256 devices in a mesh: px: 16 (over z_lo, y, core), py: 16 (over x, z_hi).
Axes of the slice: x: 4, y: 4, z: 8 (z_hi: 4, z_lo: 2; z = z_hi * 2 + z_lo), core: 2. Of those that a mesh axis runs over, the one named last changes fastest.
Arguments:
- base_flow: bfloat16 [3, 512, 384, 256], P(None, 'px', 'py'), may hold values from -3 to 3
- adjoint_start: float32 [3, 512, 384, 256], P(None, 'px', 'py'), may hold values from -2 to 3
- source: bfloat16 [3, 512, 384, 256], P(None, 'px', 'py'), may hold values from -6 to 6
- solid_mask: int32 [512, 384, 256], P('px', 'py'), may hold values 0 or 1
- outlet_ids: int32 [512, 384], P('px', 'py'), may hold values from 0 to 8
- resist: float32 [8, 8], replicated, may hold values from 5 to 20
- tile_owner: int32 [65536, 1], P(('px', 'py')), may hold values from 0 to 255; in each aligned block of 256 rows (0 to 255, 256 to 511, ...) at most 2 rows name the same one
- tile_slot: int32 [65536], P(('px', 'py')), may hold values from 0 to 31
- tile_column: int32 [65536], P(('px', 'py')), may hold values from 0 to 1535
- control_basis: float32 [8192, 128], P(('px', 'py')), may hold values from -0.0390625 to 0.0390625
Outputs:
- adjoint: float32 [3, 512, 384, 256], P(None, 'px', 'py')
- control_grad: float32 [8192], P(('px', 'py'))
The draws below stay inside these ranges and needn't reach their ends.
Inputs may be any that keep to these rules, and one draw needn't show every extreme that they name: `tile_owner`: among the tiles of one device, at most 2 share an owner.
All inputs are finite; a program needn't handle non-finite values. No bound on the sum of `solid_mask` on one device may be relied on, other than what follows from the above.
Results may differ from the reference program's by a relative error of at most 0.00035.
Values may be sent and summed in bfloat16 or wider, within the bound.
A program may use at most 64 MiB of HBM per device.

```python
import math
import jax
import jax.numpy as jnp
import numpy as np
from jax import lax

NX = 512
NY = 384
NZ = 256
SEG = 128
OUTLETS = 8
ITERS = 1
CTRL_DEV = 32
TILES_DEV = 256
CX = 32
CY = 24
CONTROLS = 8192
TILES = 65536
CAP = 2
N_PX = 16
N_PY = 16
DEVICES = 256


def draw_adjoint_start(key, part):
    key = jax.random.fold_in(key, 7)
    noise = jnp.clip(0.5 * jax.random.normal(key, (3, NX, NY, NZ), jnp.float32), -1.5, 1.5)
    lift = 1.0
    offset = jnp.where(jnp.arange(3) == 2, lift, 0.0).astype(jnp.float32)
    return noise + offset[:, None, None, None]


def plant(result, rng, smallest, top_value):
    index_at = [jax.random.randint(jax.random.fold_in(rng, axis), (), 0, length) for axis, length in enumerate(result.shape)]
    longest = result.shape.index(max(result.shape))
    beside = index_at[:longest] + [(index_at[longest] + 1) % result.shape[longest]] + index_at[longest + 1:]
    return result.at[tuple(index_at)].set(smallest).at[tuple(beside)].set(top_value)


def shard_levels(own_key, shape, cuts, least, largest):
    def one(axis_at, shards_of):
        heights = jax.random.uniform(jax.random.fold_in(jax.random.fold_in(own_key, 6), axis_at), (shards_of,), jnp.float32, least / len(cuts), largest / len(cuts))
        return jnp.repeat(jnp.exp(heights), shape[axis_at] // shards_of).reshape((-1,) + (1,) * (len(shape) - axis_at - 1))

    loudness = one(*cuts[0])
    for cut in cuts[1:]:
        loudness = loudness * one(*cut)
    return loudness


def routed_block(key, own, number, rows, number_of, top, most, skew):
    ranking = jax.random.permutation(key, number_of)
    packed, common = shares(number_of, rows * top, most, skew, True), shares(number_of, rows * top, most, skew, False)
    places = jnp.arange(number_of)

    def named(tallies, offset_by):
        used = int((tallies > 0).sum())
        fixed = max(1, used // 4)
        moved = fixed + (places - fixed + offset_by * (used - fixed)) % max(1, number_of - fixed)
        return jnp.zeros((number_of,), jnp.int32).at[ranking[jnp.where(places < fixed, places, moved)]].set(jnp.asarray(tallies, jnp.int32))

    tallies = jnp.where(number % 4 == 0, named(packed, number // 4), named(common, number - number // 4 - 1))
    mixed = jax.random.permutation(jax.random.fold_in(own, 3), number_of)
    source_of, receiver = mixed[0:number_of // 2 * 2:2], mixed[1:number_of // 2 * 2:2]
    slack = jnp.minimum(tallies[source_of] - 1, most - tallies[receiver]) // 2
    slack = jnp.where((source_of == ranking[0]) | (receiver == ranking[0]) | (tallies[receiver] == 0), 0, jnp.maximum(slack, 0))
    moved = jax.random.randint(jax.random.fold_in(own, 4), (number_of // 2,), 0, 1 << 20) % (slack + 1)
    tallies = tallies.at[source_of].add(-moved).at[receiver].add(moved)
    items = jnp.searchsorted(jnp.cumsum(tallies), jnp.arange(rows * top), side="right").astype(jnp.int32)
    listing = items.reshape(top, rows).T
    listing = listing[jax.random.permutation(jax.random.fold_in(own, 1), rows)]
    offset_by = jax.random.randint(jax.random.fold_in(own, 2), (rows, 1), 0, top)
    return jnp.take_along_axis(listing, (jnp.arange(top)[None, :] + offset_by) % top, axis=1)


def shares(number_of, total, limit, slope, full):
    weights = [(1 << 20) // math.isqrt(standing ** slope) + 1 for standing in range(1, number_of + 1)]
    largest = limit if full else min(limit, max(-(-total // number_of), total * weights[0] // sum(weights)))
    least = 1 if total - largest >= number_of - 1 else 0
    holding, rest = [largest] + [least] * (number_of - 1), total - largest - least * (number_of - 1)
    while rest > 0:
        candidates = [i for i in range(1, number_of) if holding[i] < largest] or [i for i in range(1, number_of) if holding[i] < limit]
        whole, budget = sum([weights[i] for i in candidates]), rest
        for i in candidates:
            more = min(limit - holding[i], max(1, budget * weights[i] // whole), rest)
            holding[i] = holding[i] + more
            rest = rest - more
    return np.array(holding)


def bell_draw(own_key, shape, scale, bound, shards=(), held_as=jnp.bfloat16):
    result = scale * jax.random.normal(own_key, shape, jnp.float32)
    if shards:
        result = result * shard_levels(own_key, shape, shards, -0.22, 0.18)
    return jnp.clip(result, -bound, bound).astype(held_as)


def setup_inputs(seed: int = 0) -> dict:
    arg_keys = jax.random.split(jax.random.key(seed), 11)
    base_flow = bell_draw(arg_keys[0], (3, NX, NY, NZ), 0.5, 3.0, ((1, 16), (2, 16)))
    adjoint_start = draw_adjoint_start(jax.random.fold_in(arg_keys[10], 71), 0)
    source = bell_draw(arg_keys[2], (3, NX, NY, NZ), 1.0, 6.0, ((1, 16), (2, 16)))
    solid_mask = plant((jax.random.randint(arg_keys[3], (NX, NY, NZ), 0, 4) < 1).astype(jnp.int32), jax.random.fold_in(arg_keys[3], 1), 0, 1)
    outlet_ids = plant(jax.random.randint(arg_keys[4], (NX, NY), 0, OUTLETS + 1), jax.random.fold_in(arg_keys[4], 1), 0, OUTLETS).astype(jnp.int32)
    resist = jnp.clip(jax.random.uniform(arg_keys[5], (OUTLETS, OUTLETS), jnp.float32, 5.0, 20.0), 5.0, 20.0)
    tile_owner_keys = jax.random.split(jax.random.fold_in(arg_keys[6], 1), TILES // TILES_DEV)
    tile_owner_turns = jax.random.permutation(jax.random.fold_in(arg_keys[6], 3), TILES // TILES_DEV)
    tile_owner = jax.vmap(lambda own, number: routed_block(jax.random.fold_in(arg_keys[6], 2), own, number, TILES_DEV, DEVICES, 1, CAP, 2))(tile_owner_keys, tile_owner_turns).reshape((TILES, 1))
    tile_slot = plant(jax.random.randint(arg_keys[7], (TILES,), 0, CTRL_DEV), jax.random.fold_in(arg_keys[7], 1), 0, CTRL_DEV - 1).astype(jnp.int32)
    tile_column = plant(jax.random.randint(arg_keys[8], (TILES,), 0, CX * CY * NZ // SEG), jax.random.fold_in(arg_keys[8], 1), 0, (CX * CY * NZ // SEG) - 1).astype(jnp.int32)
    control_basis = bell_draw(arg_keys[9], (CONTROLS, SEG), (25 * SEG * TILES_DEV // CTRL_DEV) ** -0.5, 0.0390625, ((0, 256),), jnp.float32)
    return dict(base_flow=base_flow, adjoint_start=adjoint_start, source=source, solid_mask=solid_mask, outlet_ids=outlet_ids, resist=resist, tile_owner=tile_owner, tile_slot=tile_slot, tile_column=tile_column, control_basis=control_basis)


DT = 0.1
NU = 0.5
ALPHA = 5.0

def shifted(padded, axis_num, offset):
    window = [slice(1, -1), slice(1, -1), slice(1, -1)]
    extent = padded.shape[padded.ndim - 3 + axis_num]
    window[axis_num] = slice(1 + offset, extent - 1 + offset)
    return padded[(slice(None),) * (padded.ndim - 3) + tuple(window)]

def central(padded, axis_num):
    return 0.5 * (shifted(padded, axis_num, 1) - shifted(padded, axis_num, -1))

def laplace(padded):
    total = -6.0 * shifted(padded, 0, 0)
    for axis_num in range(3):
        total = total + shifted(padded, axis_num, 1) + shifted(padded, axis_num, -1)
    return total

def zero_pad(field):
    return jnp.pad(field, [(0, 0)] * (field.ndim - 3) + [(1, 1)] * 3)

def cosine_table(count):
    order = jnp.arange(count).astype(jnp.float32)
    modes = order[:, None]
    points = order[None, :]
    weights = jnp.where(modes == 0.0, math.sqrt(1.0 / count), math.sqrt(2.0 / count))
    return weights * jnp.cos(jnp.pi * (points + 0.5) * modes / count)

def eigen_values(count):
    order = jnp.arange(count).astype(jnp.float32)
    return 2.0 * jnp.cos(jnp.pi * order / count) - 2.0

def solve_pressure(div):
    high = lax.Precision.HIGHEST
    table_rows = cosine_table(NX)
    table_cols = cosine_table(NY)
    table_depth = cosine_table(NZ)
    coeffs = jnp.einsum('ax,xyz->ayz', table_rows, div, precision=high)
    coeffs = jnp.einsum('by,ayz->abz', table_cols, coeffs, precision=high)
    coeffs = jnp.einsum('cz,abz->abc', table_depth, coeffs, precision=high)
    lam = eigen_values(NX)[:, None, None] + eigen_values(NY)[None, :, None] + eigen_values(NZ)[None, None, :]
    anchor = (jnp.arange(NX)[:, None, None] == 0) & (jnp.arange(NY)[None, :, None] == 0) & (jnp.arange(NZ)[None, None, :] == 0)
    coeffs = jnp.where(anchor, jnp.float32(0.0), coeffs / jnp.where(anchor, jnp.float32(-1.0), lam))
    field = jnp.einsum('ax,abc->xbc', table_rows, coeffs, precision=high)
    field = jnp.einsum('by,xbc->xyc', table_cols, field, precision=high)
    return jnp.einsum('cz,xyc->xyz', table_depth, field, precision=high)

def reference(base_flow, adjoint_start, source, solid_mask, outlet_ids, resist, tile_owner, tile_slot, tile_column, control_basis):
    flow = base_flow.astype(jnp.float32)
    forcing = source.astype(jnp.float32)
    flow_pad = zero_pad(flow)
    damping = 1.0 + DT * ALPHA * solid_mask.astype(jnp.float32)
    outlet_onehot = (outlet_ids[None] == jnp.arange(OUTLETS)[:, None, None]).astype(jnp.float32)
    velocity = adjoint_start
    for sweep in range(ITERS):
        padded = zero_pad(velocity)
        convect = flow[0][None] * central(padded, 0) + flow[1][None] * central(padded, 1) + flow[2][None] * central(padded, 2)
        transpose_term = jnp.stack([velocity[0] * central(flow_pad[0], target) + velocity[1] * central(flow_pad[1], target) + velocity[2] * central(flow_pad[2], target) for target in range(3)])
        predicted = (velocity + DT * (convect - transpose_term + NU * laplace(padded) + forcing)) / damping[None]
        flux = lax.optimization_barrier(jnp.sum(outlet_onehot * predicted[2, :, :, -1][None], axis=(1, 2))) / (NX * NY)
        press = jnp.dot(resist, flux, precision=lax.Precision.HIGHEST)
        predicted = predicted.at[2, :, :, -1].add(-DT * lax.optimization_barrier(jnp.sum(outlet_onehot * press[:, None, None], axis=0)))
        wall_pad = zero_pad(predicted)
        div = central(wall_pad[0], 0) + central(wall_pad[1], 1) + central(wall_pad[2], 2)
        pressure = solve_pressure(div)
        pressure_pad = jnp.pad(pressure, 1, mode='edge')
        velocity = predicted - jnp.stack([central(pressure_pad, target) for target in range(3)])
    sigma = -ALPHA * lax.optimization_barrier(jnp.sum(flow * velocity, axis=0))
    blocks = sigma.reshape(N_PX, CX, N_PY, CY, NZ // SEG, SEG).transpose(0, 2, 1, 3, 4, 5)
    blocks = blocks.reshape(N_PX * N_PY, CX * CY * (NZ // SEG), SEG)
    device = (jnp.arange(TILES) // TILES_DEV).astype(jnp.int32)
    rows = blocks[device, tile_column]
    control = (tile_owner[:, 0] * CTRL_DEV + tile_slot).astype(jnp.int32)
    contrib = lax.optimization_barrier(jnp.sum(rows * control_basis[control], axis=-1))
    grad = jax.ops.segment_sum(contrib, control, num_segments=CONTROLS)
    return (velocity, grad)
```

```python
import functools
import math

import jax
import jax.numpy as jnp
import numpy as np
from jax import lax
from jax.experimental import pallas as pl
from jax.experimental.pallas import tpu as pltpu
from jax.sharding import PartitionSpec as P

SEG = 128
OUTLETS = 8
DT = 0.1
NU = 0.5
ALPHA = 5.0
HALF = 128
MESH = pl.DeviceIdType.MESH
F32 = jnp.float32
BF16 = jnp.bfloat16


def table_np(count):
    order = np.arange(count).astype(np.float32)
    modes = order[:, None]
    points = order[None, :]
    weights = np.where(modes == 0.0, math.sqrt(1.0 / count), math.sqrt(2.0 / count)).astype(np.float32)
    angle = np.float32(np.pi) * (points + np.float32(0.5)) * modes / np.float32(count)
    return (weights * np.cos(angle.astype(np.float32))).astype(np.float32)


def eigen_np(count):
    order = np.arange(count).astype(np.float32)
    angle = (np.float32(np.pi) * order / np.float32(count)).astype(np.float32)
    return (np.float32(2.0) * np.cos(angle) - np.float32(2.0)).astype(np.float32)


def split_np(table, count):
    parts = []
    for _ in range(count):
        parts.append(table.astype(jnp.bfloat16))
        table = table - parts[-1].astype(np.float32)
    return tuple(parts)


def split(value, count):
    parts = []
    for _ in range(count):
        parts.append(value.astype(BF16))
        value = value - parts[-1].astype(F32)
    return tuple(parts)


def dot_parts(a_parts, b_parts, contract):
    dims = ((contract[0], contract[1]), ((), ()))
    dot = functools.partial(lax.dot_general, dimension_numbers=dims, preferred_element_type=F32)
    total = None
    for order in range(len(a_parts) - 1, -1, -1):
        for i in range(order + 1):
            term = dot(a_parts[i], b_parts[order - i])
            total = term if total is None else total + term
    return total


def swap_groups(tiles):
    lane = lax.broadcasted_iota(jnp.int32, tiles[0].shape, 1)
    odd = (lane // 32) % 2 == 1
    far = lane >= 64
    t0, t1, t2, t3 = tiles
    a0 = jnp.where(odd, pltpu.roll(t1, 32, 1), t0)
    a1 = jnp.where(odd, t1, pltpu.roll(t0, 96, 1))
    a2 = jnp.where(odd, pltpu.roll(t3, 32, 1), t2)
    a3 = jnp.where(odd, t3, pltpu.roll(t2, 96, 1))
    return (
        jnp.where(far, pltpu.roll(a2, 64, 1), a0),
        jnp.where(far, pltpu.roll(a3, 64, 1), a1),
        jnp.where(far, a2, pltpu.roll(a0, 64, 1)),
        jnp.where(far, a3, pltpu.roll(a1, 64, 1)),
    )


def z_shift(field, edge_low, edge_high):
    depth = field.shape[1]
    lane = lax.broadcasted_iota(jnp.int32, field.shape, 1)
    below = jnp.where(lane == 0, edge_low, pltpu.roll(field, 1, 1))
    above = jnp.where(lane == depth - 1, edge_high, pltpu.roll(field, depth - 1, 1))
    return below, above


def main_kernel(
    dims,
    v_hbm, u_hbm, s_hbm, m_hbm, ids, resb, tz_hbm, tx_hbm, tt_hbm, mu, muo,
    w_out, q_out,
    vp, up, ub, sb, mk, w0, w1, w2, snd_y, rcv_y, wy_snd, wy_rcv, fsum, fr1, fr2,
    div, msg, got, got2, cols, tau, kap, owner_inv, owner_phi,
    isnd, ircv, jsnd, jrcv, back, qp, qy_snd, qy_rcv, tz, tx, tt,
    load_sem, x_send, x_recv, y_send, y_recv, f_send, f_recv, a_send, a_recv, i_send, i_recv, out_sem,
):
    npx, npy, nxl, nyl, nz = dims
    nx = npx * nxl
    kzl = nz // npx
    kown = kzl // npy
    halves = nz // HALF
    me_x = lax.axis_index("px")
    me_y = lax.axis_index("py")
    right_x, left_x = lax.rem(me_x + 1, npx), lax.rem(me_x + npx - 1, npx)
    right_y, left_y = lax.rem(me_y + 1, npy), lax.rem(me_y + npy - 1, npy)
    first_x, last_x = me_x == 0, me_x == npx - 1
    first_y, last_y = me_y == 0, me_y == npy - 1
    top = 8 + nyl

    loads = []
    for c in range(3):
        for h in range(halves):
            loads.append(
                pltpu.make_async_copy(
                    v_hbm.at[c, :, :, pl.ds(h * HALF, HALF)],
                    vp.at[c, h, pl.ds(1, nxl), pl.ds(8, nyl), :],
                    load_sem.at[c * halves + h],
                )
            )
    base = 3 * halves
    load_u = pltpu.make_async_copy(u_hbm, ub, load_sem.at[base])
    load_s = pltpu.make_async_copy(s_hbm, sb, load_sem.at[base + 1])
    load_m = pltpu.make_async_copy(m_hbm, mk, load_sem.at[base + 2])
    hbm_tables = (tz_hbm, tx_hbm, tt_hbm)
    vmem_tables = (tz, tx, tt)
    load_t = [
        pltpu.make_async_copy(a, b, load_sem.at[base + 3 + n]) for n, (a, b) in enumerate(zip(hbm_tables, vmem_tables))
    ]
    load_u.start()
    for copy in loads:
        copy.start()
    load_s.start()
    load_m.start()
    for copy in load_t:
        copy.start()

    barrier = pltpu.get_barrier_semaphore()

    def greet_x(r, carry):
        pl.semaphore_signal(barrier, inc=1, device_id=(lax.rem(me_x + r, npx), me_y), device_id_type=MESH)
        return carry

    def greet_y(r, carry):
        pl.semaphore_signal(barrier, inc=1, device_id=(me_x, lax.rem(me_y + r, npy)), device_id_type=MESH)
        return carry

    lax.fori_loop(1, npx, greet_x, 0)
    lax.fori_loop(1, npy, greet_y, 0)

    load_u.wait()

    def widen(i, carry):
        for a in range(3):
            pair = ub[a, pl.ds(pl.multiple_of(i * 2 * nyl, 2 * nyl), 2 * nyl), :].astype(F32)
            for s in range(2):
                for h in range(halves):
                    up[a, h, 1 + 2 * i + s, 8:top, :] = pair[s * nyl:(s + 1) * nyl, h * HALF:(h + 1) * HALF]
        return carry

    lax.fori_loop(0, nxl // 2, widen, 0)
    for copy in loads:
        copy.wait()

    pl.semaphore_wait(barrier, npx - 1 + npy - 1)

    def remote(src, dst, send, recv, target):
        return pltpu.make_async_remote_copy(
            src_ref=src, dst_ref=dst, send_sem=send, recv_sem=recv, device_id=target, device_id_type=MESH
        )

    def x_pair(field, at, number):
        return (
            remote(at(field, nxl), at(field, 0), x_send.at[number], x_recv.at[number], (right_x, me_y)),
            remote(at(field, 1), at(field, nxl + 1), x_send.at[number + 1], x_recv.at[number + 1], (left_x, me_y)),
        )

    def at_plane(field, x):
        return field.at[:, :, x, pl.ds(8, nyl), :]

    def y_pair(send, recv, number):
        return (
            remote(send.at[0], recv.at[0], y_send.at[number], y_recv.at[number], (me_x, right_y)),
            remote(send.at[1], recv.at[1], y_send.at[number + 1], y_recv.at[number + 1], (me_x, left_y)),
        )

    for c in range(3):
        for h in range(halves):
            snd_y[0, c, h] = vp[c, h, 1:nxl + 1, top - 1, :].astype(BF16)
            snd_y[1, c, h] = vp[c, h, 1:nxl + 1, 8, :].astype(BF16)
            snd_y[0, 3 + c, h] = up[c, h, 1:nxl + 1, top - 1, :].astype(BF16)
            snd_y[1, 3 + c, h] = up[c, h, 1:nxl + 1, 8, :].astype(BF16)
    halo = y_pair(snd_y, rcv_y, 0) + x_pair(vp, at_plane, 0) + x_pair(up, at_plane, 2)
    for copy in halo:
        copy.start()

    def reduce_cell(c, g, right):
        inv = 1.0 / (c + right + g)
        return inv, c * inv

    def table_cell(i, carry):
        c, g = carry
        right = jnp.where((i == nyl - 1) & last_y, 0.0, 1.0)
        inv, k = reduce_cell(c, g, right)
        tau[i] = inv
        kap[i] = k
        return k, mu[...] + g * inv

    lax.fori_loop(1, nyl, table_cell, (jnp.ones_like(mu[...]), mu[...]))

    def owner_cell(i, carry):
        c, g, ground = carry
        inv, k = reduce_cell(c, g, 1.0)
        return k, muo[...] + g * inv, ground + k * g

    one = jnp.ones_like(muo[...])
    c, g, ground = lax.fori_loop(1, nyl - 1, owner_cell, (one, muo[...], jnp.zeros_like(one)))
    inv, link = reduce_cell(c, g, 1.0)
    from_left = g * inv
    end_ground = muo[...] + from_left + (ground + c * (g / (c + g)))
    ground = ground + link * g
    held = muo[...] + ground
    for b in range(npy - 1):
        inv = 1.0 / (link + held)
        phi = link * inv
        owner_inv[b] = inv
        owner_phi[b] = phi
        nxt = end_ground if b == npy - 2 else muo[...] + ground + from_left
        held = nxt + phi * held
    positive = held > 0.0
    owner_inv[npy - 1] = jnp.where(positive, 1.0 / jnp.where(positive, held, 1.0), 0.0)

    load_s.wait()
    load_m.wait()
    for copy in halo:
        copy.wait()

    for c in range(3):
        for h in range(halves):
            low_v, low_u = rcv_y[0, c, h].astype(F32), rcv_y[0, 3 + c, h].astype(F32)
            high_v, high_u = rcv_y[1, c, h].astype(F32), rcv_y[1, 3 + c, h].astype(F32)
            vp[c, h, 1:nxl + 1, 7, :] = jnp.where(first_y, 0.0, low_v)
            up[c, h, 1:nxl + 1, 7, :] = jnp.where(first_y, 0.0, low_u)
            vp[c, h, 1:nxl + 1, top, :] = jnp.where(last_y, 0.0, high_v)
            up[c, h, 1:nxl + 1, top, :] = jnp.where(last_y, 0.0, high_u)
    edge = jnp.zeros((nyl, HALF), F32)

    @pl.when(first_x)
    def _():
        for c in range(3):
            for h in range(halves):
                vp[c, h, 0, 8:top, :] = edge
                up[c, h, 0, 8:top, :] = edge

    @pl.when(last_x)
    def _():
        for c in range(3):
            for h in range(halves):
                vp[c, h, nxl + 1, 8:top, :] = edge
                up[c, h, nxl + 1, 8:top, :] = edge

    def whole(field, c, x):
        return jnp.concatenate([field[c, h, x] for h in range(halves)], axis=1)

    def middle(field, c, x):
        return jnp.concatenate([field[c, h, x, 8:top, :] for h in range(halves)], axis=1)

    def predict(i, carry):
        rows = pl.ds(pl.multiple_of(i * 2 * nyl, 2 * nyl), 2 * nyl)
        forcing = [sb[b, rows, :].astype(F32) for b in range(3)]
        for s in range(2):
            x = 2 * i + s
            scale = 1.0 / (1.0 + (DT * ALPHA) * mk[x].astype(F32))
            u, v = [], []
            slopes = [None] * 3
            for a in range(3):
                tall = whole(up, a, x + 1)
                u.append(tall[8:top])
                v.append(middle(vp, a, x + 1))
                below, above = z_shift(u[a], 0.0, 0.0)
                diffs = (
                    middle(up, a, x + 2) - middle(up, a, x),
                    tall[9:top + 1] - tall[7:top - 1],
                    above - below,
                )
                for b in range(3):
                    term = v[a] * diffs[b]
                    slopes[b] = term if slopes[b] is None else slopes[b] + term
            for b in range(3):
                tall = whole(vp, b, x + 1)
                xm, xp = middle(vp, b, x), middle(vp, b, x + 2)
                ym, yp = tall[7:top - 1], tall[9:top + 1]
                zm, zp = z_shift(v[b], 0.0, 0.0)
                convect = u[0] * (xp - xm) + u[1] * (yp - ym) + u[2] * (zp - zm)
                lap = (xp + xm) + (yp + ym) + (zp + zm) - 6.0 * v[b]
                change = 0.5 * (convect - slopes[b]) + NU * lap + forcing[b][s * nyl:(s + 1) * nyl]
                w = (v[b] + DT * change) * scale
                for h in range(halves):
                    part = w[:, h * HALF:(h + 1) * HALF]
                    if b == 0:
                        w0[h, x + 1] = part
                    elif b == 1:
                        w1[h, x, 8:top, :] = part
                    else:
                        w2[h, x] = part
        return carry

    lax.fori_loop(0, nxl // 2, predict, 0)

    for h in range(halves):
        wy_snd[0, h] = w1[h, :, top - 1, :]
        wy_snd[1, h] = w1[h, :, 8, :]
    halo = y_pair(wy_snd, wy_rcv, 2) + x_pair(w0, lambda field, x: field.at[:, x], 4)
    for copy in halo:
        copy.start()

    lane = lax.broadcasted_iota(jnp.int32, (nyl, HALF), 1)

    def flux_plane(x, carry):
        face = jnp.where(lane == HALF - 1, w2[halves - 1, x], 0.0)
        which = jnp.broadcast_to(ids[x], (nyl, HALF))
        return tuple(total + jnp.where(which == k, face, 0.0) for k, total in enumerate(carry))

    zero = jnp.zeros((nyl, HALF), F32)
    totals = lax.fori_loop(0, nxl, flux_plane, (zero,) * OUTLETS)
    fsum[0] = jnp.concatenate([jnp.sum(t, axis=0, keepdims=True) for t in totals], axis=0)

    def flux_x(r):
        return remote(fsum.at[0], fr1.at[me_x], f_send.at[r], f_recv.at[r], (lax.rem(me_x + r, npx), me_y))

    def flux_y(r):
        return remote(fsum.at[1], fr2.at[me_y], f_send.at[npx + r], f_recv.at[npx + r], (me_x, lax.rem(me_y + r, npy)))

    def run(first, last, action):
        def body(r, carry):
            action(r)
            return carry

        lax.fori_loop(first, last, body, 0)

    run(1, npx, lambda r: flux_x(r).start())
    fr1[me_x] = fsum[0]

    for copy in halo:
        copy.wait()
    for h in range(halves):
        w1[h, :, 7, :] = jnp.where(first_y, 0.0, wy_rcv[0, h])
        w1[h, :, top, :] = jnp.where(last_y, 0.0, wy_rcv[1, h])

    @pl.when(first_x)
    def _():
        for h in range(halves):
            w0[h, 0] = edge

    @pl.when(last_x)
    def _():
        for h in range(halves):
            w0[h, nxl + 1] = edge

    def diverge(x, carry):
        deep = jnp.concatenate([w2[h, x] for h in range(halves)], axis=1)
        below, above = z_shift(deep, 0.0, 0.0)
        for h in range(halves):
            cut = slice(h * HALF, (h + 1) * HALF)
            tall = w1[h, x]
            total = (w0[h, x + 2] - w0[h, x]) + (tall[9:top + 1] - tall[7:top - 1]) + (above - below)[:, cut]
            div[h, pl.ds(x, nyl, stride=nxl), :] = 0.5 * total
        return carry

    lax.fori_loop(0, nxl // 2, diverge, 0)
    run(1, npx, lambda r: flux_x(r).wait())
    fsum[1] = jnp.sum(fr1[...], axis=0)
    run(1, npy, lambda r: flux_y(r).start())
    fr2[me_y] = fsum[1]
    lax.fori_loop(nxl // 2, nxl, diverge, 0)
    run(1, npy, lambda r: flux_y(r).wait())
    flux = jnp.sum(fr2[...], axis=0) * (1.0 / (nx * npy * nyl))
    press = [jnp.sum(resb[k] * flux, axis=0, keepdims=True) for k in range(OUTLETS)]

    def lower(x, carry):
        which = jnp.broadcast_to(ids[x], (nyl, HALF))
        drop = jnp.zeros((nyl, HALF), F32)
        for k in range(OUTLETS):
            drop = jnp.where(which == k, jnp.broadcast_to(press[k], (nyl, HALF)), drop)
        drop = DT * jnp.where(lane == HALF - 1, drop, 0.0)
        w2[halves - 1, x] = w2[halves - 1, x] - drop
        here = pl.ds(x, nyl, stride=nxl)
        div[halves - 1, here, :] = div[halves - 1, here, :] - 0.5 * pltpu.roll(drop, HALF - 1, 1)
        return carry

    lax.fori_loop(0, nxl, lower, 0)

    outs = []
    for h in range(halves):
        cut = pl.ds(h * HALF, HALF)
        outs.append(pltpu.make_async_copy(w0.at[h, pl.ds(1, nxl)], w_out.at[0, :, :, cut], out_sem.at[3 * h]))
        outs.append(
            pltpu.make_async_copy(w1.at[h, :, pl.ds(8, nyl), :], w_out.at[1, :, :, cut], out_sem.at[3 * h + 1])
        )
        outs.append(pltpu.make_async_copy(w2.at[h], w_out.at[2, :, :, cut], out_sem.at[3 * h + 2]))
    for copy in outs:
        copy.start()

    for copy in load_t:
        copy.wait()
    cells = nxl * nyl

    def depth_chunk(j, carry):
        here = pl.ds(pl.multiple_of(j * 256, 256), 256)
        value = jnp.concatenate([div[h, here, :] for h in range(halves)], axis=1)
        out = dot_parts((tz[0], tz[1]), split(value, 2), ((1,), (1,)))
        for p in range(npx):
            msg[p, :, here] = out[p * kzl:(p + 1) * kzl]
        return carry

    lax.fori_loop(0, cells // 256, depth_chunk, 0)

    def forth(r):
        p = lax.rem(me_x + r, npx)
        return remote(msg.at[p], got.at[me_x], a_send.at[r], a_recv.at[r], (p, me_y))

    run(1, npx, lambda r: forth(r).start())
    got[me_x] = msg[me_x]
    run(1, npx, lambda r: forth(r).wait())

    groups = nyl // 4
    wides = npx // 4

    def gather(j, carry):
        yg = j // wides
        sg = lax.rem(j, wides)
        lanes = pl.ds(pl.multiple_of(yg * HALF, HALF), HALF)
        out = swap_groups([got[4 * sg + a, :, lanes] for a in range(4)])
        for b in range(4):
            rows = pl.ds(pl.multiple_of((4 * yg + b) * kzl, kzl), kzl)
            cols[rows, pl.ds(pl.multiple_of(sg * HALF, HALF), HALF)] = out[b]
        return carry

    lax.fori_loop(0, groups * wides, gather, 0)

    total_rows = nyl * kzl
    chunk = 128

    def x_transform(parts):
        def body(j, carry):
            rows = pl.ds(pl.multiple_of(j * chunk, chunk), chunk)
            cols[rows, :] = dot_parts(split(cols[rows, :], len(parts)), parts, ((1,), (0,)))
            return carry

        lax.fori_loop(0, total_rows // chunk, body, 0)

    x_transform((tt[0], tt[1]))

    def row_of(i):
        return pl.ds(pl.multiple_of(i * kzl, kzl), kzl)

    def down(i, carry):
        r, ends = carry
        ends = ends + kap[i] * r
        nxt = cols[row_of(i + 1), :] + tau[i] * r
        cols[row_of(i + 1), :] = nxt
        return nxt, ends

    r, ends = lax.fori_loop(1, nyl - 1, down, (cols[row_of(1), :], cols[row_of(0), :]))
    ends = ends + kap[nyl - 1] * r
    over = tau[nyl - 1] * r
    for j in range(npy):
        isnd[j, 0:kown, :] = ends[j * kown:(j + 1) * kown]
        isnd[j, kown:2 * kown, :] = over[j * kown:(j + 1) * kown]

    def collect(r):
        j = lax.rem(me_y + r, npy)
        return remote(isnd.at[j], ircv.at[me_y], i_send.at[r], i_recv.at[r], (me_x, j))

    run(1, npy, lambda r: collect(r).start())
    ircv[me_y] = isnd[me_y]
    run(1, npy, lambda r: collect(r).wait())

    rho = []
    for b in range(npy):
        value = ircv[b, 0:kown, :]
        if b > 0:
            value = value + ircv[b - 1, kown:2 * kown, :]
        rho.append(value)
    depth_mode = lax.broadcasted_iota(jnp.int32, (kown, nx), 0) + me_x * kzl + me_y * kown
    row_mode = lax.broadcasted_iota(jnp.int32, (kown, nx), 1)
    mean = sum(rho[1:], rho[0]) * (1.0 / (npy * nyl))
    mean = jnp.where((depth_mode == 0) & (row_mode == 0), mean, 0.0)
    half_sum = (nyl - 1) / 2.0
    for b in range(npy):
        weight = 1.0 + (0.0 if b == 0 else half_sum) + (2.0 * half_sum if b == npy - 1 else half_sum)
        rho[b] = rho[b] - weight * mean
    for b in range(npy - 1):
        rho[b + 1] = rho[b + 1] + owner_phi[b] * rho[b]
    value = -owner_inv[npy - 1] * rho[npy - 1]
    jsnd[npy - 1, 0:kown, :] = value
    jsnd[npy - 1, kown:2 * kown, :] = jnp.zeros_like(value)
    jsnd[npy - 1, 2 * kown:3 * kown, :] = mean
    for b in range(npy - 2, -1, -1):
        jsnd[b, kown:2 * kown, :] = value
        value = owner_phi[b] * value - owner_inv[b] * rho[b]
        jsnd[b, 0:kown, :] = value
        jsnd[b, 2 * kown:3 * kown, :] = mean

    def hand_back(r):
        j = lax.rem(me_y + r, npy)
        return remote(jsnd.at[j], jrcv.at[me_y], i_send.at[npy + r], i_recv.at[npy + r], (me_x, j))

    run(1, npy, lambda r: hand_back(r).start())
    jrcv[me_y] = jsnd[me_y]
    run(1, npy, lambda r: hand_back(r).wait())
    for j in range(npy):
        for part in range(3):
            back[part, j * kown:(j + 1) * kown, :] = jrcv[j, part * kown:(part + 1) * kown, :]
    first_value, mean_rows = back[0], back[2]

    def up_again(n, q):
        i = nyl - 1 - n
        share = 0.5 * (i + 1).astype(F32)
        q = tau[i] * (q - cols[row_of(i), :] + mean_rows * share) + kap[i] * first_value
        cols[row_of(i), :] = q
        return q

    lax.fori_loop(0, nyl - 1, up_again, back[1])
    cols[row_of(0), :] = first_value

    x_transform((tx[0], tx[1], tx[2]))

    def scatter(j, carry):
        yg = j // wides
        sg = lax.rem(j, wides)
        lanes = pl.ds(pl.multiple_of(sg * HALF, HALF), HALF)
        tiles = []
        for b in range(4):
            rows = pl.ds(pl.multiple_of((4 * yg + b) * kzl, kzl), kzl)
            tiles.append(cols[rows, lanes])
        out = swap_groups(tiles)
        for a in range(4):
            msg[4 * sg + a, :, pl.ds(pl.multiple_of(yg * HALF, HALF), HALF)] = out[a]
        return carry

    lax.fori_loop(0, groups * wides, scatter, 0)


    def home(r):
        p = lax.rem(me_x + r, npx)
        return remote(msg.at[p], got2.at[me_x], a_send.at[npx + r], a_recv.at[npx + r], (p, me_y))

    run(1, npx, lambda r: home(r).start())
    got2[me_x] = msg[me_x]
    run(1, npx, lambda r: home(r).wait())

    per = 256 // nxl
    for j in range(cells // 256):
        value = got2[:, :, j * 256:(j + 1) * 256].reshape(nz, 256)
        out = dot_parts(split(value.T, 3), (tz[0], tz[1], tz[2]), ((1,), (0,)))
        for y in range(per):
            for h in range(halves):
                qp[h, 1:nxl + 1, 8 + j * per + y, :] = out[y * nxl:(y + 1) * nxl, h * HALF:(h + 1) * HALF]

    for h in range(halves):
        qy_snd[0, h] = qp[h, 1:nxl + 1, top - 1, :]
        qy_snd[1, h] = qp[h, 1:nxl + 1, 8, :]
    halo = y_pair(qy_snd, qy_rcv, 4) + x_pair(qp, lambda field, x: field.at[:, x, pl.ds(8, nyl), :], 6)
    for copy in halo:
        copy.start()
    for copy in halo:
        copy.wait()
    for h in range(halves):
        qp[h, 1:nxl + 1, 7, :] = jnp.where(first_y, qy_snd[1, h], qy_rcv[0, h])
        qp[h, 1:nxl + 1, top, :] = jnp.where(last_y, qy_snd[0, h], qy_rcv[1, h])

    @pl.when(first_x)
    def _():
        for h in range(halves):
            qp[h, 0, 8:top, :] = qp[h, 1, 8:top, :]

    @pl.when(last_x)
    def _():
        for h in range(halves):
            qp[h, nxl + 1, 8:top, :] = qp[h, nxl, 8:top, :]

    give = pltpu.make_async_copy(qp, q_out, out_sem.at[3 * halves])
    give.start()
    for copy in outs:
        copy.wait()
    give.wait()


def main_call(dims, v, u, s, m, ids, resb, tables, mu, muo):
    npx, npy, nxl, nyl, nz = dims
    nx = npx * nxl
    kzl = nz // npx
    kown = kzl // npy
    halves = nz // HALF
    wide = nyl + 16
    cells = nxl * nyl
    vmem = pltpu.VMEM
    anywhere = pl.BlockSpec(memory_space=pl.ANY)
    here = pl.BlockSpec(memory_space=pltpu.VMEM)
    dma = pltpu.SemaphoreType.DMA
    scratch = [
        vmem((3, halves, nxl + 2, wide, HALF), F32),
        vmem((3, halves, nxl + 2, wide, HALF), F32),
        vmem((3, cells, nz), BF16),
        vmem((3, cells, nz), BF16),
        vmem((nxl, nyl, nz), jnp.int32),
        vmem((halves, nxl + 2, nyl, HALF), F32),
        vmem((halves, nxl, wide, HALF), F32),
        vmem((halves, nxl, nyl, HALF), F32),
        vmem((2, 6, halves, nxl, HALF), BF16),
        vmem((2, 6, halves, nxl, HALF), BF16),
        vmem((2, halves, nxl, HALF), F32),
        vmem((2, halves, nxl, HALF), F32),
        vmem((2, OUTLETS, HALF), F32),
        vmem((npx, OUTLETS, HALF), F32),
        vmem((npy, OUTLETS, HALF), F32),
        vmem((halves, cells, HALF), F32),
        vmem((npx, kzl, cells), F32),
        vmem((npx, kzl, cells), F32),
        vmem((npx, kzl, cells), F32),
        vmem((nyl * kzl, nx), F32),
        vmem((nyl, kzl, nx), F32),
        vmem((nyl, kzl, nx), F32),
        vmem((npy, kown, nx), F32),
        vmem((npy, kown, nx), F32),
        vmem((npy, 2 * kown, nx), F32),
        vmem((npy, 2 * kown, nx), F32),
        vmem((npy, 3 * kown, nx), F32),
        vmem((npy, 3 * kown, nx), F32),
        vmem((3, kzl, nx), F32),
        vmem((halves, nxl + 2, wide, HALF), F32),
        vmem((2, halves, nxl, HALF), F32),
        vmem((2, halves, nxl, HALF), F32),
    ]
    scratch += [vmem(t.shape, BF16) for t in tables]
    scratch += [
        dma((3 * halves + 3 + len(tables),)),
        dma((8,)),
        dma((8,)),
        dma((6,)),
        dma((6,)),
        dma((npx + npy,)),
        dma((npx + npy,)),
        dma((2 * npx,)),
        dma((2 * npx,)),
        dma((2 * npy,)),
        dma((2 * npy,)),
        dma((3 * halves + 1,)),
    ]
    return pl.pallas_call(
        functools.partial(main_kernel, dims),
        out_shape=(
            jax.ShapeDtypeStruct((3, nxl, nyl, nz), F32),
            jax.ShapeDtypeStruct((halves, nxl + 2, wide, HALF), F32),
        ),
        in_specs=[anywhere] * 4 + [here] * 2 + [anywhere] * len(tables) + [here] * 2,
        out_specs=(anywhere, anywhere),
        scratch_shapes=scratch,
        compiler_params=pltpu.CompilerParams(
            collective_id=0, has_side_effects=True, vmem_limit_bytes=56 * 2**20
        ),
        name="project",
    )(v, u, s, m, ids, resb, *tables, mu, muo)


def final_kernel(dims, steps, w, u, qp, slots, v_out, picked, sig):
    npx, npy, nxl, nyl, nz = dims
    halves = nz // HALF
    per = nxl // steps
    step = pl.program_id(0)
    top = 8 + nyl

    def middle(x):
        return jnp.concatenate([qp[h, x, 8:top, :] for h in range(halves)], axis=1)

    for i in range(per // 2):
        pair = [u[a, i * 2 * nyl:(i + 1) * 2 * nyl, :].astype(F32) for a in range(3)]
        for s in range(2):
            n = 2 * i + s
            x = step * per + n
            tall = jnp.concatenate([qp[h, x + 1] for h in range(halves)], axis=1)
            center = tall[8:top]
            lane = lax.broadcasted_iota(jnp.int32, center.shape, 1)
            below = jnp.where(lane == 0, center, pltpu.roll(center, 1, 1))
            above = jnp.where(lane == nz - 1, center, pltpu.roll(center, nz - 1, 1))
            slopes = (middle(x + 2) - middle(x), tall[9:top + 1] - tall[7:top - 1], above - below)
            total = None
            for b in range(3):
                v = w[b, n] - 0.5 * slopes[b]
                v_out[b, n] = v
                term = pair[b][s * nyl:(s + 1) * nyl] * v
                total = term if total is None else total + term
            total = -ALPHA * total
            for h in range(halves):
                sig[h, pl.ds(pl.multiple_of(x * nyl, 8), nyl), :] = total[:, h * HALF:(h + 1) * HALF]

    @pl.when(step == steps - 1)
    def _():
        column = slots[...]
        shape = (column.shape[0], nxl * nyl)
        cell = lax.broadcasted_iota(jnp.int32, shape, 1) * halves
        dot = functools.partial(jnp.dot, preferred_element_type=F32)
        total = None
        for h in range(halves):
            chosen = (jnp.broadcast_to(column, shape) == cell + h).astype(F32).astype(BF16)
            value = sig[h]
            first = value.astype(BF16)
            rest = value - first.astype(F32)
            second = rest.astype(BF16)
            third = (rest - second.astype(F32)).astype(BF16)
            part = dot(chosen, first) + (dot(chosen, second) + dot(chosen, third))
            total = part if total is None else total + part
        picked[...] = total


def final_call(dims, w, u, qp, slots):
    npx, npy, nxl, nyl, nz = dims
    halves = nz // HALF
    steps = 8
    per = nxl // steps
    cells = nxl * nyl
    count = slots.shape[0]
    return pl.pallas_call(
        functools.partial(final_kernel, dims, steps),
        grid=(steps,),
        out_shape=(
            jax.ShapeDtypeStruct((3, nxl, nyl, nz), F32),
            jax.ShapeDtypeStruct((count, SEG), F32),
        ),
        in_specs=[
            pl.BlockSpec((3, per, nyl, nz), lambda i: (0, i, 0, 0)),
            pl.BlockSpec((3, per * nyl, nz), lambda i: (0, i, 0)),
            pl.BlockSpec(qp.shape, lambda i: (0, 0, 0, 0)),
            pl.BlockSpec(slots.shape, lambda i: (0, 0)),
        ],
        out_specs=(
            pl.BlockSpec((3, per, nyl, nz), lambda i: (0, i, 0, 0)),
            pl.BlockSpec((count, SEG), lambda i: (0, 0)),
        ),
        scratch_shapes=[pltpu.VMEM((halves, cells, HALF), F32)],
        compiler_params=pltpu.CompilerParams(vmem_limit_bytes=40 * 2**20),
        name="correct",
    )(w, u, qp, slots)


def route_kernel(npx, npy, rows, labels, rows_out, labels_out, mid_rows, mid_labels, send, recv):
    me_x = lax.axis_index("px")
    me_y = lax.axis_index("py")
    barrier = pltpu.get_barrier_semaphore()

    def loop(count, action):
        def body(r, carry):
            action(r)
            return carry

        lax.fori_loop(1, count, body, 0)

    def at_x(r):
        return (lax.rem(me_x + r, npx), me_y)

    def at_y(r):
        return (me_x, lax.rem(me_y + r, npy))

    loop(npx, lambda r: pl.semaphore_signal(barrier, inc=1, device_id=at_x(r), device_id_type=MESH))
    loop(npy, lambda r: pl.semaphore_signal(barrier, inc=1, device_id=at_y(r), device_id_type=MESH))
    pl.semaphore_wait(barrier, npx - 1 + npy - 1)

    def remote(src, dst, number, target):
        return pltpu.make_async_remote_copy(
            src_ref=src, dst_ref=dst, send_sem=send.at[number], recv_sem=recv.at[number],
            device_id=target, device_id_type=MESH,
        )

    def rows_x(r):
        return remote(rows.at[at_x(r)[0]], mid_rows.at[me_x], r, at_x(r))

    def labels_x(r):
        return remote(labels.at[at_x(r)[0]], mid_labels.at[me_x], npx + r, at_x(r))

    def rows_y(r):
        return remote(mid_rows.at[:, at_y(r)[1]], rows_out.at[me_y], 2 * npx + r, at_y(r))

    def labels_y(r):
        return remote(mid_labels.at[:, at_y(r)[1]], labels_out.at[me_y], 2 * npx + npy + r, at_y(r))

    loop(npx, lambda r: rows_x(r).start())
    loop(npx, lambda r: labels_x(r).start())
    mid_rows[me_x] = rows[me_x]
    mid_labels[me_x] = labels[me_x]
    loop(npx, lambda r: rows_x(r).wait())
    loop(npx, lambda r: labels_x(r).wait())
    loop(npy, lambda r: rows_y(r).start())
    loop(npy, lambda r: labels_y(r).start())
    rows_out[me_y] = mid_rows[:, me_y]
    labels_out[me_y] = mid_labels[:, me_y]
    loop(npy, lambda r: rows_y(r).wait())
    loop(npy, lambda r: labels_y(r).wait())


def route_call(npx, npy, rows, labels):
    here = pl.BlockSpec(memory_space=pltpu.VMEM)
    capacity = rows.shape[2]
    return pl.pallas_call(
        functools.partial(route_kernel, npx, npy),
        out_shape=(
            jax.ShapeDtypeStruct((npy, npx, capacity, SEG), F32),
            jax.ShapeDtypeStruct((npy, npx, 1, SEG), jnp.int32),
        ),
        in_specs=[here, here],
        out_specs=(here, here),
        scratch_shapes=[
            pltpu.VMEM(rows.shape, F32),
            pltpu.VMEM(labels.shape, jnp.int32),
            pltpu.SemaphoreType.DMA((2 * (npx + npy),)),
            pltpu.SemaphoreType.DMA((2 * (npx + npy),)),
        ],
        compiler_params=pltpu.CompilerParams(
            collective_id=1, has_side_effects=True, vmem_limit_bytes=24 * 2**20
        ),
        name="route",
    )(rows, labels)


def local(
    base_flow, adjoint_start, source, solid_mask, outlet_ids, resist,
    tile_owner, tile_slot, tile_column, control_basis,
):
    _, nxl, nyl, nz = adjoint_start.shape
    npx, npy = lax.axis_size("px"), lax.axis_size("py")
    dims = (npx, npy, nxl, nyl, nz)
    nx = npx * nxl
    kzl = nz // npx
    kown = kzl // npy
    devices = npx * npy
    capacity = 2

    owners = tile_owner[:, 0]
    count = owners.shape[0]
    order = jnp.arange(count, dtype=jnp.int32)
    ranks = jnp.sum(
        ((owners[:, None] == owners[None, :]) & (order[None, :] < order[:, None])).astype(jnp.int32), axis=1
    )
    place = owners * capacity + ranks
    match = place[None, :] == jnp.arange(devices * capacity, dtype=jnp.int32)[:, None]
    column_at = jnp.sum(jnp.where(match, tile_column[None, :] + 1, 0), axis=1) - 1
    label_at = jnp.sum(jnp.where(match, tile_slot[None, :] + 1, 0), axis=1) - 1
    labels = jnp.pad(label_at.reshape(npx, npy, 1, capacity), ((0, 0), (0, 0), (0, 0), (0, SEG - capacity)))

    lam_x = jnp.asarray(-eigen_np(nx))
    lam_z = jnp.asarray(-eigen_np(nz))
    at = lax.axis_index("px") * kzl
    mine = lax.dynamic_slice(lam_z, (at,), (kzl,))
    owned = lax.dynamic_slice(lam_z, (at + lax.axis_index("py") * kown,), (kown,))
    mu = lam_x[None, :] + mine[:, None]
    muo = lam_x[None, :] + owned[:, None]
    tz, tx = table_np(nz), table_np(nx)
    tables = [split_np(tz, 3), split_np(tx, 3), split_np(np.ascontiguousarray(tx.T), 2)]
    tables = [jnp.asarray(np.stack(t)) for t in tables]

    ids = outlet_ids.reshape(nxl, nyl, 1)
    resb = jnp.broadcast_to(resist[:, :, None], (OUTLETS, OUTLETS, HALF))
    flow = base_flow.reshape(3, nxl * nyl, nz)
    w, qp = main_call(
        dims, adjoint_start, flow, source.reshape(3, nxl * nyl, nz), solid_mask, ids, resb, tables, mu, muo
    )
    velocity, picked = final_call(dims, w, flow, qp, column_at[:, None])
    rows, got_labels = route_call(npx, npy, picked.reshape(npx, npy, capacity, SEG), labels)
    rows = rows.reshape(devices * capacity, SEG)
    got_labels = got_labels[:, :, 0, :capacity].reshape(devices * capacity)
    scores = jnp.dot(rows, control_basis.T, precision=lax.Precision.HIGHEST, preferred_element_type=F32)
    chosen = got_labels[:, None] == jnp.arange(control_basis.shape[0], dtype=jnp.int32)[None, :]
    grad = jnp.sum(jnp.where(chosen, scores, jnp.float32(0.0)), axis=0)
    return velocity, grad


def solution(mesh):
    in_specs = (
        P(None, "px", "py", None),
        P(None, "px", "py", None),
        P(None, "px", "py", None),
        P("px", "py", None),
        P("px", "py"),
        P(),
        P(("px", "py"), None),
        P(("px", "py")),
        P(("px", "py")),
        P(("px", "py"), None),
    )
    out_specs = (P(None, "px", "py", None), P(("px", "py")))
    return jax.shard_map(local, mesh=mesh, in_specs=in_specs, out_specs=out_specs, check_vma=False)
```

```python
import functools
import math

import jax
import jax.numpy as jnp
import numpy as np
from jax import lax
from jax.experimental import pallas as pl
from jax.experimental.pallas import tpu as pltpu
from jax.sharding import PartitionSpec as P

SEG = 128
OUTLETS = 8
DT = 0.1
NU = 0.5
ALPHA = 5.0
HALF = 128
MESH = pl.DeviceIdType.MESH
F32 = jnp.float32
BF16 = jnp.bfloat16


def table_np(count):
    order = np.arange(count).astype(np.float32)
    modes = order[:, None]
    points = order[None, :]
    weights = np.where(modes == 0.0, math.sqrt(1.0 / count), math.sqrt(2.0 / count)).astype(np.float32)
    angle = np.float32(np.pi) * (points + np.float32(0.5)) * modes / np.float32(count)
    return (weights * np.cos(angle.astype(np.float32))).astype(np.float32)


def eigen_np(count):
    order = np.arange(count).astype(np.float32)
    angle = (np.float32(np.pi) * order / np.float32(count)).astype(np.float32)
    return (np.float32(2.0) * np.cos(angle) - np.float32(2.0)).astype(np.float32)


def split_np(table, count):
    parts = []
    for _ in range(count):
        parts.append(table.astype(jnp.bfloat16))
        table = table - parts[-1].astype(np.float32)
    return tuple(parts)


def split(value, count):
    parts = []
    for _ in range(count):
        parts.append(value.astype(BF16))
        value = value - parts[-1].astype(F32)
    return tuple(parts)


def dot_parts(a_parts, b_parts, contract):
    dims = ((contract[0], contract[1]), ((), ()))
    dot = functools.partial(lax.dot_general, dimension_numbers=dims, preferred_element_type=F32)
    total = None
    for order in range(len(a_parts) - 1, -1, -1):
        for i in range(order + 1):
            term = dot(a_parts[i], b_parts[order - i])
            total = term if total is None else total + term
    return total


def swap_groups(tiles):
    lane = lax.broadcasted_iota(jnp.int32, tiles[0].shape, 1)
    odd = (lane // 32) % 2 == 1
    far = lane >= 64
    t0, t1, t2, t3 = tiles
    a0 = jnp.where(odd, pltpu.roll(t1, 32, 1), t0)
    a1 = jnp.where(odd, t1, pltpu.roll(t0, 96, 1))
    a2 = jnp.where(odd, pltpu.roll(t3, 32, 1), t2)
    a3 = jnp.where(odd, t3, pltpu.roll(t2, 96, 1))
    return (
        jnp.where(far, pltpu.roll(a2, 64, 1), a0),
        jnp.where(far, pltpu.roll(a3, 64, 1), a1),
        jnp.where(far, a2, pltpu.roll(a0, 64, 1)),
        jnp.where(far, a3, pltpu.roll(a1, 64, 1)),
    )


def z_shift(field, edge_low, edge_high):
    depth = field.shape[1]
    lane = lax.broadcasted_iota(jnp.int32, field.shape, 1)
    below = jnp.where(lane == 0, edge_low, pltpu.roll(field, 1, 1))
    above = jnp.where(lane == depth - 1, edge_high, pltpu.roll(field, depth - 1, 1))
    return below, above


def main_kernel(
    dims,
    v_hbm, u_hbm, s_hbm, m_hbm, ids, resist, owner_col, owner_row, slot_row, column_row, basis,
    tz_hbm, tx_hbm, tt_hbm, lam_x, lam_z,
    v_out, grad_out,
    vp, up, ub, sb, mk, idb, w0, w1, w2, snd_y, rcv_y, wy_snd, wy_rcv, fsum, fr1, fr2,
    div, msg, got, got2, cols, tau, kap, owner_inv, owner_phi,
    isnd, ircv, jsnd, jrcv, back, qp, qy_snd, qy_rcv, vel, sig,
    pick, ask, asked, asks, wanted, chosen, reply, replies, fetch, fetched, give, given, gives, taken,
    tz, tx, tt,
    load_sem, x_send, x_recv, y_send, y_recv, f_send, f_recv, a_send, a_recv, i_send, i_recv, r_send, r_recv, out_sem,
):
    npx, npy, nxl, nyl, nz = dims
    nx = npx * nxl
    kzl = nz // npx
    kown = kzl // npy
    halves = nz // HALF
    cells = nxl * nyl
    per = 256 // nxl
    pieces = nyl // per
    group = 2 * npy
    places = npx * group
    me_x = lax.axis_index("px")
    me_y = lax.axis_index("py")
    right_x, left_x = lax.rem(me_x + 1, npx), lax.rem(me_x + npx - 1, npx)
    right_y, left_y = lax.rem(me_y + 1, npy), lax.rem(me_y + npy - 1, npy)
    first_x, last_x = me_x == 0, me_x == npx - 1
    first_y, last_y = me_y == 0, me_y == npy - 1
    top = 8 + nyl
    wide = nyl + 16

    def run(first, last, action):
        def body(r, carry):
            action(r)
            return carry

        lax.fori_loop(first, last, body, 0)

    def remote(src, dst, send, recv, target):
        return pltpu.make_async_remote_copy(
            src_ref=src, dst_ref=dst, send_sem=send, recv_sem=recv, device_id=target, device_id_type=MESH
        )

    def at_x(r):
        return (lax.rem(me_x + r, npx), me_y)

    def at_y(r):
        return (me_x, lax.rem(me_y + r, npy))

    loads = []
    for c in range(3):
        for h in range(halves):
            loads.append(
                pltpu.make_async_copy(
                    v_hbm.at[c, :, :, pl.ds(h * HALF, HALF)],
                    vp.at[c, h, pl.ds(1, nxl), pl.ds(8, nyl), :],
                    load_sem.at[c * halves + h],
                )
            )
    base = 3 * halves
    load_u = pltpu.make_async_copy(u_hbm, ub, load_sem.at[base])
    load_s = pltpu.make_async_copy(s_hbm, sb, load_sem.at[base + 1])
    load_m = pltpu.make_async_copy(m_hbm, mk, load_sem.at[base + 2])
    load_t = [
        pltpu.make_async_copy(a, b, load_sem.at[base + 3 + n])
        for n, (a, b) in enumerate(((tz_hbm, tz), (tx_hbm, tx), (tt_hbm, tt)))
    ]
    for copy in loads:
        copy.start()
    load_u.start()
    load_s.start()
    load_m.start()
    for copy in load_t:
        copy.start()

    barrier = pltpu.get_barrier_semaphore()
    run(1, npx, lambda r: pl.semaphore_signal(barrier, inc=1, device_id=at_x(r), device_id_type=MESH))
    run(1, npy, lambda r: pl.semaphore_signal(barrier, inc=1, device_id=at_y(r), device_id_type=MESH))

    count = owner_row.shape[1]
    owners = owner_row[...]
    same = owner_col[...] == owners
    earlier = lax.broadcasted_iota(jnp.int32, (count, count), 0) < lax.broadcasted_iota(
        jnp.int32, (count, count), 1
    )
    rank = jnp.sum(jnp.where(same & earlier, 1, 0), axis=0, keepdims=True)
    owner_x = owners // npy
    place = owner_x * group + rank * npy + (owners - owner_x * npy)
    match = lax.broadcasted_iota(jnp.int32, (places, count), 0) == place
    pick[...] = jnp.sum(jnp.where(match, column_row[...] + 1, 0), axis=1, keepdims=True) - 1
    slots = jnp.broadcast_to((slot_row[...] + 1).astype(F32), (8, count)).astype(BF16)
    requests = (
        lax.dot_general(
            slots, match.astype(F32).astype(BF16), (((1,), (1,)), ((), ())), preferred_element_type=F32
        )
        - 1.0
    )

    def pad_lanes(row):
        if row.shape[1] >= HALF:
            return row
        return jnp.concatenate([row, jnp.zeros((8, HALF - row.shape[1]), F32)], axis=1)

    def by_px(row, ref):
        row = pad_lanes(row)
        lanes = row.shape[1]
        for p in range(npx):
            ref[p] = pltpu.roll(row, (lanes - group * p) % lanes, 1)[:, :HALF]

    def by_py(rows, ref):
        for j in range(npy):
            ref[j] = pltpu.roll(rows, (HALF - j) % HALF, 1)

    by_px(requests, ask)
    seen = ids[...].T
    for x in range(nxl):
        idb[x] = jnp.broadcast_to(seen[:, x:x + 1], (nyl, HALF))

    def row_at(ref, lead, y):
        lines = ref.reshape(*ref.shape[:-3], (nxl + 2) * wide, HALF)
        return lines.at[(*lead, pl.ds(wide + y, nxl, stride=wide), slice(None))]

    def x_pair(field, at, number):
        return (
            remote(at(field, nxl), at(field, 0), x_send.at[number], x_recv.at[number], (right_x, me_y)),
            remote(at(field, 1), at(field, nxl + 1), x_send.at[number + 1], x_recv.at[number + 1], (left_x, me_y)),
        )

    def at_plane(field, x):
        return field.at[:, :, x, pl.ds(8, nyl), :]

    def y_pair(send, recv, number):
        return (
            remote(send.at[0], recv.at[0], y_send.at[number], y_recv.at[number], (me_x, right_y)),
            remote(send.at[1], recv.at[1], y_send.at[number + 1], y_recv.at[number + 1], (me_x, left_y)),
        )

    for copy in loads:
        copy.wait()
    pl.semaphore_wait(barrier, npx - 1 + npy - 1)

    def pack(field, first):
        for c in range(3):
            for h in range(halves):
                snd_y[0, first + c, h] = row_at(field, (c, h), top - 1)[...].astype(BF16)
                snd_y[1, first + c, h] = row_at(field, (c, h), 8)[...].astype(BF16)

    halo_vx = x_pair(vp, at_plane, 0)
    for copy in halo_vx:
        copy.start()

    def ask_x(r):
        return remote(ask.at[at_x(r)[0]], asked.at[me_x], r_send.at[r], r_recv.at[r], at_x(r))

    def ask_y(r):
        n = npx + r
        return remote(asks.at[at_y(r)[1]], wanted.at[me_y], r_send.at[n], r_recv.at[n], at_y(r))

    def reply_y(r):
        n = npx + npy + r
        return remote(reply.at[at_y(r)[1]], replies.at[me_y], r_send.at[n], r_recv.at[n], at_y(r))

    def reply_x(r):
        n = npx + 2 * npy + r
        return remote(fetch.at[at_x(r)[0]], fetched.at[me_x], r_send.at[n], r_recv.at[n], at_x(r))

    def give_x(r):
        n = 2 * npx + 2 * npy + r
        return remote(give.at[at_x(r)[0]], given.at[me_x], r_send.at[n], r_recv.at[n], at_x(r))

    def give_y(r):
        n = 3 * npx + 2 * npy + r
        return remote(gives.at[at_y(r)[1]], taken.at[me_y], r_send.at[n], r_recv.at[n], at_y(r))

    run(1, npx, lambda r: ask_x(r).start())
    asked[me_x] = ask[me_x]
    pack(vp, 0)
    load_u.wait()

    def widen(i, carry):
        for a in range(3):
            pair = ub[a, pl.ds(pl.multiple_of(i * 2 * nyl, 2 * nyl), 2 * nyl), :].astype(F32)
            for s in range(2):
                for h in range(halves):
                    up[a, h, 1 + 2 * i + s, 8:top, :] = pair[s * nyl:(s + 1) * nyl, h * HALF:(h + 1) * HALF]
        return carry

    lax.fori_loop(0, nxl // 2, widen, 0)
    pack(up, 3)
    halo = y_pair(snd_y, rcv_y, 0) + x_pair(up, at_plane, 2)
    for copy in halo:
        copy.start()

    run(1, npx, lambda r: ask_x(r).wait())
    by_py(asked[:, 0, :], asks)
    run(1, npy, lambda r: ask_y(r).start())
    wanted[me_y] = asks[me_y]

    def reduce_cell(c, g, right):
        inv = 1.0 / (c + right + g)
        return inv, c * inv

    mine = lam_z[pl.ds(pl.multiple_of(me_x * kzl, kzl), kzl), 0:1]
    mu = lam_x[...] + mine
    owned = lam_z[pl.ds(me_x * kzl + me_y * kown, kown), 0:1]
    muo = lam_x[...] + owned

    def owner_table():
        def owner_cell(i, carry):
            c, g, ground = carry
            inv, k = reduce_cell(c, g, 1.0)
            return k, muo + g * inv, ground + k * g

        one = jnp.ones_like(muo)
        c, g, ground = lax.fori_loop(1, nyl - 1, owner_cell, (one, muo, jnp.zeros_like(one)))
        inv, link = reduce_cell(c, g, 1.0)
        from_left = g * inv
        end_ground = muo + from_left + (ground + c * (g / (c + g)))
        ground = ground + link * g
        held = muo + ground
        for b in range(npy - 1):
            inv = 1.0 / (link + held)
            phi = link * inv
            owner_inv[b] = inv
            owner_phi[b] = phi
            nxt = end_ground if b == npy - 2 else muo + ground + from_left
            held = nxt + phi * held
        positive = held > 0.0
        owner_inv[npy - 1] = jnp.where(positive, 1.0 / jnp.where(positive, held, 1.0), 0.0)

    owner_table()
    run(1, npy, lambda r: ask_y(r).wait())

    slot_lane = lax.broadcasted_iota(jnp.int32, (npx, HALF), 1).astype(F32)

    def choose(j, carry):
        label = wanted[j]
        for r in range(2):
            hit = jnp.broadcast_to(label[:, r * npy:r * npy + 1], (npx, HALF)) == slot_lane
            chosen[pl.ds(pl.multiple_of((2 * j + r) * npx, npx), npx), :] = hit.astype(F32).astype(BF16)
        return carry

    lax.fori_loop(0, npy, choose, 0)
    controls = basis.shape[0]
    wide_basis = jnp.concatenate([basis[...], jnp.zeros((HALF - controls, SEG), F32)], axis=0)
    rows = sum(
        jnp.dot(chosen[...], part, preferred_element_type=F32) for part in reversed(split(wide_basis, 3))
    )
    for j in range(npy):
        reply[j] = rows[j * 2 * npx:(j + 1) * 2 * npx]
    run(1, npy, lambda r: reply_y(r).start())
    replies[me_y] = reply[me_y]

    load_s.wait()
    load_m.wait()
    for copy in halo_vx + halo:
        copy.wait()

    for c in range(3):
        for h in range(halves):
            for field, first in ((vp, 0), (up, 3)):
                low, high = rcv_y[0, first + c, h].astype(F32), rcv_y[1, first + c, h].astype(F32)
                row_at(field, (c, h), 7)[...] = jnp.where(first_y, 0.0, low)
                row_at(field, (c, h), top)[...] = jnp.where(last_y, 0.0, high)
    edge = jnp.zeros((nyl, HALF), F32)

    @pl.when(first_x)
    def _():
        for c in range(3):
            for h in range(halves):
                vp[c, h, 0, 8:top, :] = edge
                up[c, h, 0, 8:top, :] = edge

    @pl.when(last_x)
    def _():
        for c in range(3):
            for h in range(halves):
                vp[c, h, nxl + 1, 8:top, :] = edge
                up[c, h, nxl + 1, 8:top, :] = edge

    def tall_rows(field, c, x, y):
        return jnp.concatenate([field[c, h, x, y:y + 24, :] for h in range(halves)], axis=1)

    def tile_rows(field, c, x, y):
        return jnp.concatenate([field[c, h, x, y + 8:y + 16, :] for h in range(halves)], axis=1)

    tiles = nyl // 8

    def predict(i, carry):
        for k in range(tiles):
            rows = pl.ds(pl.multiple_of(i * 2 * nyl + 16 * k, 16), 16)
            forcing = [sb[b, rows, :].astype(F32) for b in range(3)]
            for s in range(2):
                n = 2 * k + s
                x = 2 * i + n // tiles
                y = 8 * (n % tiles)
                scale = 1.0 / (1.0 + (DT * ALPHA) * mk[x, y:y + 8, :].astype(F32))
                u, v, tall_v = [], [], []
                slopes = [None] * 3
                for a in range(3):
                    tall = tall_rows(up, a, x + 1, y)
                    tall_v.append(tall_rows(vp, a, x + 1, y))
                    u.append(tall[8:16])
                    v.append(tall_v[a][8:16])
                    below, above = z_shift(u[a], 0.0, 0.0)
                    diffs = (
                        tile_rows(up, a, x + 2, y) - tile_rows(up, a, x, y),
                        tall[9:17] - tall[7:15],
                        above - below,
                    )
                    for b in range(3):
                        term = v[a] * diffs[b]
                        slopes[b] = term if slopes[b] is None else slopes[b] + term
                for b in range(3):
                    tall = tall_v[b]
                    xm, xp = tile_rows(vp, b, x, y), tile_rows(vp, b, x + 2, y)
                    ym, yp = tall[7:15], tall[9:17]
                    zm, zp = z_shift(v[b], 0.0, 0.0)
                    convect = u[0] * (xp - xm) + u[1] * (yp - ym) + u[2] * (zp - zm)
                    lap = (xp + xm) + (yp + ym) + (zp + zm) - 6.0 * v[b]
                    change = 0.5 * (convect - slopes[b]) + NU * lap + forcing[b][8 * s:8 * s + 8]
                    w = (v[b] + DT * change) * scale
                    for h in range(halves):
                        part = w[:, h * HALF:(h + 1) * HALF]
                        if b == 0:
                            w0[h, x + 1, y:y + 8, :] = part
                        elif b == 1:
                            w1[h, x + 1, y + 8:y + 16, :] = part
                        else:
                            w2[h, x, y:y + 8, :] = part
        return carry

    lax.fori_loop(0, nxl // 2, predict, 0)

    for h in range(halves):
        wy_snd[0, h] = row_at(w1, (h,), top - 1)[...]
        wy_snd[1, h] = row_at(w1, (h,), 8)[...]
    halo = y_pair(wy_snd, wy_rcv, 2) + x_pair(w0, lambda field, x: field.at[:, x], 4)
    for copy in halo:
        copy.start()

    lane = lax.broadcasted_iota(jnp.int32, (nyl, HALF), 1)

    def flux_plane(x, carry):
        face = jnp.where(lane == HALF - 1, w2[halves - 1, x], 0.0)
        which = idb[x]
        return tuple(total + jnp.where(which == k, face, 0.0) for k, total in enumerate(carry))

    zero = jnp.zeros((nyl, HALF), F32)
    totals = lax.fori_loop(0, nxl, flux_plane, (zero,) * OUTLETS)
    fsum[0] = jnp.concatenate([jnp.sum(t, axis=0, keepdims=True) for t in totals], axis=0)

    def flux_x(r):
        return remote(fsum.at[0], fr1.at[me_x], f_send.at[r], f_recv.at[r], at_x(r))

    def flux_y(r):
        return remote(fsum.at[1], fr2.at[me_y], f_send.at[npx + r], f_recv.at[npx + r], at_y(r))

    run(1, npx, lambda r: flux_x(r).start())
    fr1[me_x] = fsum[0]

    for copy in halo:
        copy.wait()
    for h in range(halves):
        row_at(w1, (h,), 7)[...] = jnp.where(first_y, 0.0, wy_rcv[0, h])
        row_at(w1, (h,), top)[...] = jnp.where(last_y, 0.0, wy_rcv[1, h])

    @pl.when(first_x)
    def _():
        for h in range(halves):
            w0[h, 0] = edge

    @pl.when(last_x)
    def _():
        for h in range(halves):
            w0[h, nxl + 1] = edge

    def diverge(x, carry):
        deep = jnp.concatenate([w2[h, x] for h in range(halves)], axis=1)
        below, above = z_shift(deep, 0.0, 0.0)
        for h in range(halves):
            cut = slice(h * HALF, (h + 1) * HALF)
            tall = w1[h, x + 1]
            total = (w0[h, x + 2] - w0[h, x]) + (tall[9:top + 1] - tall[7:top - 1]) + (above - below)[:, cut]
            div[h, pl.ds(x, nyl, stride=nxl), :] = 0.5 * total
        return carry

    lax.fori_loop(0, nxl // 2, diverge, 0)
    run(1, npx, lambda r: flux_x(r).wait())
    fsum[1] = jnp.sum(fr1[...], axis=0)
    run(1, npy, lambda r: flux_y(r).start())
    fr2[me_y] = fsum[1]
    lax.fori_loop(nxl // 2, nxl, diverge, 0)

    run(1, npy, lambda r: reply_y(r).wait())
    lines = replies.reshape(npy * 2 * npx, SEG)
    for p in range(npx):
        for r in range(2):
            fetch[p, r * npy:(r + 1) * npy, :] = lines[pl.ds(r * npx + p, npy, stride=2 * npx), :]

    run(1, npy, lambda r: flux_y(r).wait())
    flux = jnp.sum(fr2[...], axis=0) * (1.0 / (nx * npy * nyl))
    press = []
    for k in range(OUTLETS):
        total = resist[k, 0] * flux[0:1]
        for n in range(1, OUTLETS):
            total = total + resist[k, n] * flux[n:n + 1]
        press.append(jnp.broadcast_to(total, (nyl, HALF)))

    def lower(x, carry):
        which = idb[x]
        drop = jnp.zeros((nyl, HALF), F32)
        for k in range(OUTLETS):
            drop = jnp.where(which == k, press[k], drop)
        drop = DT * jnp.where(lane == HALF - 1, drop, 0.0)
        w2[halves - 1, x] = w2[halves - 1, x] - drop
        here = pl.ds(x, nyl, stride=nxl)
        div[halves - 1, here, :] = div[halves - 1, here, :] - 0.5 * pltpu.roll(drop, HALF - 1, 1)
        return carry

    lax.fori_loop(0, nxl, lower, 0)

    for copy in load_t:
        copy.wait()

    def forth(c, r):
        p = at_x(r)[0]
        n = c * npx + r
        return remote(msg.at[p, c], got.at[me_x, c], a_send.at[n], a_recv.at[n], at_x(r))

    def depth_piece(c, carry):
        here = pl.ds(pl.multiple_of(c * 256, 256), 256)
        value = jnp.concatenate([div[h, here, :] for h in range(halves)], axis=1)
        out = dot_parts((tz[0], tz[1]), split(value, 2), ((1,), (1,)))
        for p in range(npx):
            msg[p, c] = out[p * kzl:(p + 1) * kzl]
        run(1, npx, lambda r: forth(c, r).start())
        return carry

    lax.fori_loop(0, pieces, depth_piece, 0)
    run(1, npx, lambda r: reply_x(r).start())
    fetched[me_x] = fetch[me_x]

    def table_cell(i, carry):
        c, g = carry
        right = jnp.where((i == nyl - 1) & last_y, 0.0, 1.0)
        inv, k = reduce_cell(c, g, right)
        tau[i] = inv
        kap[i] = k
        return k, mu + g * inv

    tau[0] = jnp.zeros_like(mu)
    kap[0] = jnp.ones_like(mu)
    lax.fori_loop(1, nyl, table_cell, (jnp.ones_like(mu), mu))

    wides = npx // 4

    def row_of(i):
        return pl.ds(pl.multiple_of(i * kzl, kzl), kzl)

    def piece_rows(c):
        return pl.ds(pl.multiple_of(c * per * kzl, per * kzl), per * kzl)

    def line_piece(c, carry):
        got[me_x, c] = msg[me_x, c]
        run(1, npx, lambda r: forth(c, r).wait())

        def gather(sg, inner):
            for half in range(per // 4):
                out = swap_groups([got[4 * sg + a, c, :, half * HALF:(half + 1) * HALF] for a in range(4)])
                for b in range(4):
                    y = c * per + 4 * half + b
                    cols[row_of(y), pl.ds(pl.multiple_of(sg * HALF, HALF), HALF)] = out[b]
            return inner

        lax.fori_loop(0, wides, gather, 0)
        rows = piece_rows(c)
        cols[rows, :] = dot_parts(split(cols[rows, :], 2), (tt[0], tt[1]), ((1,), (0,)))
        return carry

    lax.fori_loop(0, pieces, line_piece, 0)

    def down(i, carry):
        r, ends = carry
        ends = ends + kap[i] * r
        nxt = cols[row_of(i + 1), :] + tau[i] * r
        cols[row_of(i + 1), :] = nxt
        return nxt, ends

    r, ends = lax.fori_loop(1, nyl - 1, down, (cols[row_of(1), :], cols[row_of(0), :]))
    ends = ends + kap[nyl - 1] * r
    over = tau[nyl - 1] * r
    for j in range(npy):
        isnd[j, 0:kown, :] = ends[j * kown:(j + 1) * kown]
        isnd[j, kown:2 * kown, :] = over[j * kown:(j + 1) * kown]

    def collect(r):
        return remote(isnd.at[at_y(r)[1]], ircv.at[me_y], i_send.at[r], i_recv.at[r], at_y(r))

    run(1, npy, lambda r: collect(r).start())
    ircv[me_y] = isnd[me_y]
    run(1, npy, lambda r: collect(r).wait())

    rho = []
    for b in range(npy):
        value = ircv[b, 0:kown, :]
        if b > 0:
            value = value + ircv[b - 1, kown:2 * kown, :]
        rho.append(value)
    depth_mode = lax.broadcasted_iota(jnp.int32, (kown, nx), 0) + me_x * kzl + me_y * kown
    row_mode = lax.broadcasted_iota(jnp.int32, (kown, nx), 1)
    mean = sum(rho[1:], rho[0]) * (1.0 / (npy * nyl))
    mean = jnp.where((depth_mode == 0) & (row_mode == 0), mean, 0.0)
    half_sum = (nyl - 1) / 2.0
    for b in range(npy):
        weight = 1.0 + (0.0 if b == 0 else half_sum) + (2.0 * half_sum if b == npy - 1 else half_sum)
        rho[b] = rho[b] - weight * mean
    for b in range(npy - 1):
        rho[b + 1] = rho[b + 1] + owner_phi[b] * rho[b]
    value = -owner_inv[npy - 1] * rho[npy - 1]
    jsnd[npy - 1, 0:kown, :] = value
    jsnd[npy - 1, kown:2 * kown, :] = jnp.zeros_like(value)
    jsnd[npy - 1, 2 * kown:3 * kown, :] = mean
    for b in range(npy - 2, -1, -1):
        jsnd[b, kown:2 * kown, :] = value
        value = owner_phi[b] * value - owner_inv[b] * rho[b]
        jsnd[b, 0:kown, :] = value
        jsnd[b, 2 * kown:3 * kown, :] = mean

    def hand_back(r):
        n = npy + r
        return remote(jsnd.at[at_y(r)[1]], jrcv.at[me_y], i_send.at[n], i_recv.at[n], at_y(r))

    run(1, npy, lambda r: hand_back(r).start())
    jrcv[me_y] = jsnd[me_y]
    run(1, npy, lambda r: hand_back(r).wait())
    for j in range(npy):
        for part in range(3):
            back[part, j * kown:(j + 1) * kown, :] = jrcv[j, part * kown:(part + 1) * kown, :]
    first_value, mean_rows = back[0], back[2]

    def home(c, r):
        p = at_x(r)[0]
        n = (pieces + c) * npx + r
        return remote(msg.at[p, c], got2.at[me_x, c], a_send.at[n], a_recv.at[n], at_x(r))

    def up_piece(n, q):
        c = pieces - 1 - n

        def up_again(m, q):
            i = c * per + per - 1 - m
            share = 0.5 * (i + 1).astype(F32)
            q = tau[i] * (q - cols[row_of(i), :] + mean_rows * share) + kap[i] * first_value
            cols[row_of(i), :] = q
            return q

        q = lax.fori_loop(0, per, up_again, q)
        rows = piece_rows(c)
        cols[rows, :] = dot_parts(split(cols[rows, :], 3), (tx[0], tx[1], tx[2]), ((1,), (0,)))

        def scatter(sg, inner):
            for half in range(per // 4):
                parts = []
                for b in range(4):
                    y = c * per + 4 * half + b
                    parts.append(cols[row_of(y), pl.ds(pl.multiple_of(sg * HALF, HALF), HALF)])
                out = swap_groups(parts)
                for a in range(4):
                    msg[4 * sg + a, c, :, half * HALF:(half + 1) * HALF] = out[a]
            return inner

        lax.fori_loop(0, wides, scatter, 0)
        run(1, npx, lambda r: home(c, r).start())
        return q

    lax.fori_loop(0, pieces, up_piece, back[1])

    pressure = qp.reshape(halves, (nxl + 2) * wide, HALF)

    def rise_piece(n, carry):
        c = pieces - 1 - n
        got2[me_x, c] = msg[me_x, c]
        run(1, npx, lambda r: home(c, r).wait())
        value = got2[:, c].reshape(nz, 256)
        out = dot_parts(split(value.T, 3), (tz[0], tz[1], tz[2]), ((1,), (0,)))
        for y in range(per):
            for h in range(halves):
                pressure[h, pl.ds(wide + 8 + c * per + y, nxl, stride=wide), :] = out[
                    y * nxl:(y + 1) * nxl, h * HALF:(h + 1) * HALF
                ]
        return carry

    lax.fori_loop(0, pieces, rise_piece, 0)

    for h in range(halves):
        qy_snd[0, h] = row_at(qp, (h,), top - 1)[...]
        qy_snd[1, h] = row_at(qp, (h,), 8)[...]
    halo = y_pair(qy_snd, qy_rcv, 4) + x_pair(qp, lambda field, x: field.at[:, x, pl.ds(8, nyl), :], 6)
    for copy in halo:
        copy.start()

    def q_rows(x, y, size):
        return jnp.concatenate([qp[h, x, y:y + size, :] for h in range(halves)], axis=1)

    def join(field, x):
        return jnp.concatenate([field[h, x, 0:nyl, :] for h in range(halves)], axis=1)

    def correct_depth(x, carry):
        center = q_rows(x + 1, 8, nyl)
        spot = lax.broadcasted_iota(jnp.int32, center.shape, 1)
        below = jnp.where(spot == 0, center, pltpu.roll(center, 1, 1))
        above = jnp.where(spot == nz - 1, center, pltpu.roll(center, nz - 1, 1))
        vel[2, x] = join(w2, x) - 0.5 * (above - below)
        return carry

    lax.fori_loop(0, nxl, correct_depth, 0)
    outs = [pltpu.make_async_copy(vel.at[b], v_out.at[b], out_sem.at[b]) for b in range(3)]
    outs[2].start()

    for copy in halo:
        copy.wait()
    for h in range(halves):
        row_at(qp, (h,), 7)[...] = jnp.where(first_y, qy_snd[1, h], qy_rcv[0, h])
        row_at(qp, (h,), top)[...] = jnp.where(last_y, qy_snd[0, h], qy_rcv[1, h])

    @pl.when(first_x)
    def _():
        for h in range(halves):
            qp[h, 0, 8:top, :] = qp[h, 1, 8:top, :]

    @pl.when(last_x)
    def _():
        for h in range(halves):
            qp[h, nxl + 1, 8:top, :] = qp[h, nxl, 8:top, :]

    def correct(x, carry):
        tall = q_rows(x + 1, 0, wide)
        v0 = join(w0, x + 1) - 0.5 * (q_rows(x + 2, 8, nyl) - q_rows(x, 8, nyl))
        deep = jnp.concatenate([w1[h, x + 1, 8:top, :] for h in range(halves)], axis=1)
        v1 = deep - 0.5 * (tall[9:top + 1] - tall[7:top - 1])
        vel[0, x] = v0
        vel[1, x] = v1
        u = [jnp.concatenate([up[a, h, x + 1, 8:top, :] for h in range(halves)], axis=1) for a in range(3)]
        total = -ALPHA * (u[0] * v0 + u[1] * v1 + u[2] * vel[2, x])
        for h in range(halves):
            sig[h, pl.ds(pl.multiple_of(x * nyl, 8), nyl), :] = total[:, h * HALF:(h + 1) * HALF]
        return carry

    lax.fori_loop(0, nxl, correct, 0)
    outs[0].start()
    outs[1].start()

    shape = (places, cells)
    cell = lax.broadcasted_iota(jnp.int32, shape, 1) * halves
    picked = None
    for h in range(halves):
        hot = (jnp.broadcast_to(pick[...], shape) == cell + h).astype(F32).astype(BF16)
        for part in reversed(split(sig[h], 3)):
            term = jnp.dot(hot, part, preferred_element_type=F32)
            picked = term if picked is None else picked + term
    run(1, npx, lambda r: reply_x(r).wait())
    products = picked * fetched[...].reshape(places, SEG)
    ones = jnp.ones((8, SEG), BF16)
    totals = sum(
        lax.dot_general(ones, part, (((1,), (1,)), ((), ())), preferred_element_type=F32)
        for part in reversed(split(products, 3))
    )
    by_px(totals, give)
    run(1, npx, lambda r: give_x(r).start())
    given[me_x] = give[me_x]
    run(1, npx, lambda r: give_x(r).wait())
    by_py(given[:, 0, :], gives)
    run(1, npy, lambda r: give_y(r).start())
    taken[me_y] = gives[me_y]
    run(1, npy, lambda r: give_y(r).wait())

    def add_up(j, total):
        label, value = wanted[j], taken[j]
        for r in range(2):
            spot = slice(r * npy, r * npy + 1)
            hit = jnp.broadcast_to(label[:, spot], (npx, HALF)) == slot_lane
            total = total + jnp.where(hit, jnp.broadcast_to(value[:, spot], (npx, HALF)), 0.0)
        return total

    total = lax.fori_loop(0, npy, add_up, jnp.zeros((npx, HALF), F32))
    grad_out[...] = jnp.sum(total, axis=0, keepdims=True)[:, :controls]
    for copy in outs:
        copy.wait()


def main_call(dims, args, owner_rows):
    npx, npy, nxl, nyl, nz = dims
    nx = npx * nxl
    kzl = nz // npx
    kown = kzl // npy
    halves = nz // HALF
    wide = nyl + 16
    cells = nxl * nyl
    pieces = cells // 256
    places = 2 * npx * npy
    vmem = pltpu.VMEM
    anywhere = pl.BlockSpec(memory_space=pl.ANY)
    here = pl.BlockSpec(memory_space=pltpu.VMEM)
    scalar = pl.BlockSpec(memory_space=pltpu.SMEM)
    dma = pltpu.SemaphoreType.DMA
    tables = args[11:14]
    field = vmem((3, halves, nxl + 2, wide, HALF), F32)
    line = vmem((nyl, kzl, nx), F32)
    message = vmem((npx, pieces, kzl, 256), F32)
    scratch = [
        field,
        field,
        vmem((3, cells, nz), BF16),
        vmem((3, cells, nz), BF16),
        vmem((nxl, nyl, nz), jnp.int32),
        vmem((nxl, nyl, HALF), jnp.int32),
        vmem((halves, nxl + 2, nyl, HALF), F32),
        vmem((halves, nxl + 2, wide, HALF), F32),
        vmem((halves, nxl, nyl, HALF), F32),
        vmem((2, 6, halves, nxl, HALF), BF16),
        vmem((2, 6, halves, nxl, HALF), BF16),
        vmem((2, halves, nxl, HALF), F32),
        vmem((2, halves, nxl, HALF), F32),
        vmem((2, OUTLETS, HALF), F32),
        vmem((npx, OUTLETS, HALF), F32),
        vmem((npy, OUTLETS, HALF), F32),
        vmem((halves, cells, HALF), F32),
        message,
        message,
        message,
        vmem((nyl * kzl, nx), F32),
        line,
        line,
        vmem((npy, kown, nx), F32),
        vmem((npy, kown, nx), F32),
        vmem((npy, 2 * kown, nx), F32),
        vmem((npy, 2 * kown, nx), F32),
        vmem((npy, 3 * kown, nx), F32),
        vmem((npy, 3 * kown, nx), F32),
        vmem((3, kzl, nx), F32),
        vmem((halves, nxl + 2, wide, HALF), F32),
        vmem((2, halves, nxl, HALF), F32),
        vmem((2, halves, nxl, HALF), F32),
        vmem((3, nxl, nyl, nz), F32),
        vmem((halves, cells, HALF), F32),
        vmem((places, 1), jnp.int32),
        vmem((npx, 8, HALF), F32),
        vmem((npx, 8, HALF), F32),
        vmem((npy, npx, HALF), F32),
        vmem((npy, npx, HALF), F32),
        vmem((places, HALF), BF16),
        vmem((npy, 2 * npx, SEG), F32),
        vmem((npy, 2 * npx, SEG), F32),
        vmem((npx, 2 * npy, SEG), F32),
        vmem((npx, 2 * npy, SEG), F32),
        vmem((npx, 8, HALF), F32),
        vmem((npx, 8, HALF), F32),
        vmem((npy, npx, HALF), F32),
        vmem((npy, npx, HALF), F32),
    ]
    scratch += [vmem(t.shape, BF16) for t in tables]
    scratch += [
        dma((3 * halves + 3 + len(tables),)),
        dma((8,)),
        dma((8,)),
        dma((6,)),
        dma((6,)),
        dma((npx + npy,)),
        dma((npx + npy,)),
        dma((2 * pieces * npx,)),
        dma((2 * pieces * npx,)),
        dma((2 * npy,)),
        dma((2 * npy,)),
        dma((3 * (npx + npy),)),
        dma((3 * (npx + npy),)),
        dma((3,)),
    ]
    return pl.pallas_call(
        functools.partial(main_kernel, dims),
        out_shape=(
            jax.ShapeDtypeStruct((3, nxl, nyl, nz), F32),
            jax.ShapeDtypeStruct((1, owner_rows), F32),
        ),
        in_specs=[anywhere] * 4 + [here, scalar] + [here] * 5 + [anywhere] * len(tables) + [here] * 2,
        out_specs=(anywhere, here),
        scratch_shapes=scratch,
        compiler_params=pltpu.CompilerParams(
            collective_id=0, has_side_effects=True, vmem_limit_bytes=58 * 2**20
        ),
        name="project",
    )(*args)


def local(
    base_flow, adjoint_start, source, solid_mask, outlet_ids, resist,
    tile_owner, tile_slot, tile_column, control_basis,
):
    _, nxl, nyl, nz = adjoint_start.shape
    npx, npy = lax.axis_size("px"), lax.axis_size("py")
    nx = npx * nxl
    tz, tx = table_np(nz), table_np(nx)
    tables = [split_np(tz, 3), split_np(tx, 3), split_np(np.ascontiguousarray(tx.T), 2)]
    tables = [jnp.asarray(np.stack(t)) for t in tables]
    lam_x = jnp.asarray(-eigen_np(nx)[None, :])
    lam_z = jnp.asarray(np.repeat(-eigen_np(nz)[:, None], HALF, axis=1))
    args = (
        adjoint_start,
        base_flow.reshape(3, nxl * nyl, nz),
        source.reshape(3, nxl * nyl, nz),
        solid_mask,
        outlet_ids,
        resist,
        tile_owner,
        tile_owner.reshape(1, -1),
        tile_slot.reshape(1, -1),
        tile_column.reshape(1, -1),
        control_basis,
        *tables,
        lam_x,
        lam_z,
    )
    velocity, grad = main_call((npx, npy, nxl, nyl, nz), args, control_basis.shape[0])
    return velocity, grad.reshape(-1)


def solution(mesh):
    in_specs = (
        P(None, "px", "py", None),
        P(None, "px", "py", None),
        P(None, "px", "py", None),
        P("px", "py", None),
        P("px", "py"),
        P(),
        P(("px", "py"), None),
        P(("px", "py")),
        P(("px", "py")),
        P(("px", "py"), None),
    )
    out_specs = (P(None, "px", "py", None), P(("px", "py")))
    return jax.shard_map(local, mesh=mesh, in_specs=in_specs, out_specs=out_specs, check_vma=False)
```

```python
import functools
import math

import jax
import jax.numpy as jnp
import numpy as np
from jax import lax
from jax.experimental import pallas as pl
from jax.experimental.pallas import tpu as pltpu
from jax.sharding import PartitionSpec as P

SEG = 128
OUTLETS = 8
DT = 0.1
NU = 0.5
ALPHA = 5.0
HALF = 128
MESH = pl.DeviceIdType.MESH
F32 = jnp.float32
BF16 = jnp.bfloat16


def table_np(count):
    order = np.arange(count).astype(np.float32)
    modes = order[:, None]
    points = order[None, :]
    weights = np.where(modes == 0.0, math.sqrt(1.0 / count), math.sqrt(2.0 / count)).astype(np.float32)
    angle = np.float32(np.pi) * (points + np.float32(0.5)) * modes / np.float32(count)
    return (weights * np.cos(angle.astype(np.float32))).astype(np.float32)


def eigen_np(count):
    order = np.arange(count).astype(np.float32)
    angle = (np.float32(np.pi) * order / np.float32(count)).astype(np.float32)
    return (np.float32(2.0) * np.cos(angle) - np.float32(2.0)).astype(np.float32)


def split_np(table, count):
    parts = []
    for _ in range(count):
        parts.append(table.astype(jnp.bfloat16))
        table = table - parts[-1].astype(np.float32)
    return tuple(parts)


def split(value, count):
    parts = []
    for _ in range(count):
        parts.append(value.astype(BF16))
        value = value - parts[-1].astype(F32)
    return tuple(parts)


def dot_parts(a_parts, b_parts, contract):
    dims = ((contract[0], contract[1]), ((), ()))
    dot = functools.partial(lax.dot_general, dimension_numbers=dims, preferred_element_type=F32)
    total = None
    for order in range(len(a_parts) - 1, -1, -1):
        for i in range(order + 1):
            term = dot(a_parts[i], b_parts[order - i])
            total = term if total is None else total + term
    return total


def swap_groups(tiles):
    lane = lax.broadcasted_iota(jnp.int32, tiles[0].shape, 1)
    odd = (lane // 32) % 2 == 1
    far = lane >= 64
    t0, t1, t2, t3 = tiles
    a0 = jnp.where(odd, pltpu.roll(t1, 32, 1), t0)
    a1 = jnp.where(odd, t1, pltpu.roll(t0, 96, 1))
    a2 = jnp.where(odd, pltpu.roll(t3, 32, 1), t2)
    a3 = jnp.where(odd, t3, pltpu.roll(t2, 96, 1))
    return (
        jnp.where(far, pltpu.roll(a2, 64, 1), a0),
        jnp.where(far, pltpu.roll(a3, 64, 1), a1),
        jnp.where(far, a2, pltpu.roll(a0, 64, 1)),
        jnp.where(far, a3, pltpu.roll(a1, 64, 1)),
    )


def z_shift(field, edge_low, edge_high):
    depth = field.shape[1]
    lane = lax.broadcasted_iota(jnp.int32, field.shape, 1)
    below = jnp.where(lane == 0, edge_low, pltpu.roll(field, 1, 1))
    above = jnp.where(lane == depth - 1, edge_high, pltpu.roll(field, depth - 1, 1))
    return below, above


def main_kernel(
    dims,
    v_hbm, u_hbm, s_hbm, m_hbm, ids, resist, owner_row, slot_row, column_row, basis,
    tz_hbm, tx_hbm, tt_hbm, lam_x, lam_z,
    v_out, grad_out,
    vp, up, ub, sb, mk, idb, w0, w1, w2, snd_y, rcv_y, wy_snd, wy_rcv, fsum, fr1, fr2,
    div, msg, got, got2, cols, tau, kap, owner_inv, owner_phi,
    isnd, ircv, jsnd, jrcv, back, qp, qy_snd, qy_rcv, vel, sig,
    outlet, hot, pick, ask, asked, asks, wanted, chosen, reply, replies, fetch, fetched, give, given, gives, taken,
    tz, tx, tt,
    load_sem, x_send, x_recv, y_send, y_recv, f_send, f_recv, a_send, a_recv, i_send, i_recv, r_send, r_recv, out_sem,
):
    npx, npy, nxl, nyl, nz = dims
    nx = npx * nxl
    kzl = nz // npx
    kown = kzl // npy
    halves = nz // HALF
    cells = nxl * nyl
    per = 256 // nxl
    pieces = nyl // per
    group = 2 * npy
    places = npx * group
    me_x = lax.axis_index("px")
    me_y = lax.axis_index("py")
    right_x, left_x = lax.rem(me_x + 1, npx), lax.rem(me_x + npx - 1, npx)
    right_y, left_y = lax.rem(me_y + 1, npy), lax.rem(me_y + npy - 1, npy)
    first_x, last_x = me_x == 0, me_x == npx - 1
    first_y, last_y = me_y == 0, me_y == npy - 1
    top = 8 + nyl
    wide = nyl + 16

    def run(first, last, action):
        def body(r, carry):
            action(r)
            return carry

        lax.fori_loop(first, last, body, 0)

    def remote(src, dst, send, recv, target):
        return pltpu.make_async_remote_copy(
            src_ref=src, dst_ref=dst, send_sem=send, recv_sem=recv, device_id=target, device_id_type=MESH
        )

    def at_x(r):
        return (lax.rem(me_x + r, npx), me_y)

    def at_y(r):
        return (me_x, lax.rem(me_y + r, npy))

    def spread(count, target, src, dst, send, recv):
        run(1, count, lambda r: remote(src(r), dst, send, recv, target(r)).start())

    def settle(like, send, recv):
        pltpu.make_async_copy(like, like, send).wait()
        pltpu.make_async_copy(like, like, recv).wait()

    others_x, others_y = pl.ds(0, npx - 1), pl.ds(0, npy - 1)

    loads = []
    for c in range(3):
        for h in range(halves):
            loads.append(
                pltpu.make_async_copy(
                    v_hbm.at[c, :, :, pl.ds(h * HALF, HALF)],
                    vp.at[c, h, pl.ds(1, nxl), pl.ds(8, nyl), :],
                    load_sem.at[c * halves + h],
                )
            )
    base = 3 * halves
    load_u = pltpu.make_async_copy(u_hbm, ub, load_sem.at[base])
    load_s = pltpu.make_async_copy(s_hbm, sb, load_sem.at[base + 1])
    load_m = pltpu.make_async_copy(m_hbm, mk, load_sem.at[base + 2])
    load_t = [
        pltpu.make_async_copy(a, b, load_sem.at[base + 3 + n])
        for n, (a, b) in enumerate(((tz_hbm, tz), (tx_hbm, tx), (tt_hbm, tt)))
    ]
    for copy in loads:
        copy.start()
    load_u.start()
    load_s.start()
    load_m.start()
    for copy in load_t:
        copy.start()

    barrier = pltpu.get_barrier_semaphore()
    run(1, npx, lambda r: pl.semaphore_signal(barrier, inc=1, device_id=at_x(r), device_id_type=MESH))
    run(1, npy, lambda r: pl.semaphore_signal(barrier, inc=1, device_id=at_y(r), device_id_type=MESH))

    count = owner_row.shape[1]
    owners = owner_row[...]
    same = jnp.broadcast_to(owners, (8, count)).T[:, 0:1] == owners
    earlier = lax.broadcasted_iota(jnp.int32, (count, count), 0) < lax.broadcasted_iota(
        jnp.int32, (count, count), 1
    )
    rank = jnp.sum(jnp.where(same & earlier, 1, 0), axis=0, keepdims=True)
    owner_x = owners // npy
    place = owner_x * group + rank * npy + (owners - owner_x * npy)
    match = lax.broadcasted_iota(jnp.int32, (places, count), 0) == place
    pick[...] = jnp.sum(jnp.where(match, column_row[...] + 1, 0), axis=1, keepdims=True) - 1
    slots = jnp.broadcast_to((slot_row[...] + 1).astype(F32), (8, count)).astype(BF16)
    requests = (
        lax.dot_general(
            slots, match.astype(F32).astype(BF16), (((1,), (1,)), ((), ())), preferred_element_type=F32
        )
        - 1.0
    )

    def pad_lanes(row):
        if row.shape[1] >= HALF:
            return row
        return jnp.concatenate([row, jnp.zeros((8, HALF - row.shape[1]), F32)], axis=1)

    def by_px(row, ref):
        row = pad_lanes(row)
        lanes = row.shape[1]
        for p in range(npx):
            ref[p, 0:8, :] = pltpu.roll(row, (lanes - group * p) % lanes, 1)[:, :HALF]

    def by_py(rows, ref):
        for j in range(npy):
            ref[j] = pltpu.roll(rows, (HALF - j) % HALF, 1)

    by_px(requests, ask)
    seen = ids[...]
    padded = jnp.concatenate([seen.astype(F32), jnp.zeros((nyl, HALF - nxl), F32)], axis=1)
    for p in range(npx):
        ask[p, 8:top, :] = padded
    for x in range(nxl):
        idb[x] = jnp.broadcast_to(seen[:, x:x + 1], (nyl, HALF))

    def row_at(ref, lead, y):
        lines = ref.reshape(*ref.shape[:-3], (nxl + 2) * wide, HALF)
        return lines.at[(*lead, pl.ds(wide + y, nxl, stride=wide), slice(None))]

    def x_pair(field, at, number):
        return (
            remote(at(field, nxl), at(field, 0), x_send.at[number], x_recv.at[number], (right_x, me_y)),
            remote(at(field, 1), at(field, nxl + 1), x_send.at[number + 1], x_recv.at[number + 1], (left_x, me_y)),
        )

    def at_plane(field, x):
        return field.at[:, :, x, pl.ds(8, nyl), :]

    def y_pair(send, recv, number):
        return (
            remote(send.at[0], recv.at[0], y_send.at[number], y_recv.at[number], (me_x, right_y)),
            remote(send.at[1], recv.at[1], y_send.at[number + 1], y_recv.at[number + 1], (me_x, left_y)),
        )

    for copy in loads:
        copy.wait()
    pl.semaphore_wait(barrier, npx - 1 + npy - 1)

    def pack(field, first):
        for c in range(3):
            for h in range(halves):
                snd_y[0, first + c, h] = row_at(field, (c, h), top - 1)[...].astype(BF16)
                snd_y[1, first + c, h] = row_at(field, (c, h), 8)[...].astype(BF16)

    halo_vx = x_pair(vp, at_plane, 0)
    for copy in halo_vx:
        copy.start()

    def ask_start():
        spread(npx, at_x, lambda r: ask.at[at_x(r)[0]], asked.at[me_x], r_send.at[0], r_recv.at[0])
        asked[me_x] = ask[me_x]

    ask_start()
    pack(vp, 0)
    load_u.wait()

    def widen(i, carry):
        for a in range(3):
            pair = ub[a, pl.ds(pl.multiple_of(i * 2 * nyl, 2 * nyl), 2 * nyl), :].astype(F32)
            for s in range(2):
                for h in range(halves):
                    up[a, h, 1 + 2 * i + s, 8:top, :] = pair[s * nyl:(s + 1) * nyl, h * HALF:(h + 1) * HALF]
        return carry

    lax.fori_loop(0, nxl // 2, widen, 0)
    pack(up, 3)
    halo = y_pair(snd_y, rcv_y, 0) + x_pair(up, at_plane, 2)
    for copy in halo:
        copy.start()

    settle(asked.at[others_x], r_send.at[0], r_recv.at[0])
    by_py(asked[:, 0, :], asks)
    spread(npy, at_y, lambda r: asks.at[at_y(r)[1]], wanted.at[me_y], r_send.at[1], r_recv.at[1])
    wanted[me_y] = asks[me_y]

    def reduce_cell(c, g, right):
        inv = 1.0 / (c + right + g)
        return inv, c * inv

    mine = lam_z[pl.ds(pl.multiple_of(me_x * kzl, kzl), kzl), 0:1]
    mu = lam_x[...] + mine
    owned = lam_z[pl.ds(me_x * kzl + me_y * kown, kown), 0:1]
    muo = lam_x[...] + owned

    def owner_table():
        def owner_cell(i, carry):
            c, g, ground = carry
            inv, k = reduce_cell(c, g, 1.0)
            return k, muo + g * inv, ground + k * g

        one = jnp.ones_like(muo)
        c, g, ground = lax.fori_loop(1, nyl - 1, owner_cell, (one, muo, jnp.zeros_like(one)))
        inv, link = reduce_cell(c, g, 1.0)
        from_left = g * inv
        end_ground = muo + from_left + (ground + c * (g / (c + g)))
        ground = ground + link * g
        held = muo + ground
        for b in range(npy - 1):
            inv = 1.0 / (link + held)
            phi = link * inv
            owner_inv[b] = inv
            owner_phi[b] = phi
            nxt = end_ground if b == npy - 2 else muo + ground + from_left
            held = nxt + phi * held
        positive = held > 0.0
        owner_inv[npy - 1] = jnp.where(positive, 1.0 / jnp.where(positive, held, 1.0), 0.0)

    owner_table()
    settle(wanted.at[others_y], r_send.at[1], r_recv.at[1])

    slot_lane = lax.broadcasted_iota(jnp.int32, (npx, HALF), 1).astype(F32)

    def choose(j, carry):
        label = wanted[j]
        for r in range(2):
            hit = jnp.broadcast_to(label[:, r * npy:r * npy + 1], (npx, HALF)) == slot_lane
            chosen[pl.ds(pl.multiple_of((2 * j + r) * npx, npx), npx), :] = hit.astype(F32).astype(BF16)
        return carry

    lax.fori_loop(0, npy, choose, 0)
    controls = basis.shape[0]
    wide_basis = jnp.concatenate([basis[...], jnp.zeros((HALF - controls, SEG), F32)], axis=0)
    rows = sum(
        jnp.dot(chosen[...], part, preferred_element_type=F32) for part in reversed(split(wide_basis, 3))
    )
    for j in range(npy):
        reply[j] = rows[j * 2 * npx:(j + 1) * 2 * npx]
    spread(npy, at_y, lambda r: reply.at[at_y(r)[1]], replies.at[me_y], r_send.at[2], r_recv.at[2])
    replies[me_y] = reply[me_y]

    load_s.wait()
    load_m.wait()
    for copy in halo_vx + halo:
        copy.wait()

    for c in range(3):
        for h in range(halves):
            for field, first in ((vp, 0), (up, 3)):
                low, high = rcv_y[0, first + c, h].astype(F32), rcv_y[1, first + c, h].astype(F32)
                row_at(field, (c, h), 7)[...] = jnp.where(first_y, 0.0, low)
                row_at(field, (c, h), top)[...] = jnp.where(last_y, 0.0, high)
    edge = jnp.zeros((nyl, HALF), F32)

    @pl.when(first_x)
    def _():
        for c in range(3):
            for h in range(halves):
                vp[c, h, 0, 8:top, :] = edge
                up[c, h, 0, 8:top, :] = edge

    @pl.when(last_x)
    def _():
        for c in range(3):
            for h in range(halves):
                vp[c, h, nxl + 1, 8:top, :] = edge
                up[c, h, nxl + 1, 8:top, :] = edge

    def tall_rows(field, c, x, y):
        return jnp.concatenate([field[c, h, x, y:y + 24, :] for h in range(halves)], axis=1)

    def tile_rows(field, c, x, y):
        return jnp.concatenate([field[c, h, x, y + 8:y + 16, :] for h in range(halves)], axis=1)

    tiles = nyl // 8

    def predict(i, carry):
        for k in range(tiles):
            rows = pl.ds(pl.multiple_of(i * 2 * nyl + 16 * k, 16), 16)
            forcing = [sb[b, rows, :].astype(F32) for b in range(3)]
            for s in range(2):
                n = 2 * k + s
                x = 2 * i + n // tiles
                y = 8 * (n % tiles)
                scale = 1.0 / (1.0 + (DT * ALPHA) * mk[x, y:y + 8, :].astype(F32))
                u, v, tall_v = [], [], []
                slopes = [None] * 3
                for a in range(3):
                    tall = tall_rows(up, a, x + 1, y)
                    tall_v.append(tall_rows(vp, a, x + 1, y))
                    u.append(tall[8:16])
                    v.append(tall_v[a][8:16])
                    below, above = z_shift(u[a], 0.0, 0.0)
                    diffs = (
                        tile_rows(up, a, x + 2, y) - tile_rows(up, a, x, y),
                        tall[9:17] - tall[7:15],
                        above - below,
                    )
                    for b in range(3):
                        term = v[a] * diffs[b]
                        slopes[b] = term if slopes[b] is None else slopes[b] + term
                for b in range(3):
                    tall = tall_v[b]
                    xm, xp = tile_rows(vp, b, x, y), tile_rows(vp, b, x + 2, y)
                    ym, yp = tall[7:15], tall[9:17]
                    zm, zp = z_shift(v[b], 0.0, 0.0)
                    convect = u[0] * (xp - xm) + u[1] * (yp - ym) + u[2] * (zp - zm)
                    lap = (xp + xm) + (yp + ym) + (zp + zm) - 6.0 * v[b]
                    change = 0.5 * (convect - slopes[b]) + NU * lap + forcing[b][8 * s:8 * s + 8]
                    w = (v[b] + DT * change) * scale
                    for h in range(halves):
                        part = w[:, h * HALF:(h + 1) * HALF]
                        if b == 0:
                            w0[h, x + 1, y:y + 8, :] = part
                        elif b == 1:
                            w1[h, x + 1, y + 8:y + 16, :] = part
                        else:
                            w2[h, x, y:y + 8, :] = part
        return carry

    lax.fori_loop(0, nxl // 2, predict, 0)

    for h in range(halves):
        wy_snd[0, h] = row_at(w1, (h,), top - 1)[...]
        wy_snd[1, h] = row_at(w1, (h,), 8)[...]
    halo = y_pair(wy_snd, wy_rcv, 2) + x_pair(w0, lambda field, x: field.at[:, x], 4)
    for copy in halo:
        copy.start()

    lane = lax.broadcasted_iota(jnp.int32, (nyl, HALF), 1)

    def flux_plane(x, carry):
        face = jnp.where(lane == HALF - 1, w2[halves - 1, x], 0.0)
        which = idb[x]
        return tuple(total + jnp.where(which == k, face, 0.0) for k, total in enumerate(carry))

    zero = jnp.zeros((nyl, HALF), F32)
    totals = lax.fori_loop(0, nxl, flux_plane, (zero,) * OUTLETS)
    fsum[0] = jnp.concatenate([jnp.sum(t, axis=0, keepdims=True) for t in totals], axis=0)

    spread(npx, at_x, lambda r: fsum.at[0], fr1.at[me_x], f_send.at[0], f_recv.at[0])
    fr1[me_x] = fsum[0]

    for copy in halo:
        copy.wait()
    for h in range(halves):
        row_at(w1, (h,), 7)[...] = jnp.where(first_y, 0.0, wy_rcv[0, h])
        row_at(w1, (h,), top)[...] = jnp.where(last_y, 0.0, wy_rcv[1, h])

    @pl.when(first_x)
    def _():
        for h in range(halves):
            w0[h, 0] = edge

    @pl.when(last_x)
    def _():
        for h in range(halves):
            w0[h, nxl + 1] = edge

    def diverge(x, carry):
        deep = jnp.concatenate([w2[h, x] for h in range(halves)], axis=1)
        below, above = z_shift(deep, 0.0, 0.0)
        for h in range(halves):
            cut = slice(h * HALF, (h + 1) * HALF)
            tall = w1[h, x + 1]
            total = (w0[h, x + 2] - w0[h, x]) + (tall[9:top + 1] - tall[7:top - 1]) + (above - below)[:, cut]
            div[h, pl.ds(x, nyl, stride=nxl), :] = 0.5 * total
        return carry

    lax.fori_loop(0, nxl, diverge, 0)

    for copy in load_t:
        copy.wait()

    def depth_piece(c, carry):
        here = pl.ds(pl.multiple_of(c * 256, 256), 256)
        value = jnp.concatenate([div[h, here, :] for h in range(halves)], axis=1)
        out = dot_parts((tz[0], tz[1]), split(value, 2), ((1,), (1,)))
        for p in range(npx):
            msg[p, c] = out[p * kzl:(p + 1) * kzl]
        spread(npx, at_x, lambda r: msg.at[at_x(r)[0], c], got.at[me_x, c], a_send.at[c], a_recv.at[c])
        return carry

    lax.fori_loop(0, pieces, depth_piece, 0)

    settle(fr1.at[others_x], f_send.at[0], f_recv.at[0])
    fsum[1] = jnp.sum(fr1[...], axis=0)
    spread(npy, at_y, lambda r: fsum.at[1], fr2.at[me_y], f_send.at[1], f_recv.at[1])
    fr2[me_y] = fsum[1]
    settle(replies.at[others_y], r_send.at[2], r_recv.at[2])
    lines = replies.reshape(npy * 2 * npx, SEG)
    for p in range(npx):
        for r in range(2):
            fetch[p, r * npy:(r + 1) * npy, :] = lines[pl.ds(r * npx + p, npy, stride=2 * npx), :]
    spread(npx, at_x, lambda r: fetch.at[at_x(r)[0]], fetched.at[me_x], r_send.at[3], r_recv.at[3])
    fetched[me_x] = fetch[me_x]

    def table_cell(i, carry):
        c, g = carry
        right = jnp.where((i == nyl - 1) & last_y, 0.0, 1.0)
        inv, k = reduce_cell(c, g, right)
        tau[i] = inv
        kap[i] = k
        return k, mu + g * inv

    tau[0] = jnp.zeros_like(mu)
    kap[0] = jnp.ones_like(mu)
    lax.fori_loop(1, nyl, table_cell, (jnp.ones_like(mu), mu))

    shape = (places, cells)
    cell = lax.broadcasted_iota(jnp.int32, shape, 1) * halves
    for h in range(halves):
        hot[h] = (jnp.broadcast_to(pick[...], shape) == cell + h).astype(F32).astype(BF16)

    settle(fr2.at[others_y], f_send.at[1], f_recv.at[1])
    flux = jnp.sum(fr2[...], axis=0) * (1.0 / (nx * npy * nyl))
    press = []
    for k in range(OUTLETS):
        total = resist[k, 0] * flux[0:1]
        for n in range(1, OUTLETS):
            total = total + resist[k, n] * flux[n:n + 1]
        press.append(total[:, HALF - 1:HALF])

    def pressures(which):
        drop = jnp.zeros(which.shape, F32)
        for k in range(OUTLETS):
            drop = jnp.where(which == k, jnp.broadcast_to(press[k], which.shape), drop)
        return drop

    def lower(x, carry):
        drop = DT * jnp.where(lane == HALF - 1, pressures(idb[x]), 0.0)
        w2[halves - 1, x] = w2[halves - 1, x] - drop
        return carry

    lax.fori_loop(0, nxl, lower, 0)
    quarter = lane // nxl
    for n in range(npx // 4):
        which = asked[4 * n, 8:top, :]
        for a in range(1, 4):
            which = jnp.where(quarter == a, pltpu.roll(asked[4 * n + a, 8:top, :], a * nxl, 1), which)
        outlet[:, n * HALF:(n + 1) * HALF] = pressures(which)
    weight = jnp.broadcast_to(lam_z[pl.ds(pl.multiple_of(me_x * kzl, kzl), kzl), 1:2], (kzl, nx))

    wides = npx // 4

    def row_of(i):
        return pl.ds(pl.multiple_of(i * kzl, kzl), kzl)

    def piece_rows(c):
        return pl.ds(pl.multiple_of(c * per * kzl, per * kzl), per * kzl)

    def line_piece(c, carry):
        got[me_x, c] = msg[me_x, c]
        settle(got.at[others_x, c], a_send.at[c], a_recv.at[c])

        def gather(sg, inner):
            for half in range(per // 4):
                out = swap_groups([got[4 * sg + a, c, :, half * HALF:(half + 1) * HALF] for a in range(4)])
                for b in range(4):
                    y = c * per + 4 * half + b
                    cols[row_of(y), pl.ds(pl.multiple_of(sg * HALF, HALF), HALF)] = out[b]
            return inner

        lax.fori_loop(0, wides, gather, 0)

        def add_outlet(m, inner):
            y = c * per + m
            line = jnp.broadcast_to(outlet[pl.ds(y, 1), :], (kzl, nx))
            cols[row_of(y), :] = cols[row_of(y), :] + weight * line
            return inner

        lax.fori_loop(0, per, add_outlet, 0)
        rows = piece_rows(c)
        cols[rows, :] = dot_parts(split(cols[rows, :], 2), (tt[0], tt[1]), ((1,), (0,)))
        return carry

    lax.fori_loop(0, pieces, line_piece, 0)

    def down(i, carry):
        r, ends = carry
        ends = ends + kap[i] * r
        nxt = cols[row_of(i + 1), :] + tau[i] * r
        cols[row_of(i + 1), :] = nxt
        return nxt, ends

    r, ends = lax.fori_loop(1, nyl - 1, down, (cols[row_of(1), :], cols[row_of(0), :]))
    ends = ends + kap[nyl - 1] * r
    over = tau[nyl - 1] * r
    for j in range(npy):
        isnd[j, 0:kown, :] = ends[j * kown:(j + 1) * kown]
        isnd[j, kown:2 * kown, :] = over[j * kown:(j + 1) * kown]

    spread(npy, at_y, lambda r: isnd.at[at_y(r)[1]], ircv.at[me_y], i_send.at[0], i_recv.at[0])
    ircv[me_y] = isnd[me_y]
    settle(ircv.at[others_y], i_send.at[0], i_recv.at[0])

    rho = []
    for b in range(npy):
        value = ircv[b, 0:kown, :]
        if b > 0:
            value = value + ircv[b - 1, kown:2 * kown, :]
        rho.append(value)
    depth_mode = lax.broadcasted_iota(jnp.int32, (kown, nx), 0) + me_x * kzl + me_y * kown
    row_mode = lax.broadcasted_iota(jnp.int32, (kown, nx), 1)
    mean = sum(rho[1:], rho[0]) * (1.0 / (npy * nyl))
    mean = jnp.where((depth_mode == 0) & (row_mode == 0), mean, 0.0)
    half_sum = (nyl - 1) / 2.0
    for b in range(npy):
        weight = 1.0 + (0.0 if b == 0 else half_sum) + (2.0 * half_sum if b == npy - 1 else half_sum)
        rho[b] = rho[b] - weight * mean
    for b in range(npy - 1):
        rho[b + 1] = rho[b + 1] + owner_phi[b] * rho[b]
    value = -owner_inv[npy - 1] * rho[npy - 1]
    jsnd[npy - 1, 0:kown, :] = value
    jsnd[npy - 1, kown:2 * kown, :] = jnp.zeros_like(value)
    jsnd[npy - 1, 2 * kown:3 * kown, :] = mean
    for b in range(npy - 2, -1, -1):
        jsnd[b, kown:2 * kown, :] = value
        value = owner_phi[b] * value - owner_inv[b] * rho[b]
        jsnd[b, 0:kown, :] = value
        jsnd[b, 2 * kown:3 * kown, :] = mean

    spread(npy, at_y, lambda r: jsnd.at[at_y(r)[1]], jrcv.at[me_y], i_send.at[1], i_recv.at[1])
    jrcv[me_y] = jsnd[me_y]
    settle(jrcv.at[others_y], i_send.at[1], i_recv.at[1])
    for j in range(npy):
        for part in range(3):
            back[part, j * kown:(j + 1) * kown, :] = jrcv[j, part * kown:(part + 1) * kown, :]
    first_value, mean_rows = back[0], back[2]

    def up_piece(n, q):
        c = pieces - 1 - n

        def up_again(m, q):
            i = c * per + per - 1 - m
            share = 0.5 * (i + 1).astype(F32)
            q = tau[i] * (q - cols[row_of(i), :] + mean_rows * share) + kap[i] * first_value
            cols[row_of(i), :] = q
            return q

        q = lax.fori_loop(0, per, up_again, q)
        rows = piece_rows(c)
        cols[rows, :] = dot_parts(split(cols[rows, :], 3), (tx[0], tx[1], tx[2]), ((1,), (0,)))

        def scatter(sg, inner):
            for half in range(per // 4):
                parts = []
                for b in range(4):
                    y = c * per + 4 * half + b
                    parts.append(cols[row_of(y), pl.ds(pl.multiple_of(sg * HALF, HALF), HALF)])
                out = swap_groups(parts)
                for a in range(4):
                    msg[4 * sg + a, c, :, half * HALF:(half + 1) * HALF] = out[a]
            return inner

        lax.fori_loop(0, wides, scatter, 0)
        n = pieces + c
        spread(npx, at_x, lambda r: msg.at[at_x(r)[0], c], got2.at[me_x, c], a_send.at[n], a_recv.at[n])
        return q

    lax.fori_loop(0, pieces, up_piece, back[1])

    pressure = qp.reshape(halves, (nxl + 2) * wide, HALF)

    def rise_piece(n, carry):
        c = pieces - 1 - n
        got2[me_x, c] = msg[me_x, c]
        settle(got2.at[others_x, c], a_send.at[pieces + c], a_recv.at[pieces + c])
        value = got2[:, c].reshape(nz, 256)
        out = dot_parts(split(value.T, 3), (tz[0], tz[1], tz[2]), ((1,), (0,)))
        for y in range(per):
            for h in range(halves):
                pressure[h, pl.ds(wide + 8 + c * per + y, nxl, stride=wide), :] = out[
                    y * nxl:(y + 1) * nxl, h * HALF:(h + 1) * HALF
                ]
        return carry

    lax.fori_loop(0, pieces, rise_piece, 0)

    for h in range(halves):
        qy_snd[0, h] = row_at(qp, (h,), top - 1)[...]
        qy_snd[1, h] = row_at(qp, (h,), 8)[...]
    halo = y_pair(qy_snd, qy_rcv, 4) + x_pair(qp, lambda field, x: field.at[:, x, pl.ds(8, nyl), :], 6)
    for copy in halo:
        copy.start()

    def q_rows(x, y, size):
        return jnp.concatenate([qp[h, x, y:y + size, :] for h in range(halves)], axis=1)

    def join(field, x):
        return jnp.concatenate([field[h, x, 0:nyl, :] for h in range(halves)], axis=1)

    def flow(a, x):
        return jnp.concatenate([up[a, h, x + 1, 8:top, :] for h in range(halves)], axis=1)

    def two_parts(x, carry):
        center = q_rows(x + 1, 8, nyl)
        spot = lax.broadcasted_iota(jnp.int32, center.shape, 1)
        below = jnp.where(spot == 0, center, pltpu.roll(center, 1, 1))
        above = jnp.where(spot == nz - 1, center, pltpu.roll(center, nz - 1, 1))
        v2 = join(w2, x) - 0.5 * (above - below)
        v0 = join(w0, x + 1) - 0.5 * (q_rows(x + 2, 8, nyl) - q_rows(x, 8, nyl))
        vel[0, x] = v0
        vel[2, x] = v2
        total = flow(0, x) * v0 + flow(2, x) * v2
        for h in range(halves):
            sig[h, pl.ds(pl.multiple_of(x * nyl, 8), nyl), :] = total[:, h * HALF:(h + 1) * HALF]
        return carry

    lax.fori_loop(1, nxl - 1, two_parts, 0)
    outs = [pltpu.make_async_copy(vel.at[b], v_out.at[b], out_sem.at[b]) for b in range(3)]

    for copy in halo:
        copy.wait()
    for h in range(halves):
        row_at(qp, (h,), 7)[...] = jnp.where(first_y, qy_snd[1, h], qy_rcv[0, h])
        row_at(qp, (h,), top)[...] = jnp.where(last_y, qy_snd[0, h], qy_rcv[1, h])

    @pl.when(first_x)
    def _():
        for h in range(halves):
            qp[h, 0, 8:top, :] = qp[h, 1, 8:top, :]

    @pl.when(last_x)
    def _():
        for h in range(halves):
            qp[h, nxl + 1, 8:top, :] = qp[h, nxl, 8:top, :]

    two_parts(0, 0)
    two_parts(nxl - 1, 0)
    outs[0].start()
    outs[2].start()

    def last_part(x, carry):
        tall = q_rows(x + 1, 0, wide)
        deep = jnp.concatenate([w1[h, x + 1, 8:top, :] for h in range(halves)], axis=1)
        v1 = deep - 0.5 * (tall[9:top + 1] - tall[7:top - 1])
        vel[1, x] = v1
        rows = pl.ds(pl.multiple_of(x * nyl, 8), nyl)
        part = flow(1, x) * v1
        for h in range(halves):
            sig[h, rows, :] = -ALPHA * (sig[h, rows, :] + part[:, h * HALF:(h + 1) * HALF])
        return carry

    lax.fori_loop(0, nxl, last_part, 0)
    outs[1].start()

    picked = None
    for h in range(halves):
        for part in reversed(split(sig[h], 2)):
            term = jnp.dot(hot[h], part, preferred_element_type=F32)
            picked = term if picked is None else picked + term
    settle(fetched.at[others_x], r_send.at[3], r_recv.at[3])
    products = picked * fetched[...].reshape(places, SEG)
    ones = jnp.ones((8, SEG), BF16)
    totals = sum(
        lax.dot_general(ones, part, (((1,), (1,)), ((), ())), preferred_element_type=F32)
        for part in reversed(split(products, 3))
    )
    by_px(totals, give)
    spread(npx, at_x, lambda r: give.at[at_x(r)[0]], given.at[me_x], r_send.at[4], r_recv.at[4])
    given[me_x] = give[me_x]
    settle(given.at[others_x], r_send.at[4], r_recv.at[4])
    by_py(given[:, 0, :], gives)
    spread(npy, at_y, lambda r: gives.at[at_y(r)[1]], taken.at[me_y], r_send.at[5], r_recv.at[5])
    taken[me_y] = gives[me_y]
    settle(taken.at[others_y], r_send.at[5], r_recv.at[5])

    def add_up(j, total):
        label, value = wanted[j], taken[j]
        for r in range(2):
            spot = slice(r * npy, r * npy + 1)
            hit = jnp.broadcast_to(label[:, spot], (npx, HALF)) == slot_lane
            total = total + jnp.where(hit, jnp.broadcast_to(value[:, spot], (npx, HALF)), 0.0)
        return total

    total = lax.fori_loop(0, npy, add_up, jnp.zeros((npx, HALF), F32))
    grad_out[...] = jnp.sum(total, axis=0, keepdims=True)[:, :controls]
    for copy in outs:
        copy.wait()


def main_call(dims, args, owner_rows):
    npx, npy, nxl, nyl, nz = dims
    nx = npx * nxl
    kzl = nz // npx
    kown = kzl // npy
    halves = nz // HALF
    wide = nyl + 16
    cells = nxl * nyl
    pieces = cells // 256
    places = 2 * npx * npy
    vmem = pltpu.VMEM
    anywhere = pl.BlockSpec(memory_space=pl.ANY)
    here = pl.BlockSpec(memory_space=pltpu.VMEM)
    scalar = pl.BlockSpec(memory_space=pltpu.SMEM)
    dma = pltpu.SemaphoreType.DMA
    tables = args[10:13]
    field = vmem((3, halves, nxl + 2, wide, HALF), F32)
    line = vmem((nyl, kzl, nx), F32)
    message = vmem((npx, pieces, kzl, 256), F32)
    scratch = [
        field,
        field,
        vmem((3, cells, nz), BF16),
        vmem((3, cells, nz), BF16),
        vmem((nxl, nyl, nz), jnp.int32),
        vmem((nxl, nyl, HALF), jnp.int32),
        vmem((halves, nxl + 2, nyl, HALF), F32),
        vmem((halves, nxl + 2, wide, HALF), F32),
        vmem((halves, nxl, nyl, HALF), F32),
        vmem((2, 6, halves, nxl, HALF), BF16),
        vmem((2, 6, halves, nxl, HALF), BF16),
        vmem((2, halves, nxl, HALF), F32),
        vmem((2, halves, nxl, HALF), F32),
        vmem((2, OUTLETS, HALF), F32),
        vmem((npx, OUTLETS, HALF), F32),
        vmem((npy, OUTLETS, HALF), F32),
        vmem((halves, cells, HALF), F32),
        message,
        message,
        message,
        vmem((nyl * kzl, nx), F32),
        line,
        line,
        vmem((npy, kown, nx), F32),
        vmem((npy, kown, nx), F32),
        vmem((npy, 2 * kown, nx), F32),
        vmem((npy, 2 * kown, nx), F32),
        vmem((npy, 3 * kown, nx), F32),
        vmem((npy, 3 * kown, nx), F32),
        vmem((3, kzl, nx), F32),
        vmem((halves, nxl + 2, wide, HALF), F32),
        vmem((2, halves, nxl, HALF), F32),
        vmem((2, halves, nxl, HALF), F32),
        vmem((3, nxl, nyl, nz), F32),
        vmem((halves, cells, HALF), F32),
        vmem((nyl, nx), F32),
        vmem((halves, places, cells), BF16),
        vmem((places, 1), jnp.int32),
        vmem((npx, 8 + nyl, HALF), F32),
        vmem((npx, 8 + nyl, HALF), F32),
        vmem((npy, npx, HALF), F32),
        vmem((npy, npx, HALF), F32),
        vmem((places, HALF), BF16),
        vmem((npy, 2 * npx, SEG), F32),
        vmem((npy, 2 * npx, SEG), F32),
        vmem((npx, 2 * npy, SEG), F32),
        vmem((npx, 2 * npy, SEG), F32),
        vmem((npx, 8, HALF), F32),
        vmem((npx, 8, HALF), F32),
        vmem((npy, npx, HALF), F32),
        vmem((npy, npx, HALF), F32),
    ]
    scratch += [vmem(t.shape, BF16) for t in tables]
    scratch += [
        dma((3 * halves + 3 + len(tables),)),
        dma((8,)),
        dma((8,)),
        dma((6,)),
        dma((6,)),
        dma((2,)),
        dma((2,)),
        dma((2 * pieces,)),
        dma((2 * pieces,)),
        dma((2,)),
        dma((2,)),
        dma((6,)),
        dma((6,)),
        dma((3,)),
    ]
    return pl.pallas_call(
        functools.partial(main_kernel, dims),
        out_shape=(
            jax.ShapeDtypeStruct((3, nxl, nyl, nz), F32),
            jax.ShapeDtypeStruct((1, owner_rows), F32),
        ),
        in_specs=[anywhere] * 4 + [here, scalar] + [here] * 4 + [anywhere] * len(tables) + [here] * 2,
        out_specs=(anywhere, here),
        scratch_shapes=scratch,
        compiler_params=pltpu.CompilerParams(
            collective_id=0, has_side_effects=True, vmem_limit_bytes=58 * 2**20
        ),
        name="project",
    )(*args)


def local(
    base_flow, adjoint_start, source, solid_mask, outlet_ids, resist,
    tile_owner, tile_slot, tile_column, control_basis,
):
    _, nxl, nyl, nz = adjoint_start.shape
    npx, npy = lax.axis_size("px"), lax.axis_size("py")
    nx = npx * nxl
    tz, tx = table_np(nz), table_np(nx)
    tables = [split_np(tz, 3), split_np(tx, 3), split_np(np.ascontiguousarray(tx.T), 2)]
    tables = [jnp.asarray(np.stack(t)) for t in tables]
    lam_x = jnp.asarray(-eigen_np(nx)[None, :])
    depth = np.zeros((nz, HALF), np.float32)
    depth[:, 0] = -eigen_np(nz)
    depth[:, 1] = -0.5 * DT * tz[:, nz - 2]
    depth = jnp.asarray(depth)
    args = (
        adjoint_start,
        base_flow.reshape(3, nxl * nyl, nz),
        source.reshape(3, nxl * nyl, nz),
        solid_mask,
        outlet_ids.T,
        resist,
        tile_owner.reshape(1, -1),
        tile_slot.reshape(1, -1),
        tile_column.reshape(1, -1),
        control_basis,
        *tables,
        lam_x,
        depth,
    )
    velocity, grad = main_call((npx, npy, nxl, nyl, nz), args, control_basis.shape[0])
    return velocity, grad.reshape(-1)


def solution(mesh):
    in_specs = (
        P(None, "px", "py", None),
        P(None, "px", "py", None),
        P(None, "px", "py", None),
        P("px", "py", None),
        P("px", "py"),
        P(),
        P(("px", "py"), None),
        P(("px", "py")),
        P(("px", "py")),
        P(("px", "py"), None),
    )
    out_specs = (P(None, "px", "py", None), P(("px", "py")))
    return jax.shard_map(local, mesh=mesh, in_specs=in_specs, out_specs=out_specs, check_vma=False)
```

```python
import functools
import math

import jax
import jax.numpy as jnp
import numpy as np
from jax import lax
from jax.experimental import pallas as pl
from jax.experimental.pallas import tpu as pltpu
from jax.sharding import PartitionSpec as P

SEG = 128
OUTLETS = 8
DT = 0.1
NU = 0.5
ALPHA = 5.0
HALF = 128
MESH = pl.DeviceIdType.MESH
F32 = jnp.float32
BF16 = jnp.bfloat16


def table_np(count):
    order = np.arange(count).astype(np.float32)
    modes = order[:, None]
    points = order[None, :]
    weights = np.where(modes == 0.0, math.sqrt(1.0 / count), math.sqrt(2.0 / count)).astype(np.float32)
    angle = np.float32(np.pi) * (points + np.float32(0.5)) * modes / np.float32(count)
    return (weights * np.cos(angle.astype(np.float32))).astype(np.float32)


def eigen_np(count):
    order = np.arange(count).astype(np.float32)
    angle = (np.float32(np.pi) * order / np.float32(count)).astype(np.float32)
    return (np.float32(2.0) * np.cos(angle) - np.float32(2.0)).astype(np.float32)


def split_np(table, count):
    parts = []
    for _ in range(count):
        parts.append(table.astype(jnp.bfloat16))
        table = table - parts[-1].astype(np.float32)
    return tuple(parts)


def split(value, count):
    parts = []
    for _ in range(count):
        parts.append(value.astype(BF16))
        value = value - parts[-1].astype(F32)
    return tuple(parts)


def dot_parts(a_parts, b_parts, contract):
    dims = ((contract[0], contract[1]), ((), ()))
    dot = functools.partial(lax.dot_general, dimension_numbers=dims, preferred_element_type=F32)
    total = None
    for order in range(len(a_parts) - 1, -1, -1):
        for i in range(order + 1):
            term = dot(a_parts[i], b_parts[order - i])
            total = term if total is None else total + term
    return total


def swap_groups(tiles):
    lane = lax.broadcasted_iota(jnp.int32, tiles[0].shape, 1)
    odd = (lane // 32) % 2 == 1
    far = lane >= 64
    t0, t1, t2, t3 = tiles
    a0 = jnp.where(odd, pltpu.roll(t1, 32, 1), t0)
    a1 = jnp.where(odd, t1, pltpu.roll(t0, 96, 1))
    a2 = jnp.where(odd, pltpu.roll(t3, 32, 1), t2)
    a3 = jnp.where(odd, t3, pltpu.roll(t2, 96, 1))
    return (
        jnp.where(far, pltpu.roll(a2, 64, 1), a0),
        jnp.where(far, pltpu.roll(a3, 64, 1), a1),
        jnp.where(far, a2, pltpu.roll(a0, 64, 1)),
        jnp.where(far, a3, pltpu.roll(a1, 64, 1)),
    )


def z_shift(field, edge_low, edge_high):
    depth = field.shape[1]
    lane = lax.broadcasted_iota(jnp.int32, field.shape, 1)
    below = jnp.where(lane == 0, edge_low, pltpu.roll(field, 1, 1))
    above = jnp.where(lane == depth - 1, edge_high, pltpu.roll(field, depth - 1, 1))
    return below, above


def main_kernel(
    dims,
    v_hbm, u_hbm, s_hbm, m_hbm, ids, resist, owner_row, slot_row, column_row, basis,
    tz_hbm, tx_hbm, tt_hbm, lam_x, lam_z,
    v_out, grad_out,
    vp, up, ub, sb, mk, idb, w0, w1, w2, snd_y, rcv_y, wy_snd, wy_rcv, fsum, fr1, fr2,
    div, msg, got, got2, relay, relay2, cols, tau, kap, owner_inv, owner_phi,
    isnd, ircv, jsnd, jrcv, back, qp, qy_snd, qy_rcv, vel, sig,
    outlet, hot, pick, ask, asked, asks, wanted, chosen, reply, replies, fetch, fetched, give, given, gives, taken,
    tz, tx, tt,
    load_sem, x_send, x_recv, y_send, y_recv, f_send, f_recv, a_send, a_recv, b_send, b_recv, c_send, i_send, i_recv, r_send, r_recv, out_sem,
):
    npx, npy, nxl, nyl, nz = dims
    nx = npx * nxl
    kzl = nz // npx
    kown = kzl // npy
    halves = nz // HALF
    cells = nxl * nyl
    per = 256 // nxl
    pieces = nyl // per
    group = 2 * npy
    places = npx * group
    me_x = lax.axis_index("px")
    me_y = lax.axis_index("py")
    right_x, left_x = lax.rem(me_x + 1, npx), lax.rem(me_x + npx - 1, npx)
    right_y, left_y = lax.rem(me_y + 1, npy), lax.rem(me_y + npy - 1, npy)
    first_x, last_x = me_x == 0, me_x == npx - 1
    first_y, last_y = me_y == 0, me_y == npy - 1
    top = 8 + nyl
    wide = nyl + 16

    def run(first, last, action):
        def body(r, carry):
            action(r)
            return carry

        lax.fori_loop(first, last, body, 0)

    def remote(src, dst, send, recv, target):
        return pltpu.make_async_remote_copy(
            src_ref=src, dst_ref=dst, send_sem=send, recv_sem=recv, device_id=target, device_id_type=MESH
        )

    def at_x(r):
        return (lax.rem(me_x + r, npx), me_y)

    def at_y(r):
        return (me_x, lax.rem(me_y + r, npy))

    def spread(count, target, src, dst, send, recv):
        run(1, count, lambda r: remote(src(r), dst, send, recv, target(r)).start())

    def settle(like, send, recv):
        pltpu.make_async_copy(like, like, send).wait()
        pltpu.make_async_copy(like, like, recv).wait()

    others_x, others_y = pl.ds(0, npx - 1), pl.ds(0, npy - 1)

    ring = npx // 2
    ring_at = lax.rem(me_x, ring)
    before_x = me_x - ring_at + lax.rem(ring_at + ring - 2, ring)
    after_x = me_x - ring_at + lax.rem(ring_at + 2, ring)
    far_same = ring // 2
    far_other = jnp.where(lax.rem(me_x, 2) == 0, far_same + 1, far_same - 1)
    hops = ((before_x, after_x, far_same), (after_x, before_x, far_other))
    direct_x = pl.ds(0, npx - 5)

    def exchange(c, source, relay, sink, n):
        for way, (through, _, far) in enumerate(hops):
            for k in range(2):
                p = lax.rem(me_x + far + k * ring, npx)
                remote(
                    source.at[p, c], relay.at[2 * way + k, c], b_send.at[n], b_recv.at[n], (through, me_y)
                ).start()

        def start(r):
            step = lax.rem(r, ring)

            @pl.when((step != far_same) & (step != far_other))
            def _():
                remote(source.at[at_x(r)[0], c], sink.at[me_x, c], a_send.at[n], a_recv.at[n], at_x(r)).start()

        run(1, npx, start)

    def forward(c, relay, sink, n):
        pltpu.make_async_copy(relay.at[:, c], relay.at[:, c], b_recv.at[n]).wait()
        for way, (_, origin, far) in enumerate(hops):
            for k in range(2):
                p = lax.rem(origin + far + k * ring, npx)
                remote(
                    relay.at[2 * way + k, c], sink.at[origin, c], c_send.at[n], a_recv.at[n], (p, me_y)
                ).start()

    def complete(c, relay, sink, n):
        pltpu.make_async_copy(sink.at[direct_x, c], sink.at[direct_x, c], a_send.at[n]).wait()
        pltpu.make_async_copy(relay.at[:, c], relay.at[:, c], b_send.at[n]).wait()
        pltpu.make_async_copy(relay.at[:, c], relay.at[:, c], c_send.at[n]).wait()
        pltpu.make_async_copy(sink.at[others_x, c], sink.at[others_x, c], a_recv.at[n]).wait()

    loads = []
    for c in range(3):
        for h in range(halves):
            loads.append(
                pltpu.make_async_copy(
                    v_hbm.at[c, :, :, pl.ds(h * HALF, HALF)],
                    vp.at[c, h, pl.ds(1, nxl), pl.ds(8, nyl), :],
                    load_sem.at[c * halves + h],
                )
            )
    base = 3 * halves
    load_u = pltpu.make_async_copy(u_hbm, ub, load_sem.at[base])
    load_s = pltpu.make_async_copy(s_hbm, sb, load_sem.at[base + 1])
    load_m = pltpu.make_async_copy(m_hbm, mk, load_sem.at[base + 2])
    load_t = [
        pltpu.make_async_copy(a, b, load_sem.at[base + 3 + n])
        for n, (a, b) in enumerate(((tz_hbm, tz), (tx_hbm, tx), (tt_hbm, tt)))
    ]
    for copy in loads:
        copy.start()
    load_u.start()
    load_s.start()
    load_m.start()
    for copy in load_t:
        copy.start()

    barrier = pltpu.get_barrier_semaphore()
    run(1, npx, lambda r: pl.semaphore_signal(barrier, inc=1, device_id=at_x(r), device_id_type=MESH))
    run(1, npy, lambda r: pl.semaphore_signal(barrier, inc=1, device_id=at_y(r), device_id_type=MESH))

    def row_at(ref, lead, y):
        lines = ref.reshape(*ref.shape[:-3], (nxl + 2) * wide, HALF)
        return lines.at[(*lead, pl.ds(wide + y, nxl, stride=wide), slice(None))]

    def x_pair(field, at, number):
        return (
            remote(at(field, nxl), at(field, 0), x_send.at[number], x_recv.at[number], (right_x, me_y)),
            remote(at(field, 1), at(field, nxl + 1), x_send.at[number + 1], x_recv.at[number + 1], (left_x, me_y)),
        )

    def at_plane(field, x):
        return field.at[:, :, x, pl.ds(8, nyl), :]

    def y_pair(send, recv, number):
        return (
            remote(send.at[0], recv.at[0], y_send.at[number], y_recv.at[number], (me_x, right_y)),
            remote(send.at[1], recv.at[1], y_send.at[number + 1], y_recv.at[number + 1], (me_x, left_y)),
        )

    for copy in loads:
        copy.wait()

    def pack(field, first):
        for c in range(3):
            for h in range(halves):
                snd_y[0, first + c, h] = row_at(field, (c, h), top - 1)[...].astype(BF16)
                snd_y[1, first + c, h] = row_at(field, (c, h), 8)[...].astype(BF16)

    pack(vp, 0)
    load_u.wait()

    def widen(i, carry):
        for a in range(3):
            pair = ub[a, pl.ds(pl.multiple_of(i * 2 * nyl, 2 * nyl), 2 * nyl), :].astype(F32)
            for s in range(2):
                for h in range(halves):
                    up[a, h, 1 + 2 * i + s, 8:top, :] = pair[s * nyl:(s + 1) * nyl, h * HALF:(h + 1) * HALF]
        return carry

    lax.fori_loop(0, nxl // 2, widen, 0)
    pack(up, 3)
    pl.semaphore_wait(barrier, npx - 1 + npy - 1)
    halo = y_pair(snd_y, rcv_y, 0) + x_pair(vp, at_plane, 0) + x_pair(up, at_plane, 2)
    for copy in halo:
        copy.start()

    count = owner_row.shape[1]
    owners = owner_row[...]
    same = jnp.broadcast_to(owners, (8, count)).T[:, 0:1] == owners
    earlier = lax.broadcasted_iota(jnp.int32, (count, count), 0) < lax.broadcasted_iota(
        jnp.int32, (count, count), 1
    )
    rank = jnp.sum(jnp.where(same & earlier, 1, 0), axis=0, keepdims=True)
    owner_x = owners // npy
    place = owner_x * group + rank * npy + (owners - owner_x * npy)
    match = lax.broadcasted_iota(jnp.int32, (places, count), 0) == place
    pick[...] = jnp.sum(jnp.where(match, column_row[...] + 1, 0), axis=1, keepdims=True) - 1
    slots = jnp.broadcast_to((slot_row[...] + 1).astype(F32), (8, count)).astype(BF16)
    requests = (
        lax.dot_general(
            slots, match.astype(F32).astype(BF16), (((1,), (1,)), ((), ())), preferred_element_type=F32
        )
        - 1.0
    )

    def pad_lanes(row):
        if row.shape[1] >= HALF:
            return row
        return jnp.concatenate([row, jnp.zeros((8, HALF - row.shape[1]), F32)], axis=1)

    def by_px(row, ref):
        row = pad_lanes(row)
        lanes = row.shape[1]
        for p in range(npx):
            ref[p, 0:8, :] = pltpu.roll(row, (lanes - group * p) % lanes, 1)[:, :HALF]

    def by_py(rows, ref):
        for j in range(npy):
            ref[j] = pltpu.roll(rows, (HALF - j) % HALF, 1)

    by_px(requests, ask)
    seen = ids[...]
    padded = jnp.concatenate([seen.astype(F32), jnp.zeros((nyl, HALF - nxl), F32)], axis=1)
    for p in range(npx):
        ask[p, 8:top, :] = padded
    for x in range(nxl):
        idb[x] = jnp.broadcast_to(seen[:, x:x + 1], (nyl, HALF))

    def ask_start():
        spread(npx, at_x, lambda r: ask.at[at_x(r)[0]], asked.at[me_x], r_send.at[0], r_recv.at[0])
        asked[me_x] = ask[me_x]

    ask_start()

    def reduce_cell(c, g, right):
        inv = 1.0 / (c + right + g)
        return inv, c * inv

    mine = lam_z[pl.ds(pl.multiple_of(me_x * kzl, kzl), kzl), 0:1]
    mu = lam_x[...] + mine
    owned = lam_z[pl.ds(me_x * kzl + me_y * kown, kown), 0:1]
    muo = lam_x[...] + owned

    def owner_table():
        def owner_cell(i, carry):
            c, g, ground = carry
            inv, k = reduce_cell(c, g, 1.0)
            return k, muo + g * inv, ground + k * g

        one = jnp.ones_like(muo)
        c, g, ground = lax.fori_loop(1, nyl - 1, owner_cell, (one, muo, jnp.zeros_like(one)))
        inv, link = reduce_cell(c, g, 1.0)
        from_left = g * inv
        end_ground = muo + from_left + (ground + c * (g / (c + g)))
        ground = ground + link * g
        held = muo + ground
        for b in range(npy - 1):
            inv = 1.0 / (link + held)
            phi = link * inv
            owner_inv[b] = inv
            owner_phi[b] = phi
            nxt = end_ground if b == npy - 2 else muo + ground + from_left
            held = nxt + phi * held
        positive = held > 0.0
        owner_inv[npy - 1] = jnp.where(positive, 1.0 / jnp.where(positive, held, 1.0), 0.0)

    owner_table()
    settle(asked.at[others_x], r_send.at[0], r_recv.at[0])
    by_py(asked[:, 0, :], asks)
    spread(npy, at_y, lambda r: asks.at[at_y(r)[1]], wanted.at[me_y], r_send.at[1], r_recv.at[1])
    wanted[me_y] = asks[me_y]
    load_s.wait()
    load_m.wait()
    for copy in halo:
        copy.wait()

    for c in range(3):
        for h in range(halves):
            for field, first in ((vp, 0), (up, 3)):
                low, high = rcv_y[0, first + c, h].astype(F32), rcv_y[1, first + c, h].astype(F32)
                row_at(field, (c, h), 7)[...] = jnp.where(first_y, 0.0, low)
                row_at(field, (c, h), top)[...] = jnp.where(last_y, 0.0, high)
    edge = jnp.zeros((nyl, HALF), F32)

    @pl.when(first_x)
    def _():
        for c in range(3):
            for h in range(halves):
                vp[c, h, 0, 8:top, :] = edge
                up[c, h, 0, 8:top, :] = edge

    @pl.when(last_x)
    def _():
        for c in range(3):
            for h in range(halves):
                vp[c, h, nxl + 1, 8:top, :] = edge
                up[c, h, nxl + 1, 8:top, :] = edge

    def tall_rows(field, c, x, y):
        return jnp.concatenate([field[c, h, x, y:y + 24, :] for h in range(halves)], axis=1)

    def tile_rows(field, c, x, y):
        return jnp.concatenate([field[c, h, x, y + 8:y + 16, :] for h in range(halves)], axis=1)

    tiles = nyl // 8

    def predict(i, carry):
        for k in range(tiles):
            rows = pl.ds(pl.multiple_of(i * 2 * nyl + 16 * k, 16), 16)
            forcing = [sb[b, rows, :].astype(F32) for b in range(3)]
            for s in range(2):
                n = 2 * k + s
                x = 2 * i + n // tiles
                y = 8 * (n % tiles)
                scale = 1.0 / (1.0 + (DT * ALPHA) * mk[x, y:y + 8, :].astype(F32))
                u, v, tall_v = [], [], []
                slopes = [None] * 3
                for a in range(3):
                    tall = tall_rows(up, a, x + 1, y)
                    tall_v.append(tall_rows(vp, a, x + 1, y))
                    u.append(tall[8:16])
                    v.append(tall_v[a][8:16])
                    below, above = z_shift(u[a], 0.0, 0.0)
                    diffs = (
                        tile_rows(up, a, x + 2, y) - tile_rows(up, a, x, y),
                        tall[9:17] - tall[7:15],
                        above - below,
                    )
                    for b in range(3):
                        term = v[a] * diffs[b]
                        slopes[b] = term if slopes[b] is None else slopes[b] + term
                for b in range(3):
                    tall = tall_v[b]
                    xm, xp = tile_rows(vp, b, x, y), tile_rows(vp, b, x + 2, y)
                    ym, yp = tall[7:15], tall[9:17]
                    zm, zp = z_shift(v[b], 0.0, 0.0)
                    convect = u[0] * (xp - xm) + u[1] * (yp - ym) + u[2] * (zp - zm)
                    lap = (xp + xm) + (yp + ym) + (zp + zm) - 6.0 * v[b]
                    change = 0.5 * (convect - slopes[b]) + NU * lap + forcing[b][8 * s:8 * s + 8]
                    w = (v[b] + DT * change) * scale
                    for h in range(halves):
                        part = w[:, h * HALF:(h + 1) * HALF]
                        if b == 0:
                            w0[h, x + 1, y:y + 8, :] = part
                        elif b == 1:
                            w1[h, x + 1, y + 8:y + 16, :] = part
                        else:
                            w2[h, x, y:y + 8, :] = part
        return carry

    lax.fori_loop(0, nxl // 2, predict, 0)

    for h in range(halves):
        wy_snd[0, h] = row_at(w1, (h,), top - 1)[...]
        wy_snd[1, h] = row_at(w1, (h,), 8)[...]
    halo = y_pair(wy_snd, wy_rcv, 2) + x_pair(w0, lambda field, x: field.at[:, x], 4)
    for copy in halo:
        copy.start()

    settle(wanted.at[others_y], r_send.at[1], r_recv.at[1])

    slot_lane = lax.broadcasted_iota(jnp.int32, (npx, HALF), 1).astype(F32)

    def choose(j, carry):
        label = wanted[j]
        for r in range(2):
            hit = jnp.broadcast_to(label[:, r * npy:r * npy + 1], (npx, HALF)) == slot_lane
            chosen[pl.ds(pl.multiple_of((2 * j + r) * npx, npx), npx), :] = hit.astype(F32).astype(BF16)
        return carry

    lax.fori_loop(0, npy, choose, 0)
    controls = basis.shape[0]
    wide_basis = jnp.concatenate([basis[...], jnp.zeros((HALF - controls, SEG), F32)], axis=0)
    rows = sum(
        jnp.dot(chosen[...], part, preferred_element_type=F32) for part in reversed(split(wide_basis, 3))
    )
    for j in range(npy):
        reply[j] = rows[j * 2 * npx:(j + 1) * 2 * npx]
    spread(npy, at_y, lambda r: reply.at[at_y(r)[1]], replies.at[me_y], r_send.at[2], r_recv.at[2])
    replies[me_y] = reply[me_y]

    lane = lax.broadcasted_iota(jnp.int32, (nyl, HALF), 1)

    def flux_plane(x, carry):
        face = jnp.where(lane == HALF - 1, w2[halves - 1, x], 0.0)
        which = idb[x]
        return tuple(total + jnp.where(which == k, face, 0.0) for k, total in enumerate(carry))

    zero = jnp.zeros((nyl, HALF), F32)
    totals = lax.fori_loop(0, nxl, flux_plane, (zero,) * OUTLETS)
    fsum[0] = jnp.concatenate([jnp.sum(t, axis=0, keepdims=True) for t in totals], axis=0)

    spread(npx, at_x, lambda r: fsum.at[0], fr1.at[me_x], f_send.at[0], f_recv.at[0])
    fr1[me_x] = fsum[0]

    for copy in halo:
        copy.wait()
    for h in range(halves):
        row_at(w1, (h,), 7)[...] = jnp.where(first_y, 0.0, wy_rcv[0, h])
        row_at(w1, (h,), top)[...] = jnp.where(last_y, 0.0, wy_rcv[1, h])

    @pl.when(first_x)
    def _():
        for h in range(halves):
            w0[h, 0] = edge

    @pl.when(last_x)
    def _():
        for h in range(halves):
            w0[h, nxl + 1] = edge

    def diverge(x, carry):
        deep = jnp.concatenate([w2[h, x] for h in range(halves)], axis=1)
        below, above = z_shift(deep, 0.0, 0.0)
        for h in range(halves):
            cut = slice(h * HALF, (h + 1) * HALF)
            tall = w1[h, x + 1]
            total = (w0[h, x + 2] - w0[h, x]) + (tall[9:top + 1] - tall[7:top - 1]) + (above - below)[:, cut]
            div[h, pl.ds(x, nyl, stride=nxl), :] = 0.5 * total
        return carry

    lax.fori_loop(0, nxl, diverge, 0)

    for copy in load_t:
        copy.wait()

    def depth_piece(c, carry):
        here = pl.ds(pl.multiple_of(c * 256, 256), 256)
        value = jnp.concatenate([div[h, here, :] for h in range(halves)], axis=1)
        out = dot_parts((tz[0], tz[1]), split(value, 2), ((1,), (1,)))
        for p in range(npx):
            msg[p, c] = out[p * kzl:(p + 1) * kzl]
        exchange(c, msg, relay, got, c)
        return carry

    lax.fori_loop(0, pieces, depth_piece, 0)
    run(0, pieces, lambda c: forward(c, relay, got, c))

    settle(fr1.at[others_x], f_send.at[0], f_recv.at[0])
    fsum[1] = jnp.sum(fr1[...], axis=0)
    spread(npy, at_y, lambda r: fsum.at[1], fr2.at[me_y], f_send.at[1], f_recv.at[1])
    fr2[me_y] = fsum[1]
    settle(replies.at[others_y], r_send.at[2], r_recv.at[2])
    lines = replies.reshape(npy * 2 * npx, SEG)
    for p in range(npx):
        for r in range(2):
            fetch[p, r * npy:(r + 1) * npy, :] = lines[pl.ds(r * npx + p, npy, stride=2 * npx), :]
    spread(npx, at_x, lambda r: fetch.at[at_x(r)[0]], fetched.at[me_x], r_send.at[3], r_recv.at[3])
    fetched[me_x] = fetch[me_x]

    def table_cell(i, carry):
        c, g = carry
        right = jnp.where((i == nyl - 1) & last_y, 0.0, 1.0)
        inv, k = reduce_cell(c, g, right)
        tau[i] = inv
        kap[i] = k
        return k, mu + g * inv

    tau[0] = jnp.zeros_like(mu)
    kap[0] = jnp.ones_like(mu)
    lax.fori_loop(1, nyl, table_cell, (jnp.ones_like(mu), mu))

    shape = (places, cells)
    cell = lax.broadcasted_iota(jnp.int32, shape, 1) * halves
    for h in range(halves):
        hot[h] = (jnp.broadcast_to(pick[...], shape) == cell + h).astype(F32).astype(BF16)

    settle(fr2.at[others_y], f_send.at[1], f_recv.at[1])
    flux = jnp.sum(fr2[...], axis=0) * (1.0 / (nx * npy * nyl))
    press = []
    for k in range(OUTLETS):
        total = resist[k, 0] * flux[0:1]
        for n in range(1, OUTLETS):
            total = total + resist[k, n] * flux[n:n + 1]
        press.append(total[:, HALF - 1:HALF])

    def pressures(which):
        drop = jnp.zeros(which.shape, F32)
        for k in range(OUTLETS):
            drop = jnp.where(which == k, jnp.broadcast_to(press[k], which.shape), drop)
        return drop

    def lower(x, carry):
        drop = DT * jnp.where(lane == HALF - 1, pressures(idb[x]), 0.0)
        w2[halves - 1, x] = w2[halves - 1, x] - drop
        return carry

    lax.fori_loop(0, nxl, lower, 0)
    quarter = lane // nxl
    for n in range(npx // 4):
        which = asked[4 * n, 8:top, :]
        for a in range(1, 4):
            which = jnp.where(quarter == a, pltpu.roll(asked[4 * n + a, 8:top, :], a * nxl, 1), which)
        outlet[:, n * HALF:(n + 1) * HALF] = pressures(which)
    weight = jnp.broadcast_to(lam_z[pl.ds(pl.multiple_of(me_x * kzl, kzl), kzl), 1:2], (kzl, nx))

    wides = npx // 4

    def row_of(i):
        return pl.ds(pl.multiple_of(i * kzl, kzl), kzl)

    def piece_rows(c):
        return pl.ds(pl.multiple_of(c * per * kzl, per * kzl), per * kzl)

    def line_piece(c, carry):
        got[me_x, c] = msg[me_x, c]
        complete(c, relay, got, c)

        def gather(sg, inner):
            for half in range(per // 4):
                out = swap_groups([got[4 * sg + a, c, :, half * HALF:(half + 1) * HALF] for a in range(4)])
                for b in range(4):
                    y = c * per + 4 * half + b
                    cols[row_of(y), pl.ds(pl.multiple_of(sg * HALF, HALF), HALF)] = out[b]
            return inner

        lax.fori_loop(0, wides, gather, 0)

        def add_outlet(m, inner):
            y = c * per + m
            line = jnp.broadcast_to(outlet[pl.ds(y, 1), :], (kzl, nx))
            cols[row_of(y), :] = cols[row_of(y), :] + weight * line
            return inner

        lax.fori_loop(0, per, add_outlet, 0)
        rows = piece_rows(c)
        cols[rows, :] = dot_parts(split(cols[rows, :], 2), (tt[0], tt[1]), ((1,), (0,)))
        return carry

    lax.fori_loop(0, pieces, line_piece, 0)

    def down(i, carry):
        r, ends = carry
        ends = ends + kap[i] * r
        nxt = cols[row_of(i + 1), :] + tau[i] * r
        cols[row_of(i + 1), :] = nxt
        return nxt, ends

    r, ends = lax.fori_loop(1, nyl - 1, down, (cols[row_of(1), :], cols[row_of(0), :]))
    ends = ends + kap[nyl - 1] * r
    over = tau[nyl - 1] * r
    for j in range(npy):
        isnd[j, 0:kown, :] = ends[j * kown:(j + 1) * kown]
        isnd[j, kown:2 * kown, :] = over[j * kown:(j + 1) * kown]

    spread(npy, at_y, lambda r: isnd.at[at_y(r)[1]], ircv.at[me_y], i_send.at[0], i_recv.at[0])
    ircv[me_y] = isnd[me_y]
    settle(ircv.at[others_y], i_send.at[0], i_recv.at[0])

    rho = []
    for b in range(npy):
        value = ircv[b, 0:kown, :]
        if b > 0:
            value = value + ircv[b - 1, kown:2 * kown, :]
        rho.append(value)
    depth_mode = lax.broadcasted_iota(jnp.int32, (kown, nx), 0) + me_x * kzl + me_y * kown
    row_mode = lax.broadcasted_iota(jnp.int32, (kown, nx), 1)
    mean = sum(rho[1:], rho[0]) * (1.0 / (npy * nyl))
    mean = jnp.where((depth_mode == 0) & (row_mode == 0), mean, 0.0)
    half_sum = (nyl - 1) / 2.0
    for b in range(npy):
        weight = 1.0 + (0.0 if b == 0 else half_sum) + (2.0 * half_sum if b == npy - 1 else half_sum)
        rho[b] = rho[b] - weight * mean
    for b in range(npy - 1):
        rho[b + 1] = rho[b + 1] + owner_phi[b] * rho[b]
    value = -owner_inv[npy - 1] * rho[npy - 1]
    jsnd[npy - 1, 0:kown, :] = value
    jsnd[npy - 1, kown:2 * kown, :] = jnp.zeros_like(value)
    jsnd[npy - 1, 2 * kown:3 * kown, :] = mean
    for b in range(npy - 2, -1, -1):
        jsnd[b, kown:2 * kown, :] = value
        value = owner_phi[b] * value - owner_inv[b] * rho[b]
        jsnd[b, 0:kown, :] = value
        jsnd[b, 2 * kown:3 * kown, :] = mean

    spread(npy, at_y, lambda r: jsnd.at[at_y(r)[1]], jrcv.at[me_y], i_send.at[1], i_recv.at[1])
    jrcv[me_y] = jsnd[me_y]
    settle(jrcv.at[others_y], i_send.at[1], i_recv.at[1])
    for j in range(npy):
        for part in range(3):
            back[part, j * kown:(j + 1) * kown, :] = jrcv[j, part * kown:(part + 1) * kown, :]
    first_value, mean_rows = back[0], back[2]

    def up_piece(n, q):
        c = pieces - 1 - n

        def up_again(m, q):
            i = c * per + per - 1 - m
            share = 0.5 * (i + 1).astype(F32)
            q = tau[i] * (q - cols[row_of(i), :] + mean_rows * share) + kap[i] * first_value
            cols[row_of(i), :] = q
            return q

        q = lax.fori_loop(0, per, up_again, q)
        rows = piece_rows(c)
        cols[rows, :] = dot_parts(split(cols[rows, :], 3), (tx[0], tx[1], tx[2]), ((1,), (0,)))

        def scatter(sg, inner):
            for half in range(per // 4):
                parts = []
                for b in range(4):
                    y = c * per + 4 * half + b
                    parts.append(cols[row_of(y), pl.ds(pl.multiple_of(sg * HALF, HALF), HALF)])
                out = swap_groups(parts)
                for a in range(4):
                    msg[4 * sg + a, c, :, half * HALF:(half + 1) * HALF] = out[a]
            return inner

        lax.fori_loop(0, wides, scatter, 0)
        exchange(c, msg, relay2, got2, pieces + c)

        @pl.when(n > 0)
        def _():
            forward(c + 1, relay2, got2, pieces + c + 1)

        return q

    lax.fori_loop(0, pieces, up_piece, back[1])
    forward(0, relay2, got2, pieces)

    pressure = qp.reshape(halves, (nxl + 2) * wide, HALF)

    def rise_piece(n, carry):
        c = pieces - 1 - n
        got2[me_x, c] = msg[me_x, c]
        complete(c, relay2, got2, pieces + c)
        value = got2[:, c].reshape(nz, 256)
        out = dot_parts(split(value.T, 3), (tz[0], tz[1], tz[2]), ((1,), (0,)))
        for y in range(per):
            for h in range(halves):
                pressure[h, pl.ds(wide + 8 + c * per + y, nxl, stride=wide), :] = out[
                    y * nxl:(y + 1) * nxl, h * HALF:(h + 1) * HALF
                ]
        return carry

    lax.fori_loop(0, pieces, rise_piece, 0)

    for h in range(halves):
        qy_snd[0, h] = row_at(qp, (h,), top - 1)[...]
        qy_snd[1, h] = row_at(qp, (h,), 8)[...]
    halo = y_pair(qy_snd, qy_rcv, 4) + x_pair(qp, lambda field, x: field.at[:, x, pl.ds(8, nyl), :], 6)
    for copy in halo:
        copy.start()

    def q_rows(x, y, size):
        return jnp.concatenate([qp[h, x, y:y + size, :] for h in range(halves)], axis=1)

    def join(field, x):
        return jnp.concatenate([field[h, x, 0:nyl, :] for h in range(halves)], axis=1)

    def flow(a, x):
        return jnp.concatenate([up[a, h, x + 1, 8:top, :] for h in range(halves)], axis=1)

    def two_parts(x, carry):
        center = q_rows(x + 1, 8, nyl)
        spot = lax.broadcasted_iota(jnp.int32, center.shape, 1)
        below = jnp.where(spot == 0, center, pltpu.roll(center, 1, 1))
        above = jnp.where(spot == nz - 1, center, pltpu.roll(center, nz - 1, 1))
        v2 = join(w2, x) - 0.5 * (above - below)
        v0 = join(w0, x + 1) - 0.5 * (q_rows(x + 2, 8, nyl) - q_rows(x, 8, nyl))
        vel[0, x] = v0
        vel[2, x] = v2
        total = flow(0, x) * v0 + flow(2, x) * v2
        for h in range(halves):
            sig[h, pl.ds(pl.multiple_of(x * nyl, 8), nyl), :] = total[:, h * HALF:(h + 1) * HALF]
        return carry

    lax.fori_loop(1, nxl - 1, two_parts, 0)
    outs = [pltpu.make_async_copy(vel.at[b], v_out.at[b], out_sem.at[b]) for b in range(3)]

    for copy in halo:
        copy.wait()
    for h in range(halves):
        row_at(qp, (h,), 7)[...] = jnp.where(first_y, qy_snd[1, h], qy_rcv[0, h])
        row_at(qp, (h,), top)[...] = jnp.where(last_y, qy_snd[0, h], qy_rcv[1, h])

    @pl.when(first_x)
    def _():
        for h in range(halves):
            qp[h, 0, 8:top, :] = qp[h, 1, 8:top, :]

    @pl.when(last_x)
    def _():
        for h in range(halves):
            qp[h, nxl + 1, 8:top, :] = qp[h, nxl, 8:top, :]

    two_parts(0, 0)
    two_parts(nxl - 1, 0)
    outs[0].start()
    outs[2].start()

    def last_part(x, carry):
        tall = q_rows(x + 1, 0, wide)
        deep = jnp.concatenate([w1[h, x + 1, 8:top, :] for h in range(halves)], axis=1)
        v1 = deep - 0.5 * (tall[9:top + 1] - tall[7:top - 1])
        vel[1, x] = v1
        rows = pl.ds(pl.multiple_of(x * nyl, 8), nyl)
        part = flow(1, x) * v1
        for h in range(halves):
            sig[h, rows, :] = -ALPHA * (sig[h, rows, :] + part[:, h * HALF:(h + 1) * HALF])
        return carry

    lax.fori_loop(0, nxl, last_part, 0)
    outs[1].start()

    picked = None
    for h in range(halves):
        for part in reversed(split(sig[h], 2)):
            term = jnp.dot(hot[h], part, preferred_element_type=F32)
            picked = term if picked is None else picked + term
    settle(fetched.at[others_x], r_send.at[3], r_recv.at[3])
    products = picked * fetched[...].reshape(places, SEG)
    ones = jnp.ones((8, SEG), BF16)
    totals = sum(
        lax.dot_general(ones, part, (((1,), (1,)), ((), ())), preferred_element_type=F32)
        for part in reversed(split(products, 3))
    )
    by_px(totals, give)
    spread(npx, at_x, lambda r: give.at[at_x(r)[0]], given.at[me_x], r_send.at[4], r_recv.at[4])
    given[me_x] = give[me_x]
    settle(given.at[others_x], r_send.at[4], r_recv.at[4])
    by_py(given[:, 0, :], gives)
    spread(npy, at_y, lambda r: gives.at[at_y(r)[1]], taken.at[me_y], r_send.at[5], r_recv.at[5])
    taken[me_y] = gives[me_y]
    settle(taken.at[others_y], r_send.at[5], r_recv.at[5])

    def add_up(j, total):
        label, value = wanted[j], taken[j]
        for r in range(2):
            spot = slice(r * npy, r * npy + 1)
            hit = jnp.broadcast_to(label[:, spot], (npx, HALF)) == slot_lane
            total = total + jnp.where(hit, jnp.broadcast_to(value[:, spot], (npx, HALF)), 0.0)
        return total

    total = lax.fori_loop(0, npy, add_up, jnp.zeros((npx, HALF), F32))
    grad_out[...] = jnp.sum(total, axis=0, keepdims=True)[:, :controls]
    for copy in outs:
        copy.wait()


def main_call(dims, args, owner_rows):
    npx, npy, nxl, nyl, nz = dims
    nx = npx * nxl
    kzl = nz // npx
    kown = kzl // npy
    halves = nz // HALF
    wide = nyl + 16
    cells = nxl * nyl
    pieces = cells // 256
    places = 2 * npx * npy
    vmem = pltpu.VMEM
    anywhere = pl.BlockSpec(memory_space=pl.ANY)
    here = pl.BlockSpec(memory_space=pltpu.VMEM)
    scalar = pl.BlockSpec(memory_space=pltpu.SMEM)
    dma = pltpu.SemaphoreType.DMA
    tables = args[10:13]
    field = vmem((3, halves, nxl + 2, wide, HALF), F32)
    line = vmem((nyl, kzl, nx), F32)
    message = vmem((npx, pieces, kzl, 256), F32)
    scratch = [
        field,
        field,
        vmem((3, cells, nz), BF16),
        vmem((3, cells, nz), BF16),
        vmem((nxl, nyl, nz), jnp.int32),
        vmem((nxl, nyl, HALF), jnp.int32),
        vmem((halves, nxl + 2, nyl, HALF), F32),
        vmem((halves, nxl + 2, wide, HALF), F32),
        vmem((halves, nxl, nyl, HALF), F32),
        vmem((2, 6, halves, nxl, HALF), BF16),
        vmem((2, 6, halves, nxl, HALF), BF16),
        vmem((2, halves, nxl, HALF), F32),
        vmem((2, halves, nxl, HALF), F32),
        vmem((2, OUTLETS, HALF), F32),
        vmem((npx, OUTLETS, HALF), F32),
        vmem((npy, OUTLETS, HALF), F32),
        vmem((halves, cells, HALF), F32),
        message,
        message,
        message,
        vmem((4, pieces, kzl, 256), F32),
        vmem((4, pieces, kzl, 256), F32),
        vmem((nyl * kzl, nx), F32),
        line,
        line,
        vmem((npy, kown, nx), F32),
        vmem((npy, kown, nx), F32),
        vmem((npy, 2 * kown, nx), F32),
        vmem((npy, 2 * kown, nx), F32),
        vmem((npy, 3 * kown, nx), F32),
        vmem((npy, 3 * kown, nx), F32),
        vmem((3, kzl, nx), F32),
        vmem((halves, nxl + 2, wide, HALF), F32),
        vmem((2, halves, nxl, HALF), F32),
        vmem((2, halves, nxl, HALF), F32),
        vmem((3, nxl, nyl, nz), F32),
        vmem((halves, cells, HALF), F32),
        vmem((nyl, nx), F32),
        vmem((halves, places, cells), BF16),
        vmem((places, 1), jnp.int32),
        vmem((npx, 8 + nyl, HALF), F32),
        vmem((npx, 8 + nyl, HALF), F32),
        vmem((npy, npx, HALF), F32),
        vmem((npy, npx, HALF), F32),
        vmem((places, HALF), BF16),
        vmem((npy, 2 * npx, SEG), F32),
        vmem((npy, 2 * npx, SEG), F32),
        vmem((npx, 2 * npy, SEG), F32),
        vmem((npx, 2 * npy, SEG), F32),
        vmem((npx, 8, HALF), F32),
        vmem((npx, 8, HALF), F32),
        vmem((npy, npx, HALF), F32),
        vmem((npy, npx, HALF), F32),
    ]
    scratch += [vmem(t.shape, BF16) for t in tables]
    scratch += [
        dma((3 * halves + 3 + len(tables),)),
        dma((8,)),
        dma((8,)),
        dma((6,)),
        dma((6,)),
        dma((2,)),
        dma((2,)),
        dma((2 * pieces,)),
        dma((2 * pieces,)),
        dma((2 * pieces,)),
        dma((2 * pieces,)),
        dma((2 * pieces,)),
        dma((2,)),
        dma((2,)),
        dma((6,)),
        dma((6,)),
        dma((3,)),
    ]
    return pl.pallas_call(
        functools.partial(main_kernel, dims),
        out_shape=(
            jax.ShapeDtypeStruct((3, nxl, nyl, nz), F32),
            jax.ShapeDtypeStruct((1, owner_rows), F32),
        ),
        in_specs=[anywhere] * 4 + [here, scalar] + [here] * 4 + [anywhere] * len(tables) + [here] * 2,
        out_specs=(anywhere, here),
        scratch_shapes=scratch,
        compiler_params=pltpu.CompilerParams(
            collective_id=0, has_side_effects=True, vmem_limit_bytes=36 * 2**20
        ),
        name="project",
    )(*args)


def local(
    base_flow, adjoint_start, source, solid_mask, outlet_ids, resist,
    tile_owner, tile_slot, tile_column, control_basis,
):
    _, nxl, nyl, nz = adjoint_start.shape
    npx, npy = lax.axis_size("px"), lax.axis_size("py")
    nx = npx * nxl
    tz, tx = table_np(nz), table_np(nx)
    tables = [split_np(tz, 3), split_np(tx, 3), split_np(np.ascontiguousarray(tx.T), 2)]
    tables = [jnp.asarray(np.stack(t)) for t in tables]
    lam_x = jnp.asarray(-eigen_np(nx)[None, :])
    depth = np.zeros((nz, HALF), np.float32)
    depth[:, 0] = -eigen_np(nz)
    depth[:, 1] = -0.5 * DT * tz[:, nz - 2]
    depth = jnp.asarray(depth)
    args = (
        adjoint_start,
        base_flow.reshape(3, nxl * nyl, nz),
        source.reshape(3, nxl * nyl, nz),
        solid_mask,
        outlet_ids.T,
        resist,
        tile_owner.reshape(1, -1),
        tile_slot.reshape(1, -1),
        tile_column.reshape(1, -1),
        control_basis,
        *tables,
        lam_x,
        depth,
    )
    velocity, grad = main_call((npx, npy, nxl, nyl, nz), args, control_basis.shape[0])
    return velocity, grad.reshape(-1)


def solution(mesh):
    in_specs = (
        P(None, "px", "py", None),
        P(None, "px", "py", None),
        P(None, "px", "py", None),
        P("px", "py", None),
        P("px", "py"),
        P(),
        P(("px", "py"), None),
        P(("px", "py")),
        P(("px", "py")),
        P(("px", "py"), None),
    )
    out_specs = (P(None, "px", "py", None), P(("px", "py")))
    return jax.shard_map(local, mesh=mesh, in_specs=in_specs, out_specs=out_specs, check_vma=False)
```

```python
import functools
import math

import jax
import jax.numpy as jnp
import numpy as np
from jax import lax
from jax.experimental import pallas as pl
from jax.experimental.pallas import tpu as pltpu
from jax.sharding import PartitionSpec as P

SEG = 128
OUTLETS = 8
DT = 0.1
NU = 0.5
ALPHA = 5.0
HALF = 128
MESH = pl.DeviceIdType.MESH
F32 = jnp.float32
BF16 = jnp.bfloat16


def table_np(count):
    order = np.arange(count).astype(np.float32)
    modes = order[:, None]
    points = order[None, :]
    weights = np.where(modes == 0.0, math.sqrt(1.0 / count), math.sqrt(2.0 / count)).astype(np.float32)
    angle = np.float32(np.pi) * (points + np.float32(0.5)) * modes / np.float32(count)
    return (weights * np.cos(angle.astype(np.float32))).astype(np.float32)


def eigen_np(count):
    order = np.arange(count).astype(np.float32)
    angle = (np.float32(np.pi) * order / np.float32(count)).astype(np.float32)
    return (np.float32(2.0) * np.cos(angle) - np.float32(2.0)).astype(np.float32)


def split_np(table, count):
    parts = []
    for _ in range(count):
        parts.append(table.astype(jnp.bfloat16))
        table = table - parts[-1].astype(np.float32)
    return tuple(parts)


def split(value, count):
    parts = []
    for _ in range(count):
        parts.append(value.astype(BF16))
        value = value - parts[-1].astype(F32)
    return tuple(parts)


def dot_parts(a_parts, b_parts, contract):
    dims = ((contract[0], contract[1]), ((), ()))
    count, rows = len(a_parts), a_parts[0].shape[0]
    terms = {}
    for j in range(count):
        stacked = jnp.concatenate(a_parts[:count - j], axis=0) if j < count - 1 else a_parts[0]
        out = lax.dot_general(stacked, b_parts[j], dimension_numbers=dims, preferred_element_type=F32)
        for i in range(count - j):
            terms[i, j] = out[i * rows:(i + 1) * rows]
    total = None
    for i, j in sorted(terms, key=lambda at: -(at[0] + at[1])):
        total = terms[i, j] if total is None else total + terms[i, j]
    return total


def swap_groups(tiles):
    lane = lax.broadcasted_iota(jnp.int32, tiles[0].shape, 1)
    odd = (lane // 32) % 2 == 1
    far = lane >= 64
    t0, t1, t2, t3 = tiles
    a0 = jnp.where(odd, pltpu.roll(t1, 32, 1), t0)
    a1 = jnp.where(odd, t1, pltpu.roll(t0, 96, 1))
    a2 = jnp.where(odd, pltpu.roll(t3, 32, 1), t2)
    a3 = jnp.where(odd, t3, pltpu.roll(t2, 96, 1))
    return (
        jnp.where(far, pltpu.roll(a2, 64, 1), a0),
        jnp.where(far, pltpu.roll(a3, 64, 1), a1),
        jnp.where(far, a2, pltpu.roll(a0, 64, 1)),
        jnp.where(far, a3, pltpu.roll(a1, 64, 1)),
    )


def z_shift(field, edge_low, edge_high):
    depth = field.shape[1]
    lane = lax.broadcasted_iota(jnp.int32, field.shape, 1)
    below = jnp.where(lane == 0, edge_low, pltpu.roll(field, 1, 1))
    above = jnp.where(lane == depth - 1, edge_high, pltpu.roll(field, depth - 1, 1))
    return below, above


def main_kernel(
    dims,
    v_hbm, u_hbm, s_hbm, m_hbm, ids_hbm, resist_hbm, owner_hbm, slot_hbm, column_hbm, basis_hbm,
    tz_hbm, tx_hbm, tt_hbm, lam_x_hbm, lam_z_hbm,
    v_out, grad_out,
    vp, up, ub, sb, mk, idb, w0, w1, w2, snd_y, rcv_y, wy_snd, wy_rcv, fsum, fr1, fr2,
    div, msg, got, got2, cols, tau, kap, owner_inv, owner_phi,
    isnd, ircv, jsnd, jrcv, back, qp, qy_snd, qy_rcv, vel, sig,
    outlet, hot, pick, ask, asked, asks, wanted, chosen, reply, replies, fetch, fetched, give, given, gives, taken,
    tz, tx, tt, ids, resist, owner_row, slot_row, column_row, basis, lam_x, lam_z,
    load_sem, x_send, x_recv, y_send, y_recv, f_send, f_recv, a_send, a_recv, i_send, i_recv, r_send, r_recv, out_sem,
):
    npx, npy, nxl, nyl, nz = dims
    nx = npx * nxl
    kzl = nz // npx
    kown = kzl // npy
    halves = nz // HALF
    cells = nxl * nyl
    per = 256 // nxl
    pieces = nyl // per
    group = 2 * npy
    places = npx * group
    me_x = lax.axis_index("px")
    me_y = lax.axis_index("py")
    right_x, left_x = lax.rem(me_x + 1, npx), lax.rem(me_x + npx - 1, npx)
    right_y, left_y = lax.rem(me_y + 1, npy), lax.rem(me_y + npy - 1, npy)
    first_x, last_x = me_x == 0, me_x == npx - 1
    first_y, last_y = me_y == 0, me_y == npy - 1
    top = 8 + nyl
    wide = nyl + 16
    zero_at = jnp.minimum(me_x, 0)

    def run(first, last, action):
        def body(r, carry):
            action(r)
            return carry

        lax.fori_loop(first, last, body, 0)

    def remote(src, dst, send, recv, target):
        return pltpu.make_async_remote_copy(
            src_ref=src, dst_ref=dst, send_sem=send, recv_sem=recv, device_id=target, device_id_type=MESH
        )

    def at_x(r):
        return (lax.rem(me_x + r, npx), me_y)

    def at_y(r):
        return (me_x, lax.rem(me_y + r, npy))

    def spread(count, target, src, dst, send, recv):
        run(1, count, lambda r: remote(src(r), dst, send, recv, target(r)).start())

    def settle(like, send, recv):
        pltpu.make_async_copy(like, like, send).wait()
        pltpu.make_async_copy(like, like, recv).wait()

    others_x, others_y = pl.ds(0, npx - 1), pl.ds(0, npy - 1)

    loads = []
    for c in range(3):
        for h in range(halves):
            loads.append(
                pltpu.make_async_copy(
                    v_hbm.at[c, :, :, pl.ds(h * HALF, HALF)],
                    vp.at[c, h, pl.ds(1, nxl), pl.ds(8, nyl), :],
                    load_sem.at[c * halves + h],
                )
            )
    base = 3 * halves
    load_u = pltpu.make_async_copy(u_hbm, ub, load_sem.at[base])
    load_s = pltpu.make_async_copy(s_hbm, sb, load_sem.at[base + 1])
    load_m = pltpu.make_async_copy(m_hbm, mk, load_sem.at[base + 2])
    load_t = [
        pltpu.make_async_copy(a, b, load_sem.at[base + 3 + n])
        for n, (a, b) in enumerate(((tz_hbm, tz), (tx_hbm, tx), (tt_hbm, tt)))
    ]
    load_small = [
        pltpu.make_async_copy(a, b, load_sem.at[base + 6 + n])
        for n, (a, b) in enumerate(
            (
                (ids_hbm, ids), (resist_hbm, resist), (owner_hbm, owner_row), (slot_hbm, slot_row),
                (column_hbm, column_row), (basis_hbm, basis), (lam_x_hbm, lam_x), (lam_z_hbm, lam_z),
            )
        )
    ]
    for copy in loads:
        copy.start()
    load_u.start()
    for copy in load_small:
        copy.start()
    load_s.start()
    load_m.start()
    for copy in load_t:
        copy.start()

    barrier = pltpu.get_barrier_semaphore()
    run(1, npx, lambda r: pl.semaphore_signal(barrier, inc=1, device_id=at_x(r), device_id_type=MESH))
    run(1, npy, lambda r: pl.semaphore_signal(barrier, inc=1, device_id=at_y(r), device_id_type=MESH))

    def row_at(ref, lead, y):
        lines = ref.reshape(*ref.shape[:-3], (nxl + 2) * wide, HALF)
        return lines.at[(*lead, pl.ds(wide + y, nxl, stride=wide), slice(None))]

    def x_pair(field, at, number):
        return (
            remote(at(field, nxl), at(field, 0), x_send.at[number], x_recv.at[number], (right_x, me_y)),
            remote(at(field, 1), at(field, nxl + 1), x_send.at[number + 1], x_recv.at[number + 1], (left_x, me_y)),
        )

    def at_plane(field, x):
        return field.at[:, :, x, pl.ds(8, nyl), :]

    def y_pair(send, recv, number):
        return (
            remote(send.at[0], recv.at[0], y_send.at[number], y_recv.at[number], (me_x, right_y)),
            remote(send.at[1], recv.at[1], y_send.at[number + 1], y_recv.at[number + 1], (me_x, left_y)),
        )

    for copy in loads:
        copy.wait()

    def pack(field, first):
        for c in range(3):
            for h in range(halves):
                snd_y[0, first + c, h] = row_at(field, (c, h), top - 1)[...].astype(BF16)
                snd_y[1, first + c, h] = row_at(field, (c, h), 8)[...].astype(BF16)

    pack(vp, 0)
    load_u.wait()

    def widen(i, carry):
        for a in range(3):
            pair = ub[a, pl.ds(pl.multiple_of(i * 2 * nyl, 2 * nyl), 2 * nyl), :].astype(F32)
            for s in range(2):
                for h in range(halves):
                    up[a, h, 1 + 2 * i + s, 8:top, :] = pair[s * nyl:(s + 1) * nyl, h * HALF:(h + 1) * HALF]
        return carry

    lax.fori_loop(0, nxl // 2, widen, 0)
    pack(up, 3)
    pl.semaphore_wait(barrier, npx - 1 + npy - 1)
    halo = y_pair(snd_y, rcv_y, 0) + x_pair(vp, at_plane, 0) + x_pair(up, at_plane, 2)
    for copy in halo:
        copy.start()
    for copy in load_small:
        copy.wait()

    count = owner_row.shape[1]
    owners = owner_row[...]
    same = jnp.broadcast_to(owners, (8, count)).T[:, 0:1] == owners
    earlier = lax.broadcasted_iota(jnp.int32, (count, count), 0) < lax.broadcasted_iota(
        jnp.int32, (count, count), 1
    )
    rank = jnp.sum(jnp.where(same & earlier, 1, 0), axis=0, keepdims=True)
    owner_x = owners // npy
    place = owner_x * group + rank * npy + (owners - owner_x * npy)
    match = lax.broadcasted_iota(jnp.int32, (places, count), 0) == place
    pick[...] = jnp.sum(jnp.where(match, column_row[...] + 1, 0), axis=1, keepdims=True) - 1
    slots = jnp.broadcast_to((slot_row[...] + 1).astype(F32), (8, count)).astype(BF16)
    requests = (
        lax.dot_general(
            slots, match.astype(F32).astype(BF16), (((1,), (1,)), ((), ())), preferred_element_type=F32
        )
        - 1.0
    )

    def pad_lanes(row):
        if row.shape[1] >= HALF:
            return row
        return jnp.concatenate([row, jnp.zeros((8, HALF - row.shape[1]), F32)], axis=1)

    def by_px(row, ref):
        row = pad_lanes(row)
        lanes = row.shape[1]
        for p in range(npx):
            ref[p, 0:8, :] = pltpu.roll(row, (lanes - group * p) % lanes, 1)[:, :HALF]

    def by_py(rows, ref):
        for j in range(npy):
            ref[j] = pltpu.roll(rows, (HALF - j) % HALF, 1)

    by_px(requests, ask)
    seen = ids[...]
    padded = jnp.concatenate([seen.astype(F32), jnp.zeros((nyl, HALF - nxl), F32)], axis=1)
    for p in range(npx):
        ask[p, 8:top, :] = padded
    for x in range(nxl):
        idb[x] = jnp.broadcast_to(seen[:, x:x + 1], (nyl, HALF))

    def ask_start():
        spread(npx, at_x, lambda r: ask.at[at_x(r)[0]], asked.at[me_x], r_send.at[0], r_recv.at[0])
        asked[me_x] = ask[me_x]

    ask_start()

    def reduce_cell(c, g, right):
        inv = 1.0 / (c + right + g)
        return inv, c * inv

    mine = lam_z[pl.ds(pl.multiple_of(me_x * kzl, kzl), kzl), 0:1]
    mu = lam_x[...] + mine
    owned = lam_z[pl.ds(me_x * kzl + me_y * kown, kown), 0:1]
    muo = lam_x[...] + owned

    def owner_table():
        def owner_cell(i, carry):
            c, g, ground = carry
            inv, k = reduce_cell(c, g, 1.0)
            return k, muo + g * inv, ground + k * g

        one = jnp.ones_like(muo)
        c, g, ground = lax.fori_loop(1, nyl - 1, owner_cell, (one, muo, jnp.zeros_like(one)))
        inv, link = reduce_cell(c, g, 1.0)
        from_left = g * inv
        end_ground = muo + from_left + (ground + c * (g / (c + g)))
        ground = ground + link * g
        held = muo + ground
        for b in range(npy - 1):
            inv = 1.0 / (link + held)
            phi = link * inv
            owner_inv[b] = inv
            owner_phi[b] = phi
            nxt = end_ground if b == npy - 2 else muo + ground + from_left
            held = nxt + phi * held
        positive = held > 0.0
        owner_inv[npy - 1] = jnp.where(positive, 1.0 / jnp.where(positive, held, 1.0), 0.0)

    owner_table()
    settle(asked.at[others_x], r_send.at[0], r_recv.at[0])
    by_py(asked[:, 0, :], asks)
    spread(npy, at_y, lambda r: asks.at[at_y(r)[1]], wanted.at[me_y], r_send.at[1], r_recv.at[1])
    wanted[me_y] = asks[me_y]
    load_s.wait()
    load_m.wait()
    for copy in halo:
        copy.wait()

    for c in range(3):
        for h in range(halves):
            for field, first in ((vp, 0), (up, 3)):
                low, high = rcv_y[0, first + c, h].astype(F32), rcv_y[1, first + c, h].astype(F32)
                row_at(field, (c, h), 7)[...] = jnp.where(first_y, 0.0, low)
                row_at(field, (c, h), top)[...] = jnp.where(last_y, 0.0, high)
    edge = jnp.zeros((nyl, HALF), F32)

    @pl.when(first_x)
    def _():
        for c in range(3):
            for h in range(halves):
                vp[c, h, 0, 8:top, :] = edge
                up[c, h, 0, 8:top, :] = edge

    @pl.when(last_x)
    def _():
        for c in range(3):
            for h in range(halves):
                vp[c, h, nxl + 1, 8:top, :] = edge
                up[c, h, nxl + 1, 8:top, :] = edge

    def rows_at(field, c, x, start, size=8):
        return jnp.concatenate([field[c, h, x, pl.ds(start, size), :] for h in range(halves)], axis=1)

    tiles = nyl // 8

    def predict(i, carry):
        for k in range(tiles):
            rows = pl.ds(pl.multiple_of(i * 2 * nyl + 16 * k, 16), 16)
            forcing = [sb[b, rows, :].astype(F32) for b in range(3)]
            for s in range(2):
                n = 2 * k + s
                x = 2 * i + n // tiles
                y = 8 * (n % tiles)
                scale = 1.0 / (1.0 + (DT * ALPHA) * mk[x, y:y + 8, :].astype(F32))
                u = [rows_at(up, a, x + 1, y + 8) for a in range(3)]
                v = [rows_at(vp, a, x + 1, y + 8) for a in range(3)]
                low, high = y + 7 + zero_at, y + 9 + zero_at
                slopes = [None] * 3
                for a in range(3):
                    below, above = z_shift(u[a], 0.0, 0.0)
                    diffs = (
                        rows_at(up, a, x + 2, y + 8) - rows_at(up, a, x, y + 8),
                        rows_at(up, a, x + 1, high) - rows_at(up, a, x + 1, low),
                        above - below,
                    )
                    for b in range(3):
                        term = v[a] * diffs[b]
                        slopes[b] = term if slopes[b] is None else slopes[b] + term
                for b in range(3):
                    xm, xp = rows_at(vp, b, x, y + 8), rows_at(vp, b, x + 2, y + 8)
                    ym, yp = rows_at(vp, b, x + 1, low), rows_at(vp, b, x + 1, high)
                    zm, zp = z_shift(v[b], 0.0, 0.0)
                    convect = u[0] * (xp - xm) + u[1] * (yp - ym) + u[2] * (zp - zm)
                    lap = (xp + xm) + (yp + ym) + (zp + zm) - 6.0 * v[b]
                    change = 0.5 * (convect - slopes[b]) + NU * lap + forcing[b][8 * s:8 * s + 8]
                    w = (v[b] + DT * change) * scale
                    for h in range(halves):
                        part = w[:, h * HALF:(h + 1) * HALF]
                        if b == 0:
                            w0[h, x + 1, y:y + 8, :] = part
                        elif b == 1:
                            w1[h, x + 1, y + 8:y + 16, :] = part
                        else:
                            w2[h, x, y:y + 8, :] = part
        return carry

    lax.fori_loop(0, nxl // 2, predict, 0)

    for h in range(halves):
        wy_snd[0, h] = row_at(w1, (h,), top - 1)[...]
        wy_snd[1, h] = row_at(w1, (h,), 8)[...]
    halo = y_pair(wy_snd, wy_rcv, 2) + x_pair(w0, lambda field, x: field.at[:, x], 4)
    for copy in halo:
        copy.start()

    settle(wanted.at[others_y], r_send.at[1], r_recv.at[1])

    slot_lane = lax.broadcasted_iota(jnp.int32, (npx, HALF), 1).astype(F32)

    def choose(j, carry):
        label = wanted[j]
        for r in range(2):
            hit = jnp.broadcast_to(label[:, r * npy:r * npy + 1], (npx, HALF)) == slot_lane
            chosen[pl.ds(pl.multiple_of((2 * j + r) * npx, npx), npx), :] = hit.astype(F32).astype(BF16)
        return carry

    lax.fori_loop(0, npy, choose, 0)
    controls = basis.shape[0]
    wide_basis = jnp.concatenate([basis[...], jnp.zeros((HALF - controls, SEG), F32)], axis=0)
    rows = sum(
        jnp.dot(chosen[...], part, preferred_element_type=F32) for part in reversed(split(wide_basis, 3))
    )
    for j in range(npy):
        reply[j] = rows[j * 2 * npx:(j + 1) * 2 * npx]
    spread(npy, at_y, lambda r: reply.at[at_y(r)[1]], replies.at[me_y], r_send.at[2], r_recv.at[2])
    replies[me_y] = reply[me_y]

    lane = lax.broadcasted_iota(jnp.int32, (nyl, HALF), 1)

    def flux_plane(x, carry):
        face = jnp.where(lane == HALF - 1, w2[halves - 1, x], 0.0)
        which = idb[x]
        return tuple(total + jnp.where(which == k, face, 0.0) for k, total in enumerate(carry))

    zero = jnp.zeros((nyl, HALF), F32)
    totals = lax.fori_loop(0, nxl, flux_plane, (zero,) * OUTLETS)
    fsum[0] = jnp.concatenate([jnp.sum(t, axis=0, keepdims=True) for t in totals], axis=0)

    spread(npx, at_x, lambda r: fsum.at[0], fr1.at[me_x], f_send.at[0], f_recv.at[0])
    fr1[me_x] = fsum[0]

    for copy in halo:
        copy.wait()
    for h in range(halves):
        row_at(w1, (h,), 7)[...] = jnp.where(first_y, 0.0, wy_rcv[0, h])
        row_at(w1, (h,), top)[...] = jnp.where(last_y, 0.0, wy_rcv[1, h])

    @pl.when(first_x)
    def _():
        for h in range(halves):
            w0[h, 0] = edge

    @pl.when(last_x)
    def _():
        for h in range(halves):
            w0[h, nxl + 1] = edge

    def diverge(x, carry):
        deep = jnp.concatenate([w2[h, x] for h in range(halves)], axis=1)
        below, above = z_shift(deep, 0.0, 0.0)
        for h in range(halves):
            cut = slice(h * HALF, (h + 1) * HALF)
            rise = w1[h, x + 1, pl.ds(9 + zero_at, nyl), :] - w1[h, x + 1, pl.ds(7 + zero_at, nyl), :]
            total = (w0[h, x + 2] - w0[h, x]) + rise + (above - below)[:, cut]
            div[h, pl.ds(x, nyl, stride=nxl), :] = 0.5 * total
        return carry

    lax.fori_loop(0, nxl, diverge, 0)

    for copy in load_t:
        copy.wait()

    def depth_piece(c, carry):
        here = pl.ds(pl.multiple_of(c * 256, 256), 256)
        value = jnp.concatenate([div[h, here, :] for h in range(halves)], axis=1)
        out = dot_parts((tz[0], tz[1]), split(value, 2), ((1,), (1,)))
        for p in range(npx):
            msg[p, c] = out[p * kzl:(p + 1) * kzl]
        spread(npx, at_x, lambda r: msg.at[at_x(r)[0], c], got.at[me_x, c], a_send.at[c], a_recv.at[c])
        return carry

    lax.fori_loop(0, pieces, depth_piece, 0)

    settle(fr1.at[others_x], f_send.at[0], f_recv.at[0])
    fsum[1] = jnp.sum(fr1[...], axis=0)
    spread(npy, at_y, lambda r: fsum.at[1], fr2.at[me_y], f_send.at[1], f_recv.at[1])
    fr2[me_y] = fsum[1]
    settle(replies.at[others_y], r_send.at[2], r_recv.at[2])
    lines = replies.reshape(npy * 2 * npx, SEG)
    for p in range(npx):
        for r in range(2):
            fetch[p, r * npy:(r + 1) * npy, :] = lines[pl.ds(r * npx + p, npy, stride=2 * npx), :]
    spread(npx, at_x, lambda r: fetch.at[at_x(r)[0]], fetched.at[me_x], r_send.at[3], r_recv.at[3])
    fetched[me_x] = fetch[me_x]

    def table_cell(i, carry):
        c, g = carry
        right = jnp.where((i == nyl - 1) & last_y, 0.0, 1.0)
        inv, k = reduce_cell(c, g, right)
        tau[i] = inv
        kap[i] = k
        return k, mu + g * inv

    tau[0] = jnp.zeros_like(mu)
    kap[0] = jnp.ones_like(mu)
    lax.fori_loop(1, nyl, table_cell, (jnp.ones_like(mu), mu))

    shape = (places, cells)
    cell = lax.broadcasted_iota(jnp.int32, shape, 1) * halves
    for h in range(halves):
        hot[h] = (jnp.broadcast_to(pick[...], shape) == cell + h).astype(F32).astype(BF16)

    settle(fr2.at[others_y], f_send.at[1], f_recv.at[1])
    flux = jnp.sum(fr2[...], axis=0) * (1.0 / (nx * npy * nyl))
    press = []
    for k in range(OUTLETS):
        total = resist[k, 0] * flux[0:1]
        for n in range(1, OUTLETS):
            total = total + resist[k, n] * flux[n:n + 1]
        press.append(total[:, HALF - 1:HALF])

    def pressures(which):
        drop = jnp.zeros(which.shape, F32)
        for k in range(OUTLETS):
            drop = jnp.where(which == k, jnp.broadcast_to(press[k], which.shape), drop)
        return drop

    def lower(x, carry):
        drop = DT * jnp.where(lane == HALF - 1, pressures(idb[x]), 0.0)
        w2[halves - 1, x] = w2[halves - 1, x] - drop
        return carry

    lax.fori_loop(0, nxl, lower, 0)
    quarter = lane // nxl
    for n in range(npx // 4):
        which = asked[4 * n, 8:top, :]
        for a in range(1, 4):
            which = jnp.where(quarter == a, pltpu.roll(asked[4 * n + a, 8:top, :], a * nxl, 1), which)
        outlet[:, n * HALF:(n + 1) * HALF] = pressures(which)
    weight = jnp.broadcast_to(lam_z[pl.ds(pl.multiple_of(me_x * kzl, kzl), kzl), 1:2], (kzl, nx))

    wides = npx // 4

    def row_of(i):
        return pl.ds(pl.multiple_of(i * kzl, kzl), kzl)

    def piece_rows(c):
        return pl.ds(pl.multiple_of(c * per * kzl, per * kzl), per * kzl)

    def line_piece(c, carry):
        got[me_x, c] = msg[me_x, c]
        settle(got.at[others_x, c], a_send.at[c], a_recv.at[c])

        def gather(sg, inner):
            for half in range(per // 4):
                out = swap_groups([got[4 * sg + a, c, :, half * HALF:(half + 1) * HALF] for a in range(4)])
                for b in range(4):
                    y = c * per + 4 * half + b
                    cols[row_of(y), pl.ds(pl.multiple_of(sg * HALF, HALF), HALF)] = out[b]
            return inner

        lax.fori_loop(0, wides, gather, 0)

        def add_outlet(m, inner):
            y = c * per + m
            line = jnp.broadcast_to(outlet[pl.ds(y, 1), :], (kzl, nx))
            cols[row_of(y), :] = cols[row_of(y), :] + weight * line
            return inner

        lax.fori_loop(0, per, add_outlet, 0)
        rows = piece_rows(c)
        cols[rows, :] = dot_parts(split(cols[rows, :], 2), (tt[0], tt[1]), ((1,), (0,)))
        return carry

    lax.fori_loop(0, pieces, line_piece, 0)

    def down(i, carry):
        r, ends = carry
        ends = ends + kap[i] * r
        nxt = cols[row_of(i + 1), :] + tau[i] * r
        cols[row_of(i + 1), :] = nxt
        return nxt, ends

    r, ends = lax.fori_loop(1, nyl - 1, down, (cols[row_of(1), :], cols[row_of(0), :]))
    ends = ends + kap[nyl - 1] * r
    over = tau[nyl - 1] * r
    for j in range(npy):
        isnd[j, 0:kown, :] = ends[j * kown:(j + 1) * kown]
        isnd[j, kown:2 * kown, :] = over[j * kown:(j + 1) * kown]

    spread(npy, at_y, lambda r: isnd.at[at_y(r)[1]], ircv.at[me_y], i_send.at[0], i_recv.at[0])
    ircv[me_y] = isnd[me_y]
    settle(ircv.at[others_y], i_send.at[0], i_recv.at[0])

    rho = []
    for b in range(npy):
        value = ircv[b, 0:kown, :]
        if b > 0:
            value = value + ircv[b - 1, kown:2 * kown, :]
        rho.append(value)
    depth_mode = lax.broadcasted_iota(jnp.int32, (kown, nx), 0) + me_x * kzl + me_y * kown
    row_mode = lax.broadcasted_iota(jnp.int32, (kown, nx), 1)
    mean = sum(rho[1:], rho[0]) * (1.0 / (npy * nyl))
    mean = jnp.where((depth_mode == 0) & (row_mode == 0), mean, 0.0)
    half_sum = (nyl - 1) / 2.0
    for b in range(npy):
        weight = 1.0 + (0.0 if b == 0 else half_sum) + (2.0 * half_sum if b == npy - 1 else half_sum)
        rho[b] = rho[b] - weight * mean
    for b in range(npy - 1):
        rho[b + 1] = rho[b + 1] + owner_phi[b] * rho[b]
    value = -owner_inv[npy - 1] * rho[npy - 1]
    jsnd[npy - 1, 0:kown, :] = value
    jsnd[npy - 1, kown:2 * kown, :] = jnp.zeros_like(value)
    jsnd[npy - 1, 2 * kown:3 * kown, :] = mean
    for b in range(npy - 2, -1, -1):
        jsnd[b, kown:2 * kown, :] = value
        value = owner_phi[b] * value - owner_inv[b] * rho[b]
        jsnd[b, 0:kown, :] = value
        jsnd[b, 2 * kown:3 * kown, :] = mean

    spread(npy, at_y, lambda r: jsnd.at[at_y(r)[1]], jrcv.at[me_y], i_send.at[1], i_recv.at[1])
    jrcv[me_y] = jsnd[me_y]
    settle(jrcv.at[others_y], i_send.at[1], i_recv.at[1])
    for j in range(npy):
        for part in range(3):
            back[part, j * kown:(j + 1) * kown, :] = jrcv[j, part * kown:(part + 1) * kown, :]
    first_value, mean_rows = back[0], back[2]

    def up_piece(n, q):
        c = pieces - 1 - n

        def up_again(m, q):
            i = c * per + per - 1 - m
            share = 0.5 * (i + 1).astype(F32)
            q = tau[i] * (q - cols[row_of(i), :] + mean_rows * share) + kap[i] * first_value
            cols[row_of(i), :] = q
            return q

        q = lax.fori_loop(0, per, up_again, q)
        rows = piece_rows(c)
        cols[rows, :] = dot_parts(split(cols[rows, :], 3), (tx[0], tx[1], tx[2]), ((1,), (0,)))

        def scatter(sg, inner):
            for half in range(per // 4):
                parts = []
                for b in range(4):
                    y = c * per + 4 * half + b
                    parts.append(cols[row_of(y), pl.ds(pl.multiple_of(sg * HALF, HALF), HALF)])
                out = swap_groups(parts)
                for a in range(4):
                    msg[4 * sg + a, c, :, half * HALF:(half + 1) * HALF] = out[a]
            return inner

        lax.fori_loop(0, wides, scatter, 0)
        n = pieces + c
        spread(npx, at_x, lambda r: msg.at[at_x(r)[0], c], got2.at[me_x, c], a_send.at[n], a_recv.at[n])
        return q

    lax.fori_loop(0, pieces, up_piece, back[1])

    pressure = qp.reshape(halves, (nxl + 2) * wide, HALF)

    def rise_piece(n, carry):
        c = pieces - 1 - n
        got2[me_x, c] = msg[me_x, c]
        settle(got2.at[others_x, c], a_send.at[pieces + c], a_recv.at[pieces + c])
        value = got2[:, c].reshape(nz, 256)
        out = dot_parts(split(value.T, 3), (tz[0], tz[1], tz[2]), ((1,), (0,)))
        for y in range(per):
            for h in range(halves):
                pressure[h, pl.ds(wide + 8 + c * per + y, nxl, stride=wide), :] = out[
                    y * nxl:(y + 1) * nxl, h * HALF:(h + 1) * HALF
                ]
        return carry

    lax.fori_loop(0, pieces, rise_piece, 0)

    for h in range(halves):
        qy_snd[0, h] = row_at(qp, (h,), top - 1)[...]
        qy_snd[1, h] = row_at(qp, (h,), 8)[...]
    halo = y_pair(qy_snd, qy_rcv, 4) + x_pair(qp, lambda field, x: field.at[:, x, pl.ds(8, nyl), :], 6)
    for copy in halo:
        copy.start()

    def q_rows(x, y, size):
        return jnp.concatenate([qp[h, x, pl.ds(y, size), :] for h in range(halves)], axis=1)

    def join(field, x):
        return jnp.concatenate([field[h, x, 0:nyl, :] for h in range(halves)], axis=1)

    def flow(a, x):
        return jnp.concatenate([up[a, h, x + 1, 8:top, :] for h in range(halves)], axis=1)

    def two_parts(x, carry):
        center = q_rows(x + 1, 8, nyl)
        spot = lax.broadcasted_iota(jnp.int32, center.shape, 1)
        below = jnp.where(spot == 0, center, pltpu.roll(center, 1, 1))
        above = jnp.where(spot == nz - 1, center, pltpu.roll(center, nz - 1, 1))
        v2 = join(w2, x) - 0.5 * (above - below)
        v0 = join(w0, x + 1) - 0.5 * (q_rows(x + 2, 8, nyl) - q_rows(x, 8, nyl))
        vel[0, x] = v0
        vel[2, x] = v2
        total = flow(0, x) * v0 + flow(2, x) * v2
        for h in range(halves):
            sig[h, pl.ds(pl.multiple_of(x * nyl, 8), nyl), :] = total[:, h * HALF:(h + 1) * HALF]
        return carry

    lax.fori_loop(1, nxl - 1, two_parts, 0)
    outs = [pltpu.make_async_copy(vel.at[b], v_out.at[b], out_sem.at[b]) for b in range(3)]

    for copy in halo:
        copy.wait()
    for h in range(halves):
        row_at(qp, (h,), 7)[...] = jnp.where(first_y, qy_snd[1, h], qy_rcv[0, h])
        row_at(qp, (h,), top)[...] = jnp.where(last_y, qy_snd[0, h], qy_rcv[1, h])

    @pl.when(first_x)
    def _():
        for h in range(halves):
            qp[h, 0, 8:top, :] = qp[h, 1, 8:top, :]

    @pl.when(last_x)
    def _():
        for h in range(halves):
            qp[h, nxl + 1, 8:top, :] = qp[h, nxl, 8:top, :]

    two_parts(0, 0)
    two_parts(nxl - 1, 0)
    outs[0].start()
    outs[2].start()

    def last_part(x, carry):
        deep = jnp.concatenate([w1[h, x + 1, 8:top, :] for h in range(halves)], axis=1)
        v1 = deep - 0.5 * (q_rows(x + 1, 9 + zero_at, nyl) - q_rows(x + 1, 7 + zero_at, nyl))
        vel[1, x] = v1
        rows = pl.ds(pl.multiple_of(x * nyl, 8), nyl)
        part = flow(1, x) * v1
        for h in range(halves):
            sig[h, rows, :] = -ALPHA * (sig[h, rows, :] + part[:, h * HALF:(h + 1) * HALF])
        return carry

    lax.fori_loop(0, nxl, last_part, 0)
    outs[1].start()

    picked = None
    for h in range(halves):
        both = jnp.dot(hot[h], jnp.concatenate(split(sig[h], 2), axis=1), preferred_element_type=F32)
        term = both[:, :SEG] + both[:, SEG:]
        picked = term if picked is None else picked + term
    settle(fetched.at[others_x], r_send.at[3], r_recv.at[3])
    products = picked * fetched[...].reshape(places, SEG)
    ones = jnp.ones((8, SEG), BF16)
    totals = sum(
        lax.dot_general(ones, part, (((1,), (1,)), ((), ())), preferred_element_type=F32)
        for part in reversed(split(products, 3))
    )
    by_px(totals, give)
    spread(npx, at_x, lambda r: give.at[at_x(r)[0]], given.at[me_x], r_send.at[4], r_recv.at[4])
    given[me_x] = give[me_x]
    settle(given.at[others_x], r_send.at[4], r_recv.at[4])
    by_py(given[:, 0, :], gives)
    spread(npy, at_y, lambda r: gives.at[at_y(r)[1]], taken.at[me_y], r_send.at[5], r_recv.at[5])
    taken[me_y] = gives[me_y]
    settle(taken.at[others_y], r_send.at[5], r_recv.at[5])

    def add_up(j, total):
        label, value = wanted[j], taken[j]
        for r in range(2):
            spot = slice(r * npy, r * npy + 1)
            hit = jnp.broadcast_to(label[:, spot], (npx, HALF)) == slot_lane
            total = total + jnp.where(hit, jnp.broadcast_to(value[:, spot], (npx, HALF)), 0.0)
        return total

    total = lax.fori_loop(0, npy, add_up, jnp.zeros((npx, HALF), F32))
    grad_out[...] = jnp.sum(total, axis=0, keepdims=True)[:, :controls]
    for copy in outs:
        copy.wait()


def main_call(dims, args, owner_rows):
    npx, npy, nxl, nyl, nz = dims
    nx = npx * nxl
    kzl = nz // npx
    kown = kzl // npy
    halves = nz // HALF
    wide = nyl + 16
    cells = nxl * nyl
    pieces = cells // 256
    places = 2 * npx * npy
    vmem = pltpu.VMEM
    anywhere = pl.BlockSpec(memory_space=pl.ANY)
    here = pl.BlockSpec(memory_space=pltpu.VMEM)
    far = pl.BlockSpec(memory_space=pltpu.HBM)
    dma = pltpu.SemaphoreType.DMA
    tables = args[10:13]
    field = vmem((3, halves, nxl + 2, wide, HALF), F32)
    line = vmem((nyl, kzl, nx), F32)
    message = vmem((npx, pieces, kzl, 256), F32)
    scratch = [
        field,
        field,
        vmem((3, cells, nz), BF16),
        vmem((3, cells, nz), BF16),
        vmem((nxl, nyl, nz), jnp.int32),
        vmem((nxl, nyl, HALF), jnp.int32),
        vmem((halves, nxl + 2, nyl, HALF), F32),
        vmem((halves, nxl + 2, wide, HALF), F32),
        vmem((halves, nxl, nyl, HALF), F32),
        vmem((2, 6, halves, nxl, HALF), BF16),
        vmem((2, 6, halves, nxl, HALF), BF16),
        vmem((2, halves, nxl, HALF), F32),
        vmem((2, halves, nxl, HALF), F32),
        vmem((2, OUTLETS, HALF), F32),
        vmem((npx, OUTLETS, HALF), F32),
        vmem((npy, OUTLETS, HALF), F32),
        vmem((halves, cells, HALF), F32),
        message,
        message,
        message,
        vmem((nyl * kzl, nx), F32),
        line,
        line,
        vmem((npy, kown, nx), F32),
        vmem((npy, kown, nx), F32),
        vmem((npy, 2 * kown, nx), F32),
        vmem((npy, 2 * kown, nx), F32),
        vmem((npy, 3 * kown, nx), F32),
        vmem((npy, 3 * kown, nx), F32),
        vmem((3, kzl, nx), F32),
        vmem((halves, nxl + 2, wide, HALF), F32),
        vmem((2, halves, nxl, HALF), F32),
        vmem((2, halves, nxl, HALF), F32),
        vmem((3, nxl, nyl, nz), F32),
        vmem((halves, cells, HALF), F32),
        vmem((nyl, nx), F32),
        vmem((halves, places, cells), BF16),
        vmem((places, 1), jnp.int32),
        vmem((npx, 8 + nyl, HALF), F32),
        vmem((npx, 8 + nyl, HALF), F32),
        vmem((npy, npx, HALF), F32),
        vmem((npy, npx, HALF), F32),
        vmem((places, HALF), BF16),
        vmem((npy, 2 * npx, SEG), F32),
        vmem((npy, 2 * npx, SEG), F32),
        vmem((npx, 2 * npy, SEG), F32),
        vmem((npx, 2 * npy, SEG), F32),
        vmem((npx, 8, HALF), F32),
        vmem((npx, 8, HALF), F32),
        vmem((npy, npx, HALF), F32),
        vmem((npy, npx, HALF), F32),
    ]
    scratch += [vmem(t.shape, BF16) for t in tables]
    scratch += [
        pltpu.SMEM(a.shape, a.dtype) if n == 5 else vmem(a.shape, a.dtype)
        for n, a in enumerate(args)
        if n > 3 and not 10 <= n < 13
    ]
    scratch += [
        dma((3 * halves + 14,)),
        dma((8,)),
        dma((8,)),
        dma((6,)),
        dma((6,)),
        dma((2,)),
        dma((2,)),
        dma((2 * pieces,)),
        dma((2 * pieces,)),
        dma((2,)),
        dma((2,)),
        dma((6,)),
        dma((6,)),
        dma((3,)),
    ]
    return pl.pallas_call(
        functools.partial(main_kernel, dims),
        out_shape=(
            jax.ShapeDtypeStruct((3, nxl, nyl, nz), F32),
            jax.ShapeDtypeStruct((1, owner_rows), F32),
        ),
        in_specs=[far] * len(args),
        out_specs=(anywhere, here),
        scratch_shapes=scratch,
        compiler_params=pltpu.CompilerParams(
            collective_id=0, has_side_effects=True, vmem_limit_bytes=58 * 2**20
        ),
        name="project",
    )(*args)


def local(
    base_flow, adjoint_start, source, solid_mask, outlet_ids, resist,
    tile_owner, tile_slot, tile_column, control_basis,
):
    _, nxl, nyl, nz = adjoint_start.shape
    npx, npy = lax.axis_size("px"), lax.axis_size("py")
    nx = npx * nxl
    tz, tx = table_np(nz), table_np(nx)
    tables = [split_np(tz, 3), split_np(tx, 3), split_np(np.ascontiguousarray(tx.T), 2)]
    tables = [jnp.asarray(np.stack(t)) for t in tables]
    lam_x = jnp.asarray(-eigen_np(nx)[None, :])
    depth = np.zeros((nz, HALF), np.float32)
    depth[:, 0] = -eigen_np(nz)
    depth[:, 1] = -0.5 * DT * tz[:, nz - 2]
    depth = jnp.asarray(depth)
    args = (
        adjoint_start,
        base_flow.reshape(3, nxl * nyl, nz),
        source.reshape(3, nxl * nyl, nz),
        solid_mask,
        outlet_ids.T,
        resist,
        tile_owner.reshape(1, -1),
        tile_slot.reshape(1, -1),
        tile_column.reshape(1, -1),
        control_basis,
        *tables,
        lam_x,
        depth,
    )
    velocity, grad = main_call((npx, npy, nxl, nyl, nz), args, control_basis.shape[0])
    return velocity, grad.reshape(-1)


def solution(mesh):
    in_specs = (
        P(None, "px", "py", None),
        P(None, "px", "py", None),
        P(None, "px", "py", None),
        P("px", "py", None),
        P("px", "py"),
        P(),
        P(("px", "py"), None),
        P(("px", "py")),
        P(("px", "py")),
        P(("px", "py"), None),
    )
    out_specs = (P(None, "px", "py", None), P(("px", "py")))
    return jax.shard_map(local, mesh=mesh, in_specs=in_specs, out_specs=out_specs, check_vma=False)
```

```python
import functools
import math

import jax
import jax.numpy as jnp
import numpy as np
from jax import lax
from jax.experimental import pallas as pl
from jax.experimental.pallas import tpu as pltpu
from jax.sharding import PartitionSpec as P

SEG = 128
OUTLETS = 8
DT = 0.1
NU = 0.5
ALPHA = 5.0
HALF = 128
MESH = pl.DeviceIdType.MESH
F32 = jnp.float32
BF16 = jnp.bfloat16


def table_np(count):
    order = np.arange(count).astype(np.float32)
    modes = order[:, None]
    points = order[None, :]
    weights = np.where(modes == 0.0, math.sqrt(1.0 / count), math.sqrt(2.0 / count)).astype(np.float32)
    angle = np.float32(np.pi) * (points + np.float32(0.5)) * modes / np.float32(count)
    return (weights * np.cos(angle.astype(np.float32))).astype(np.float32)


def eigen_np(count):
    order = np.arange(count).astype(np.float32)
    angle = (np.float32(np.pi) * order / np.float32(count)).astype(np.float32)
    return (np.float32(2.0) * np.cos(angle) - np.float32(2.0)).astype(np.float32)


def split_np(table, count):
    parts = []
    for _ in range(count):
        parts.append(table.astype(jnp.bfloat16))
        table = table - parts[-1].astype(np.float32)
    return tuple(parts)


def split(value, count):
    parts = []
    for _ in range(count):
        parts.append(value.astype(BF16))
        value = value - parts[-1].astype(F32)
    return tuple(parts)


def dot_parts(a_parts, b_parts, contract):
    dims = ((contract[0], contract[1]), ((), ()))
    count, rows = len(a_parts), a_parts[0].shape[0]
    terms = {}
    for j in range(count):
        stacked = jnp.concatenate(a_parts[:count - j], axis=0) if j < count - 1 else a_parts[0]
        out = lax.dot_general(stacked, b_parts[j], dimension_numbers=dims, preferred_element_type=F32)
        for i in range(count - j):
            terms[i, j] = out[i * rows:(i + 1) * rows]
    total = None
    for i, j in sorted(terms, key=lambda at: -(at[0] + at[1])):
        total = terms[i, j] if total is None else total + terms[i, j]
    return total


def swap_groups(tiles):
    lane = lax.broadcasted_iota(jnp.int32, tiles[0].shape, 1)
    odd = (lane // 32) % 2 == 1
    far = lane >= 64
    t0, t1, t2, t3 = tiles
    a0 = jnp.where(odd, pltpu.roll(t1, 32, 1), t0)
    a1 = jnp.where(odd, t1, pltpu.roll(t0, 96, 1))
    a2 = jnp.where(odd, pltpu.roll(t3, 32, 1), t2)
    a3 = jnp.where(odd, t3, pltpu.roll(t2, 96, 1))
    return (
        jnp.where(far, pltpu.roll(a2, 64, 1), a0),
        jnp.where(far, pltpu.roll(a3, 64, 1), a1),
        jnp.where(far, a2, pltpu.roll(a0, 64, 1)),
        jnp.where(far, a3, pltpu.roll(a1, 64, 1)),
    )


def z_shift(field, edge_low, edge_high):
    depth = field.shape[1]
    lane = lax.broadcasted_iota(jnp.int32, field.shape, 1)
    below = jnp.where(lane == 0, edge_low, pltpu.roll(field, 1, 1))
    above = jnp.where(lane == depth - 1, edge_high, pltpu.roll(field, depth - 1, 1))
    return below, above


def main_kernel(
    dims,
    v_hbm, u_hbm, s_hbm, m_hbm, ids_hbm, resist_hbm, owner_hbm, slot_hbm, column_hbm, basis_hbm,
    tz_hbm, tx_hbm, tt_hbm, lam_x_hbm, lam_z_hbm,
    v_out, grad_out,
    vp, up, ub, sb, mk, idb, w0, w1, w2, snd_y, rcv_y, wy_snd, wy_rcv, fsum, fr1, fr2,
    div, msg, got, got2, cols, tau, kap, owner_inv, owner_phi,
    isnd, ircv, jsnd, jrcv, back, qp, qy_snd, qy_rcv, vel, sig,
    outlet, hot, pick, ask, asked, asks, wanted, chosen, reply, replies, fetch, fetched, give, given, gives, taken,
    tz, tx, tt, ids, resist, owner_row, slot_row, column_row, basis, lam_x, lam_z,
    load_sem, x_send, x_recv, y_send, y_recv, f_send, f_recv, a_send, a_recv, i_send, i_recv, r_send, r_recv, out_sem,
):
    npx, npy, nxl, nyl, nz = dims
    nx = npx * nxl
    kzl = nz // npx
    kown = kzl // npy
    halves = nz // HALF
    cells = nxl * nyl
    per = 256 // nxl
    pieces = nyl // per
    group = 2 * npy
    places = npx * group
    me_x = lax.axis_index("px")
    me_y = lax.axis_index("py")
    right_x, left_x = lax.rem(me_x + 1, npx), lax.rem(me_x + npx - 1, npx)
    right_y, left_y = lax.rem(me_y + 1, npy), lax.rem(me_y + npy - 1, npy)
    first_x, last_x = me_x == 0, me_x == npx - 1
    first_y, last_y = me_y == 0, me_y == npy - 1
    top = 8 + nyl
    wide = nyl + 16
    zero_at = jnp.minimum(me_x, 0)

    def run(first, last, action):
        def body(r, carry):
            action(r)
            return carry

        lax.fori_loop(first, last, body, 0)

    def remote(src, dst, send, recv, target):
        return pltpu.make_async_remote_copy(
            src_ref=src, dst_ref=dst, send_sem=send, recv_sem=recv, device_id=target, device_id_type=MESH
        )

    def at_x(r):
        return (lax.rem(me_x + r, npx), me_y)

    def at_y(r):
        return (me_x, lax.rem(me_y + r, npy))

    def spread(count, target, src, dst, send, recv):
        def start(n):
            r = lax.rem(n + (count // 2 - 2), count - 1) + 1
            remote(src(r), dst, send, recv, target(r)).start()

        run(1, count, start)

    def settle(like, send, recv):
        pltpu.make_async_copy(like, like, send).wait()
        pltpu.make_async_copy(like, like, recv).wait()

    others_x, others_y = pl.ds(0, npx - 1), pl.ds(0, npy - 1)

    loads = []
    for c in range(3):
        for h in range(halves):
            loads.append(
                pltpu.make_async_copy(
                    v_hbm.at[c, :, :, pl.ds(h * HALF, HALF)],
                    vp.at[c, h, pl.ds(1, nxl), pl.ds(8, nyl), :],
                    load_sem.at[c * halves + h],
                )
            )
    base = 3 * halves
    load_u = pltpu.make_async_copy(u_hbm, ub, load_sem.at[base])
    load_s = pltpu.make_async_copy(s_hbm, sb, load_sem.at[base + 1])
    load_m = pltpu.make_async_copy(m_hbm, mk, load_sem.at[base + 2])
    load_t = [
        pltpu.make_async_copy(a, b, load_sem.at[base + 3 + n])
        for n, (a, b) in enumerate(((tz_hbm, tz), (tx_hbm, tx), (tt_hbm, tt)))
    ]
    load_small = [
        pltpu.make_async_copy(a, b, load_sem.at[base + 6 + n])
        for n, (a, b) in enumerate(
            (
                (ids_hbm, ids), (resist_hbm, resist), (owner_hbm, owner_row), (slot_hbm, slot_row),
                (column_hbm, column_row), (basis_hbm, basis), (lam_x_hbm, lam_x), (lam_z_hbm, lam_z),
            )
        )
    ]
    for copy in loads:
        copy.start()
    load_u.start()
    for copy in load_small:
        copy.start()
    load_s.start()
    load_m.start()
    for copy in load_t:
        copy.start()

    barrier = pltpu.get_barrier_semaphore()
    run(1, npx, lambda r: pl.semaphore_signal(barrier, inc=1, device_id=at_x(r), device_id_type=MESH))
    run(1, npy, lambda r: pl.semaphore_signal(barrier, inc=1, device_id=at_y(r), device_id_type=MESH))

    def row_at(ref, lead, y):
        lines = ref.reshape(*ref.shape[:-3], (nxl + 2) * wide, HALF)
        return lines.at[(*lead, pl.ds(wide + y, nxl, stride=wide), slice(None))]

    def x_pair(field, at, number):
        return (
            remote(at(field, nxl), at(field, 0), x_send.at[number], x_recv.at[number], (right_x, me_y)),
            remote(at(field, 1), at(field, nxl + 1), x_send.at[number + 1], x_recv.at[number + 1], (left_x, me_y)),
        )

    def at_plane(field, x):
        return field.at[:, :, x, pl.ds(8, nyl), :]

    def y_pair(send, recv, number):
        return (
            remote(send.at[0], recv.at[0], y_send.at[number], y_recv.at[number], (me_x, right_y)),
            remote(send.at[1], recv.at[1], y_send.at[number + 1], y_recv.at[number + 1], (me_x, left_y)),
        )

    for copy in loads:
        copy.wait()

    def pack(field, first):
        for c in range(3):
            for h in range(halves):
                snd_y[0, first + c, h] = row_at(field, (c, h), top - 1)[...].astype(BF16)
                snd_y[1, first + c, h] = row_at(field, (c, h), 8)[...].astype(BF16)

    pack(vp, 0)
    load_u.wait()

    def widen(i, carry):
        for a in range(3):
            pair = ub[a, pl.ds(pl.multiple_of(i * 2 * nyl, 2 * nyl), 2 * nyl), :].astype(F32)
            for s in range(2):
                for h in range(halves):
                    up[a, h, 1 + 2 * i + s, 8:top, :] = pair[s * nyl:(s + 1) * nyl, h * HALF:(h + 1) * HALF]
        return carry

    lax.fori_loop(0, nxl // 2, widen, 0)
    pack(up, 3)
    pl.semaphore_wait(barrier, npx - 1 + npy - 1)
    halo = y_pair(snd_y, rcv_y, 0) + x_pair(vp, at_plane, 0) + x_pair(up, at_plane, 2)
    for copy in halo:
        copy.start()
    for copy in load_small:
        copy.wait()

    count = owner_row.shape[1]
    owners = owner_row[...]
    same = jnp.broadcast_to(owners, (8, count)).T[:, 0:1] == owners
    earlier = lax.broadcasted_iota(jnp.int32, (count, count), 0) < lax.broadcasted_iota(
        jnp.int32, (count, count), 1
    )
    rank = jnp.sum(jnp.where(same & earlier, 1, 0), axis=0, keepdims=True)
    owner_x = owners // npy
    place = owner_x * group + rank * npy + (owners - owner_x * npy)
    match = lax.broadcasted_iota(jnp.int32, (places, count), 0) == place
    pick[...] = jnp.sum(jnp.where(match, column_row[...] + 1, 0), axis=1, keepdims=True) - 1
    slots = jnp.broadcast_to((slot_row[...] + 1).astype(F32), (8, count)).astype(BF16)
    requests = (
        lax.dot_general(
            slots, match.astype(F32).astype(BF16), (((1,), (1,)), ((), ())), preferred_element_type=F32
        )
        - 1.0
    )

    def pad_lanes(row):
        if row.shape[1] >= HALF:
            return row
        return jnp.concatenate([row, jnp.zeros((8, HALF - row.shape[1]), F32)], axis=1)

    def by_px(row, ref):
        row = pad_lanes(row)
        lanes = row.shape[1]
        for p in range(npx):
            ref[p, 0:8, :] = pltpu.roll(row, (lanes - group * p) % lanes, 1)[:, :HALF]

    def by_py(rows, ref):
        for j in range(npy):
            ref[j] = pltpu.roll(rows, (HALF - j) % HALF, 1)

    by_px(requests, ask)
    seen = ids[...]
    padded = jnp.concatenate([seen.astype(F32), jnp.zeros((nyl, HALF - nxl), F32)], axis=1)
    for p in range(npx):
        ask[p, 8:top, :] = padded
    for x in range(nxl):
        idb[x] = jnp.broadcast_to(seen[:, x:x + 1], (nyl, HALF))

    def ask_start():
        spread(npx, at_x, lambda r: ask.at[at_x(r)[0]], asked.at[me_x], r_send.at[0], r_recv.at[0])
        asked[me_x] = ask[me_x]

    ask_start()

    def reduce_cell(c, g, right):
        inv = 1.0 / (c + right + g)
        return inv, c * inv

    mine = lam_z[pl.ds(pl.multiple_of(me_x * kzl, kzl), kzl), 0:1]
    mu = lam_x[...] + mine
    owned = lam_z[pl.ds(me_x * kzl + me_y * kown, kown), 0:1]
    muo = lam_x[...] + owned

    def owner_table():
        def owner_cell(i, carry):
            c, g, ground = carry
            inv, k = reduce_cell(c, g, 1.0)
            return k, muo + g * inv, ground + k * g

        one = jnp.ones_like(muo)
        c, g, ground = lax.fori_loop(1, nyl - 1, owner_cell, (one, muo, jnp.zeros_like(one)))
        inv, link = reduce_cell(c, g, 1.0)
        from_left = g * inv
        end_ground = muo + from_left + (ground + c * (g / (c + g)))
        ground = ground + link * g
        held = muo + ground
        for b in range(npy - 1):
            inv = 1.0 / (link + held)
            phi = link * inv
            owner_inv[b] = inv
            owner_phi[b] = phi
            nxt = end_ground if b == npy - 2 else muo + ground + from_left
            held = nxt + phi * held
        positive = held > 0.0
        owner_inv[npy - 1] = jnp.where(positive, 1.0 / jnp.where(positive, held, 1.0), 0.0)

    load_s.wait()
    load_m.wait()

    blank = jnp.zeros((nxl, HALF), F32)
    for c in range(3):
        for h in range(halves):
            for field in (vp, up):
                row_at(field, (c, h), 7)[...] = blank
                row_at(field, (c, h), top)[...] = blank

    def rows_at(field, c, x, start, size=8):
        return jnp.concatenate([field[c, h, x, pl.ds(start, size), :] for h in range(halves)], axis=1)

    tiles = nyl // 8

    def predict(i, planes):
        for k in range(tiles):
            if all((2 * k + s) // tiles not in planes for s in range(2)):
                continue
            rows = pl.ds(pl.multiple_of(i * 2 * nyl + 16 * k, 16), 16)
            forcing = [sb[b, rows, :].astype(F32) for b in range(3)]
            for s in range(2):
                n = 2 * k + s
                if n // tiles not in planes:
                    continue
                x = 2 * i + n // tiles
                y = 8 * (n % tiles)
                scale = 1.0 / (1.0 + (DT * ALPHA) * mk[x, y:y + 8, :].astype(F32))
                u = [rows_at(up, a, x + 1, y + 8) for a in range(3)]
                v = [rows_at(vp, a, x + 1, y + 8) for a in range(3)]
                low, high = y + 7 + zero_at, y + 9 + zero_at
                slopes = [None] * 3
                for a in range(3):
                    below, above = z_shift(u[a], 0.0, 0.0)
                    diffs = (
                        rows_at(up, a, x + 2, y + 8) - rows_at(up, a, x, y + 8),
                        rows_at(up, a, x + 1, high) - rows_at(up, a, x + 1, low),
                        above - below,
                    )
                    for b in range(3):
                        term = v[a] * diffs[b]
                        slopes[b] = term if slopes[b] is None else slopes[b] + term
                for b in range(3):
                    xm, xp = rows_at(vp, b, x, y + 8), rows_at(vp, b, x + 2, y + 8)
                    ym, yp = rows_at(vp, b, x + 1, low), rows_at(vp, b, x + 1, high)
                    zm, zp = z_shift(v[b], 0.0, 0.0)
                    convect = u[0] * (xp - xm) + u[1] * (yp - ym) + u[2] * (zp - zm)
                    lap = (xp + xm) + (yp + ym) + (zp + zm) - 6.0 * v[b]
                    change = 0.5 * (convect - slopes[b]) + NU * lap + forcing[b][8 * s:8 * s + 8]
                    w = (v[b] + DT * change) * scale
                    for h in range(halves):
                        part = w[:, h * HALF:(h + 1) * HALF]
                        if b == 0:
                            w0[h, x + 1, y:y + 8, :] = part
                        elif b == 1:
                            w1[h, x + 1, y + 8:y + 16, :] = part
                        else:
                            w2[h, x, y:y + 8, :] = part

    pairs = nxl // 2
    run(1, pairs // 2, lambda i: predict(i, (0, 1)))
    settle(asked.at[others_x], r_send.at[0], r_recv.at[0])
    by_py(asked[:, 0, :], asks)
    spread(npy, at_y, lambda r: asks.at[at_y(r)[1]], wanted.at[me_y], r_send.at[1], r_recv.at[1])
    wanted[me_y] = asks[me_y]
    run(pairs // 2, pairs - 1, lambda i: predict(i, (0, 1)))
    predict(0, (1,))
    predict(pairs - 1, (0,))
    for copy in halo:
        copy.wait()
    edge = jnp.zeros((nyl, HALF), F32)

    @pl.when(first_x)
    def _():
        for c in range(3):
            for h in range(halves):
                vp[c, h, 0, 8:top, :] = edge
                up[c, h, 0, 8:top, :] = edge

    @pl.when(last_x)
    def _():
        for c in range(3):
            for h in range(halves):
                vp[c, h, nxl + 1, 8:top, :] = edge
                up[c, h, nxl + 1, 8:top, :] = edge
    predict(0, (0,))
    predict(pairs - 1, (1,))

    flat0 = w0.reshape(halves, (nxl + 2) * nyl, HALF)
    flat2 = w2.reshape(halves, nxl * nyl, HALF)
    for side, y, inside in ((0, 0, first_y), (1, nyl - 1, last_y)):
        sign = -0.5 if side == 0 else 0.5
        for h in range(halves):
            solid = mk[:, y, h * HALF:(h + 1) * HALF].astype(F32)
            scale = jnp.where(inside, 0.0, DT / (1.0 + (DT * ALPHA) * solid))
            beyond = [rcv_y[side, n, h].astype(F32) for n in range(6)]
            weigh = scale * (NU + sign * row_at(up, (1, h), y + 8)[...])
            slope = sum(row_at(vp, (a, h), y + 8)[...] * beyond[3 + a] for a in range(3))
            here = flat0.at[h, pl.ds(nyl + y, nxl, stride=nyl), :]
            here[...] = here[...] + weigh * beyond[0]
            here = row_at(w1, (h,), y + 8)
            here[...] = here[...] + (weigh * beyond[1] - (sign * scale) * slope)
            here = flat2.at[h, pl.ds(y, nxl, stride=nyl), :]
            here[...] = here[...] + weigh * beyond[2]

    for h in range(halves):
        wy_snd[0, h] = row_at(w1, (h,), top - 1)[...]
        wy_snd[1, h] = row_at(w1, (h,), 8)[...]
    halo = y_pair(wy_snd, wy_rcv, 2) + x_pair(w0, lambda field, x: field.at[:, x], 4)
    for copy in halo:
        copy.start()

    settle(wanted.at[others_y], r_send.at[1], r_recv.at[1])

    slot_lane = lax.broadcasted_iota(jnp.int32, (npx, HALF), 1).astype(F32)

    def choose(j, carry):
        label = wanted[j]
        for r in range(2):
            hit = jnp.broadcast_to(label[:, r * npy:r * npy + 1], (npx, HALF)) == slot_lane
            chosen[pl.ds(pl.multiple_of((2 * j + r) * npx, npx), npx), :] = hit.astype(F32).astype(BF16)
        return carry

    lax.fori_loop(0, npy, choose, 0)
    controls = basis.shape[0]
    wide_basis = jnp.concatenate([basis[...], jnp.zeros((HALF - controls, SEG), F32)], axis=0)
    rows = sum(
        jnp.dot(chosen[...], part, preferred_element_type=F32) for part in reversed(split(wide_basis, 3))
    )
    for j in range(npy):
        reply[j] = rows[j * 2 * npx:(j + 1) * 2 * npx]
    spread(npy, at_y, lambda r: reply.at[at_y(r)[1]], replies.at[me_y], r_send.at[2], r_recv.at[2])
    replies[me_y] = reply[me_y]

    lane = lax.broadcasted_iota(jnp.int32, (nyl, HALF), 1)

    def flux_plane(x, carry):
        face = jnp.where(lane == HALF - 1, w2[halves - 1, x], 0.0)
        which = idb[x]
        return tuple(total + jnp.where(which == k, face, 0.0) for k, total in enumerate(carry))

    zero = jnp.zeros((nyl, HALF), F32)
    totals = lax.fori_loop(0, nxl, flux_plane, (zero,) * OUTLETS)
    fsum[0] = jnp.concatenate([jnp.sum(t, axis=0, keepdims=True) for t in totals], axis=0)

    spread(npx, at_x, lambda r: fsum.at[0], fr1.at[me_x], f_send.at[0], f_recv.at[0])
    fr1[me_x] = fsum[0]

    for copy in halo:
        copy.wait()
    for h in range(halves):
        row_at(w1, (h,), 7)[...] = jnp.where(first_y, 0.0, wy_rcv[0, h])
        row_at(w1, (h,), top)[...] = jnp.where(last_y, 0.0, wy_rcv[1, h])

    @pl.when(first_x)
    def _():
        for h in range(halves):
            w0[h, 0] = edge

    @pl.when(last_x)
    def _():
        for h in range(halves):
            w0[h, nxl + 1] = edge

    def diverge(x, carry):
        deep = jnp.concatenate([w2[h, x] for h in range(halves)], axis=1)
        below, above = z_shift(deep, 0.0, 0.0)
        for h in range(halves):
            cut = slice(h * HALF, (h + 1) * HALF)
            rise = w1[h, x + 1, pl.ds(9 + zero_at, nyl), :] - w1[h, x + 1, pl.ds(7 + zero_at, nyl), :]
            total = (w0[h, x + 2] - w0[h, x]) + rise + (above - below)[:, cut]
            div[h, pl.ds(x, nyl, stride=nxl), :] = 0.5 * total
        return carry

    lax.fori_loop(0, nxl, diverge, 0)

    for copy in load_t:
        copy.wait()

    def depth_piece(c, carry):
        here = pl.ds(pl.multiple_of(c * 256, 256), 256)
        value = jnp.concatenate([div[h, here, :] for h in range(halves)], axis=1)
        out = dot_parts((tz[0], tz[1]), split(value, 2), ((1,), (1,)))
        for p in range(npx):
            msg[p, c] = out[p * kzl:(p + 1) * kzl]
        spread(npx, at_x, lambda r: msg.at[at_x(r)[0], c], got.at[me_x, c], a_send.at[c], a_recv.at[c])
        return carry

    lax.fori_loop(0, pieces, depth_piece, 0)

    settle(fr1.at[others_x], f_send.at[0], f_recv.at[0])
    fsum[1] = jnp.sum(fr1[...], axis=0)
    spread(npy, at_y, lambda r: fsum.at[1], fr2.at[me_y], f_send.at[1], f_recv.at[1])
    fr2[me_y] = fsum[1]
    settle(replies.at[others_y], r_send.at[2], r_recv.at[2])
    lines = replies.reshape(npy * 2 * npx, SEG)
    for p in range(npx):
        for r in range(2):
            fetch[p, r * npy:(r + 1) * npy, :] = lines[pl.ds(r * npx + p, npy, stride=2 * npx), :]
    spread(npx, at_x, lambda r: fetch.at[at_x(r)[0]], fetched.at[me_x], r_send.at[3], r_recv.at[3])
    fetched[me_x] = fetch[me_x]

    owner_table()

    def table_cell(i, carry):
        c, g = carry
        right = jnp.where((i == nyl - 1) & last_y, 0.0, 1.0)
        inv, k = reduce_cell(c, g, right)
        tau[i] = inv
        kap[i] = k
        return k, mu + g * inv

    tau[0] = jnp.zeros_like(mu)
    kap[0] = jnp.ones_like(mu)
    lax.fori_loop(1, nyl, table_cell, (jnp.ones_like(mu), mu))

    settle(fr2.at[others_y], f_send.at[1], f_recv.at[1])
    flux = jnp.sum(fr2[...], axis=0) * (1.0 / (nx * npy * nyl))
    press = []
    for k in range(OUTLETS):
        total = resist[k, 0] * flux[0:1]
        for n in range(1, OUTLETS):
            total = total + resist[k, n] * flux[n:n + 1]
        press.append(total[:, HALF - 1:HALF])

    def pressures(which):
        drop = jnp.zeros(which.shape, F32)
        for k in range(OUTLETS):
            drop = jnp.where(which == k, jnp.broadcast_to(press[k], which.shape), drop)
        return drop

    quarter = lane // nxl
    for n in range(npx // 4):
        which = asked[4 * n, 8:top, :]
        for a in range(1, 4):
            which = jnp.where(quarter == a, pltpu.roll(asked[4 * n + a, 8:top, :], a * nxl, 1), which)
        outlet[:, n * HALF:(n + 1) * HALF] = pressures(which)
    weight = jnp.broadcast_to(lam_z[pl.ds(pl.multiple_of(me_x * kzl, kzl), kzl), 1:2], (kzl, nx))

    wides = npx // 4

    def row_of(i):
        return pl.ds(pl.multiple_of(i * kzl, kzl), kzl)

    def piece_rows(c):
        return pl.ds(pl.multiple_of(c * per * kzl, per * kzl), per * kzl)

    def line_piece(c, carry):
        got[me_x, c] = msg[me_x, c]
        settle(got.at[others_x, c], a_send.at[c], a_recv.at[c])

        def gather(sg, inner):
            for half in range(per // 4):
                out = swap_groups([got[4 * sg + a, c, :, half * HALF:(half + 1) * HALF] for a in range(4)])
                for b in range(4):
                    y = c * per + 4 * half + b
                    cols[row_of(y), pl.ds(pl.multiple_of(sg * HALF, HALF), HALF)] = out[b]
            return inner

        lax.fori_loop(0, wides, gather, 0)

        def add_outlet(m, inner):
            y = c * per + m
            line = jnp.broadcast_to(outlet[pl.ds(y, 1), :], (kzl, nx))
            cols[row_of(y), :] = cols[row_of(y), :] + weight * line
            return inner

        lax.fori_loop(0, per, add_outlet, 0)
        rows = piece_rows(c)
        cols[rows, :] = dot_parts(split(cols[rows, :], 2), (tt[0], tt[1]), ((1,), (0,)))
        return carry

    lax.fori_loop(0, pieces, line_piece, 0)

    def down(i, carry):
        r, ends = carry
        ends = ends + kap[i] * r
        nxt = cols[row_of(i + 1), :] + tau[i] * r
        cols[row_of(i + 1), :] = nxt
        return nxt, ends

    r, ends = lax.fori_loop(1, nyl - 1, down, (cols[row_of(1), :], cols[row_of(0), :]))
    ends = ends + kap[nyl - 1] * r
    over = tau[nyl - 1] * r
    for j in range(npy):
        isnd[j, 0:kown, :] = ends[j * kown:(j + 1) * kown]
        isnd[j, kown:2 * kown, :] = over[j * kown:(j + 1) * kown]

    spread(npy, at_y, lambda r: isnd.at[at_y(r)[1]], ircv.at[me_y], i_send.at[0], i_recv.at[0])
    ircv[me_y] = isnd[me_y]
    settle(ircv.at[others_y], i_send.at[0], i_recv.at[0])

    rho = []
    for b in range(npy):
        value = ircv[b, 0:kown, :]
        if b > 0:
            value = value + ircv[b - 1, kown:2 * kown, :]
        rho.append(value)
    depth_mode = lax.broadcasted_iota(jnp.int32, (kown, nx), 0) + me_x * kzl + me_y * kown
    row_mode = lax.broadcasted_iota(jnp.int32, (kown, nx), 1)
    mean = sum(rho[1:], rho[0]) * (1.0 / (npy * nyl))
    mean = jnp.where((depth_mode == 0) & (row_mode == 0), mean, 0.0)
    half_sum = (nyl - 1) / 2.0
    for b in range(npy):
        weight = 1.0 + (0.0 if b == 0 else half_sum) + (2.0 * half_sum if b == npy - 1 else half_sum)
        rho[b] = rho[b] - weight * mean
    for b in range(npy - 1):
        rho[b + 1] = rho[b + 1] + owner_phi[b] * rho[b]
    value = -owner_inv[npy - 1] * rho[npy - 1]
    jsnd[npy - 1, 0:kown, :] = value
    jsnd[npy - 1, kown:2 * kown, :] = jnp.zeros_like(value)
    jsnd[npy - 1, 2 * kown:3 * kown, :] = mean
    for b in range(npy - 2, -1, -1):
        jsnd[b, kown:2 * kown, :] = value
        value = owner_phi[b] * value - owner_inv[b] * rho[b]
        jsnd[b, 0:kown, :] = value
        jsnd[b, 2 * kown:3 * kown, :] = mean

    spread(npy, at_y, lambda r: jsnd.at[at_y(r)[1]], jrcv.at[me_y], i_send.at[1], i_recv.at[1])
    jrcv[me_y] = jsnd[me_y]
    settle(jrcv.at[others_y], i_send.at[1], i_recv.at[1])
    for j in range(npy):
        for part in range(3):
            back[part, j * kown:(j + 1) * kown, :] = jrcv[j, part * kown:(part + 1) * kown, :]
    first_value, mean_rows = back[0], back[2]

    def up_piece(n, q):
        c = pieces - 1 - n

        def up_again(m, q):
            i = c * per + per - 1 - m
            share = 0.5 * (i + 1).astype(F32)
            q = tau[i] * (q - cols[row_of(i), :] + mean_rows * share) + kap[i] * first_value
            cols[row_of(i), :] = q
            return q

        q = lax.fori_loop(0, per, up_again, q)
        rows = piece_rows(c)
        cols[rows, :] = dot_parts(split(cols[rows, :], 3), (tx[0], tx[1], tx[2]), ((1,), (0,)))

        def scatter(sg, inner):
            for half in range(per // 4):
                parts = []
                for b in range(4):
                    y = c * per + 4 * half + b
                    parts.append(cols[row_of(y), pl.ds(pl.multiple_of(sg * HALF, HALF), HALF)])
                out = swap_groups(parts)
                for a in range(4):
                    msg[4 * sg + a, c, :, half * HALF:(half + 1) * HALF] = out[a]
            return inner

        lax.fori_loop(0, wides, scatter, 0)
        n = pieces + c
        spread(npx, at_x, lambda r: msg.at[at_x(r)[0], c], got2.at[me_x, c], a_send.at[n], a_recv.at[n])
        return q

    lax.fori_loop(0, pieces, up_piece, back[1])

    shape = (places, cells)
    cell = lax.broadcasted_iota(jnp.int32, shape, 1) * halves
    for h in range(halves):
        hot[h] = (jnp.broadcast_to(pick[...], shape) == cell + h).astype(F32).astype(BF16)

    def lower(x, carry):
        drop = DT * jnp.where(lane == HALF - 1, pressures(idb[x]), 0.0)
        w2[halves - 1, x] = w2[halves - 1, x] - drop
        return carry

    lax.fori_loop(0, nxl, lower, 0)

    pressure = qp.reshape(halves, (nxl + 2) * wide, HALF)

    def rise_piece(n, carry):
        c = pieces - 1 - n
        got2[me_x, c] = msg[me_x, c]
        settle(got2.at[others_x, c], a_send.at[pieces + c], a_recv.at[pieces + c])
        value = got2[:, c].reshape(nz, 256)
        out = dot_parts(split(value.T, 3), (tz[0], tz[1], tz[2]), ((1,), (0,)))
        for y in range(per):
            for h in range(halves):
                pressure[h, pl.ds(wide + 8 + c * per + y, nxl, stride=wide), :] = out[
                    y * nxl:(y + 1) * nxl, h * HALF:(h + 1) * HALF
                ]
        return carry

    lax.fori_loop(0, pieces, rise_piece, 0)

    for h in range(halves):
        qy_snd[0, h] = row_at(qp, (h,), top - 1)[...]
        qy_snd[1, h] = row_at(qp, (h,), 8)[...]
    halo = y_pair(qy_snd, qy_rcv, 4) + x_pair(qp, lambda field, x: field.at[:, x, pl.ds(8, nyl), :], 6)
    for copy in halo:
        copy.start()

    def q_rows(x, y, size):
        return jnp.concatenate([qp[h, x, pl.ds(y, size), :] for h in range(halves)], axis=1)

    def join(field, x):
        return jnp.concatenate([field[h, x, 0:nyl, :] for h in range(halves)], axis=1)

    def flow(a, x):
        return jnp.concatenate([up[a, h, x + 1, 8:top, :] for h in range(halves)], axis=1)

    def two_parts(x, carry):
        center = q_rows(x + 1, 8, nyl)
        spot = lax.broadcasted_iota(jnp.int32, center.shape, 1)
        below = jnp.where(spot == 0, center, pltpu.roll(center, 1, 1))
        above = jnp.where(spot == nz - 1, center, pltpu.roll(center, nz - 1, 1))
        v2 = join(w2, x) - 0.5 * (above - below)
        v0 = join(w0, x + 1) - 0.5 * (q_rows(x + 2, 8, nyl) - q_rows(x, 8, nyl))
        vel[0, x] = v0
        vel[2, x] = v2
        total = flow(0, x) * v0 + flow(2, x) * v2
        for h in range(halves):
            sig[h, pl.ds(pl.multiple_of(x * nyl, 8), nyl), :] = total[:, h * HALF:(h + 1) * HALF]
        return carry

    lax.fori_loop(1, nxl - 1, two_parts, 0)
    outs = [pltpu.make_async_copy(vel.at[b], v_out.at[b], out_sem.at[b]) for b in range(3)]

    for copy in halo:
        copy.wait()
    for h in range(halves):
        row_at(qp, (h,), 7)[...] = jnp.where(first_y, qy_snd[1, h], qy_rcv[0, h])
        row_at(qp, (h,), top)[...] = jnp.where(last_y, qy_snd[0, h], qy_rcv[1, h])

    @pl.when(first_x)
    def _():
        for h in range(halves):
            qp[h, 0, 8:top, :] = qp[h, 1, 8:top, :]

    @pl.when(last_x)
    def _():
        for h in range(halves):
            qp[h, nxl + 1, 8:top, :] = qp[h, nxl, 8:top, :]

    two_parts(0, 0)
    two_parts(nxl - 1, 0)
    outs[0].start()
    outs[2].start()

    def last_part(x, carry):
        deep = jnp.concatenate([w1[h, x + 1, 8:top, :] for h in range(halves)], axis=1)
        v1 = deep - 0.5 * (q_rows(x + 1, 9 + zero_at, nyl) - q_rows(x + 1, 7 + zero_at, nyl))
        vel[1, x] = v1
        rows = pl.ds(pl.multiple_of(x * nyl, 8), nyl)
        part = flow(1, x) * v1
        for h in range(halves):
            sig[h, rows, :] = -ALPHA * (sig[h, rows, :] + part[:, h * HALF:(h + 1) * HALF])
        return carry

    lax.fori_loop(0, nxl, last_part, 0)
    outs[1].start()

    picked = None
    for h in range(halves):
        both = jnp.dot(hot[h], jnp.concatenate(split(sig[h], 2), axis=1), preferred_element_type=F32)
        term = both[:, :SEG] + both[:, SEG:]
        picked = term if picked is None else picked + term
    settle(fetched.at[others_x], r_send.at[3], r_recv.at[3])
    products = picked * fetched[...].reshape(places, SEG)
    ones = jnp.ones((8, SEG), BF16)
    totals = sum(
        lax.dot_general(ones, part, (((1,), (1,)), ((), ())), preferred_element_type=F32)
        for part in reversed(split(products, 3))
    )
    by_px(totals, give)
    spread(npx, at_x, lambda r: give.at[at_x(r)[0]], given.at[me_x], r_send.at[4], r_recv.at[4])
    given[me_x] = give[me_x]
    settle(given.at[others_x], r_send.at[4], r_recv.at[4])
    by_py(given[:, 0, :], gives)
    spread(npy, at_y, lambda r: gives.at[at_y(r)[1]], taken.at[me_y], r_send.at[5], r_recv.at[5])
    taken[me_y] = gives[me_y]
    settle(taken.at[others_y], r_send.at[5], r_recv.at[5])

    def add_up(j, total):
        label, value = wanted[j], taken[j]
        for r in range(2):
            spot = slice(r * npy, r * npy + 1)
            hit = jnp.broadcast_to(label[:, spot], (npx, HALF)) == slot_lane
            total = total + jnp.where(hit, jnp.broadcast_to(value[:, spot], (npx, HALF)), 0.0)
        return total

    total = lax.fori_loop(0, npy, add_up, jnp.zeros((npx, HALF), F32))
    grad_out[...] = jnp.sum(total, axis=0, keepdims=True)[:, :controls]
    for copy in outs:
        copy.wait()


def main_call(dims, args, owner_rows):
    npx, npy, nxl, nyl, nz = dims
    nx = npx * nxl
    kzl = nz // npx
    kown = kzl // npy
    halves = nz // HALF
    wide = nyl + 16
    cells = nxl * nyl
    pieces = cells // 256
    places = 2 * npx * npy
    vmem = pltpu.VMEM
    anywhere = pl.BlockSpec(memory_space=pl.ANY)
    here = pl.BlockSpec(memory_space=pltpu.VMEM)
    far = pl.BlockSpec(memory_space=pltpu.HBM)
    dma = pltpu.SemaphoreType.DMA
    tables = args[10:13]
    field = vmem((3, halves, nxl + 2, wide, HALF), F32)
    line = vmem((nyl, kzl, nx), F32)
    message = vmem((npx, pieces, kzl, 256), F32)
    scratch = [
        field,
        field,
        vmem((3, cells, nz), BF16),
        vmem((3, cells, nz), BF16),
        vmem((nxl, nyl, nz), jnp.int32),
        vmem((nxl, nyl, HALF), jnp.int32),
        vmem((halves, nxl + 2, nyl, HALF), F32),
        vmem((halves, nxl + 2, wide, HALF), F32),
        vmem((halves, nxl, nyl, HALF), F32),
        vmem((2, 6, halves, nxl, HALF), BF16),
        vmem((2, 6, halves, nxl, HALF), BF16),
        vmem((2, halves, nxl, HALF), F32),
        vmem((2, halves, nxl, HALF), F32),
        vmem((2, OUTLETS, HALF), F32),
        vmem((npx, OUTLETS, HALF), F32),
        vmem((npy, OUTLETS, HALF), F32),
        vmem((halves, cells, HALF), F32),
        message,
        message,
        message,
        vmem((nyl * kzl, nx), F32),
        line,
        line,
        vmem((npy, kown, nx), F32),
        vmem((npy, kown, nx), F32),
        vmem((npy, 2 * kown, nx), F32),
        vmem((npy, 2 * kown, nx), F32),
        vmem((npy, 3 * kown, nx), F32),
        vmem((npy, 3 * kown, nx), F32),
        vmem((3, kzl, nx), F32),
        vmem((halves, nxl + 2, wide, HALF), F32),
        vmem((2, halves, nxl, HALF), F32),
        vmem((2, halves, nxl, HALF), F32),
        vmem((3, nxl, nyl, nz), F32),
        vmem((halves, cells, HALF), F32),
        vmem((nyl, nx), F32),
        vmem((halves, places, cells), BF16),
        vmem((places, 1), jnp.int32),
        vmem((npx, 8 + nyl, HALF), F32),
        vmem((npx, 8 + nyl, HALF), F32),
        vmem((npy, npx, HALF), F32),
        vmem((npy, npx, HALF), F32),
        vmem((places, HALF), BF16),
        vmem((npy, 2 * npx, SEG), F32),
        vmem((npy, 2 * npx, SEG), F32),
        vmem((npx, 2 * npy, SEG), F32),
        vmem((npx, 2 * npy, SEG), F32),
        vmem((npx, 8, HALF), F32),
        vmem((npx, 8, HALF), F32),
        vmem((npy, npx, HALF), F32),
        vmem((npy, npx, HALF), F32),
    ]
    scratch += [vmem(t.shape, BF16) for t in tables]
    scratch += [
        pltpu.SMEM(a.shape, a.dtype) if n == 5 else vmem(a.shape, a.dtype)
        for n, a in enumerate(args)
        if n > 3 and not 10 <= n < 13
    ]
    scratch += [
        dma((3 * halves + 14,)),
        dma((8,)),
        dma((8,)),
        dma((6,)),
        dma((6,)),
        dma((2,)),
        dma((2,)),
        dma((2 * pieces,)),
        dma((2 * pieces,)),
        dma((2,)),
        dma((2,)),
        dma((6,)),
        dma((6,)),
        dma((3,)),
    ]
    return pl.pallas_call(
        functools.partial(main_kernel, dims),
        out_shape=(
            jax.ShapeDtypeStruct((3, nxl, nyl, nz), F32),
            jax.ShapeDtypeStruct((1, owner_rows), F32),
        ),
        in_specs=[far] * len(args),
        out_specs=(anywhere, here),
        scratch_shapes=scratch,
        compiler_params=pltpu.CompilerParams(
            collective_id=0, has_side_effects=True, vmem_limit_bytes=58 * 2**20
        ),
        name="project",
    )(*args)


def local(
    base_flow, adjoint_start, source, solid_mask, outlet_ids, resist,
    tile_owner, tile_slot, tile_column, control_basis,
):
    _, nxl, nyl, nz = adjoint_start.shape
    npx, npy = lax.axis_size("px"), lax.axis_size("py")
    nx = npx * nxl
    tz, tx = table_np(nz), table_np(nx)
    tables = [split_np(tz, 3), split_np(tx, 3), split_np(np.ascontiguousarray(tx.T), 2)]
    tables = [jnp.asarray(np.stack(t)) for t in tables]
    lam_x = jnp.asarray(-eigen_np(nx)[None, :])
    depth = np.zeros((nz, HALF), np.float32)
    depth[:, 0] = -eigen_np(nz)
    depth[:, 1] = -0.5 * DT * tz[:, nz - 2]
    depth = jnp.asarray(depth)
    args = (
        adjoint_start,
        base_flow.reshape(3, nxl * nyl, nz),
        source.reshape(3, nxl * nyl, nz),
        solid_mask,
        outlet_ids.T,
        resist,
        tile_owner.reshape(1, -1),
        tile_slot.reshape(1, -1),
        tile_column.reshape(1, -1),
        control_basis,
        *tables,
        lam_x,
        depth,
    )
    velocity, grad = main_call((npx, npy, nxl, nyl, nz), args, control_basis.shape[0])
    return velocity, grad.reshape(-1)


def solution(mesh):
    in_specs = (
        P(None, "px", "py", None),
        P(None, "px", "py", None),
        P(None, "px", "py", None),
        P("px", "py", None),
        P("px", "py"),
        P(),
        P(("px", "py"), None),
        P(("px", "py")),
        P(("px", "py")),
        P(("px", "py"), None),
    )
    out_specs = (P(None, "px", "py", None), P(("px", "py")))
    return jax.shard_map(local, mesh=mesh, in_specs=in_specs, out_specs=out_specs, check_vma=False)
```

```python
import functools
import math

import jax
import jax.numpy as jnp
import numpy as np
from jax import lax
from jax.experimental import pallas as pl
from jax.experimental.pallas import tpu as pltpu
from jax.sharding import PartitionSpec as P

SEG = 128
OUTLETS = 8
DT = 0.1
NU = 0.5
ALPHA = 5.0
HALF = 128
MESH = pl.DeviceIdType.MESH
F32 = jnp.float32
BF16 = jnp.bfloat16


def table_np(count):
    order = np.arange(count).astype(np.float32)
    modes = order[:, None]
    points = order[None, :]
    weights = np.where(modes == 0.0, math.sqrt(1.0 / count), math.sqrt(2.0 / count)).astype(np.float32)
    angle = np.float32(np.pi) * (points + np.float32(0.5)) * modes / np.float32(count)
    return (weights * np.cos(angle.astype(np.float32))).astype(np.float32)


def eigen_np(count):
    order = np.arange(count).astype(np.float32)
    angle = (np.float32(np.pi) * order / np.float32(count)).astype(np.float32)
    return (np.float32(2.0) * np.cos(angle) - np.float32(2.0)).astype(np.float32)


def split_np(table, count):
    parts = []
    for _ in range(count):
        parts.append(table.astype(jnp.bfloat16))
        table = table - parts[-1].astype(np.float32)
    return tuple(parts)


def split(value, count):
    parts = []
    for _ in range(count):
        parts.append(value.astype(BF16))
        value = value - parts[-1].astype(F32)
    return tuple(parts)


def dot_parts(a_parts, b_parts, contract):
    dims = ((contract[0], contract[1]), ((), ()))
    count, rows = len(a_parts), a_parts[0].shape[0]
    terms = {}
    for j in range(count):
        stacked = jnp.concatenate(a_parts[:count - j], axis=0) if j < count - 1 else a_parts[0]
        out = lax.dot_general(stacked, b_parts[j], dimension_numbers=dims, preferred_element_type=F32)
        for i in range(count - j):
            terms[i, j] = out[i * rows:(i + 1) * rows]
    total = None
    for i, j in sorted(terms, key=lambda at: -(at[0] + at[1])):
        total = terms[i, j] if total is None else total + terms[i, j]
    return total


def swap_groups(tiles):
    lane = lax.broadcasted_iota(jnp.int32, tiles[0].shape, 1)
    odd = (lane // 32) % 2 == 1
    far = lane >= 64
    t0, t1, t2, t3 = tiles
    a0 = jnp.where(odd, pltpu.roll(t1, 32, 1), t0)
    a1 = jnp.where(odd, t1, pltpu.roll(t0, 96, 1))
    a2 = jnp.where(odd, pltpu.roll(t3, 32, 1), t2)
    a3 = jnp.where(odd, t3, pltpu.roll(t2, 96, 1))
    return (
        jnp.where(far, pltpu.roll(a2, 64, 1), a0),
        jnp.where(far, pltpu.roll(a3, 64, 1), a1),
        jnp.where(far, a2, pltpu.roll(a0, 64, 1)),
        jnp.where(far, a3, pltpu.roll(a1, 64, 1)),
    )


def z_shift(field, edge_low, edge_high):
    depth = field.shape[1]
    lane = lax.broadcasted_iota(jnp.int32, field.shape, 1)
    below = jnp.where(lane == 0, edge_low, pltpu.roll(field, 1, 1))
    above = jnp.where(lane == depth - 1, edge_high, pltpu.roll(field, depth - 1, 1))
    return below, above


def main_kernel(
    dims,
    v_hbm, u_hbm, s_hbm, m_hbm, ids_hbm, resist_hbm, owner_hbm, slot_hbm, column_hbm, basis_hbm,
    tz_hbm, tx_hbm, tt_hbm, lam_x_hbm, lam_z_hbm,
    v_out, grad_out,
    vp, up, ub, sb, mk, idb, w0, w1, w2, snd_y, rcv_y, wy_snd, wy_rcv, fsum, fr1, fr2,
    div, msg, got, got2, cols, tau, kap, owner_inv, owner_phi,
    isnd, ircv, jsnd, jrcv, back, qp, qy_snd, qy_rcv, vel, sig,
    outlet, hot, pick, ask, asked, asks, wanted, chosen, reply, replies, fetch, fetched, give, given, gives, taken,
    tz, tx, tt, ids, resist, owner_row, slot_row, column_row, basis, lam_x, lam_z,
    load_sem, x_send, x_recv, y_send, y_recv, f_send, f_recv, a_send, a_recv, i_send, i_recv, r_send, r_recv, out_sem,
):
    npx, npy, nxl, nyl, nz = dims
    nx = npx * nxl
    kzl = nz // npx
    kown = kzl // npy
    halves = nz // HALF
    cells = nxl * nyl
    per = 256 // nxl
    pieces = nyl // per
    group = 2 * npy
    places = npx * group
    me_x = lax.axis_index("px")
    me_y = lax.axis_index("py")
    right_x, left_x = lax.rem(me_x + 1, npx), lax.rem(me_x + npx - 1, npx)
    right_y, left_y = lax.rem(me_y + 1, npy), lax.rem(me_y + npy - 1, npy)
    first_x, last_x = me_x == 0, me_x == npx - 1
    first_y, last_y = me_y == 0, me_y == npy - 1
    top = 8 + nyl
    wide = nyl + 16
    zero_at = jnp.minimum(me_x, 0)

    def run(first, last, action):
        def body(r, carry):
            action(r)
            return carry

        lax.fori_loop(first, last, body, 0)

    def remote(src, dst, send, recv, target):
        return pltpu.make_async_remote_copy(
            src_ref=src, dst_ref=dst, send_sem=send, recv_sem=recv, device_id=target, device_id_type=MESH
        )

    def at_x(r):
        return (lax.rem(me_x + r, npx), me_y)

    def at_y(r):
        return (me_x, lax.rem(me_y + r, npy))

    def spread(count, target, src, dst, send, recv):
        def start(n):
            r = (n + (count // 2 - 2)) % (count - 1) + 1
            remote(src(r), dst, send, recv, target(r)).start()

        for n in range(1, count):
            start(n)

    def settle(like, send, recv):
        pltpu.make_async_copy(like, like, send).wait()
        pltpu.make_async_copy(like, like, recv).wait()

    others_x, others_y = pl.ds(0, npx - 1), pl.ds(0, npy - 1)

    loads = []
    for c in range(3):
        for h in range(halves):
            loads.append(
                pltpu.make_async_copy(
                    v_hbm.at[c, :, :, pl.ds(h * HALF, HALF)],
                    vp.at[c, h, pl.ds(1, nxl), pl.ds(8, nyl), :],
                    load_sem.at[c * halves + h],
                )
            )
    base = 3 * halves
    load_u = pltpu.make_async_copy(u_hbm, ub, load_sem.at[base])
    load_s = pltpu.make_async_copy(s_hbm, sb, load_sem.at[base + 1])
    load_m = pltpu.make_async_copy(m_hbm, mk, load_sem.at[base + 2])
    load_t = [
        pltpu.make_async_copy(a, b, load_sem.at[base + 3 + n])
        for n, (a, b) in enumerate(((tz_hbm, tz), (tx_hbm, tx), (tt_hbm, tt)))
    ]
    load_small = [
        pltpu.make_async_copy(a, b, load_sem.at[base + 6 + n])
        for n, (a, b) in enumerate(
            (
                (ids_hbm, ids), (resist_hbm, resist), (owner_hbm, owner_row), (slot_hbm, slot_row),
                (column_hbm, column_row), (basis_hbm, basis), (lam_x_hbm, lam_x), (lam_z_hbm, lam_z),
            )
        )
    ]
    for copy in load_small:
        copy.start()
    for copy in loads:
        copy.start()
    load_u.start()
    load_s.start()
    load_m.start()
    for copy in load_t:
        copy.start()

    barrier = pltpu.get_barrier_semaphore()
    for r in range(1, npx):
        pl.semaphore_signal(barrier, inc=1, device_id=at_x(r), device_id_type=MESH)
    for r in range(1, npy):
        pl.semaphore_signal(barrier, inc=1, device_id=at_y(r), device_id_type=MESH)

    def row_at(ref, lead, y):
        lines = ref.reshape(*ref.shape[:-3], (nxl + 2) * wide, HALF)
        return lines.at[(*lead, pl.ds(wide + y, nxl, stride=wide), slice(None))]

    def x_pair(field, at, number):
        return (
            remote(at(field, nxl), at(field, 0), x_send.at[number], x_recv.at[number], (right_x, me_y)),
            remote(at(field, 1), at(field, nxl + 1), x_send.at[number + 1], x_recv.at[number + 1], (left_x, me_y)),
        )

    def at_plane(field, x):
        return field.at[:, :, x, pl.ds(8, nyl), :]

    def y_pair(send, recv, number):
        return (
            remote(send.at[0], recv.at[0], y_send.at[number], y_recv.at[number], (me_x, right_y)),
            remote(send.at[1], recv.at[1], y_send.at[number + 1], y_recv.at[number + 1], (me_x, left_y)),
        )

    for copy in load_small:
        copy.wait()

    count = owner_row.shape[1]
    owners = owner_row[...]
    same = jnp.broadcast_to(owners, (8, count)).T[:, 0:1] == owners
    earlier = lax.broadcasted_iota(jnp.int32, (count, count), 0) < lax.broadcasted_iota(
        jnp.int32, (count, count), 1
    )
    rank = jnp.sum(jnp.where(same & earlier, 1, 0), axis=0, keepdims=True)
    owner_x = owners // npy
    place = owner_x * group + rank * npy + (owners - owner_x * npy)
    match = lax.broadcasted_iota(jnp.int32, (places, count), 0) == place
    pick[...] = jnp.sum(jnp.where(match, column_row[...] + 1, 0), axis=1, keepdims=True) - 1
    slots = jnp.broadcast_to((slot_row[...] + 1).astype(F32), (8, count)).astype(BF16)
    requests = (
        lax.dot_general(
            slots, match.astype(F32).astype(BF16), (((1,), (1,)), ((), ())), preferred_element_type=F32
        )
        - 1.0
    )

    def pad_lanes(row):
        if row.shape[1] >= HALF:
            return row
        return jnp.concatenate([row, jnp.zeros((8, HALF - row.shape[1]), F32)], axis=1)

    def by_px(row, ref):
        row = pad_lanes(row)
        lanes = row.shape[1]
        for p in range(npx):
            ref[p, 0:8, :] = pltpu.roll(row, (lanes - group * p) % lanes, 1)[:, :HALF]

    def by_py(rows, ref):
        for j in range(npy):
            ref[j] = pltpu.roll(rows, (HALF - j) % HALF, 1)

    by_px(requests, ask)
    seen = ids[...]
    padded = jnp.concatenate([seen.astype(F32), jnp.zeros((nyl, HALF - nxl), F32)], axis=1)
    for p in range(npx):
        ask[p, 8:top, :] = padded
    for x in range(nxl):
        idb[x] = jnp.broadcast_to(seen[:, x:x + 1], (nyl, HALF))

    def ask_start():
        spread(npx, at_x, lambda r: ask.at[at_x(r)[0]], asked.at[me_x], r_send.at[0], r_recv.at[0])
        asked[me_x] = ask[me_x]

    for copy in loads:
        copy.wait()

    def pack(field, first):
        for c in range(3):
            for h in range(halves):
                snd_y[0, first + c, h] = row_at(field, (c, h), top - 1)[...].astype(BF16)
                snd_y[1, first + c, h] = row_at(field, (c, h), 8)[...].astype(BF16)

    pack(vp, 0)
    load_u.wait()

    def widen(i, carry):
        for a in range(3):
            pair = ub[a, pl.ds(pl.multiple_of(i * 2 * nyl, 2 * nyl), 2 * nyl), :].astype(F32)
            for s in range(2):
                for h in range(halves):
                    up[a, h, 1 + 2 * i + s, 8:top, :] = pair[s * nyl:(s + 1) * nyl, h * HALF:(h + 1) * HALF]
        return carry

    lax.fori_loop(0, nxl // 2, widen, 0)
    pack(up, 3)
    pl.semaphore_wait(barrier, npx - 1 + npy - 1)
    ask_start()
    halo = y_pair(snd_y, rcv_y, 0) + x_pair(vp, at_plane, 0) + x_pair(up, at_plane, 2)
    for copy in halo:
        copy.start()
    def reduce_cell(c, g, right):
        inv = 1.0 / (c + right + g)
        return inv, c * inv

    mine = lam_z[pl.ds(pl.multiple_of(me_x * kzl, kzl), kzl), 0:1]
    mu = lam_x[...] + mine
    owned = lam_z[pl.ds(me_x * kzl + me_y * kown, kown), 0:1]
    muo = lam_x[...] + owned

    def owner_table():
        def owner_cell(i, carry):
            c, g, ground = carry
            inv, k = reduce_cell(c, g, 1.0)
            return k, muo + g * inv, ground + k * g

        one = jnp.ones_like(muo)
        c, g, ground = lax.fori_loop(1, nyl - 1, owner_cell, (one, muo, jnp.zeros_like(one)))
        inv, link = reduce_cell(c, g, 1.0)
        from_left = g * inv
        end_ground = muo + from_left + (ground + c * (g / (c + g)))
        ground = ground + link * g
        held = muo + ground
        for b in range(npy - 1):
            inv = 1.0 / (link + held)
            phi = link * inv
            owner_inv[b] = inv
            owner_phi[b] = phi
            nxt = end_ground if b == npy - 2 else muo + ground + from_left
            held = nxt + phi * held
        positive = held > 0.0
        owner_inv[npy - 1] = jnp.where(positive, 1.0 / jnp.where(positive, held, 1.0), 0.0)

    load_s.wait()
    load_m.wait()

    blank = jnp.zeros((nxl, HALF), F32)
    for c in range(3):
        for h in range(halves):
            for field in (vp, up):
                row_at(field, (c, h), 7)[...] = blank
                row_at(field, (c, h), top)[...] = blank

    def rows_at(field, c, x, start, size=8):
        return jnp.concatenate([field[c, h, x, pl.ds(start, size), :] for h in range(halves)], axis=1)

    tiles = nyl // 8

    def predict(i, planes):
        for k in range(tiles):
            if all((2 * k + s) // tiles not in planes for s in range(2)):
                continue
            rows = pl.ds(pl.multiple_of(i * 2 * nyl + 16 * k, 16), 16)
            forcing = [sb[b, rows, :].astype(F32) for b in range(3)]
            for s in range(2):
                n = 2 * k + s
                if n // tiles not in planes:
                    continue
                x = 2 * i + n // tiles
                y = 8 * (n % tiles)
                scale = 1.0 - (DT * ALPHA / (1.0 + DT * ALPHA)) * mk[x, y:y + 8, :].astype(F32)
                u = [rows_at(up, a, x + 1, y + 8) for a in range(3)]
                v = [rows_at(vp, a, x + 1, y + 8) for a in range(3)]
                low, high = y + 7 + zero_at, y + 9 + zero_at
                slopes = [None] * 3
                for a in range(3):
                    below, above = z_shift(u[a], 0.0, 0.0)
                    diffs = (
                        rows_at(up, a, x + 2, y + 8) - rows_at(up, a, x, y + 8),
                        rows_at(up, a, x + 1, high) - rows_at(up, a, x + 1, low),
                        above - below,
                    )
                    for b in range(3):
                        term = v[a] * diffs[b]
                        slopes[b] = term if slopes[b] is None else slopes[b] + term
                for b in range(3):
                    xm, xp = rows_at(vp, b, x, y + 8), rows_at(vp, b, x + 2, y + 8)
                    ym, yp = rows_at(vp, b, x + 1, low), rows_at(vp, b, x + 1, high)
                    zm, zp = z_shift(v[b], 0.0, 0.0)
                    convect = u[0] * (xp - xm) + u[1] * (yp - ym) + u[2] * (zp - zm)
                    lap = (xp + xm) + (yp + ym) + (zp + zm) - 6.0 * v[b]
                    change = 0.5 * (convect - slopes[b]) + NU * lap + forcing[b][8 * s:8 * s + 8]
                    w = (v[b] + DT * change) * scale
                    for h in range(halves):
                        part = w[:, h * HALF:(h + 1) * HALF]
                        if b == 0:
                            w0[h, x + 1, y:y + 8, :] = part
                        elif b == 1:
                            w1[h, x + 1, y + 8:y + 16, :] = part
                        else:
                            w2[h, x, y:y + 8, :] = part

    pairs = nxl // 2
    settle(asked.at[others_x], r_send.at[0], r_recv.at[0])
    by_py(asked[:, 0, :], asks)
    spread(npy, at_y, lambda r: asks.at[at_y(r)[1]], wanted.at[me_y], r_send.at[1], r_recv.at[1])
    wanted[me_y] = asks[me_y]
    run(1, pairs // 2 + 1, lambda i: predict(i, (0, 1)))
    settle(wanted.at[others_y], r_send.at[1], r_recv.at[1])

    slot_lane = lax.broadcasted_iota(jnp.int32, (npx, HALF), 1).astype(F32)

    def choose(j, carry):
        label = wanted[j]
        for r in range(2):
            hit = jnp.broadcast_to(label[:, r * npy:r * npy + 1], (npx, HALF)) == slot_lane
            chosen[pl.ds(pl.multiple_of((2 * j + r) * npx, npx), npx), :] = hit.astype(F32).astype(BF16)
        return carry

    lax.fori_loop(0, npy, choose, 0)
    controls = basis.shape[0]
    wide_basis = jnp.concatenate([basis[...], jnp.zeros((HALF - controls, SEG), F32)], axis=0)
    rows = sum(
        jnp.dot(chosen[...], part, preferred_element_type=F32) for part in reversed(split(wide_basis, 3))
    )
    for j in range(npy):
        reply[j] = rows[j * 2 * npx:(j + 1) * 2 * npx]
    spread(npy, at_y, lambda r: reply.at[at_y(r)[1]], replies.at[me_y], r_send.at[2], r_recv.at[2])
    replies[me_y] = reply[me_y]
    run(pairs // 2 + 1, pairs - 1, lambda i: predict(i, (0, 1)))
    predict(0, (1,))
    predict(pairs - 1, (0,))
    for copy in halo:
        copy.wait()
    edge = jnp.zeros((nyl, HALF), F32)

    @pl.when(first_x)
    def _():
        for c in range(3):
            for h in range(halves):
                vp[c, h, 0, 8:top, :] = edge
                up[c, h, 0, 8:top, :] = edge

    @pl.when(last_x)
    def _():
        for c in range(3):
            for h in range(halves):
                vp[c, h, nxl + 1, 8:top, :] = edge
                up[c, h, nxl + 1, 8:top, :] = edge
    predict(0, (0,))
    predict(pairs - 1, (1,))

    flat0 = w0.reshape(halves, (nxl + 2) * nyl, HALF)
    flat2 = w2.reshape(halves, nxl * nyl, HALF)
    for side, y, inside in ((0, 0, first_y), (1, nyl - 1, last_y)):
        sign = -0.5 if side == 0 else 0.5
        for h in range(halves):
            solid = mk[:, y, h * HALF:(h + 1) * HALF].astype(F32)
            scale = jnp.where(inside, 0.0, DT - (DT * DT * ALPHA / (1.0 + DT * ALPHA)) * solid)
            beyond = [rcv_y[side, n, h].astype(F32) for n in range(6)]
            weigh = scale * (NU + sign * row_at(up, (1, h), y + 8)[...])
            slope = sum(row_at(vp, (a, h), y + 8)[...] * beyond[3 + a] for a in range(3))
            here = flat0.at[h, pl.ds(nyl + y, nxl, stride=nyl), :]
            here[...] = here[...] + weigh * beyond[0]
            here = row_at(w1, (h,), y + 8)
            here[...] = here[...] + (weigh * beyond[1] - (sign * scale) * slope)
            here = flat2.at[h, pl.ds(y, nxl, stride=nyl), :]
            here[...] = here[...] + weigh * beyond[2]

    for h in range(halves):
        wy_snd[0, h] = row_at(w1, (h,), top - 1)[...]
        wy_snd[1, h] = row_at(w1, (h,), 8)[...]
    halo = y_pair(wy_snd, wy_rcv, 2) + x_pair(w0, lambda field, x: field.at[:, x], 4)
    for copy in halo:
        copy.start()

    lane = lax.broadcasted_iota(jnp.int32, (nyl, HALF), 1)

    def flux_plane(x, carry):
        face = jnp.where(lane == HALF - 1, w2[halves - 1, x], 0.0)
        which = idb[x]
        return tuple(total + jnp.where(which == k, face, 0.0) for k, total in enumerate(carry))

    zero = jnp.zeros((nyl, HALF), F32)
    totals = lax.fori_loop(0, nxl, flux_plane, (zero,) * OUTLETS)
    fsum[0] = jnp.concatenate([jnp.sum(t, axis=0, keepdims=True) for t in totals], axis=0)

    spread(npx, at_x, lambda r: fsum.at[0], fr1.at[me_x], f_send.at[0], f_recv.at[0])
    fr1[me_x] = fsum[0]

    for copy in halo:
        copy.wait()
    for h in range(halves):
        row_at(w1, (h,), 7)[...] = jnp.where(first_y, 0.0, wy_rcv[0, h])
        row_at(w1, (h,), top)[...] = jnp.where(last_y, 0.0, wy_rcv[1, h])

    @pl.when(first_x)
    def _():
        for h in range(halves):
            w0[h, 0] = edge

    @pl.when(last_x)
    def _():
        for h in range(halves):
            w0[h, nxl + 1] = edge

    def diverge(x, carry):
        deep = jnp.concatenate([w2[h, x] for h in range(halves)], axis=1)
        below, above = z_shift(deep, 0.0, 0.0)
        for h in range(halves):
            cut = slice(h * HALF, (h + 1) * HALF)
            rise = w1[h, x + 1, pl.ds(9 + zero_at, nyl), :] - w1[h, x + 1, pl.ds(7 + zero_at, nyl), :]
            total = (w0[h, x + 2] - w0[h, x]) + rise + (above - below)[:, cut]
            div[h, pl.ds(x, nyl, stride=nxl), :] = 0.5 * total
        return carry

    lax.fori_loop(0, nxl, diverge, 0)

    for copy in load_t:
        copy.wait()

    def depth_piece(c, carry):
        here = pl.ds(pl.multiple_of(c * 256, 256), 256)
        value = jnp.concatenate([div[h, here, :] for h in range(halves)], axis=1)
        out = dot_parts((tz[0], tz[1]), split(value, 2), ((1,), (1,)))
        for p in range(npx):
            msg[p, c] = out[p * kzl:(p + 1) * kzl]
        spread(npx, at_x, lambda r: msg.at[at_x(r)[0], c], got.at[me_x, c], a_send.at[c], a_recv.at[c])

        @pl.when(c == 0)
        def _():
            settle(fr1.at[others_x], f_send.at[0], f_recv.at[0])
            fsum[1] = jnp.sum(fr1[...], axis=0)
            spread(npy, at_y, lambda r: fsum.at[1], fr2.at[me_y], f_send.at[1], f_recv.at[1])
            fr2[me_y] = fsum[1]

        return carry

    lax.fori_loop(0, pieces, depth_piece, 0)

    owner_table()

    def table_cell(i, carry):
        c, g = carry
        right = jnp.where((i == nyl - 1) & last_y, 0.0, 1.0)
        inv, k = reduce_cell(c, g, right)
        tau[i] = inv
        kap[i] = k
        return k, mu + g * inv

    tau[0] = jnp.zeros_like(mu)
    kap[0] = jnp.ones_like(mu)
    lax.fori_loop(1, nyl, table_cell, (jnp.ones_like(mu), mu))

    settle(fr2.at[others_y], f_send.at[1], f_recv.at[1])
    flux = jnp.sum(fr2[...], axis=0) * (1.0 / (nx * npy * nyl))
    press = []
    for k in range(OUTLETS):
        total = resist[k, 0] * flux[0:1]
        for n in range(1, OUTLETS):
            total = total + resist[k, n] * flux[n:n + 1]
        press.append(total[:, HALF - 1:HALF])

    def pressures(which):
        drop = jnp.zeros(which.shape, F32)
        for k in range(OUTLETS):
            drop = jnp.where(which == k, jnp.broadcast_to(press[k], which.shape), drop)
        return drop

    quarter = lane // nxl
    for n in range(npx // 4):
        which = asked[4 * n, 8:top, :]
        for a in range(1, 4):
            which = jnp.where(quarter == a, pltpu.roll(asked[4 * n + a, 8:top, :], a * nxl, 1), which)
        outlet[:, n * HALF:(n + 1) * HALF] = pressures(which)
    weight = jnp.broadcast_to(lam_z[pl.ds(pl.multiple_of(me_x * kzl, kzl), kzl), 1:2], (kzl, nx))

    wides = npx // 4

    def row_of(i):
        return pl.ds(pl.multiple_of(i * kzl, kzl), kzl)

    def piece_rows(c):
        return pl.ds(pl.multiple_of(c * per * kzl, per * kzl), per * kzl)

    def line_piece(c, carry):
        got[me_x, c] = msg[me_x, c]
        settle(got.at[others_x, c], a_send.at[c], a_recv.at[c])

        def gather(sg, inner):
            for half in range(per // 4):
                out = swap_groups([got[4 * sg + a, c, :, half * HALF:(half + 1) * HALF] for a in range(4)])
                for b in range(4):
                    y = c * per + 4 * half + b
                    cols[row_of(y), pl.ds(pl.multiple_of(sg * HALF, HALF), HALF)] = out[b]
            return inner

        lax.fori_loop(0, wides, gather, 0)

        def add_outlet(m, inner):
            y = c * per + m
            line = jnp.broadcast_to(outlet[pl.ds(y, 1), :], (kzl, nx))
            cols[row_of(y), :] = cols[row_of(y), :] + weight * line
            return inner

        lax.fori_loop(0, per, add_outlet, 0)
        rows = piece_rows(c)
        cols[rows, :] = dot_parts(split(cols[rows, :], 2), (tt[0], tt[1]), ((1,), (0,)))
        return carry

    lax.fori_loop(0, pieces, line_piece, 0)

    def down(i, carry):
        r, ends = carry
        ends = ends + kap[i] * r
        nxt = cols[row_of(i + 1), :] + tau[i] * r
        cols[row_of(i + 1), :] = nxt
        return nxt, ends

    r, ends = lax.fori_loop(1, nyl - 1, down, (cols[row_of(1), :], cols[row_of(0), :]))
    ends = ends + kap[nyl - 1] * r
    over = tau[nyl - 1] * r
    for j in range(npy):
        isnd[j, 0:kown, :] = ends[j * kown:(j + 1) * kown]
        isnd[j, kown:2 * kown, :] = over[j * kown:(j + 1) * kown]

    spread(npy, at_y, lambda r: isnd.at[at_y(r)[1]], ircv.at[me_y], i_send.at[0], i_recv.at[0])
    ircv[me_y] = isnd[me_y]
    settle(replies.at[others_y], r_send.at[2], r_recv.at[2])
    lines = replies.reshape(npy * 2 * npx, SEG)
    for p in range(npx):
        for r in range(2):
            fetch[p, r * npy:(r + 1) * npy, :] = lines[pl.ds(r * npx + p, npy, stride=2 * npx), :]
    spread(npx, at_x, lambda r: fetch.at[at_x(r)[0]], fetched.at[me_x], r_send.at[3], r_recv.at[3])
    fetched[me_x] = fetch[me_x]
    settle(ircv.at[others_y], i_send.at[0], i_recv.at[0])

    rho = []
    for b in range(npy):
        value = ircv[b, 0:kown, :]
        if b > 0:
            value = value + ircv[b - 1, kown:2 * kown, :]
        rho.append(value)
    depth_mode = lax.broadcasted_iota(jnp.int32, (kown, nx), 0) + me_x * kzl + me_y * kown
    row_mode = lax.broadcasted_iota(jnp.int32, (kown, nx), 1)
    mean = sum(rho[1:], rho[0]) * (1.0 / (npy * nyl))
    mean = jnp.where((depth_mode == 0) & (row_mode == 0), mean, 0.0)
    half_sum = (nyl - 1) / 2.0
    for b in range(npy):
        weight = 1.0 + (0.0 if b == 0 else half_sum) + (2.0 * half_sum if b == npy - 1 else half_sum)
        rho[b] = rho[b] - weight * mean
    for b in range(npy - 1):
        rho[b + 1] = rho[b + 1] + owner_phi[b] * rho[b]
    value = -owner_inv[npy - 1] * rho[npy - 1]
    jsnd[npy - 1, 0:kown, :] = value
    jsnd[npy - 1, kown:2 * kown, :] = jnp.zeros_like(value)
    jsnd[npy - 1, 2 * kown:3 * kown, :] = mean
    for b in range(npy - 2, -1, -1):
        jsnd[b, kown:2 * kown, :] = value
        value = owner_phi[b] * value - owner_inv[b] * rho[b]
        jsnd[b, 0:kown, :] = value
        jsnd[b, 2 * kown:3 * kown, :] = mean

    spread(npy, at_y, lambda r: jsnd.at[at_y(r)[1]], jrcv.at[me_y], i_send.at[1], i_recv.at[1])
    jrcv[me_y] = jsnd[me_y]
    settle(jrcv.at[others_y], i_send.at[1], i_recv.at[1])
    for j in range(npy):
        for part in range(3):
            back[part, j * kown:(j + 1) * kown, :] = jrcv[j, part * kown:(part + 1) * kown, :]
    first_value, mean_rows = back[0], back[2]

    def up_piece(n, q):
        c = pieces - 1 - n

        def up_again(m, q):
            i = c * per + per - 1 - m
            share = 0.5 * (i + 1).astype(F32)
            q = tau[i] * (q - cols[row_of(i), :] + mean_rows * share) + kap[i] * first_value
            cols[row_of(i), :] = q
            return q

        q = lax.fori_loop(0, per, up_again, q)
        rows = piece_rows(c)
        cols[rows, :] = dot_parts(split(cols[rows, :], 3), (tx[0], tx[1], tx[2]), ((1,), (0,)))

        def scatter(sg, inner):
            for half in range(per // 4):
                parts = []
                for b in range(4):
                    y = c * per + 4 * half + b
                    parts.append(cols[row_of(y), pl.ds(pl.multiple_of(sg * HALF, HALF), HALF)])
                out = swap_groups(parts)
                for a in range(4):
                    msg[4 * sg + a, c, :, half * HALF:(half + 1) * HALF] = out[a]
            return inner

        lax.fori_loop(0, wides, scatter, 0)
        n = pieces + c
        spread(npx, at_x, lambda r: msg.at[at_x(r)[0], c], got2.at[me_x, c], a_send.at[n], a_recv.at[n])
        return q

    lax.fori_loop(0, pieces, up_piece, back[1])

    shape = (places, cells)
    cell = lax.broadcasted_iota(jnp.int32, shape, 1) * halves
    for h in range(halves):
        hot[h] = (jnp.broadcast_to(pick[...], shape) == cell + h).astype(F32).astype(BF16)

    def lower(x, carry):
        drop = DT * jnp.where(lane == HALF - 1, pressures(idb[x]), 0.0)
        w2[halves - 1, x] = w2[halves - 1, x] - drop
        return carry

    lax.fori_loop(0, nxl, lower, 0)

    pressure = qp.reshape(halves, (nxl + 2) * wide, HALF)

    def rise_piece(n, carry):
        c = pieces - 1 - n
        got2[me_x, c] = msg[me_x, c]
        settle(got2.at[others_x, c], a_send.at[pieces + c], a_recv.at[pieces + c])
        value = got2[:, c].reshape(nz, 256)
        out = dot_parts(split(value.T, 3), (tz[0], tz[1], tz[2]), ((1,), (0,)))
        for y in range(per):
            for h in range(halves):
                pressure[h, pl.ds(wide + 8 + c * per + y, nxl, stride=wide), :] = out[
                    y * nxl:(y + 1) * nxl, h * HALF:(h + 1) * HALF
                ]
        return carry

    lax.fori_loop(0, pieces, rise_piece, 0)

    for h in range(halves):
        qy_snd[0, h] = row_at(qp, (h,), top - 1)[...]
        qy_snd[1, h] = row_at(qp, (h,), 8)[...]
    halo = y_pair(qy_snd, qy_rcv, 4) + x_pair(qp, lambda field, x: field.at[:, x, pl.ds(8, nyl), :], 6)
    for copy in halo:
        copy.start()

    def q_rows(x, y, size):
        return jnp.concatenate([qp[h, x, pl.ds(y, size), :] for h in range(halves)], axis=1)

    def join(field, x):
        return jnp.concatenate([field[h, x, 0:nyl, :] for h in range(halves)], axis=1)

    def flow(a, x):
        return jnp.concatenate([up[a, h, x + 1, 8:top, :] for h in range(halves)], axis=1)

    def two_parts(x, carry):
        center = q_rows(x + 1, 8, nyl)
        spot = lax.broadcasted_iota(jnp.int32, center.shape, 1)
        below = jnp.where(spot == 0, center, pltpu.roll(center, 1, 1))
        above = jnp.where(spot == nz - 1, center, pltpu.roll(center, nz - 1, 1))
        v2 = join(w2, x) - 0.5 * (above - below)
        v0 = join(w0, x + 1) - 0.5 * (q_rows(x + 2, 8, nyl) - q_rows(x, 8, nyl))
        vel[0, x] = v0
        vel[2, x] = v2
        total = flow(0, x) * v0 + flow(2, x) * v2
        for h in range(halves):
            sig[h, pl.ds(pl.multiple_of(x * nyl, 8), nyl), :] = total[:, h * HALF:(h + 1) * HALF]
        return carry

    lax.fori_loop(1, nxl - 1, two_parts, 0)
    outs = [pltpu.make_async_copy(vel.at[b], v_out.at[b], out_sem.at[b]) for b in range(3)]

    for copy in halo:
        copy.wait()
    for h in range(halves):
        row_at(qp, (h,), 7)[...] = jnp.where(first_y, qy_snd[1, h], qy_rcv[0, h])
        row_at(qp, (h,), top)[...] = jnp.where(last_y, qy_snd[0, h], qy_rcv[1, h])

    @pl.when(first_x)
    def _():
        for h in range(halves):
            qp[h, 0, 8:top, :] = qp[h, 1, 8:top, :]

    @pl.when(last_x)
    def _():
        for h in range(halves):
            qp[h, nxl + 1, 8:top, :] = qp[h, nxl, 8:top, :]

    two_parts(0, 0)
    two_parts(nxl - 1, 0)
    outs[0].start()
    outs[2].start()

    def last_part(x, carry):
        deep = jnp.concatenate([w1[h, x + 1, 8:top, :] for h in range(halves)], axis=1)
        v1 = deep - 0.5 * (q_rows(x + 1, 9 + zero_at, nyl) - q_rows(x + 1, 7 + zero_at, nyl))
        vel[1, x] = v1
        rows = pl.ds(pl.multiple_of(x * nyl, 8), nyl)
        part = flow(1, x) * v1
        for h in range(halves):
            sig[h, rows, :] = -ALPHA * (sig[h, rows, :] + part[:, h * HALF:(h + 1) * HALF])
        return carry

    lax.fori_loop(0, nxl, last_part, 0)
    outs[1].start()

    picked = None
    for h in range(halves):
        both = jnp.dot(hot[h], jnp.concatenate(split(sig[h], 2), axis=1), preferred_element_type=F32)
        term = both[:, :SEG] + both[:, SEG:]
        picked = term if picked is None else picked + term
    settle(fetched.at[others_x], r_send.at[3], r_recv.at[3])
    products = picked * fetched[...].reshape(places, SEG)
    totals = jnp.broadcast_to(jnp.sum(products, axis=1, keepdims=True), (places, HALF))
    for p in range(npx):
        give[p] = totals[p * group:(p + 1) * group]
    spread(npx, at_x, lambda r: give.at[at_x(r)[0]], given.at[me_x], r_send.at[4], r_recv.at[4])
    given[me_x] = give[me_x]
    settle(given.at[others_x], r_send.at[4], r_recv.at[4])
    lines = given.reshape(npx * group, HALF)
    for j in range(npy):
        for r in range(2):
            gives[j, r * npx:(r + 1) * npx, :] = lines[pl.ds(r * npy + j, npx, stride=group), :]
    spread(npy, at_y, lambda r: gives.at[at_y(r)[1]], taken.at[me_y], r_send.at[5], r_recv.at[5])
    taken[me_y] = gives[me_y]
    settle(taken.at[others_y], r_send.at[5], r_recv.at[5])

    def add_up(j, total):
        label = wanted[j]
        for r in range(2):
            spot = slice(r * npy, r * npy + 1)
            hit = jnp.broadcast_to(label[:, spot], (npx, HALF)) == slot_lane
            total = total + jnp.where(hit, taken[j, r * npx:(r + 1) * npx, :], 0.0)
        return total

    total = lax.fori_loop(0, npy, add_up, jnp.zeros((npx, HALF), F32))
    grad_out[...] = jnp.sum(total, axis=0, keepdims=True)[:, :controls]
    for copy in outs:
        copy.wait()


def main_call(dims, args, owner_rows):
    npx, npy, nxl, nyl, nz = dims
    nx = npx * nxl
    kzl = nz // npx
    kown = kzl // npy
    halves = nz // HALF
    wide = nyl + 16
    cells = nxl * nyl
    pieces = cells // 256
    places = 2 * npx * npy
    vmem = pltpu.VMEM
    anywhere = pl.BlockSpec(memory_space=pl.ANY)
    here = pl.BlockSpec(memory_space=pltpu.VMEM)
    far = pl.BlockSpec(memory_space=pltpu.HBM)
    dma = pltpu.SemaphoreType.DMA
    tables = args[10:13]
    field = vmem((3, halves, nxl + 2, wide, HALF), F32)
    line = vmem((nyl, kzl, nx), F32)
    message = vmem((npx, pieces, kzl, 256), F32)
    scratch = [
        field,
        field,
        vmem((3, cells, nz), BF16),
        vmem((3, cells, nz), BF16),
        vmem((nxl, nyl, nz), jnp.int32),
        vmem((nxl, nyl, HALF), jnp.int32),
        vmem((halves, nxl + 2, nyl, HALF), F32),
        vmem((halves, nxl + 2, wide, HALF), F32),
        vmem((halves, nxl, nyl, HALF), F32),
        vmem((2, 6, halves, nxl, HALF), BF16),
        vmem((2, 6, halves, nxl, HALF), BF16),
        vmem((2, halves, nxl, HALF), F32),
        vmem((2, halves, nxl, HALF), F32),
        vmem((2, OUTLETS, HALF), F32),
        vmem((npx, OUTLETS, HALF), F32),
        vmem((npy, OUTLETS, HALF), F32),
        vmem((halves, cells, HALF), F32),
        message,
        message,
        message,
        vmem((nyl * kzl, nx), F32),
        line,
        line,
        vmem((npy, kown, nx), F32),
        vmem((npy, kown, nx), F32),
        vmem((npy, 2 * kown, nx), F32),
        vmem((npy, 2 * kown, nx), F32),
        vmem((npy, 3 * kown, nx), F32),
        vmem((npy, 3 * kown, nx), F32),
        vmem((3, kzl, nx), F32),
        vmem((halves, nxl + 2, wide, HALF), F32),
        vmem((2, halves, nxl, HALF), F32),
        vmem((2, halves, nxl, HALF), F32),
        vmem((3, nxl, nyl, nz), F32),
        vmem((halves, cells, HALF), F32),
        vmem((nyl, nx), F32),
        vmem((halves, places, cells), BF16),
        vmem((places, 1), jnp.int32),
        vmem((npx, 8 + nyl, HALF), F32),
        vmem((npx, 8 + nyl, HALF), F32),
        vmem((npy, npx, HALF), F32),
        vmem((npy, npx, HALF), F32),
        vmem((places, HALF), BF16),
        vmem((npy, 2 * npx, SEG), F32),
        vmem((npy, 2 * npx, SEG), F32),
        vmem((npx, 2 * npy, SEG), F32),
        vmem((npx, 2 * npy, SEG), F32),
        vmem((npx, 2 * npy, HALF), F32),
        vmem((npx, 2 * npy, HALF), F32),
        vmem((npy, 2 * npx, HALF), F32),
        vmem((npy, 2 * npx, HALF), F32),
    ]
    scratch += [vmem(t.shape, BF16) for t in tables]
    scratch += [
        pltpu.SMEM(a.shape, a.dtype) if n == 5 else vmem(a.shape, a.dtype)
        for n, a in enumerate(args)
        if n > 3 and not 10 <= n < 13
    ]
    scratch += [
        dma((3 * halves + 14,)),
        dma((8,)),
        dma((8,)),
        dma((6,)),
        dma((6,)),
        dma((2,)),
        dma((2,)),
        dma((2 * pieces,)),
        dma((2 * pieces,)),
        dma((2,)),
        dma((2,)),
        dma((6,)),
        dma((6,)),
        dma((3,)),
    ]
    return pl.pallas_call(
        functools.partial(main_kernel, dims),
        out_shape=(
            jax.ShapeDtypeStruct((3, nxl, nyl, nz), F32),
            jax.ShapeDtypeStruct((1, owner_rows), F32),
        ),
        in_specs=[far] * len(args),
        out_specs=(anywhere, here),
        scratch_shapes=scratch,
        compiler_params=pltpu.CompilerParams(
            collective_id=0, has_side_effects=True, vmem_limit_bytes=58 * 2**20
        ),
        name="project",
    )(*args)


def local(
    base_flow, adjoint_start, source, solid_mask, outlet_ids, resist,
    tile_owner, tile_slot, tile_column, control_basis,
):
    _, nxl, nyl, nz = adjoint_start.shape
    npx, npy = lax.axis_size("px"), lax.axis_size("py")
    nx = npx * nxl
    tz, tx = table_np(nz), table_np(nx)
    tables = [split_np(tz, 3), split_np(tx, 3), split_np(np.ascontiguousarray(tx.T), 2)]
    tables = [jnp.asarray(np.stack(t)) for t in tables]
    lam_x = jnp.asarray(-eigen_np(nx)[None, :])
    depth = np.zeros((nz, HALF), np.float32)
    depth[:, 0] = -eigen_np(nz)
    depth[:, 1] = -0.5 * DT * tz[:, nz - 2]
    depth = jnp.asarray(depth)
    args = (
        adjoint_start,
        base_flow.reshape(3, nxl * nyl, nz),
        source.reshape(3, nxl * nyl, nz),
        solid_mask,
        outlet_ids.T,
        resist,
        tile_owner.reshape(1, -1),
        tile_slot.reshape(1, -1),
        tile_column.reshape(1, -1),
        control_basis,
        *tables,
        lam_x,
        depth,
    )
    velocity, grad = main_call((npx, npy, nxl, nyl, nz), args, control_basis.shape[0])
    return velocity, grad.reshape(-1)


def solution(mesh):
    in_specs = (
        P(None, "px", "py", None),
        P(None, "px", "py", None),
        P(None, "px", "py", None),
        P("px", "py", None),
        P("px", "py"),
        P(),
        P(("px", "py"), None),
        P(("px", "py")),
        P(("px", "py")),
        P(("px", "py"), None),
    )
    out_specs = (P(None, "px", "py", None), P(("px", "py")))
    return jax.shard_map(local, mesh=mesh, in_specs=in_specs, out_specs=out_specs, check_vma=False)
```

```python
import functools
import math

import jax
import jax.numpy as jnp
import numpy as np
from jax import lax
from jax.experimental import pallas as pl
from jax.experimental.pallas import tpu as pltpu
from jax.sharding import PartitionSpec as P

SEG = 128
OUTLETS = 8
DT = 0.1
NU = 0.5
ALPHA = 5.0
HALF = 128
MESH = pl.DeviceIdType.MESH
F32 = jnp.float32
BF16 = jnp.bfloat16


def table_np(count):
    order = np.arange(count).astype(np.float32)
    modes = order[:, None]
    points = order[None, :]
    weights = np.where(modes == 0.0, math.sqrt(1.0 / count), math.sqrt(2.0 / count)).astype(np.float32)
    angle = np.float32(np.pi) * (points + np.float32(0.5)) * modes / np.float32(count)
    return (weights * np.cos(angle.astype(np.float32))).astype(np.float32)


def eigen_np(count):
    order = np.arange(count).astype(np.float32)
    angle = (np.float32(np.pi) * order / np.float32(count)).astype(np.float32)
    return (np.float32(2.0) * np.cos(angle) - np.float32(2.0)).astype(np.float32)


def split_np(table, count):
    parts = []
    for _ in range(count):
        parts.append(table.astype(jnp.bfloat16))
        table = table - parts[-1].astype(np.float32)
    return tuple(parts)


def split(value, count):
    parts = []
    for _ in range(count):
        parts.append(value.astype(BF16))
        value = value - parts[-1].astype(F32)
    return tuple(parts)


def dot_parts(a_parts, b_parts, contract):
    dims = ((contract[0], contract[1]), ((), ()))
    count, rows = len(a_parts), a_parts[0].shape[0]
    terms = {}
    for j in range(count):
        stacked = jnp.concatenate(a_parts[:count - j], axis=0) if j < count - 1 else a_parts[0]
        out = lax.dot_general(stacked, b_parts[j], dimension_numbers=dims, preferred_element_type=F32)
        for i in range(count - j):
            terms[i, j] = out[i * rows:(i + 1) * rows]
    total = None
    for i, j in sorted(terms, key=lambda at: -(at[0] + at[1])):
        total = terms[i, j] if total is None else total + terms[i, j]
    return total


def swap_groups(tiles):
    lane = lax.broadcasted_iota(jnp.int32, tiles[0].shape, 1)
    odd = (lane // 32) % 2 == 1
    far = lane >= 64
    t0, t1, t2, t3 = tiles
    a0 = jnp.where(odd, pltpu.roll(t1, 32, 1), t0)
    a1 = jnp.where(odd, t1, pltpu.roll(t0, 96, 1))
    a2 = jnp.where(odd, pltpu.roll(t3, 32, 1), t2)
    a3 = jnp.where(odd, t3, pltpu.roll(t2, 96, 1))
    return (
        jnp.where(far, pltpu.roll(a2, 64, 1), a0),
        jnp.where(far, pltpu.roll(a3, 64, 1), a1),
        jnp.where(far, a2, pltpu.roll(a0, 64, 1)),
        jnp.where(far, a3, pltpu.roll(a1, 64, 1)),
    )


def z_shift(field, edge_low, edge_high):
    depth = field.shape[1]
    lane = lax.broadcasted_iota(jnp.int32, field.shape, 1)
    below = jnp.where(lane == 0, edge_low, pltpu.roll(field, 1, 1))
    above = jnp.where(lane == depth - 1, edge_high, pltpu.roll(field, depth - 1, 1))
    return below, above


def main_kernel(
    dims,
    v_hbm, u_hbm, s_hbm, m_hbm, ids_hbm, resist_hbm, owner_hbm, slot_hbm, column_hbm, basis_hbm,
    tz_hbm, tx_hbm, tt_hbm, lam_x_hbm, lam_z_hbm,
    v_out, grad_out,
    vp, up, ub, sb, mk, idb, w0, w1, w2, snd_y, rcv_y, wy_snd, wy_rcv, fsum, fr1, fr2,
    div, msg, got, got2, cols, tau, kap, owner_inv, owner_phi,
    isnd, ircv, jsnd, jrcv, back, qp, qy_snd, qy_rcv, vel, sig,
    outlet, hot, pick, ask, asked, asks, wanted, chosen, reply, replies, fetch, fetched, give, given, gives, taken, stack, level,
    tz, tx, tt, ids, resist, owner_row, slot_row, column_row, basis, lam_x, lam_z,
    load_sem, x_send, x_recv, y_send, y_recv, f_send, f_recv, a_send, a_recv, i_send, i_recv, l_send, l_recv, r_send, r_recv, out_sem,
):
    npx, npy, nxl, nyl, nz = dims
    nx = npx * nxl
    kzl = nz // npx
    kown = kzl // npy
    halves = nz // HALF
    cells = nxl * nyl
    per = 256 // nxl
    pieces = nyl // per
    group = 2 * npy
    places = npx * group
    me_x = lax.axis_index("px")
    me_y = lax.axis_index("py")
    right_x, left_x = lax.rem(me_x + 1, npx), lax.rem(me_x + npx - 1, npx)
    right_y, left_y = lax.rem(me_y + 1, npy), lax.rem(me_y + npy - 1, npy)
    first_x, last_x = me_x == 0, me_x == npx - 1
    first_y, last_y = me_y == 0, me_y == npy - 1
    top = 8 + nyl
    wide = nyl + 16
    zero_at = jnp.minimum(me_x, 0)

    def run(first, last, action):
        def body(r, carry):
            action(r)
            return carry

        lax.fori_loop(first, last, body, 0)

    def remote(src, dst, send, recv, target):
        return pltpu.make_async_remote_copy(
            src_ref=src, dst_ref=dst, send_sem=send, recv_sem=recv, device_id=target, device_id_type=MESH
        )

    def at_x(r):
        return (lax.rem(me_x + r, npx), me_y)

    def at_y(r):
        return (me_x, lax.rem(me_y + r, npy))

    def spread(count, target, src, dst, send, recv):
        def start(n):
            r = lax.rem(n + (count // 2 - 2), count - 1) + 1
            remote(src(r), dst, send, recv, target(r)).start()

        run(1, count, start)

    def settle(like, send, recv):
        pltpu.make_async_copy(like, like, send).wait()
        pltpu.make_async_copy(like, like, recv).wait()

    others_x, others_y = pl.ds(0, npx - 1), pl.ds(0, npy - 1)

    loads = []
    for c in range(3):
        for h in range(halves):
            loads.append(
                pltpu.make_async_copy(
                    v_hbm.at[c, :, :, pl.ds(h * HALF, HALF)],
                    vp.at[c, h, pl.ds(1, nxl), pl.ds(8, nyl), :],
                    load_sem.at[c * halves + h],
                )
            )
    base = 3 * halves
    load_u = pltpu.make_async_copy(u_hbm, ub, load_sem.at[base])
    load_s = pltpu.make_async_copy(s_hbm, sb, load_sem.at[base + 1])
    load_m = pltpu.make_async_copy(m_hbm, mk, load_sem.at[base + 2])
    load_t = [
        pltpu.make_async_copy(a, b, load_sem.at[base + 3 + n])
        for n, (a, b) in enumerate(((tz_hbm, tz), (tx_hbm, tx), (tt_hbm, tt)))
    ]
    load_small = [
        pltpu.make_async_copy(a, b, load_sem.at[base + 6 + n])
        for n, (a, b) in enumerate(
            (
                (ids_hbm, ids), (resist_hbm, resist), (owner_hbm, owner_row), (slot_hbm, slot_row),
                (column_hbm, column_row), (basis_hbm, basis), (lam_x_hbm, lam_x), (lam_z_hbm, lam_z),
            )
        )
    ]
    for copy in load_small:
        copy.start()
    for copy in loads:
        copy.start()
    load_u.start()
    load_s.start()
    load_m.start()
    for copy in load_t:
        copy.start()

    barrier = pltpu.get_barrier_semaphore()
    run(1, npx, lambda r: pl.semaphore_signal(barrier, inc=1, device_id=at_x(r), device_id_type=MESH))
    run(1, npy, lambda r: pl.semaphore_signal(barrier, inc=1, device_id=at_y(r), device_id_type=MESH))

    def row_at(ref, lead, y):
        lines = ref.reshape(*ref.shape[:-3], (nxl + 2) * wide, HALF)
        return lines.at[(*lead, pl.ds(wide + y, nxl, stride=wide), slice(None))]

    def x_pair(field, at, number):
        return (
            remote(at(field, nxl), at(field, 0), x_send.at[number], x_recv.at[number], (right_x, me_y)),
            remote(at(field, 1), at(field, nxl + 1), x_send.at[number + 1], x_recv.at[number + 1], (left_x, me_y)),
        )

    def at_plane(field, x):
        return field.at[:, :, x, pl.ds(8, nyl), :]

    def y_pair(send, recv, number):
        return (
            remote(send.at[0], recv.at[0], y_send.at[number], y_recv.at[number], (me_x, right_y)),
            remote(send.at[1], recv.at[1], y_send.at[number + 1], y_recv.at[number + 1], (me_x, left_y)),
        )

    for copy in loads:
        copy.wait()

    def pack(field, first):
        for c in range(3):
            for h in range(halves):
                snd_y[0, first + c, h] = row_at(field, (c, h), top - 1)[...].astype(BF16)
                snd_y[1, first + c, h] = row_at(field, (c, h), 8)[...].astype(BF16)

    pack(vp, 0)
    load_u.wait()

    def widen(i, carry):
        for a in range(3):
            pair = ub[a, pl.ds(pl.multiple_of(i * 2 * nyl, 2 * nyl), 2 * nyl), :].astype(F32)
            for s in range(2):
                for h in range(halves):
                    up[a, h, 1 + 2 * i + s, 8:top, :] = pair[s * nyl:(s + 1) * nyl, h * HALF:(h + 1) * HALF]
        return carry

    lax.fori_loop(0, nxl // 2, widen, 0)
    pack(up, 3)
    pl.semaphore_wait(barrier, npx - 1 + npy - 1)
    halo = y_pair(snd_y, rcv_y, 0) + x_pair(vp, at_plane, 0) + x_pair(up, at_plane, 2)
    for copy in halo:
        copy.start()
    for copy in load_small:
        copy.wait()

    count = owner_row.shape[1]
    owners = owner_row[...]
    same = jnp.broadcast_to(owners, (8, count)).T[:, 0:1] == owners
    earlier = lax.broadcasted_iota(jnp.int32, (count, count), 0) < lax.broadcasted_iota(
        jnp.int32, (count, count), 1
    )
    rank = jnp.sum(jnp.where(same & earlier, 1, 0), axis=0, keepdims=True)
    owner_x = owners // npy
    place = owner_x * group + rank * npy + (owners - owner_x * npy)
    match = lax.broadcasted_iota(jnp.int32, (places, count), 0) == place
    pick[...] = jnp.sum(jnp.where(match, column_row[...] + 1, 0), axis=1, keepdims=True) - 1
    slots = jnp.broadcast_to((slot_row[...] + 1).astype(F32), (8, count)).astype(BF16)
    requests = (
        lax.dot_general(
            slots, match.astype(F32).astype(BF16), (((1,), (1,)), ((), ())), preferred_element_type=F32
        )
        - 1.0
    )

    def pad_lanes(row):
        if row.shape[1] >= HALF:
            return row
        return jnp.concatenate([row, jnp.zeros((8, HALF - row.shape[1]), F32)], axis=1)

    def by_px(row, ref):
        row = pad_lanes(row)
        lanes = row.shape[1]
        for p in range(npx):
            ref[p, 0:8, :] = pltpu.roll(row, (lanes - group * p) % lanes, 1)[:, :HALF]

    def by_py(rows, ref):
        full = jnp.concatenate([rows, jnp.zeros((HALF - npx, HALF), F32)], axis=0).T
        for j in range(npy):
            for r in range(2):
                ref[j, r:r + 1, :] = full[r * npy + j:r * npy + j + 1]

    def from_py(ref):
        for j in range(npy):
            stack[2 * j:2 * j + 2, :] = ref[j]
        return stack[...].T[0:npx]

    by_px(requests, ask)
    seen = ids[...]
    padded = jnp.concatenate([seen.astype(F32), jnp.zeros((nyl, HALF - nxl), F32)], axis=1)
    for p in range(npx):
        ask[p, 8:top, :] = padded
    for x in range(nxl):
        idb[x] = jnp.broadcast_to(seen[:, x:x + 1], (nyl, HALF))

    def ask_start():
        spread(npx, at_x, lambda r: ask.at[at_x(r)[0]], asked.at[me_x], r_send.at[0], r_recv.at[0])
        asked[me_x] = ask[me_x]

    ask_start()

    def reduce_cell(c, g, right):
        inv = 1.0 / (c + right + g)
        return inv, c * inv

    mine = lam_z[pl.ds(pl.multiple_of(me_x * kzl, kzl), kzl), 0:1]
    mu = lam_x[...] + mine
    owned = lam_z[pl.ds(me_x * kzl + me_y * kown, kown), 0:1]
    muo = lam_x[...] + owned

    def owner_table():
        def owner_cell(i, carry):
            c, g, ground = carry
            inv, k = reduce_cell(c, g, 1.0)
            return k, muo + g * inv, ground + k * g

        one = jnp.ones_like(muo)
        c, g, ground = lax.fori_loop(1, nyl - 1, owner_cell, (one, muo, jnp.zeros_like(one)))
        inv, link = reduce_cell(c, g, 1.0)
        from_left = g * inv
        end_ground = muo + from_left + (ground + c * (g / (c + g)))
        ground = ground + link * g
        held = muo + ground
        for b in range(npy - 1):
            inv = 1.0 / (link + held)
            phi = link * inv
            owner_inv[b] = inv
            owner_phi[b] = phi
            nxt = end_ground if b == npy - 2 else muo + ground + from_left
            held = nxt + phi * held
        positive = held > 0.0
        owner_inv[npy - 1] = jnp.where(positive, 1.0 / jnp.where(positive, held, 1.0), 0.0)

    load_s.wait()
    load_m.wait()

    blank = jnp.zeros((nxl, HALF), F32)
    for c in range(3):
        for h in range(halves):
            for field in (vp, up):
                row_at(field, (c, h), 7)[...] = blank
                row_at(field, (c, h), top)[...] = blank

    def rows_at(field, c, x, start, size=8):
        return jnp.concatenate([field[c, h, x, pl.ds(start, size), :] for h in range(halves)], axis=1)

    tiles = nyl // 8

    def predict(i, planes):
        for k in range(tiles):
            if all((2 * k + s) // tiles not in planes for s in range(2)):
                continue
            rows = pl.ds(pl.multiple_of(i * 2 * nyl + 16 * k, 16), 16)
            forcing = [sb[b, rows, :].astype(F32) for b in range(3)]
            for s in range(2):
                n = 2 * k + s
                if n // tiles not in planes:
                    continue
                x = 2 * i + n // tiles
                y = 8 * (n % tiles)
                scale = 1.0 - (DT * ALPHA / (1.0 + DT * ALPHA)) * mk[x, y:y + 8, :].astype(F32)
                u = [rows_at(up, a, x + 1, y + 8) for a in range(3)]
                v = [rows_at(vp, a, x + 1, y + 8) for a in range(3)]
                low, high = y + 7 + zero_at, y + 9 + zero_at
                slopes = [None] * 3
                for a in range(3):
                    below, above = z_shift(u[a], 0.0, 0.0)
                    diffs = (
                        rows_at(up, a, x + 2, y + 8) - rows_at(up, a, x, y + 8),
                        rows_at(up, a, x + 1, high) - rows_at(up, a, x + 1, low),
                        above - below,
                    )
                    for b in range(3):
                        term = v[a] * diffs[b]
                        slopes[b] = term if slopes[b] is None else slopes[b] + term
                for b in range(3):
                    xm, xp = rows_at(vp, b, x, y + 8), rows_at(vp, b, x + 2, y + 8)
                    ym, yp = rows_at(vp, b, x + 1, low), rows_at(vp, b, x + 1, high)
                    zm, zp = z_shift(v[b], 0.0, 0.0)
                    convect = u[0] * (xp - xm) + u[1] * (yp - ym) + u[2] * (zp - zm)
                    lap = (xp + xm) + (yp + ym) + (zp + zm) - 6.0 * v[b]
                    change = 0.5 * (convect - slopes[b]) + NU * lap + forcing[b][8 * s:8 * s + 8]
                    w = (v[b] + DT * change) * scale
                    for h in range(halves):
                        part = w[:, h * HALF:(h + 1) * HALF]
                        if b == 0:
                            w0[h, x + 1, y:y + 8, :] = part
                        elif b == 1:
                            w1[h, x + 1, y + 8:y + 16, :] = part
                        else:
                            w2[h, x, y:y + 8, :] = part

    pairs = nxl // 2
    run(1, pairs // 2, lambda i: predict(i, (0, 1)))
    settle(asked.at[others_x], r_send.at[0], r_recv.at[0])
    by_py(asked[:, 0, :], asks)
    spread(npy, at_y, lambda r: asks.at[at_y(r)[1]], wanted.at[me_y], r_send.at[1], r_recv.at[1])
    wanted[me_y] = asks[me_y]
    run(pairs // 2, pairs - 1, lambda i: predict(i, (0, 1)))
    predict(0, (1,))
    predict(pairs - 1, (0,))
    for copy in halo:
        copy.wait()
    edge = jnp.zeros((nyl, HALF), F32)

    @pl.when(first_x)
    def _():
        for c in range(3):
            for h in range(halves):
                vp[c, h, 0, 8:top, :] = edge
                up[c, h, 0, 8:top, :] = edge

    @pl.when(last_x)
    def _():
        for c in range(3):
            for h in range(halves):
                vp[c, h, nxl + 1, 8:top, :] = edge
                up[c, h, nxl + 1, 8:top, :] = edge
    predict(0, (0,))
    predict(pairs - 1, (1,))

    flat0 = w0.reshape(halves, (nxl + 2) * nyl, HALF)
    flat2 = w2.reshape(halves, nxl * nyl, HALF)
    for side, y, inside in ((0, 0, first_y), (1, nyl - 1, last_y)):
        sign = -0.5 if side == 0 else 0.5
        for h in range(halves):
            solid = mk[:, y, h * HALF:(h + 1) * HALF].astype(F32)
            scale = jnp.where(inside, 0.0, DT - (DT * DT * ALPHA / (1.0 + DT * ALPHA)) * solid)
            beyond = [rcv_y[side, n, h].astype(F32) for n in range(6)]
            weigh = scale * (NU + sign * row_at(up, (1, h), y + 8)[...])
            slope = sum(row_at(vp, (a, h), y + 8)[...] * beyond[3 + a] for a in range(3))
            here = flat0.at[h, pl.ds(nyl + y, nxl, stride=nyl), :]
            here[...] = here[...] + weigh * beyond[0]
            here = row_at(w1, (h,), y + 8)
            here[...] = here[...] + (weigh * beyond[1] - (sign * scale) * slope)
            here = flat2.at[h, pl.ds(y, nxl, stride=nyl), :]
            here[...] = here[...] + weigh * beyond[2]

    for h in range(halves):
        wy_snd[0, h] = row_at(w1, (h,), top - 1)[...]
        wy_snd[1, h] = row_at(w1, (h,), 8)[...]
    halo = y_pair(wy_snd, wy_rcv, 2) + x_pair(w0, lambda field, x: field.at[:, x], 4)
    for copy in halo:
        copy.start()

    settle(wanted.at[others_y], r_send.at[1], r_recv.at[1])

    slot_lane = lax.broadcasted_iota(jnp.int32, (npx, HALF), 1).astype(F32)

    labels = from_py(wanted)
    for n in range(2 * npy):
        hit = jnp.broadcast_to(labels[:, n:n + 1], (npx, HALF)) == slot_lane
        chosen[n * npx:(n + 1) * npx, :] = hit.astype(F32).astype(BF16)
    controls = basis.shape[0]
    wide_basis = jnp.concatenate([basis[...], jnp.zeros((HALF - controls, SEG), F32)], axis=0)
    rows = sum(
        jnp.dot(chosen[...], part, preferred_element_type=F32) for part in reversed(split(wide_basis, 3))
    )
    for j in range(npy):
        reply[j] = rows[j * 2 * npx:(j + 1) * 2 * npx]

    lane = lax.broadcasted_iota(jnp.int32, (nyl, HALF), 1)

    def flux_plane(x, carry):
        face = jnp.where(lane == HALF - 1, w2[halves - 1, x], 0.0)
        which = idb[x]
        return tuple(total + jnp.where(which == k, face, 0.0) for k, total in enumerate(carry))

    zero = jnp.zeros((nyl, HALF), F32)
    totals = lax.fori_loop(0, nxl, flux_plane, (zero,) * OUTLETS)
    fsum[0] = jnp.concatenate([jnp.sum(t, axis=0, keepdims=True) for t in totals], axis=0)

    spread(npx, at_x, lambda r: fsum.at[0], fr1.at[me_x], f_send.at[0], f_recv.at[0])
    fr1[me_x] = fsum[0]

    for copy in halo:
        copy.wait()
    for h in range(halves):
        row_at(w1, (h,), 7)[...] = jnp.where(first_y, 0.0, wy_rcv[0, h])
        row_at(w1, (h,), top)[...] = jnp.where(last_y, 0.0, wy_rcv[1, h])

    @pl.when(first_x)
    def _():
        for h in range(halves):
            w0[h, 0] = edge

    @pl.when(last_x)
    def _():
        for h in range(halves):
            w0[h, nxl + 1] = edge

    def diverge(x, carry):
        deep = jnp.concatenate([w2[h, x] for h in range(halves)], axis=1)
        below, above = z_shift(deep, 0.0, 0.0)
        for h in range(halves):
            cut = slice(h * HALF, (h + 1) * HALF)
            rise = w1[h, x + 1, pl.ds(9 + zero_at, nyl), :] - w1[h, x + 1, pl.ds(7 + zero_at, nyl), :]
            total = (w0[h, x + 2] - w0[h, x]) + rise + (above - below)[:, cut]
            div[h, pl.ds(x, nyl, stride=nxl), :] = 0.5 * total
        return carry

    lax.fori_loop(0, nxl, diverge, 0)

    for copy in load_t:
        copy.wait()

    def depth_piece(c, carry):
        here = pl.ds(pl.multiple_of(c * 256, 256), 256)
        value = jnp.concatenate([div[h, here, :] for h in range(halves)], axis=1)
        out = dot_parts((tz[0], tz[1]), split(value, 2), ((1,), (1,)))
        for p in range(npx):
            msg[p, c] = out[p * kzl:(p + 1) * kzl]
        spread(npx, at_x, lambda r: msg.at[at_x(r)[0], c], got.at[me_x, c], a_send.at[c], a_recv.at[c])

        @pl.when(c == 0)
        def _():
            settle(fr1.at[others_x], f_send.at[0], f_recv.at[0])
            fsum[1] = jnp.sum(fr1[...], axis=0)
            spread(npy, at_y, lambda r: fsum.at[1], fr2.at[me_y], f_send.at[1], f_recv.at[1])
            fr2[me_y] = fsum[1]

        return carry

    lax.fori_loop(0, pieces, depth_piece, 0)

    spread(npy, at_y, lambda r: reply.at[at_y(r)[1]], replies.at[me_y], r_send.at[2], r_recv.at[2])
    replies[me_y] = reply[me_y]
    owner_table()

    def table_cell(i, carry):
        c, g = carry
        right = jnp.where((i == nyl - 1) & last_y, 0.0, 1.0)
        inv, k = reduce_cell(c, g, right)
        tau[i] = inv
        kap[i] = k
        return k, mu + g * inv

    tau[0] = jnp.zeros_like(mu)
    kap[0] = jnp.ones_like(mu)
    lax.fori_loop(1, nyl, table_cell, (jnp.ones_like(mu), mu))

    settle(fr2.at[others_y], f_send.at[1], f_recv.at[1])
    flux = jnp.sum(fr2[...], axis=0) * (1.0 / (nx * npy * nyl))
    press = []
    for k in range(OUTLETS):
        total = resist[k, 0] * flux[0:1]
        for n in range(1, OUTLETS):
            total = total + resist[k, n] * flux[n:n + 1]
        press.append(total[:, HALF - 1:HALF])

    def pressures(which):
        drop = jnp.zeros(which.shape, F32)
        for k in range(OUTLETS):
            drop = jnp.where(which == k, jnp.broadcast_to(press[k], which.shape), drop)
        return drop

    quarter = lane // nxl
    for n in range(npx // 4):
        which = asked[4 * n, 8:top, :]
        for a in range(1, 4):
            which = jnp.where(quarter == a, pltpu.roll(asked[4 * n + a, 8:top, :], a * nxl, 1), which)
        outlet[:, n * HALF:(n + 1) * HALF] = pressures(which)
    weight = jnp.broadcast_to(lam_z[pl.ds(pl.multiple_of(me_x * kzl, kzl), kzl), 1:2], (kzl, nx))

    wides = npx // 4

    def row_of(i):
        return pl.ds(pl.multiple_of(i * kzl, kzl), kzl)

    def piece_rows(c):
        return pl.ds(pl.multiple_of(c * per * kzl, per * kzl), per * kzl)

    def line_piece(c, carry):
        got[me_x, c] = msg[me_x, c]
        settle(got.at[others_x, c], a_send.at[c], a_recv.at[c])

        def gather(sg, inner):
            for half in range(per // 4):
                out = swap_groups([got[4 * sg + a, c, :, half * HALF:(half + 1) * HALF] for a in range(4)])
                for b in range(4):
                    y = c * per + 4 * half + b
                    cols[row_of(y), pl.ds(pl.multiple_of(sg * HALF, HALF), HALF)] = out[b]
            return inner

        lax.fori_loop(0, wides, gather, 0)

        def add_outlet(m, inner):
            y = c * per + m
            line = jnp.broadcast_to(outlet[pl.ds(y, 1), :], (kzl, nx))
            cols[row_of(y), :] = cols[row_of(y), :] + weight * line
            return inner

        lax.fori_loop(0, per, add_outlet, 0)
        rows = piece_rows(c)
        cols[rows, :] = dot_parts(split(cols[rows, :], 2), (tt[0], tt[1]), ((1,), (0,)))
        return carry

    lax.fori_loop(0, pieces, line_piece, 0)

    def down(i, carry):
        r, ends = carry
        ends = ends + kap[i] * r
        nxt = cols[row_of(i + 1), :] + tau[i] * r
        cols[row_of(i + 1), :] = nxt
        return nxt, ends

    r, ends = lax.fori_loop(1, nyl - 1, down, (cols[row_of(1), :], cols[row_of(0), :]))
    ends = ends + kap[nyl - 1] * r
    over = tau[nyl - 1] * r
    for j in range(npy):
        isnd[j, 0:kown, :] = ends[j * kown:(j + 1) * kown]
        isnd[j, kown:2 * kown, :] = over[j * kown:(j + 1) * kown]

    spread(npy, at_y, lambda r: isnd.at[at_y(r)[1]], ircv.at[me_y], i_send.at[0], i_recv.at[0])
    ircv[me_y] = isnd[me_y]
    settle(ircv.at[others_y], i_send.at[0], i_recv.at[0])

    rho = []
    for b in range(npy):
        value = ircv[b, 0:kown, :]
        if b > 0:
            value = value + ircv[b - 1, kown:2 * kown, :]
        rho.append(value)
    depth_mode = lax.broadcasted_iota(jnp.int32, (kown, nx), 0) + me_x * kzl + me_y * kown
    row_mode = lax.broadcasted_iota(jnp.int32, (kown, nx), 1)
    mean = sum(rho[1:], rho[0]) * (1.0 / (npy * nyl))
    mean = jnp.where((depth_mode == 0) & (row_mode == 0), mean, 0.0)
    half_sum = (nyl - 1) / 2.0
    for b in range(npy):
        weight = 1.0 + (0.0 if b == 0 else half_sum) + (2.0 * half_sum if b == npy - 1 else half_sum)
        rho[b] = rho[b] - weight * mean
    for b in range(npy - 1):
        rho[b + 1] = rho[b + 1] + owner_phi[b] * rho[b]
    value = -owner_inv[npy - 1] * rho[npy - 1]
    jsnd[npy - 1, 0:kown, :] = value
    jsnd[npy - 1, kown:2 * kown, :] = jnp.zeros_like(value)
    for b in range(npy - 2, -1, -1):
        jsnd[b, kown:2 * kown, :] = value
        value = owner_phi[b] * value - owner_inv[b] * rho[b]
        jsnd[b, 0:kown, :] = value

    level[0] = mean[0:1, 0:HALF]
    has_mean = (me_x == 0) & first_y

    def tell(r):
        return remote(level.at[0], level.at[1], l_send.at[r], l_recv.at[0], at_y(r))

    @pl.when(has_mean)
    def _():
        run(1, npy, lambda r: tell(r).start())

    spread(npy, at_y, lambda r: jsnd.at[at_y(r)[1]], jrcv.at[me_y], i_send.at[1], i_recv.at[1])
    jrcv[me_y] = jsnd[me_y]
    settle(replies.at[others_y], r_send.at[2], r_recv.at[2])
    lines = replies.reshape(npy * 2 * npx, SEG)
    for p in range(npx):
        for r in range(2):
            fetch[p, r * npy:(r + 1) * npy, :] = lines[pl.ds(r * npx + p, npy, stride=2 * npx), :]
    spread(npx, at_x, lambda r: fetch.at[at_x(r)[0]], fetched.at[me_x], r_send.at[3], r_recv.at[3])
    fetched[me_x] = fetch[me_x]

    settle(jrcv.at[others_y], i_send.at[1], i_recv.at[1])

    @pl.when(has_mean)
    def _():
        run(1, npy, lambda r: tell(r).wait_send())
        level[1] = level[0]

    @pl.when((me_x == 0) & (me_y > 0))
    def _():
        pltpu.make_async_copy(level.at[1], level.at[1], l_recv.at[0]).wait()

    @pl.when(me_x > 0)
    def _():
        level[1] = jnp.zeros((1, HALF), F32)

    for j in range(npy):
        for part in range(2):
            back[part, j * kown:(j + 1) * kown, :] = jrcv[j, part * kown:(part + 1) * kown, :]
    first_value = back[0]
    corner = (lax.broadcasted_iota(jnp.int32, (kzl, nx), 0) == 0) & (
        lax.broadcasted_iota(jnp.int32, (kzl, nx), 1) == 0
    )
    mean_rows = jnp.where(corner, jnp.broadcast_to(level[1, :, 0:1], (kzl, nx)), 0.0)

    def up_piece(n, q):
        c = pieces - 1 - n

        def up_again(m, q):
            i = c * per + per - 1 - m
            share = 0.5 * (i + 1).astype(F32)
            q = tau[i] * (q - cols[row_of(i), :] + mean_rows * share) + kap[i] * first_value
            cols[row_of(i), :] = q
            return q

        q = lax.fori_loop(0, per, up_again, q)
        rows = piece_rows(c)
        cols[rows, :] = dot_parts(split(cols[rows, :], 3), (tx[0], tx[1], tx[2]), ((1,), (0,)))

        def scatter(sg, inner):
            for half in range(per // 4):
                parts = []
                for b in range(4):
                    y = c * per + 4 * half + b
                    parts.append(cols[row_of(y), pl.ds(pl.multiple_of(sg * HALF, HALF), HALF)])
                out = swap_groups(parts)
                for a in range(4):
                    msg[4 * sg + a, c, :, half * HALF:(half + 1) * HALF] = out[a]
            return inner

        lax.fori_loop(0, wides, scatter, 0)
        n = pieces + c
        spread(npx, at_x, lambda r: msg.at[at_x(r)[0], c], got2.at[me_x, c], a_send.at[n], a_recv.at[n])
        return q

    lax.fori_loop(0, pieces, up_piece, back[1])

    shape = (places, cells)
    cell = lax.broadcasted_iota(jnp.int32, shape, 1) * halves
    for h in range(halves):
        hot[h] = (jnp.broadcast_to(pick[...], shape) == cell + h).astype(F32).astype(BF16)

    def lower(x, carry):
        drop = DT * jnp.where(lane == HALF - 1, pressures(idb[x]), 0.0)
        w2[halves - 1, x] = w2[halves - 1, x] - drop
        return carry

    lax.fori_loop(0, nxl, lower, 0)

    pressure = qp.reshape(halves, (nxl + 2) * wide, HALF)

    def rise_piece(n, carry):
        c = pieces - 1 - n
        got2[me_x, c] = msg[me_x, c]
        settle(got2.at[others_x, c], a_send.at[pieces + c], a_recv.at[pieces + c])
        value = got2[:, c].reshape(nz, 256)
        out = dot_parts(split(value.T, 3), (tz[0], tz[1], tz[2]), ((1,), (0,)))
        for y in range(per):
            for h in range(halves):
                pressure[h, pl.ds(wide + 8 + c * per + y, nxl, stride=wide), :] = out[
                    y * nxl:(y + 1) * nxl, h * HALF:(h + 1) * HALF
                ]
        return carry

    lax.fori_loop(0, pieces, rise_piece, 0)

    for h in range(halves):
        qy_snd[0, h] = row_at(qp, (h,), top - 1)[...]
        qy_snd[1, h] = row_at(qp, (h,), 8)[...]
    halo = y_pair(qy_snd, qy_rcv, 4) + x_pair(qp, lambda field, x: field.at[:, x, pl.ds(8, nyl), :], 6)
    for copy in halo:
        copy.start()

    def q_rows(x, y, size):
        return jnp.concatenate([qp[h, x, pl.ds(y, size), :] for h in range(halves)], axis=1)

    def join(field, x):
        return jnp.concatenate([field[h, x, 0:nyl, :] for h in range(halves)], axis=1)

    def flow(a, x):
        return jnp.concatenate([up[a, h, x + 1, 8:top, :] for h in range(halves)], axis=1)

    def two_parts(x, carry):
        center = q_rows(x + 1, 8, nyl)
        spot = lax.broadcasted_iota(jnp.int32, center.shape, 1)
        below = jnp.where(spot == 0, center, pltpu.roll(center, 1, 1))
        above = jnp.where(spot == nz - 1, center, pltpu.roll(center, nz - 1, 1))
        v2 = join(w2, x) - 0.5 * (above - below)
        v0 = join(w0, x + 1) - 0.5 * (q_rows(x + 2, 8, nyl) - q_rows(x, 8, nyl))
        vel[0, x] = v0
        vel[2, x] = v2
        total = flow(0, x) * v0 + flow(2, x) * v2
        for h in range(halves):
            sig[h, pl.ds(pl.multiple_of(x * nyl, 8), nyl), :] = total[:, h * HALF:(h + 1) * HALF]
        return carry

    lax.fori_loop(1, nxl - 1, two_parts, 0)
    outs = [pltpu.make_async_copy(vel.at[b], v_out.at[b], out_sem.at[b]) for b in range(3)]

    for copy in halo:
        copy.wait()
    for h in range(halves):
        row_at(qp, (h,), 7)[...] = jnp.where(first_y, qy_snd[1, h], qy_rcv[0, h])
        row_at(qp, (h,), top)[...] = jnp.where(last_y, qy_snd[0, h], qy_rcv[1, h])

    @pl.when(first_x)
    def _():
        for h in range(halves):
            qp[h, 0, 8:top, :] = qp[h, 1, 8:top, :]

    @pl.when(last_x)
    def _():
        for h in range(halves):
            qp[h, nxl + 1, 8:top, :] = qp[h, nxl, 8:top, :]

    two_parts(0, 0)
    two_parts(nxl - 1, 0)
    outs[0].start()
    outs[2].start()

    def last_part(x, carry):
        deep = jnp.concatenate([w1[h, x + 1, 8:top, :] for h in range(halves)], axis=1)
        v1 = deep - 0.5 * (q_rows(x + 1, 9 + zero_at, nyl) - q_rows(x + 1, 7 + zero_at, nyl))
        vel[1, x] = v1
        rows = pl.ds(pl.multiple_of(x * nyl, 8), nyl)
        part = flow(1, x) * v1
        for h in range(halves):
            sig[h, rows, :] = -ALPHA * (sig[h, rows, :] + part[:, h * HALF:(h + 1) * HALF])
        return carry

    lax.fori_loop(0, nxl, last_part, 0)
    outs[1].start()

    picked = None
    for h in range(halves):
        both = jnp.dot(hot[h], jnp.concatenate(split(sig[h], 2), axis=1), preferred_element_type=F32)
        term = both[:, :SEG] + both[:, SEG:]
        picked = term if picked is None else picked + term
    settle(fetched.at[others_x], r_send.at[3], r_recv.at[3])
    products = picked * fetched[...].reshape(places, SEG)
    totals = jnp.broadcast_to(jnp.sum(products, axis=1, keepdims=True), (places, HALF)).T[0:8]
    by_px(totals, give)
    spread(npx, at_x, lambda r: give.at[at_x(r)[0]], given.at[me_x], r_send.at[4], r_recv.at[4])
    given[me_x] = give[me_x]
    settle(given.at[others_x], r_send.at[4], r_recv.at[4])
    by_py(given[:, 0, :], gives)
    spread(npy, at_y, lambda r: gives.at[at_y(r)[1]], taken.at[me_y], r_send.at[5], r_recv.at[5])
    taken[me_y] = gives[me_y]
    settle(taken.at[others_y], r_send.at[5], r_recv.at[5])

    values = from_py(taken)
    total = jnp.zeros((npx, HALF), F32)
    for n in range(2 * npy):
        hit = jnp.broadcast_to(labels[:, n:n + 1], (npx, HALF)) == slot_lane
        total = total + jnp.where(hit, jnp.broadcast_to(values[:, n:n + 1], (npx, HALF)), 0.0)
    grad_out[...] = jnp.sum(total, axis=0, keepdims=True)[:, :controls]
    for copy in outs:
        copy.wait()


def main_call(dims, args, owner_rows):
    npx, npy, nxl, nyl, nz = dims
    nx = npx * nxl
    kzl = nz // npx
    kown = kzl // npy
    halves = nz // HALF
    wide = nyl + 16
    cells = nxl * nyl
    pieces = cells // 256
    places = 2 * npx * npy
    vmem = pltpu.VMEM
    anywhere = pl.BlockSpec(memory_space=pl.ANY)
    here = pl.BlockSpec(memory_space=pltpu.VMEM)
    far = pl.BlockSpec(memory_space=pltpu.HBM)
    dma = pltpu.SemaphoreType.DMA
    tables = args[10:13]
    field = vmem((3, halves, nxl + 2, wide, HALF), F32)
    line = vmem((nyl, kzl, nx), F32)
    message = vmem((npx, pieces, kzl, 256), F32)
    scratch = [
        field,
        field,
        vmem((3, cells, nz), BF16),
        vmem((3, cells, nz), BF16),
        vmem((nxl, nyl, nz), jnp.int32),
        vmem((nxl, nyl, HALF), jnp.int32),
        vmem((halves, nxl + 2, nyl, HALF), F32),
        vmem((halves, nxl + 2, wide, HALF), F32),
        vmem((halves, nxl, nyl, HALF), F32),
        vmem((2, 6, halves, nxl, HALF), BF16),
        vmem((2, 6, halves, nxl, HALF), BF16),
        vmem((2, halves, nxl, HALF), F32),
        vmem((2, halves, nxl, HALF), F32),
        vmem((2, OUTLETS, HALF), F32),
        vmem((npx, OUTLETS, HALF), F32),
        vmem((npy, OUTLETS, HALF), F32),
        vmem((halves, cells, HALF), F32),
        message,
        message,
        message,
        vmem((nyl * kzl, nx), F32),
        line,
        line,
        vmem((npy, kown, nx), F32),
        vmem((npy, kown, nx), F32),
        vmem((npy, 2 * kown, nx), F32),
        vmem((npy, 2 * kown, nx), F32),
        vmem((npy, 2 * kown, nx), F32),
        vmem((npy, 2 * kown, nx), F32),
        vmem((2, kzl, nx), F32),
        vmem((halves, nxl + 2, wide, HALF), F32),
        vmem((2, halves, nxl, HALF), F32),
        vmem((2, halves, nxl, HALF), F32),
        vmem((3, nxl, nyl, nz), F32),
        vmem((halves, cells, HALF), F32),
        vmem((nyl, nx), F32),
        vmem((halves, places, cells), BF16),
        vmem((places, 1), jnp.int32),
        vmem((npx, 8 + nyl, HALF), F32),
        vmem((npx, 8 + nyl, HALF), F32),
        vmem((npy, 2, HALF), F32),
        vmem((npy, 2, HALF), F32),
        vmem((places, HALF), BF16),
        vmem((npy, 2 * npx, SEG), F32),
        vmem((npy, 2 * npx, SEG), F32),
        vmem((npx, 2 * npy, SEG), F32),
        vmem((npx, 2 * npy, SEG), F32),
        vmem((npx, 8, HALF), F32),
        vmem((npx, 8, HALF), F32),
        vmem((npy, 2, HALF), F32),
        vmem((npy, 2, HALF), F32),
        vmem((2 * npy, HALF), F32),
        vmem((2, 1, HALF), F32),
    ]
    scratch += [vmem(t.shape, BF16) for t in tables]
    scratch += [
        pltpu.SMEM(a.shape, a.dtype) if n == 5 else vmem(a.shape, a.dtype)
        for n, a in enumerate(args)
        if n > 3 and not 10 <= n < 13
    ]
    scratch += [
        dma((3 * halves + 14,)),
        dma((8,)),
        dma((8,)),
        dma((6,)),
        dma((6,)),
        dma((2,)),
        dma((2,)),
        dma((2 * pieces,)),
        dma((2 * pieces,)),
        dma((2,)),
        dma((2,)),
        dma((npy,)),
        dma((1,)),
        dma((6,)),
        dma((6,)),
        dma((3,)),
    ]
    return pl.pallas_call(
        functools.partial(main_kernel, dims),
        out_shape=(
            jax.ShapeDtypeStruct((3, nxl, nyl, nz), F32),
            jax.ShapeDtypeStruct((1, owner_rows), F32),
        ),
        in_specs=[far] * len(args),
        out_specs=(anywhere, here),
        scratch_shapes=scratch,
        compiler_params=pltpu.CompilerParams(
            collective_id=0, has_side_effects=True, vmem_limit_bytes=58 * 2**20
        ),
        name="project",
    )(*args)


def local(
    base_flow, adjoint_start, source, solid_mask, outlet_ids, resist,
    tile_owner, tile_slot, tile_column, control_basis,
):
    _, nxl, nyl, nz = adjoint_start.shape
    npx, npy = lax.axis_size("px"), lax.axis_size("py")
    nx = npx * nxl
    tz, tx = table_np(nz), table_np(nx)
    tables = [split_np(tz, 3), split_np(tx, 3), split_np(np.ascontiguousarray(tx.T), 2)]
    tables = [jnp.asarray(np.stack(t)) for t in tables]
    lam_x = jnp.asarray(-eigen_np(nx)[None, :])
    depth = np.zeros((nz, HALF), np.float32)
    depth[:, 0] = -eigen_np(nz)
    depth[:, 1] = -0.5 * DT * tz[:, nz - 2]
    depth = jnp.asarray(depth)
    args = (
        adjoint_start,
        base_flow.reshape(3, nxl * nyl, nz),
        source.reshape(3, nxl * nyl, nz),
        solid_mask,
        outlet_ids.T,
        resist,
        tile_owner.reshape(1, -1),
        tile_slot.reshape(1, -1),
        tile_column.reshape(1, -1),
        control_basis,
        *tables,
        lam_x,
        depth,
    )
    velocity, grad = main_call((npx, npy, nxl, nyl, nz), args, control_basis.shape[0])
    return velocity, grad.reshape(-1)


def solution(mesh):
    in_specs = (
        P(None, "px", "py", None),
        P(None, "px", "py", None),
        P(None, "px", "py", None),
        P("px", "py", None),
        P("px", "py"),
        P(),
        P(("px", "py"), None),
        P(("px", "py")),
        P(("px", "py")),
        P(("px", "py"), None),
    )
    out_specs = (P(None, "px", "py", None), P(("px", "py")))
    return jax.shard_map(local, mesh=mesh, in_specs=in_specs, out_specs=out_specs, check_vma=False)
```

```python
import functools
import math

import jax
import jax.numpy as jnp
import numpy as np
from jax import lax
from jax.experimental import pallas as pl
from jax.experimental.pallas import tpu as pltpu
from jax.sharding import PartitionSpec as P

SEG = 128
OUTLETS = 8
DT = 0.1
NU = 0.5
ALPHA = 5.0
HALF = 128
MESH = pl.DeviceIdType.MESH
F32 = jnp.float32
BF16 = jnp.bfloat16


def table_np(count):
    order = np.arange(count).astype(np.float32)
    modes = order[:, None]
    points = order[None, :]
    weights = np.where(modes == 0.0, math.sqrt(1.0 / count), math.sqrt(2.0 / count)).astype(np.float32)
    angle = np.float32(np.pi) * (points + np.float32(0.5)) * modes / np.float32(count)
    return (weights * np.cos(angle.astype(np.float32))).astype(np.float32)


def eigen_np(count):
    order = np.arange(count).astype(np.float32)
    angle = (np.float32(np.pi) * order / np.float32(count)).astype(np.float32)
    return (np.float32(2.0) * np.cos(angle) - np.float32(2.0)).astype(np.float32)


def split_np(table, count):
    parts = []
    for _ in range(count):
        parts.append(table.astype(jnp.bfloat16))
        table = table - parts[-1].astype(np.float32)
    return tuple(parts)


def split(value, count):
    parts = []
    for _ in range(count):
        parts.append(value.astype(BF16))
        value = value - parts[-1].astype(F32)
    return tuple(parts)


def dot_parts(a_parts, b_parts, contract):
    dims = ((contract[0], contract[1]), ((), ()))
    count, rows = len(a_parts), a_parts[0].shape[0]
    terms = {}
    for j in range(count):
        stacked = jnp.concatenate(a_parts[:count - j], axis=0) if j < count - 1 else a_parts[0]
        out = lax.dot_general(stacked, b_parts[j], dimension_numbers=dims, preferred_element_type=F32)
        for i in range(count - j):
            terms[i, j] = out[i * rows:(i + 1) * rows]
    total = None
    for i, j in sorted(terms, key=lambda at: -(at[0] + at[1])):
        total = terms[i, j] if total is None else total + terms[i, j]
    return total


def swap_groups(tiles):
    lane = lax.broadcasted_iota(jnp.int32, tiles[0].shape, 1)
    odd = (lane // 32) % 2 == 1
    far = lane >= 64
    t0, t1, t2, t3 = tiles
    a0 = jnp.where(odd, pltpu.roll(t1, 32, 1), t0)
    a1 = jnp.where(odd, t1, pltpu.roll(t0, 96, 1))
    a2 = jnp.where(odd, pltpu.roll(t3, 32, 1), t2)
    a3 = jnp.where(odd, t3, pltpu.roll(t2, 96, 1))
    return (
        jnp.where(far, pltpu.roll(a2, 64, 1), a0),
        jnp.where(far, pltpu.roll(a3, 64, 1), a1),
        jnp.where(far, a2, pltpu.roll(a0, 64, 1)),
        jnp.where(far, a3, pltpu.roll(a1, 64, 1)),
    )


def z_shift(field, edge_low, edge_high):
    depth = field.shape[1]
    lane = lax.broadcasted_iota(jnp.int32, field.shape, 1)
    below = jnp.where(lane == 0, edge_low, pltpu.roll(field, 1, 1))
    above = jnp.where(lane == depth - 1, edge_high, pltpu.roll(field, depth - 1, 1))
    return below, above


def main_kernel(
    dims,
    v_hbm, u_hbm, s_hbm, m_hbm, ids_hbm, resist_hbm, owner_hbm, slot_hbm, column_hbm, basis_hbm,
    tz_hbm, tx_hbm, tt_hbm, lam_x_hbm, lam_z_hbm,
    v_out, grad_out,
    vp, up, ub, sb, mk, idb, w0, w1, w2, snd_y, rcv_y, wy_snd, wy_rcv, fsum, fr1, fr2,
    div, msg, got, got2, cols, tau, kap, owner_inv, owner_phi,
    isnd, ircv, jsnd, jrcv, back, qp, qy_snd, qy_rcv, vel, sig,
    outlet, hot, pick, ask, asked, asks, wanted, chosen, reply, replies, fetch, fetched, give, given, gives, taken, stack, level,
    tz, tx, tt, ids, resist, owner_row, slot_row, column_row, basis, lam_x, lam_z,
    load_sem, x_send, x_recv, y_send, y_recv, f_send, f_recv, a_send, a_recv, i_send, i_recv, l_send, l_recv, r_send, r_recv, out_sem,
):
    npx, npy, nxl, nyl, nz = dims
    nx = npx * nxl
    kzl = nz // npx
    kown = kzl // npy
    halves = nz // HALF
    cells = nxl * nyl
    per = 256 // nxl
    pieces = nyl // per
    group = 2 * npy
    places = npx * group
    me_x = lax.axis_index("px")
    me_y = lax.axis_index("py")
    right_x, left_x = lax.rem(me_x + 1, npx), lax.rem(me_x + npx - 1, npx)
    right_y, left_y = lax.rem(me_y + 1, npy), lax.rem(me_y + npy - 1, npy)
    first_x, last_x = me_x == 0, me_x == npx - 1
    first_y, last_y = me_y == 0, me_y == npy - 1
    top = 8 + nyl
    wide = nyl + 16
    zero_at = jnp.minimum(me_x, 0)

    def run(first, last, action):
        def body(r, carry):
            action(r)
            return carry

        lax.fori_loop(first, last, body, 0)

    def remote(src, dst, send, recv, target):
        return pltpu.make_async_remote_copy(
            src_ref=src, dst_ref=dst, send_sem=send, recv_sem=recv, device_id=target, device_id_type=MESH
        )

    def at_x(r):
        return (lax.rem(me_x + r, npx), me_y)

    def at_y(r):
        return (me_x, lax.rem(me_y + r, npy))

    def spread(count, target, src, dst, send, recv):
        def start(n):
            r = (n + (count // 2 - 2)) % (count - 1) + 1
            remote(src(r), dst, send, recv, target(r)).start()

        for n in range(1, count):
            start(n)

    def settle(like, send, recv):
        pltpu.make_async_copy(like, like, send).wait()
        pltpu.make_async_copy(like, like, recv).wait()

    others_x, others_y = pl.ds(0, npx - 1), pl.ds(0, npy - 1)

    loads = []
    for c in range(3):
        for h in range(halves):
            loads.append(
                pltpu.make_async_copy(
                    v_hbm.at[c, :, :, pl.ds(h * HALF, HALF)],
                    vp.at[c, h, pl.ds(1, nxl), pl.ds(8, nyl), :],
                    load_sem.at[c * halves + h],
                )
            )
    base = 3 * halves
    load_u = pltpu.make_async_copy(u_hbm, ub, load_sem.at[base])
    load_s = pltpu.make_async_copy(s_hbm, sb, load_sem.at[base + 1])
    load_m = pltpu.make_async_copy(m_hbm, mk, load_sem.at[base + 2])
    load_t = [
        pltpu.make_async_copy(a, b, load_sem.at[base + 3 + n])
        for n, (a, b) in enumerate(((tz_hbm, tz), (tx_hbm, tx), (tt_hbm, tt)))
    ]
    load_small = [
        pltpu.make_async_copy(a, b, load_sem.at[base + 6 + n])
        for n, (a, b) in enumerate(
            (
                (ids_hbm, ids), (resist_hbm, resist), (owner_hbm, owner_row), (slot_hbm, slot_row),
                (column_hbm, column_row), (basis_hbm, basis), (lam_x_hbm, lam_x), (lam_z_hbm, lam_z),
            )
        )
    ]
    for copy in load_small:
        copy.start()
    for copy in loads:
        copy.start()
    load_u.start()
    load_s.start()
    load_m.start()
    for copy in load_t:
        copy.start()

    barrier = pltpu.get_barrier_semaphore()
    for r in range(1, npx):
        pl.semaphore_signal(barrier, inc=1, device_id=at_x(r), device_id_type=MESH)
    for r in range(1, npy):
        pl.semaphore_signal(barrier, inc=1, device_id=at_y(r), device_id_type=MESH)

    def row_at(ref, lead, y):
        lines = ref.reshape(*ref.shape[:-3], (nxl + 2) * wide, HALF)
        return lines.at[(*lead, pl.ds(wide + y, nxl, stride=wide), slice(None))]

    def x_pair(field, at, number):
        return (
            remote(at(field, nxl), at(field, 0), x_send.at[number], x_recv.at[number], (right_x, me_y)),
            remote(at(field, 1), at(field, nxl + 1), x_send.at[number + 1], x_recv.at[number + 1], (left_x, me_y)),
        )

    def at_plane(field, x):
        return field.at[:, :, x, pl.ds(8, nyl), :]

    def y_pair(send, recv, number):
        return (
            remote(send.at[0], recv.at[0], y_send.at[number], y_recv.at[number], (me_x, right_y)),
            remote(send.at[1], recv.at[1], y_send.at[number + 1], y_recv.at[number + 1], (me_x, left_y)),
        )

    for copy in loads:
        copy.wait()

    def pack(field, first):
        for c in range(3):
            for h in range(halves):
                snd_y[0, first + c, h] = row_at(field, (c, h), top - 1)[...].astype(BF16)
                snd_y[1, first + c, h] = row_at(field, (c, h), 8)[...].astype(BF16)

    pack(vp, 0)
    load_u.wait()

    def widen(i, carry):
        for a in range(3):
            pair = ub[a, pl.ds(pl.multiple_of(i * 2 * nyl, 2 * nyl), 2 * nyl), :].astype(F32)
            for s in range(2):
                for h in range(halves):
                    up[a, h, 1 + 2 * i + s, 8:top, :] = pair[s * nyl:(s + 1) * nyl, h * HALF:(h + 1) * HALF]
        return carry

    lax.fori_loop(0, nxl // 2, widen, 0)
    pack(up, 3)
    pl.semaphore_wait(barrier, npx - 1 + npy - 1)
    halo = y_pair(snd_y, rcv_y, 0) + x_pair(vp, at_plane, 0) + x_pair(up, at_plane, 2)
    for copy in halo:
        copy.start()
    for copy in load_small:
        copy.wait()

    count = owner_row.shape[1]
    owners = owner_row[...]
    same = jnp.broadcast_to(owners, (8, count)).T[:, 0:1] == owners
    earlier = lax.broadcasted_iota(jnp.int32, (count, count), 0) < lax.broadcasted_iota(
        jnp.int32, (count, count), 1
    )
    rank = jnp.sum(jnp.where(same & earlier, 1, 0), axis=0, keepdims=True)
    owner_x = owners // npy
    place = owner_x * group + rank * npy + (owners - owner_x * npy)
    match = lax.broadcasted_iota(jnp.int32, (places, count), 0) == place
    pick[...] = jnp.sum(jnp.where(match, column_row[...] + 1, 0), axis=1, keepdims=True) - 1
    slots = jnp.broadcast_to((slot_row[...] + 1).astype(F32), (8, count)).astype(BF16)
    requests = (
        lax.dot_general(
            slots, match.astype(F32).astype(BF16), (((1,), (1,)), ((), ())), preferred_element_type=F32
        )
        - 1.0
    )

    def pad_lanes(row):
        if row.shape[1] >= HALF:
            return row
        return jnp.concatenate([row, jnp.zeros((8, HALF - row.shape[1]), F32)], axis=1)

    def by_px(row, ref, rows=8):
        row = pad_lanes(row)
        lanes = row.shape[1]
        for p in range(npx):
            ref[p, 0:rows, :] = pltpu.roll(row, (lanes - group * p) % lanes, 1)[0:rows, :HALF]

    def by_py(rows, ref):
        full = jnp.concatenate([rows, jnp.zeros((HALF - npx, HALF), F32)], axis=0).T
        for j in range(npy):
            for r in range(2):
                ref[j, r:r + 1, :] = full[r * npy + j:r * npy + j + 1]

    def from_py(ref):
        for j in range(npy):
            stack[2 * j:2 * j + 2, :] = ref[j]
        return stack[...].T[0:npx]

    by_px(requests, ask)
    seen = ids[...]
    padded = jnp.concatenate([seen.astype(F32), jnp.zeros((nyl, HALF - nxl), F32)], axis=1)
    for p in range(npx):
        ask[p, 8:top, :] = padded
    for x in range(nxl):
        idb[x] = jnp.broadcast_to(seen[:, x:x + 1], (nyl, HALF))

    def ask_start():
        spread(npx, at_x, lambda r: ask.at[at_x(r)[0]], asked.at[me_x], r_send.at[0], r_recv.at[0])
        asked[me_x] = ask[me_x]

    ask_start()

    def reduce_cell(c, g, right):
        inv = 1.0 / (c + right + g)
        return inv, c * inv

    mine = lam_z[pl.ds(pl.multiple_of(me_x * kzl, kzl), kzl), 0:1]
    mu = lam_x[...] + mine
    owned = lam_z[pl.ds(me_x * kzl + me_y * kown, kown), 0:1]
    muo = lam_x[...] + owned

    def owner_table():
        def owner_cell(i, carry):
            c, g, ground = carry
            inv, k = reduce_cell(c, g, 1.0)
            return k, muo + g * inv, ground + k * g

        one = jnp.ones_like(muo)
        c, g, ground = lax.fori_loop(1, nyl - 1, owner_cell, (one, muo, jnp.zeros_like(one)))
        inv, link = reduce_cell(c, g, 1.0)
        from_left = g * inv
        end_ground = muo + from_left + (ground + c * (g / (c + g)))
        ground = ground + link * g
        held = muo + ground
        for b in range(npy - 1):
            inv = 1.0 / (link + held)
            phi = link * inv
            owner_inv[b] = inv
            owner_phi[b] = phi
            nxt = end_ground if b == npy - 2 else muo + ground + from_left
            held = nxt + phi * held
        positive = held > 0.0
        owner_inv[npy - 1] = jnp.where(positive, 1.0 / jnp.where(positive, held, 1.0), 0.0)

    load_s.wait()
    load_m.wait()

    blank = jnp.zeros((nxl, HALF), F32)
    for c in range(3):
        for h in range(halves):
            for field in (vp, up):
                row_at(field, (c, h), 7)[...] = blank
                row_at(field, (c, h), top)[...] = blank

    def rows_at(field, c, x, start, size=8):
        return jnp.concatenate([field[c, h, x, pl.ds(start, size), :] for h in range(halves)], axis=1)

    tiles = nyl // 8

    def predict(i, planes):
        for k in range(tiles):
            if all((2 * k + s) // tiles not in planes for s in range(2)):
                continue
            rows = pl.ds(pl.multiple_of(i * 2 * nyl + 16 * k, 16), 16)
            forcing = [sb[b, rows, :].astype(F32) for b in range(3)]
            for s in range(2):
                n = 2 * k + s
                if n // tiles not in planes:
                    continue
                x = 2 * i + n // tiles
                y = 8 * (n % tiles)
                scale = 1.0 - (DT * ALPHA / (1.0 + DT * ALPHA)) * mk[x, y:y + 8, :].astype(F32)
                u = [rows_at(up, a, x + 1, y + 8) for a in range(3)]
                v = [rows_at(vp, a, x + 1, y + 8) for a in range(3)]
                low, high = y + 7 + zero_at, y + 9 + zero_at
                slopes = [None] * 3
                for a in range(3):
                    below, above = z_shift(u[a], 0.0, 0.0)
                    diffs = (
                        rows_at(up, a, x + 2, y + 8) - rows_at(up, a, x, y + 8),
                        rows_at(up, a, x + 1, high) - rows_at(up, a, x + 1, low),
                        above - below,
                    )
                    for b in range(3):
                        term = v[a] * diffs[b]
                        slopes[b] = term if slopes[b] is None else slopes[b] + term
                for b in range(3):
                    xm, xp = rows_at(vp, b, x, y + 8), rows_at(vp, b, x + 2, y + 8)
                    ym, yp = rows_at(vp, b, x + 1, low), rows_at(vp, b, x + 1, high)
                    zm, zp = z_shift(v[b], 0.0, 0.0)
                    convect = u[0] * (xp - xm) + u[1] * (yp - ym) + u[2] * (zp - zm)
                    lap = (xp + xm) + (yp + ym) + (zp + zm) - 6.0 * v[b]
                    change = 0.5 * (convect - slopes[b]) + NU * lap + forcing[b][8 * s:8 * s + 8]
                    w = (v[b] + DT * change) * scale
                    for h in range(halves):
                        part = w[:, h * HALF:(h + 1) * HALF]
                        if b == 0:
                            w0[h, x + 1, y:y + 8, :] = part
                        elif b == 1:
                            w1[h, x + 1, y + 8:y + 16, :] = part
                        else:
                            w2[h, x, y:y + 8, :] = part

    pairs = nxl // 2
    run(1, pairs // 2, lambda i: predict(i, (0, 1)))
    settle(asked.at[others_x], r_send.at[0], r_recv.at[0])
    by_py(asked[:, 0, :], asks)
    spread(npy, at_y, lambda r: asks.at[at_y(r)[1]], wanted.at[me_y], r_send.at[1], r_recv.at[1])
    wanted[me_y] = asks[me_y]
    run(pairs // 2, pairs - 1, lambda i: predict(i, (0, 1)))
    predict(0, (1,))
    predict(pairs - 1, (0,))
    for copy in halo:
        copy.wait()
    edge = jnp.zeros((nyl, HALF), F32)

    @pl.when(first_x)
    def _():
        for c in range(3):
            for h in range(halves):
                vp[c, h, 0, 8:top, :] = edge
                up[c, h, 0, 8:top, :] = edge

    @pl.when(last_x)
    def _():
        for c in range(3):
            for h in range(halves):
                vp[c, h, nxl + 1, 8:top, :] = edge
                up[c, h, nxl + 1, 8:top, :] = edge
    predict(0, (0,))
    predict(pairs - 1, (1,))

    flat0 = w0.reshape(halves, (nxl + 2) * nyl, HALF)
    flat2 = w2.reshape(halves, nxl * nyl, HALF)
    for side, y, inside in ((0, 0, first_y), (1, nyl - 1, last_y)):
        sign = -0.5 if side == 0 else 0.5
        for h in range(halves):
            solid = mk[:, y, h * HALF:(h + 1) * HALF].astype(F32)
            scale = jnp.where(inside, 0.0, DT - (DT * DT * ALPHA / (1.0 + DT * ALPHA)) * solid)
            beyond = [rcv_y[side, n, h].astype(F32) for n in range(6)]
            weigh = scale * (NU + sign * row_at(up, (1, h), y + 8)[...])
            slope = sum(row_at(vp, (a, h), y + 8)[...] * beyond[3 + a] for a in range(3))
            here = flat0.at[h, pl.ds(nyl + y, nxl, stride=nyl), :]
            here[...] = here[...] + weigh * beyond[0]
            here = row_at(w1, (h,), y + 8)
            here[...] = here[...] + (weigh * beyond[1] - (sign * scale) * slope)
            here = flat2.at[h, pl.ds(y, nxl, stride=nyl), :]
            here[...] = here[...] + weigh * beyond[2]

    for h in range(halves):
        wy_snd[0, h] = row_at(w1, (h,), top - 1)[...]
        wy_snd[1, h] = row_at(w1, (h,), 8)[...]
    halo = y_pair(wy_snd, wy_rcv, 2) + x_pair(w0, lambda field, x: field.at[:, x], 4)
    for copy in halo:
        copy.start()

    settle(wanted.at[others_y], r_send.at[1], r_recv.at[1])

    slot_lane = lax.broadcasted_iota(jnp.int32, (npx, HALF), 1).astype(F32)

    labels = from_py(wanted)
    for n in range(2 * npy):
        hit = jnp.broadcast_to(labels[:, n:n + 1], (npx, HALF)) == slot_lane
        chosen[n * npx:(n + 1) * npx, :] = hit.astype(F32).astype(BF16)
    controls = basis.shape[0]
    wide_basis = jnp.concatenate([basis[...], jnp.zeros((HALF - controls, SEG), F32)], axis=0)
    rows = sum(
        jnp.dot(chosen[...], part, preferred_element_type=F32) for part in reversed(split(wide_basis, 3))
    )
    for j in range(npy):
        reply[j] = rows[j * 2 * npx:(j + 1) * 2 * npx]

    lane = lax.broadcasted_iota(jnp.int32, (nyl, HALF), 1)

    def flux_plane(x, carry):
        face = jnp.where(lane == HALF - 1, w2[halves - 1, x], 0.0)
        which = idb[x]
        return tuple(total + jnp.where(which == k, face, 0.0) for k, total in enumerate(carry))

    zero = jnp.zeros((nyl, HALF), F32)
    totals = lax.fori_loop(0, nxl, flux_plane, (zero,) * OUTLETS)
    fsum[0] = jnp.concatenate([jnp.sum(t, axis=0, keepdims=True) for t in totals], axis=0)

    spread(npx, at_x, lambda r: fsum.at[0], fr1.at[me_x], f_send.at[0], f_recv.at[0])
    fr1[me_x] = fsum[0]

    for copy in halo:
        copy.wait()
    for h in range(halves):
        row_at(w1, (h,), 7)[...] = jnp.where(first_y, 0.0, wy_rcv[0, h])
        row_at(w1, (h,), top)[...] = jnp.where(last_y, 0.0, wy_rcv[1, h])

    @pl.when(first_x)
    def _():
        for h in range(halves):
            w0[h, 0] = edge

    @pl.when(last_x)
    def _():
        for h in range(halves):
            w0[h, nxl + 1] = edge

    def diverge(x, carry):
        deep = jnp.concatenate([w2[h, x] for h in range(halves)], axis=1)
        below, above = z_shift(deep, 0.0, 0.0)
        for h in range(halves):
            cut = slice(h * HALF, (h + 1) * HALF)
            rise = w1[h, x + 1, pl.ds(9 + zero_at, nyl), :] - w1[h, x + 1, pl.ds(7 + zero_at, nyl), :]
            total = (w0[h, x + 2] - w0[h, x]) + rise + (above - below)[:, cut]
            div[h, pl.ds(x, nyl, stride=nxl), :] = 0.5 * total
        return carry

    lax.fori_loop(0, nxl, diverge, 0)

    for copy in load_t:
        copy.wait()

    def depth_piece(c, carry):
        here = pl.ds(pl.multiple_of(c * 256, 256), 256)
        value = jnp.concatenate([div[h, here, :] for h in range(halves)], axis=1)
        out = dot_parts((tz[0], tz[1]), split(value, 2), ((1,), (1,)))
        for p in range(npx):
            msg[p, c] = out[p * kzl:(p + 1) * kzl]
        spread(npx, at_x, lambda r: msg.at[at_x(r)[0], c], got.at[me_x, c], a_send.at[c], a_recv.at[c])

        @pl.when(c == 0)
        def _():
            settle(fr1.at[others_x], f_send.at[0], f_recv.at[0])
            fsum[1] = jnp.sum(fr1[...], axis=0)
            spread(npy, at_y, lambda r: fsum.at[1], fr2.at[me_y], f_send.at[1], f_recv.at[1])
            fr2[me_y] = fsum[1]

        return carry

    lax.fori_loop(0, pieces, depth_piece, 0)

    spread(npy, at_y, lambda r: reply.at[at_y(r)[1]], replies.at[me_y], r_send.at[2], r_recv.at[2])
    replies[me_y] = reply[me_y]
    owner_table()

    def table_cell(i, carry):
        c, g = carry
        right = jnp.where((i == nyl - 1) & last_y, 0.0, 1.0)
        inv, k = reduce_cell(c, g, right)
        tau[i] = inv
        kap[i] = k
        return k, mu + g * inv

    tau[0] = jnp.zeros_like(mu)
    kap[0] = jnp.ones_like(mu)
    lax.fori_loop(1, nyl, table_cell, (jnp.ones_like(mu), mu))

    settle(fr2.at[others_y], f_send.at[1], f_recv.at[1])
    flux = jnp.sum(fr2[...], axis=0) * (1.0 / (nx * npy * nyl))
    press = []
    for k in range(OUTLETS):
        total = resist[k, 0] * flux[0:1]
        for n in range(1, OUTLETS):
            total = total + resist[k, n] * flux[n:n + 1]
        press.append(total[:, HALF - 1:HALF])

    def pressures(which):
        drop = jnp.zeros(which.shape, F32)
        for k in range(OUTLETS):
            drop = jnp.where(which == k, jnp.broadcast_to(press[k], which.shape), drop)
        return drop

    quarter = lane // nxl
    for n in range(npx // 4):
        which = asked[4 * n, 8:top, :]
        for a in range(1, 4):
            which = jnp.where(quarter == a, pltpu.roll(asked[4 * n + a, 8:top, :], a * nxl, 1), which)
        outlet[:, n * HALF:(n + 1) * HALF] = pressures(which)
    weight = jnp.broadcast_to(lam_z[pl.ds(pl.multiple_of(me_x * kzl, kzl), kzl), 1:2], (kzl, nx))

    wides = npx // 4

    def row_of(i):
        return pl.ds(pl.multiple_of(i * kzl, kzl), kzl)

    def piece_rows(c):
        return pl.ds(pl.multiple_of(c * per * kzl, per * kzl), per * kzl)

    def line_piece(c, carry):
        got[me_x, c] = msg[me_x, c]
        settle(got.at[others_x, c], a_send.at[c], a_recv.at[c])

        def gather(sg, inner):
            for half in range(per // 4):
                out = swap_groups([got[4 * sg + a, c, :, half * HALF:(half + 1) * HALF] for a in range(4)])
                for b in range(4):
                    y = c * per + 4 * half + b
                    cols[row_of(y), pl.ds(pl.multiple_of(sg * HALF, HALF), HALF)] = out[b]
            return inner

        lax.fori_loop(0, wides, gather, 0)

        def add_outlet(m, inner):
            y = c * per + m
            line = jnp.broadcast_to(outlet[pl.ds(y, 1), :], (kzl, nx))
            cols[row_of(y), :] = cols[row_of(y), :] + weight * line
            return inner

        lax.fori_loop(0, per, add_outlet, 0)
        rows = piece_rows(c)
        cols[rows, :] = dot_parts(split(cols[rows, :], 2), (tt[0], tt[1]), ((1,), (0,)))
        return carry

    lax.fori_loop(0, pieces, line_piece, 0)

    def down(i, carry):
        r, ends = carry
        ends = ends + kap[i] * r
        nxt = cols[row_of(i + 1), :] + tau[i] * r
        cols[row_of(i + 1), :] = nxt
        return nxt, ends

    r, ends = lax.fori_loop(1, nyl - 1, down, (cols[row_of(1), :], cols[row_of(0), :]))
    ends = ends + kap[nyl - 1] * r
    over = tau[nyl - 1] * r
    for j in range(npy):
        isnd[j, 0:kown, :] = ends[j * kown:(j + 1) * kown]
        isnd[j, kown:2 * kown, :] = over[j * kown:(j + 1) * kown]

    spread(npy, at_y, lambda r: isnd.at[at_y(r)[1]], ircv.at[me_y], i_send.at[0], i_recv.at[0])
    ircv[me_y] = isnd[me_y]
    settle(ircv.at[others_y], i_send.at[0], i_recv.at[0])

    rho = []
    for b in range(npy):
        value = ircv[b, 0:kown, :]
        if b > 0:
            value = value + ircv[b - 1, kown:2 * kown, :]
        rho.append(value)
    depth_mode = lax.broadcasted_iota(jnp.int32, (kown, nx), 0) + me_x * kzl + me_y * kown
    row_mode = lax.broadcasted_iota(jnp.int32, (kown, nx), 1)
    mean = sum(rho[1:], rho[0]) * (1.0 / (npy * nyl))
    mean = jnp.where((depth_mode == 0) & (row_mode == 0), mean, 0.0)
    half_sum = (nyl - 1) / 2.0
    for b in range(npy):
        weight = 1.0 + (0.0 if b == 0 else half_sum) + (2.0 * half_sum if b == npy - 1 else half_sum)
        rho[b] = rho[b] - weight * mean
    for b in range(npy - 1):
        rho[b + 1] = rho[b + 1] + owner_phi[b] * rho[b]
    value = -owner_inv[npy - 1] * rho[npy - 1]
    jsnd[npy - 1, 0:kown, :] = value
    jsnd[npy - 1, kown:2 * kown, :] = jnp.zeros_like(value)
    for b in range(npy - 2, -1, -1):
        jsnd[b, kown:2 * kown, :] = value
        value = owner_phi[b] * value - owner_inv[b] * rho[b]
        jsnd[b, 0:kown, :] = value

    level[0] = mean[0:1, 0:HALF]
    has_mean = (me_x == 0) & first_y

    def tell(r):
        return remote(level.at[0], level.at[1], l_send.at[r], l_recv.at[0], at_y(r))

    @pl.when(has_mean)
    def _():
        run(1, npy, lambda r: tell(r).start())

    spread(npy, at_y, lambda r: jsnd.at[at_y(r)[1]], jrcv.at[me_y], i_send.at[1], i_recv.at[1])
    jrcv[me_y] = jsnd[me_y]
    settle(replies.at[others_y], r_send.at[2], r_recv.at[2])
    lines = replies.reshape(npy * 2 * npx, SEG)
    for p in range(npx):
        for r in range(2):
            fetch[p, r * npy:(r + 1) * npy, :] = lines[pl.ds(r * npx + p, npy, stride=2 * npx), :]
    spread(npx, at_x, lambda r: fetch.at[at_x(r)[0]], fetched.at[me_x], r_send.at[3], r_recv.at[3])
    fetched[me_x] = fetch[me_x]

    settle(jrcv.at[others_y], i_send.at[1], i_recv.at[1])

    @pl.when(has_mean)
    def _():
        run(1, npy, lambda r: tell(r).wait_send())
        level[1] = level[0]

    @pl.when((me_x == 0) & (me_y > 0))
    def _():
        pltpu.make_async_copy(level.at[1], level.at[1], l_recv.at[0]).wait()

    @pl.when(me_x > 0)
    def _():
        level[1] = jnp.zeros((1, HALF), F32)

    for j in range(npy):
        for part in range(2):
            back[part, j * kown:(j + 1) * kown, :] = jrcv[j, part * kown:(part + 1) * kown, :]
    first_value = back[0]
    corner = (lax.broadcasted_iota(jnp.int32, (kzl, nx), 0) == 0) & (
        lax.broadcasted_iota(jnp.int32, (kzl, nx), 1) == 0
    )
    mean_rows = jnp.where(corner, jnp.broadcast_to(level[1, :, 0:1], (kzl, nx)), 0.0)

    def up_piece(n, q):
        c = pieces - 1 - n

        def up_again(m, q):
            i = c * per + per - 1 - m
            share = 0.5 * (i + 1).astype(F32)
            q = tau[i] * (q - cols[row_of(i), :] + mean_rows * share) + kap[i] * first_value
            cols[row_of(i), :] = q
            return q

        q = lax.fori_loop(0, per, up_again, q)
        rows = piece_rows(c)
        cols[rows, :] = dot_parts(split(cols[rows, :], 3), (tx[0], tx[1], tx[2]), ((1,), (0,)))

        def scatter(sg, inner):
            for half in range(per // 4):
                parts = []
                for b in range(4):
                    y = c * per + 4 * half + b
                    parts.append(cols[row_of(y), pl.ds(pl.multiple_of(sg * HALF, HALF), HALF)])
                out = swap_groups(parts)
                for a in range(4):
                    msg[4 * sg + a, c, :, half * HALF:(half + 1) * HALF] = out[a]
            return inner

        lax.fori_loop(0, wides, scatter, 0)
        n = pieces + c
        spread(npx, at_x, lambda r: msg.at[at_x(r)[0], c], got2.at[me_x, c], a_send.at[n], a_recv.at[n])
        return q

    lax.fori_loop(0, pieces, up_piece, back[1])

    shape = (places, cells)
    cell = lax.broadcasted_iota(jnp.int32, shape, 1) * halves
    for h in range(halves):
        hot[h] = (jnp.broadcast_to(pick[...], shape) == cell + h).astype(F32).astype(BF16)

    def lower(x, carry):
        drop = DT * jnp.where(lane == HALF - 1, pressures(idb[x]), 0.0)
        w2[halves - 1, x] = w2[halves - 1, x] - drop
        return carry

    lax.fori_loop(0, nxl, lower, 0)

    pressure = qp.reshape(halves, (nxl + 2) * wide, HALF)

    def rise_piece(n, carry):
        c = pieces - 1 - n
        got2[me_x, c] = msg[me_x, c]
        settle(got2.at[others_x, c], a_send.at[pieces + c], a_recv.at[pieces + c])
        value = got2[:, c].reshape(nz, 256)
        out = dot_parts(split(value.T, 3), (tz[0], tz[1], tz[2]), ((1,), (0,)))
        for y in range(per):
            for h in range(halves):
                pressure[h, pl.ds(wide + 8 + c * per + y, nxl, stride=wide), :] = out[
                    y * nxl:(y + 1) * nxl, h * HALF:(h + 1) * HALF
                ]
        return carry

    lax.fori_loop(0, pieces, rise_piece, 0)

    for h in range(halves):
        qy_snd[0, h] = row_at(qp, (h,), top - 1)[...]
        qy_snd[1, h] = row_at(qp, (h,), 8)[...]
    halo = y_pair(qy_snd, qy_rcv, 4) + x_pair(qp, lambda field, x: field.at[:, x, pl.ds(8, nyl), :], 6)
    for copy in halo:
        copy.start()

    def q_rows(x, y, size):
        return jnp.concatenate([qp[h, x, pl.ds(y, size), :] for h in range(halves)], axis=1)

    def join(field, x):
        return jnp.concatenate([field[h, x, 0:nyl, :] for h in range(halves)], axis=1)

    def flow(a, x):
        return jnp.concatenate([up[a, h, x + 1, 8:top, :] for h in range(halves)], axis=1)

    def two_parts(x, carry):
        center = q_rows(x + 1, 8, nyl)
        spot = lax.broadcasted_iota(jnp.int32, center.shape, 1)
        below = jnp.where(spot == 0, center, pltpu.roll(center, 1, 1))
        above = jnp.where(spot == nz - 1, center, pltpu.roll(center, nz - 1, 1))
        v2 = join(w2, x) - 0.5 * (above - below)
        v0 = join(w0, x + 1) - 0.5 * (q_rows(x + 2, 8, nyl) - q_rows(x, 8, nyl))
        vel[0, x] = v0
        vel[2, x] = v2
        total = flow(0, x) * v0 + flow(2, x) * v2
        for h in range(halves):
            sig[h, pl.ds(pl.multiple_of(x * nyl, 8), nyl), :] = total[:, h * HALF:(h + 1) * HALF]
        return carry

    lax.fori_loop(1, nxl - 1, two_parts, 0)
    outs = [pltpu.make_async_copy(vel.at[b], v_out.at[b], out_sem.at[b]) for b in range(3)]

    for copy in halo:
        copy.wait()
    for h in range(halves):
        row_at(qp, (h,), 7)[...] = jnp.where(first_y, qy_snd[1, h], qy_rcv[0, h])
        row_at(qp, (h,), top)[...] = jnp.where(last_y, qy_snd[0, h], qy_rcv[1, h])

    @pl.when(first_x)
    def _():
        for h in range(halves):
            qp[h, 0, 8:top, :] = qp[h, 1, 8:top, :]

    @pl.when(last_x)
    def _():
        for h in range(halves):
            qp[h, nxl + 1, 8:top, :] = qp[h, nxl, 8:top, :]

    two_parts(0, 0)
    two_parts(nxl - 1, 0)
    outs[0].start()
    outs[2].start()

    def last_part(x, carry):
        deep = jnp.concatenate([w1[h, x + 1, 8:top, :] for h in range(halves)], axis=1)
        v1 = deep - 0.5 * (q_rows(x + 1, 9 + zero_at, nyl) - q_rows(x + 1, 7 + zero_at, nyl))
        vel[1, x] = v1
        rows = pl.ds(pl.multiple_of(x * nyl, 8), nyl)
        part = flow(1, x) * v1
        for h in range(halves):
            sig[h, rows, :] = -ALPHA * (sig[h, rows, :] + part[:, h * HALF:(h + 1) * HALF])
        return carry

    lax.fori_loop(0, nxl, last_part, 0)
    outs[1].start()

    picked = None
    for h in range(halves):
        both = jnp.dot(hot[h], jnp.concatenate(split(sig[h], 2), axis=1), preferred_element_type=F32)
        term = both[:, :SEG] + both[:, SEG:]
        picked = term if picked is None else picked + term
    settle(fetched.at[others_x], r_send.at[3], r_recv.at[3])
    products = picked * fetched[...].reshape(places, SEG)
    totals = jnp.broadcast_to(jnp.sum(products, axis=1, keepdims=True), (places, HALF)).T[0:8]
    by_px(totals, give, 1)
    spread(npx, at_x, lambda r: give.at[at_x(r)[0]], given.at[me_x], r_send.at[4], r_recv.at[4])
    given[me_x] = give[me_x]
    settle(given.at[others_x], r_send.at[4], r_recv.at[4])
    for p in range(npx):
        stack[p:p + 1, :] = given[p]
    by_py(stack[0:npx, :], gives)
    spread(npy, at_y, lambda r: gives.at[at_y(r)[1]], taken.at[me_y], r_send.at[5], r_recv.at[5])
    taken[me_y] = gives[me_y]
    settle(taken.at[others_y], r_send.at[5], r_recv.at[5])

    values = from_py(taken)
    total = jnp.zeros((npx, HALF), F32)
    for n in range(2 * npy):
        hit = jnp.broadcast_to(labels[:, n:n + 1], (npx, HALF)) == slot_lane
        total = total + jnp.where(hit, jnp.broadcast_to(values[:, n:n + 1], (npx, HALF)), 0.0)
    grad_out[...] = jnp.sum(total, axis=0, keepdims=True)[:, :controls]
    for copy in outs:
        copy.wait()


def main_call(dims, args, owner_rows):
    npx, npy, nxl, nyl, nz = dims
    nx = npx * nxl
    kzl = nz // npx
    kown = kzl // npy
    halves = nz // HALF
    wide = nyl + 16
    cells = nxl * nyl
    pieces = cells // 256
    places = 2 * npx * npy
    vmem = pltpu.VMEM
    anywhere = pl.BlockSpec(memory_space=pl.ANY)
    here = pl.BlockSpec(memory_space=pltpu.VMEM)
    far = pl.BlockSpec(memory_space=pltpu.HBM)
    dma = pltpu.SemaphoreType.DMA
    tables = args[10:13]
    field = vmem((3, halves, nxl + 2, wide, HALF), F32)
    line = vmem((nyl, kzl, nx), F32)
    message = vmem((npx, pieces, kzl, 256), F32)
    scratch = [
        field,
        field,
        vmem((3, cells, nz), BF16),
        vmem((3, cells, nz), BF16),
        vmem((nxl, nyl, nz), jnp.int32),
        vmem((nxl, nyl, HALF), jnp.int32),
        vmem((halves, nxl + 2, nyl, HALF), F32),
        vmem((halves, nxl + 2, wide, HALF), F32),
        vmem((halves, nxl, nyl, HALF), F32),
        vmem((2, 6, halves, nxl, HALF), BF16),
        vmem((2, 6, halves, nxl, HALF), BF16),
        vmem((2, halves, nxl, HALF), F32),
        vmem((2, halves, nxl, HALF), F32),
        vmem((2, OUTLETS, HALF), F32),
        vmem((npx, OUTLETS, HALF), F32),
        vmem((npy, OUTLETS, HALF), F32),
        vmem((halves, cells, HALF), F32),
        message,
        message,
        message,
        vmem((nyl * kzl, nx), F32),
        line,
        line,
        vmem((npy, kown, nx), F32),
        vmem((npy, kown, nx), F32),
        vmem((npy, 2 * kown, nx), F32),
        vmem((npy, 2 * kown, nx), F32),
        vmem((npy, 2 * kown, nx), F32),
        vmem((npy, 2 * kown, nx), F32),
        vmem((2, kzl, nx), F32),
        vmem((halves, nxl + 2, wide, HALF), F32),
        vmem((2, halves, nxl, HALF), F32),
        vmem((2, halves, nxl, HALF), F32),
        vmem((3, nxl, nyl, nz), F32),
        vmem((halves, cells, HALF), F32),
        vmem((nyl, nx), F32),
        vmem((halves, places, cells), BF16),
        vmem((places, 1), jnp.int32),
        vmem((npx, 8 + nyl, HALF), F32),
        vmem((npx, 8 + nyl, HALF), F32),
        vmem((npy, 2, HALF), F32),
        vmem((npy, 2, HALF), F32),
        vmem((places, HALF), BF16),
        vmem((npy, 2 * npx, SEG), F32),
        vmem((npy, 2 * npx, SEG), F32),
        vmem((npx, 2 * npy, SEG), F32),
        vmem((npx, 2 * npy, SEG), F32),
        vmem((npx, 1, HALF), F32),
        vmem((npx, 1, HALF), F32),
        vmem((npy, 2, HALF), F32),
        vmem((npy, 2, HALF), F32),
        vmem((2 * npy, HALF), F32),
        vmem((2, 1, HALF), F32),
    ]
    scratch += [vmem(t.shape, BF16) for t in tables]
    scratch += [
        pltpu.SMEM(a.shape, a.dtype) if n == 5 else vmem(a.shape, a.dtype)
        for n, a in enumerate(args)
        if n > 3 and not 10 <= n < 13
    ]
    scratch += [
        dma((3 * halves + 14,)),
        dma((8,)),
        dma((8,)),
        dma((6,)),
        dma((6,)),
        dma((2,)),
        dma((2,)),
        dma((2 * pieces,)),
        dma((2 * pieces,)),
        dma((2,)),
        dma((2,)),
        dma((npy,)),
        dma((1,)),
        dma((6,)),
        dma((6,)),
        dma((3,)),
    ]
    return pl.pallas_call(
        functools.partial(main_kernel, dims),
        out_shape=(
            jax.ShapeDtypeStruct((3, nxl, nyl, nz), F32),
            jax.ShapeDtypeStruct((1, owner_rows), F32),
        ),
        in_specs=[far] * len(args),
        out_specs=(anywhere, here),
        scratch_shapes=scratch,
        compiler_params=pltpu.CompilerParams(
            collective_id=0, has_side_effects=True, vmem_limit_bytes=58 * 2**20
        ),
        name="project",
    )(*args)


def local(
    base_flow, adjoint_start, source, solid_mask, outlet_ids, resist,
    tile_owner, tile_slot, tile_column, control_basis,
):
    _, nxl, nyl, nz = adjoint_start.shape
    npx, npy = lax.axis_size("px"), lax.axis_size("py")
    nx = npx * nxl
    tz, tx = table_np(nz), table_np(nx)
    tables = [split_np(tz, 3), split_np(tx, 3), split_np(np.ascontiguousarray(tx.T), 2)]
    tables = [jnp.asarray(np.stack(t)) for t in tables]
    lam_x = jnp.asarray(-eigen_np(nx)[None, :])
    depth = np.zeros((nz, HALF), np.float32)
    depth[:, 0] = -eigen_np(nz)
    depth[:, 1] = -0.5 * DT * tz[:, nz - 2]
    depth = jnp.asarray(depth)
    args = (
        adjoint_start,
        base_flow.reshape(3, nxl * nyl, nz),
        source.reshape(3, nxl * nyl, nz),
        solid_mask,
        outlet_ids.T,
        resist,
        tile_owner.reshape(1, -1),
        tile_slot.reshape(1, -1),
        tile_column.reshape(1, -1),
        control_basis,
        *tables,
        lam_x,
        depth,
    )
    velocity, grad = main_call((npx, npy, nxl, nyl, nz), args, control_basis.shape[0])
    return velocity, grad.reshape(-1)


def solution(mesh):
    in_specs = (
        P(None, "px", "py", None),
        P(None, "px", "py", None),
        P(None, "px", "py", None),
        P("px", "py", None),
        P("px", "py"),
        P(),
        P(("px", "py"), None),
        P(("px", "py")),
        P(("px", "py")),
        P(("px", "py"), None),
    )
    out_specs = (P(None, "px", "py", None), P(("px", "py")))
    return jax.shard_map(local, mesh=mesh, in_specs=in_specs, out_specs=out_specs, check_vma=False)
```

```python
import functools
import math

import jax
import jax.numpy as jnp
import numpy as np
from jax import lax
from jax.experimental import pallas as pl
from jax.experimental.pallas import tpu as pltpu
from jax.sharding import PartitionSpec as P

SEG = 128
OUTLETS = 8
DT = 0.1
NU = 0.5
ALPHA = 5.0
HALF = 128
MESH = pl.DeviceIdType.MESH
F32 = jnp.float32
BF16 = jnp.bfloat16


def table_np(count):
    order = np.arange(count).astype(np.float32)
    modes = order[:, None]
    points = order[None, :]
    weights = np.where(modes == 0.0, math.sqrt(1.0 / count), math.sqrt(2.0 / count)).astype(np.float32)
    angle = np.float32(np.pi) * (points + np.float32(0.5)) * modes / np.float32(count)
    return (weights * np.cos(angle.astype(np.float32))).astype(np.float32)


def eigen_np(count):
    order = np.arange(count).astype(np.float32)
    angle = (np.float32(np.pi) * order / np.float32(count)).astype(np.float32)
    return (np.float32(2.0) * np.cos(angle) - np.float32(2.0)).astype(np.float32)


def split_np(table, count):
    parts = []
    for _ in range(count):
        parts.append(table.astype(jnp.bfloat16))
        table = table - parts[-1].astype(np.float32)
    return tuple(parts)


def split(value, count):
    parts = []
    for _ in range(count):
        parts.append(value.astype(BF16))
        value = value - parts[-1].astype(F32)
    return tuple(parts)


def dot_parts(a_parts, b_parts, contract):
    dims = ((contract[0], contract[1]), ((), ()))
    count, rows = len(a_parts), a_parts[0].shape[0]
    terms = {}
    for j in range(count):
        stacked = jnp.concatenate(a_parts[:count - j], axis=0) if j < count - 1 else a_parts[0]
        out = lax.dot_general(stacked, b_parts[j], dimension_numbers=dims, preferred_element_type=F32)
        for i in range(count - j):
            terms[i, j] = out[i * rows:(i + 1) * rows]
    total = None
    for i, j in sorted(terms, key=lambda at: -(at[0] + at[1])):
        total = terms[i, j] if total is None else total + terms[i, j]
    return total


def swap_groups(tiles):
    lane = lax.broadcasted_iota(jnp.int32, tiles[0].shape, 1)
    odd = (lane // 32) % 2 == 1
    far = lane >= 64
    t0, t1, t2, t3 = tiles
    a0 = jnp.where(odd, pltpu.roll(t1, 32, 1), t0)
    a1 = jnp.where(odd, t1, pltpu.roll(t0, 96, 1))
    a2 = jnp.where(odd, pltpu.roll(t3, 32, 1), t2)
    a3 = jnp.where(odd, t3, pltpu.roll(t2, 96, 1))
    return (
        jnp.where(far, pltpu.roll(a2, 64, 1), a0),
        jnp.where(far, pltpu.roll(a3, 64, 1), a1),
        jnp.where(far, a2, pltpu.roll(a0, 64, 1)),
        jnp.where(far, a3, pltpu.roll(a1, 64, 1)),
    )


def z_shift(field, edge_low, edge_high):
    depth = field.shape[1]
    lane = lax.broadcasted_iota(jnp.int32, field.shape, 1)
    below = jnp.where(lane == 0, edge_low, pltpu.roll(field, 1, 1))
    above = jnp.where(lane == depth - 1, edge_high, pltpu.roll(field, depth - 1, 1))
    return below, above


def main_kernel(
    dims,
    v_hbm, u_hbm, s_hbm, m_hbm, ids_hbm, resist_hbm, owner_hbm, slot_hbm, column_hbm, basis_hbm,
    tz_hbm, tx_hbm, tt_hbm, lam_x_hbm, lam_z_hbm,
    v_out, grad_out,
    vp, up, ub, sb, mk, idb, w0, w1, w2, snd_y, rcv_y, wy_snd, wy_rcv, fsum, fr1, fr2,
    div, msg, got, got2, cols, tau, kap, owner_inv, owner_phi,
    isnd, ircv, jsnd, jrcv, back, qp, qy_snd, qy_rcv, vel, sig,
    outlet, hot, pick, ask, asked, asks, wanted, chosen, reply, replies, fetch, fetched, give, given, gives, taken, stack, level,
    tz, tx, tt, ids, resist, owner_row, slot_row, column_row, basis, lam_x, lam_z,
    load_sem, x_send, x_recv, y_send, y_recv, f_send, f_recv, a_send, a_recv, i_send, i_recv, l_send, l_recv, r_send, r_recv, out_sem,
):
    npx, npy, nxl, nyl, nz = dims
    nx = npx * nxl
    kzl = nz // npx
    kown = kzl // npy
    halves = nz // HALF
    cells = nxl * nyl
    per = 256 // nxl
    pieces = nyl // per
    group = 2 * npy
    places = npx * group
    me_x = lax.axis_index("px")
    me_y = lax.axis_index("py")
    right_x, left_x = lax.rem(me_x + 1, npx), lax.rem(me_x + npx - 1, npx)
    right_y, left_y = lax.rem(me_y + 1, npy), lax.rem(me_y + npy - 1, npy)
    first_x, last_x = me_x == 0, me_x == npx - 1
    first_y, last_y = me_y == 0, me_y == npy - 1
    top = 8 + nyl
    wide = nyl + 16
    zero_at = jnp.minimum(me_x, 0)

    def run(first, last, action):
        def body(r, carry):
            action(r)
            return carry

        lax.fori_loop(first, last, body, 0)

    def remote(src, dst, send, recv, target):
        return pltpu.make_async_remote_copy(
            src_ref=src, dst_ref=dst, send_sem=send, recv_sem=recv, device_id=target, device_id_type=MESH
        )

    def at_x(r):
        return (lax.rem(me_x + r, npx), me_y)

    def at_y(r):
        return (me_x, lax.rem(me_y + r, npy))

    def by_twos(first, last, body):
        def step(i, carry):
            body(first + 2 * i, 0)
            body(first + 2 * i + 1, 0)
            return carry

        lax.fori_loop(0, (last - first) // 2, step, 0)

    def spread(count, target, src, dst, send, recv):
        def start(n):
            r = (n + (count // 2 - 2)) % (count - 1) + 1
            remote(src(r), dst, send, recv, target(r)).start()

        for n in range(1, count):
            start(n)

    def settle(like, send, recv):
        pltpu.make_async_copy(like, like, send).wait()
        pltpu.make_async_copy(like, like, recv).wait()

    others_x, others_y = pl.ds(0, npx - 1), pl.ds(0, npy - 1)

    loads = []
    for c in range(3):
        for h in range(halves):
            loads.append(
                pltpu.make_async_copy(
                    v_hbm.at[c, :, :, pl.ds(h * HALF, HALF)],
                    vp.at[c, h, pl.ds(1, nxl), pl.ds(8, nyl), :],
                    load_sem.at[c * halves + h],
                )
            )
    base = 3 * halves
    load_u = pltpu.make_async_copy(u_hbm, ub, load_sem.at[base])
    load_s = pltpu.make_async_copy(s_hbm, sb, load_sem.at[base + 1])
    load_m = pltpu.make_async_copy(m_hbm, mk, load_sem.at[base + 2])
    load_t = [
        pltpu.make_async_copy(a, b, load_sem.at[base + 3 + n])
        for n, (a, b) in enumerate(((tz_hbm, tz), (tx_hbm, tx), (tt_hbm, tt)))
    ]
    load_small = [
        pltpu.make_async_copy(a, b, load_sem.at[base + 6 + n])
        for n, (a, b) in enumerate(
            (
                (ids_hbm, ids), (resist_hbm, resist), (owner_hbm, owner_row), (slot_hbm, slot_row),
                (column_hbm, column_row), (basis_hbm, basis), (lam_x_hbm, lam_x), (lam_z_hbm, lam_z),
            )
        )
    ]
    for copy in load_small:
        copy.start()
    for copy in loads:
        copy.start()
    load_u.start()
    load_s.start()
    load_m.start()
    for copy in load_t:
        copy.start()

    barrier = pltpu.get_barrier_semaphore()
    for r in range(1, npx):
        pl.semaphore_signal(barrier, inc=1, device_id=at_x(r), device_id_type=MESH)
    for r in range(1, npy):
        pl.semaphore_signal(barrier, inc=1, device_id=at_y(r), device_id_type=MESH)

    def row_at(ref, lead, y):
        lines = ref.reshape(*ref.shape[:-3], (nxl + 2) * wide, HALF)
        return lines.at[(*lead, pl.ds(wide + y, nxl, stride=wide), slice(None))]

    def x_pair(field, at, number):
        return (
            remote(at(field, nxl), at(field, 0), x_send.at[number], x_recv.at[number], (right_x, me_y)),
            remote(at(field, 1), at(field, nxl + 1), x_send.at[number + 1], x_recv.at[number + 1], (left_x, me_y)),
        )

    def at_plane(field, x):
        return field.at[:, :, x, pl.ds(8, nyl), :]

    def y_pair(send, recv, number):
        return (
            remote(send.at[0], recv.at[0], y_send.at[number], y_recv.at[number], (me_x, right_y)),
            remote(send.at[1], recv.at[1], y_send.at[number + 1], y_recv.at[number + 1], (me_x, left_y)),
        )

    for copy in loads:
        copy.wait()

    def pack(field, first):
        for c in range(3):
            for h in range(halves):
                snd_y[0, first + c, h] = row_at(field, (c, h), top - 1)[...].astype(BF16)
                snd_y[1, first + c, h] = row_at(field, (c, h), 8)[...].astype(BF16)

    pack(vp, 0)
    load_u.wait()

    def widen(i, carry):
        for a in range(3):
            pair = ub[a, pl.ds(pl.multiple_of(i * 2 * nyl, 2 * nyl), 2 * nyl), :].astype(F32)
            for s in range(2):
                for h in range(halves):
                    up[a, h, 1 + 2 * i + s, 8:top, :] = pair[s * nyl:(s + 1) * nyl, h * HALF:(h + 1) * HALF]
        return carry

    lax.fori_loop(0, nxl // 2, widen, 0)
    pack(up, 3)
    pl.semaphore_wait(barrier, npx - 1 + npy - 1)
    halo = y_pair(snd_y, rcv_y, 0) + x_pair(vp, at_plane, 0) + x_pair(up, at_plane, 2)
    for copy in halo:
        copy.start()
    for copy in load_small:
        copy.wait()

    count = owner_row.shape[1]
    owners = owner_row[...]
    same = jnp.broadcast_to(owners, (8, count)).T[:, 0:1] == owners
    earlier = lax.broadcasted_iota(jnp.int32, (count, count), 0) < lax.broadcasted_iota(
        jnp.int32, (count, count), 1
    )
    rank = jnp.sum(jnp.where(same & earlier, 1, 0), axis=0, keepdims=True)
    owner_x = owners // npy
    place = owner_x * group + rank * npy + (owners - owner_x * npy)
    match = lax.broadcasted_iota(jnp.int32, (places, count), 0) == place
    pick[...] = jnp.sum(jnp.where(match, column_row[...] + 1, 0), axis=1, keepdims=True) - 1
    slots = jnp.broadcast_to((slot_row[...] + 1).astype(F32), (8, count)).astype(BF16)
    requests = (
        lax.dot_general(
            slots, match.astype(F32).astype(BF16), (((1,), (1,)), ((), ())), preferred_element_type=F32
        )
        - 1.0
    )

    def pad_lanes(row):
        if row.shape[1] >= HALF:
            return row
        return jnp.concatenate([row, jnp.zeros((8, HALF - row.shape[1]), F32)], axis=1)

    def by_px(row, ref, rows=8):
        row = pad_lanes(row)
        lanes = row.shape[1]
        for p in range(npx):
            ref[p, 0:rows, :] = pltpu.roll(row, (lanes - group * p) % lanes, 1)[0:rows, :HALF]

    def by_py(rows, ref):
        full = jnp.concatenate([rows, jnp.zeros((HALF - npx, HALF), F32)], axis=0).T
        for j in range(npy):
            for r in range(2):
                ref[j, r:r + 1, :] = full[r * npy + j:r * npy + j + 1]

    def from_py(ref):
        for j in range(npy):
            stack[2 * j:2 * j + 2, :] = ref[j]
        return stack[...].T[0:npx]

    by_px(requests, ask)
    seen = ids[...]
    padded = jnp.concatenate([seen.astype(F32), jnp.zeros((nyl, HALF - nxl), F32)], axis=1)
    for p in range(npx):
        ask[p, 8:top, :] = padded
    for x in range(nxl):
        idb[x] = jnp.broadcast_to(seen[:, x:x + 1], (nyl, HALF))

    def ask_start():
        spread(npx, at_x, lambda r: ask.at[at_x(r)[0]], asked.at[me_x], r_send.at[0], r_recv.at[0])
        asked[me_x] = ask[me_x]

    ask_start()

    def reduce_cell(c, g, right):
        inv = 1.0 / (c + right + g)
        return inv, c * inv

    mine = lam_z[pl.ds(pl.multiple_of(me_x * kzl, kzl), kzl), 0:1]
    mu = lam_x[...] + mine
    owned = lam_z[pl.ds(me_x * kzl + me_y * kown, kown), 0:1]
    muo = lam_x[...] + owned

    def owner_table():
        def owner_cell(i, carry):
            c, g, ground = carry
            inv, k = reduce_cell(c, g, 1.0)
            return k, muo + g * inv, ground + k * g

        one = jnp.ones_like(muo)
        c, g, ground = lax.fori_loop(1, nyl - 1, owner_cell, (one, muo, jnp.zeros_like(one)))
        inv, link = reduce_cell(c, g, 1.0)
        from_left = g * inv
        end_ground = muo + from_left + (ground + c * (g / (c + g)))
        ground = ground + link * g
        held = muo + ground
        for b in range(npy - 1):
            inv = 1.0 / (link + held)
            phi = link * inv
            owner_inv[b] = inv
            owner_phi[b] = phi
            nxt = end_ground if b == npy - 2 else muo + ground + from_left
            held = nxt + phi * held
        positive = held > 0.0
        owner_inv[npy - 1] = jnp.where(positive, 1.0 / jnp.where(positive, held, 1.0), 0.0)

    load_s.wait()
    load_m.wait()

    blank = jnp.zeros((nxl, HALF), F32)
    for c in range(3):
        for h in range(halves):
            for field in (vp, up):
                row_at(field, (c, h), 7)[...] = blank
                row_at(field, (c, h), top)[...] = blank

    def rows_at(field, c, x, start, size=8):
        return jnp.concatenate([field[c, h, x, pl.ds(start, size), :] for h in range(halves)], axis=1)

    tiles = nyl // 8

    def predict(i, planes):
        for k in range(tiles):
            if all((2 * k + s) // tiles not in planes for s in range(2)):
                continue
            rows = pl.ds(pl.multiple_of(i * 2 * nyl + 16 * k, 16), 16)
            forcing = [sb[b, rows, :].astype(F32) for b in range(3)]
            for s in range(2):
                n = 2 * k + s
                if n // tiles not in planes:
                    continue
                x = 2 * i + n // tiles
                y = 8 * (n % tiles)
                scale = 1.0 - (DT * ALPHA / (1.0 + DT * ALPHA)) * mk[x, y:y + 8, :].astype(F32)
                u = [rows_at(up, a, x + 1, y + 8) for a in range(3)]
                v = [rows_at(vp, a, x + 1, y + 8) for a in range(3)]
                low, high = y + 7 + zero_at, y + 9 + zero_at
                slopes = [None] * 3
                for a in range(3):
                    below, above = z_shift(u[a], 0.0, 0.0)
                    diffs = (
                        rows_at(up, a, x + 2, y + 8) - rows_at(up, a, x, y + 8),
                        rows_at(up, a, x + 1, high) - rows_at(up, a, x + 1, low),
                        above - below,
                    )
                    for b in range(3):
                        term = v[a] * diffs[b]
                        slopes[b] = term if slopes[b] is None else slopes[b] + term
                for b in range(3):
                    xm, xp = rows_at(vp, b, x, y + 8), rows_at(vp, b, x + 2, y + 8)
                    ym, yp = rows_at(vp, b, x + 1, low), rows_at(vp, b, x + 1, high)
                    zm, zp = z_shift(v[b], 0.0, 0.0)
                    convect = u[0] * (xp - xm) + u[1] * (yp - ym) + u[2] * (zp - zm)
                    lap = (xp + xm) + (yp + ym) + (zp + zm) - 6.0 * v[b]
                    change = 0.5 * (convect - slopes[b]) + NU * lap + forcing[b][8 * s:8 * s + 8]
                    w = (v[b] + DT * change) * scale
                    for h in range(halves):
                        part = w[:, h * HALF:(h + 1) * HALF]
                        if b == 0:
                            w0[h, x + 1, y:y + 8, :] = part
                        elif b == 1:
                            w1[h, x + 1, y + 8:y + 16, :] = part
                        else:
                            w2[h, x, y:y + 8, :] = part

    pairs = nxl // 2
    run(1, pairs // 2, lambda i: predict(i, (0, 1)))
    settle(asked.at[others_x], r_send.at[0], r_recv.at[0])
    by_py(asked[:, 0, :], asks)
    spread(npy, at_y, lambda r: asks.at[at_y(r)[1]], wanted.at[me_y], r_send.at[1], r_recv.at[1])
    wanted[me_y] = asks[me_y]
    run(pairs // 2, pairs - 1, lambda i: predict(i, (0, 1)))
    predict(0, (1,))
    predict(pairs - 1, (0,))
    for copy in halo:
        copy.wait()
    edge = jnp.zeros((nyl, HALF), F32)

    @pl.when(first_x)
    def _():
        for c in range(3):
            for h in range(halves):
                vp[c, h, 0, 8:top, :] = edge
                up[c, h, 0, 8:top, :] = edge

    @pl.when(last_x)
    def _():
        for c in range(3):
            for h in range(halves):
                vp[c, h, nxl + 1, 8:top, :] = edge
                up[c, h, nxl + 1, 8:top, :] = edge
    predict(0, (0,))
    predict(pairs - 1, (1,))

    flat0 = w0.reshape(halves, (nxl + 2) * nyl, HALF)
    flat2 = w2.reshape(halves, nxl * nyl, HALF)
    for side, y, inside in ((0, 0, first_y), (1, nyl - 1, last_y)):
        sign = -0.5 if side == 0 else 0.5
        for h in range(halves):
            solid = mk[:, y, h * HALF:(h + 1) * HALF].astype(F32)
            scale = jnp.where(inside, 0.0, DT - (DT * DT * ALPHA / (1.0 + DT * ALPHA)) * solid)
            beyond = [rcv_y[side, n, h].astype(F32) for n in range(6)]
            weigh = scale * (NU + sign * row_at(up, (1, h), y + 8)[...])
            slope = sum(row_at(vp, (a, h), y + 8)[...] * beyond[3 + a] for a in range(3))
            here = flat0.at[h, pl.ds(nyl + y, nxl, stride=nyl), :]
            here[...] = here[...] + weigh * beyond[0]
            here = row_at(w1, (h,), y + 8)
            here[...] = here[...] + (weigh * beyond[1] - (sign * scale) * slope)
            here = flat2.at[h, pl.ds(y, nxl, stride=nyl), :]
            here[...] = here[...] + weigh * beyond[2]

    for h in range(halves):
        wy_snd[0, h] = row_at(w1, (h,), top - 1)[...]
        wy_snd[1, h] = row_at(w1, (h,), 8)[...]
    halo = y_pair(wy_snd, wy_rcv, 2) + x_pair(w0, lambda field, x: field.at[:, x], 4)
    for copy in halo:
        copy.start()

    settle(wanted.at[others_y], r_send.at[1], r_recv.at[1])

    slot_lane = lax.broadcasted_iota(jnp.int32, (npx, HALF), 1).astype(F32)

    labels = from_py(wanted)
    for n in range(2 * npy):
        hit = jnp.broadcast_to(labels[:, n:n + 1], (npx, HALF)) == slot_lane
        chosen[n * npx:(n + 1) * npx, :] = hit.astype(F32).astype(BF16)
    controls = basis.shape[0]
    wide_basis = jnp.concatenate([basis[...], jnp.zeros((HALF - controls, SEG), F32)], axis=0)
    rows = sum(
        jnp.dot(chosen[...], part, preferred_element_type=F32) for part in reversed(split(wide_basis, 3))
    )
    for j in range(npy):
        reply[j] = rows[j * 2 * npx:(j + 1) * 2 * npx]

    lane = lax.broadcasted_iota(jnp.int32, (nyl, HALF), 1)

    def flux_plane(x, carry):
        face = jnp.where(lane == HALF - 1, w2[halves - 1, x], 0.0)
        which = idb[x]
        return tuple(total + jnp.where(which == k, face, 0.0) for k, total in enumerate(carry))

    zero = jnp.zeros((nyl, HALF), F32)
    totals = lax.fori_loop(0, nxl, flux_plane, (zero,) * OUTLETS)
    fsum[0] = jnp.concatenate([jnp.sum(t, axis=0, keepdims=True) for t in totals], axis=0)

    spread(npx, at_x, lambda r: fsum.at[0], fr1.at[me_x], f_send.at[0], f_recv.at[0])
    fr1[me_x] = fsum[0]

    for copy in halo:
        copy.wait()
    for h in range(halves):
        row_at(w1, (h,), 7)[...] = jnp.where(first_y, 0.0, wy_rcv[0, h])
        row_at(w1, (h,), top)[...] = jnp.where(last_y, 0.0, wy_rcv[1, h])

    @pl.when(first_x)
    def _():
        for h in range(halves):
            w0[h, 0] = edge

    @pl.when(last_x)
    def _():
        for h in range(halves):
            w0[h, nxl + 1] = edge

    def diverge(x, carry):
        deep = jnp.concatenate([w2[h, x] for h in range(halves)], axis=1)
        below, above = z_shift(deep, 0.0, 0.0)
        for h in range(halves):
            cut = slice(h * HALF, (h + 1) * HALF)
            rise = w1[h, x + 1, pl.ds(9 + zero_at, nyl), :] - w1[h, x + 1, pl.ds(7 + zero_at, nyl), :]
            total = (w0[h, x + 2] - w0[h, x]) + rise + (above - below)[:, cut]
            div[h, pl.ds(x, nyl, stride=nxl), :] = 0.5 * total
        return carry

    by_twos(0, nxl, diverge)

    for copy in load_t:
        copy.wait()

    def depth_piece(c, carry):
        here = pl.ds(pl.multiple_of(c * 256, 256), 256)
        value = jnp.concatenate([div[h, here, :] for h in range(halves)], axis=1)
        out = dot_parts((tz[0], tz[1]), split(value, 2), ((1,), (1,)))
        for p in range(npx):
            msg[p, c] = out[p * kzl:(p + 1) * kzl]
        spread(npx, at_x, lambda r: msg.at[at_x(r)[0], c], got.at[me_x, c], a_send.at[c], a_recv.at[c])

        @pl.when(c == 0)
        def _():
            settle(fr1.at[others_x], f_send.at[0], f_recv.at[0])
            fsum[1] = jnp.sum(fr1[...], axis=0)
            spread(npy, at_y, lambda r: fsum.at[1], fr2.at[me_y], f_send.at[1], f_recv.at[1])
            fr2[me_y] = fsum[1]

        return carry

    lax.fori_loop(0, pieces, depth_piece, 0)

    spread(npy, at_y, lambda r: reply.at[at_y(r)[1]], replies.at[me_y], r_send.at[2], r_recv.at[2])
    replies[me_y] = reply[me_y]
    owner_table()

    def table_cell(i, carry):
        c, g = carry
        right = jnp.where((i == nyl - 1) & last_y, 0.0, 1.0)
        inv, k = reduce_cell(c, g, right)
        tau[i] = inv
        kap[i] = k
        return k, mu + g * inv

    tau[0] = jnp.zeros_like(mu)
    kap[0] = jnp.ones_like(mu)
    lax.fori_loop(1, nyl, table_cell, (jnp.ones_like(mu), mu))

    settle(fr2.at[others_y], f_send.at[1], f_recv.at[1])
    flux = jnp.sum(fr2[...], axis=0) * (1.0 / (nx * npy * nyl))
    press = []
    for k in range(OUTLETS):
        total = resist[k, 0] * flux[0:1]
        for n in range(1, OUTLETS):
            total = total + resist[k, n] * flux[n:n + 1]
        press.append(total[:, HALF - 1:HALF])

    def pressures(which):
        drop = jnp.zeros(which.shape, F32)
        for k in range(OUTLETS):
            drop = jnp.where(which == k, jnp.broadcast_to(press[k], which.shape), drop)
        return drop

    quarter = lane // nxl
    for n in range(npx // 4):
        which = asked[4 * n, 8:top, :]
        for a in range(1, 4):
            which = jnp.where(quarter == a, pltpu.roll(asked[4 * n + a, 8:top, :], a * nxl, 1), which)
        outlet[:, n * HALF:(n + 1) * HALF] = pressures(which)
    weight = jnp.broadcast_to(lam_z[pl.ds(pl.multiple_of(me_x * kzl, kzl), kzl), 1:2], (kzl, nx))

    wides = npx // 4

    def row_of(i):
        return pl.ds(pl.multiple_of(i * kzl, kzl), kzl)

    def piece_rows(c):
        return pl.ds(pl.multiple_of(c * per * kzl, per * kzl), per * kzl)

    def line_piece(c, carry):
        got[me_x, c] = msg[me_x, c]
        settle(got.at[others_x, c], a_send.at[c], a_recv.at[c])

        def gather(sg, inner):
            for half in range(per // 4):
                out = swap_groups([got[4 * sg + a, c, :, half * HALF:(half + 1) * HALF] for a in range(4)])
                for b in range(4):
                    y = c * per + 4 * half + b
                    cols[row_of(y), pl.ds(pl.multiple_of(sg * HALF, HALF), HALF)] = out[b]
            return inner

        lax.fori_loop(0, wides, gather, 0)

        def add_outlet(m, inner):
            y = c * per + m
            line = jnp.broadcast_to(outlet[pl.ds(y, 1), :], (kzl, nx))
            cols[row_of(y), :] = cols[row_of(y), :] + weight * line
            return inner

        lax.fori_loop(0, per, add_outlet, 0)
        rows = piece_rows(c)
        cols[rows, :] = dot_parts(split(cols[rows, :], 2), (tt[0], tt[1]), ((1,), (0,)))
        return carry

    lax.fori_loop(0, pieces, line_piece, 0)

    def down(i, carry):
        r, ends = carry
        ends = ends + kap[i] * r
        nxt = cols[row_of(i + 1), :] + tau[i] * r
        cols[row_of(i + 1), :] = nxt
        return nxt, ends

    r, ends = lax.fori_loop(1, nyl - 1, down, (cols[row_of(1), :], cols[row_of(0), :]))
    ends = ends + kap[nyl - 1] * r
    over = tau[nyl - 1] * r
    for j in range(npy):
        isnd[j, 0:kown, :] = ends[j * kown:(j + 1) * kown]
        isnd[j, kown:2 * kown, :] = over[j * kown:(j + 1) * kown]

    spread(npy, at_y, lambda r: isnd.at[at_y(r)[1]], ircv.at[me_y], i_send.at[0], i_recv.at[0])
    ircv[me_y] = isnd[me_y]
    settle(ircv.at[others_y], i_send.at[0], i_recv.at[0])

    rho = []
    for b in range(npy):
        value = ircv[b, 0:kown, :]
        if b > 0:
            value = value + ircv[b - 1, kown:2 * kown, :]
        rho.append(value)
    depth_mode = lax.broadcasted_iota(jnp.int32, (kown, nx), 0) + me_x * kzl + me_y * kown
    row_mode = lax.broadcasted_iota(jnp.int32, (kown, nx), 1)
    mean = sum(rho[1:], rho[0]) * (1.0 / (npy * nyl))
    mean = jnp.where((depth_mode == 0) & (row_mode == 0), mean, 0.0)
    half_sum = (nyl - 1) / 2.0
    for b in range(npy):
        weight = 1.0 + (0.0 if b == 0 else half_sum) + (2.0 * half_sum if b == npy - 1 else half_sum)
        rho[b] = rho[b] - weight * mean
    for b in range(npy - 1):
        rho[b + 1] = rho[b + 1] + owner_phi[b] * rho[b]
    value = -owner_inv[npy - 1] * rho[npy - 1]
    jsnd[npy - 1, 0:kown, :] = value
    jsnd[npy - 1, kown:2 * kown, :] = jnp.zeros_like(value)
    for b in range(npy - 2, -1, -1):
        jsnd[b, kown:2 * kown, :] = value
        value = owner_phi[b] * value - owner_inv[b] * rho[b]
        jsnd[b, 0:kown, :] = value

    level[0] = mean[0:1, 0:HALF]
    has_mean = (me_x == 0) & first_y

    def tell(r):
        return remote(level.at[0], level.at[1], l_send.at[r], l_recv.at[0], at_y(r))

    @pl.when(has_mean)
    def _():
        run(1, npy, lambda r: tell(r).start())

    spread(npy, at_y, lambda r: jsnd.at[at_y(r)[1]], jrcv.at[me_y], i_send.at[1], i_recv.at[1])
    jrcv[me_y] = jsnd[me_y]
    settle(replies.at[others_y], r_send.at[2], r_recv.at[2])
    lines = replies.reshape(npy * 2 * npx, SEG)
    for p in range(npx):
        for r in range(2):
            fetch[p, r * npy:(r + 1) * npy, :] = lines[pl.ds(r * npx + p, npy, stride=2 * npx), :]
    spread(npx, at_x, lambda r: fetch.at[at_x(r)[0]], fetched.at[me_x], r_send.at[3], r_recv.at[3])
    fetched[me_x] = fetch[me_x]

    settle(jrcv.at[others_y], i_send.at[1], i_recv.at[1])

    @pl.when(has_mean)
    def _():
        run(1, npy, lambda r: tell(r).wait_send())
        level[1] = level[0]

    @pl.when((me_x == 0) & (me_y > 0))
    def _():
        pltpu.make_async_copy(level.at[1], level.at[1], l_recv.at[0]).wait()

    @pl.when(me_x > 0)
    def _():
        level[1] = jnp.zeros((1, HALF), F32)

    for j in range(npy):
        for part in range(2):
            back[part, j * kown:(j + 1) * kown, :] = jrcv[j, part * kown:(part + 1) * kown, :]
    first_value = back[0]
    corner = (lax.broadcasted_iota(jnp.int32, (kzl, nx), 0) == 0) & (
        lax.broadcasted_iota(jnp.int32, (kzl, nx), 1) == 0
    )
    mean_rows = jnp.where(corner, jnp.broadcast_to(level[1, :, 0:1], (kzl, nx)), 0.0)

    def up_piece(n, q):
        c = pieces - 1 - n

        def up_again(m, q):
            i = c * per + per - 1 - m
            share = 0.5 * (i + 1).astype(F32)
            q = tau[i] * (q - cols[row_of(i), :] + mean_rows * share) + kap[i] * first_value
            cols[row_of(i), :] = q
            return q

        q = lax.fori_loop(0, per, up_again, q)
        rows = piece_rows(c)
        cols[rows, :] = dot_parts(split(cols[rows, :], 3), (tx[0], tx[1], tx[2]), ((1,), (0,)))

        def scatter(sg, inner):
            for half in range(per // 4):
                parts = []
                for b in range(4):
                    y = c * per + 4 * half + b
                    parts.append(cols[row_of(y), pl.ds(pl.multiple_of(sg * HALF, HALF), HALF)])
                out = swap_groups(parts)
                for a in range(4):
                    msg[4 * sg + a, c, :, half * HALF:(half + 1) * HALF] = out[a]
            return inner

        lax.fori_loop(0, wides, scatter, 0)
        n = pieces + c
        spread(npx, at_x, lambda r: msg.at[at_x(r)[0], c], got2.at[me_x, c], a_send.at[n], a_recv.at[n])
        return q

    lax.fori_loop(0, pieces, up_piece, back[1])

    shape = (places, cells)
    cell = lax.broadcasted_iota(jnp.int32, shape, 1) * halves
    for h in range(halves):
        hot[h] = (jnp.broadcast_to(pick[...], shape) == cell + h).astype(F32).astype(BF16)

    def lower(x, carry):
        drop = DT * jnp.where(lane == HALF - 1, pressures(idb[x]), 0.0)
        w2[halves - 1, x] = w2[halves - 1, x] - drop
        return carry

    lax.fori_loop(0, nxl, lower, 0)

    pressure = qp.reshape(halves, (nxl + 2) * wide, HALF)

    def rise_piece(n, carry):
        c = pieces - 1 - n
        got2[me_x, c] = msg[me_x, c]
        settle(got2.at[others_x, c], a_send.at[pieces + c], a_recv.at[pieces + c])
        value = got2[:, c].reshape(nz, 256)
        out = dot_parts(split(value.T, 3), (tz[0], tz[1], tz[2]), ((1,), (0,)))
        for y in range(per):
            for h in range(halves):
                pressure[h, pl.ds(wide + 8 + c * per + y, nxl, stride=wide), :] = out[
                    y * nxl:(y + 1) * nxl, h * HALF:(h + 1) * HALF
                ]
        return carry

    lax.fori_loop(0, pieces, rise_piece, 0)

    for h in range(halves):
        qy_snd[0, h] = row_at(qp, (h,), top - 1)[...]
        qy_snd[1, h] = row_at(qp, (h,), 8)[...]
    halo = y_pair(qy_snd, qy_rcv, 4) + x_pair(qp, lambda field, x: field.at[:, x, pl.ds(8, nyl), :], 6)
    for copy in halo:
        copy.start()

    def q_rows(x, y, size):
        return jnp.concatenate([qp[h, x, pl.ds(y, size), :] for h in range(halves)], axis=1)

    def join(field, x):
        return jnp.concatenate([field[h, x, 0:nyl, :] for h in range(halves)], axis=1)

    def flow(a, x):
        return jnp.concatenate([up[a, h, x + 1, 8:top, :] for h in range(halves)], axis=1)

    def two_parts(x, carry):
        center = q_rows(x + 1, 8, nyl)
        spot = lax.broadcasted_iota(jnp.int32, center.shape, 1)
        below = jnp.where(spot == 0, center, pltpu.roll(center, 1, 1))
        above = jnp.where(spot == nz - 1, center, pltpu.roll(center, nz - 1, 1))
        v2 = join(w2, x) - 0.5 * (above - below)
        v0 = join(w0, x + 1) - 0.5 * (q_rows(x + 2, 8, nyl) - q_rows(x, 8, nyl))
        vel[0, x] = v0
        vel[2, x] = v2
        total = flow(0, x) * v0 + flow(2, x) * v2
        for h in range(halves):
            sig[h, pl.ds(pl.multiple_of(x * nyl, 8), nyl), :] = total[:, h * HALF:(h + 1) * HALF]
        return carry

    by_twos(1, nxl - 1, two_parts)
    outs = [pltpu.make_async_copy(vel.at[b], v_out.at[b], out_sem.at[b]) for b in range(3)]

    for copy in halo:
        copy.wait()
    for h in range(halves):
        row_at(qp, (h,), 7)[...] = jnp.where(first_y, qy_snd[1, h], qy_rcv[0, h])
        row_at(qp, (h,), top)[...] = jnp.where(last_y, qy_snd[0, h], qy_rcv[1, h])

    @pl.when(first_x)
    def _():
        for h in range(halves):
            qp[h, 0, 8:top, :] = qp[h, 1, 8:top, :]

    @pl.when(last_x)
    def _():
        for h in range(halves):
            qp[h, nxl + 1, 8:top, :] = qp[h, nxl, 8:top, :]

    two_parts(0, 0)
    two_parts(nxl - 1, 0)
    outs[0].start()
    outs[2].start()

    def last_part(x, carry):
        deep = jnp.concatenate([w1[h, x + 1, 8:top, :] for h in range(halves)], axis=1)
        v1 = deep - 0.5 * (q_rows(x + 1, 9 + zero_at, nyl) - q_rows(x + 1, 7 + zero_at, nyl))
        vel[1, x] = v1
        rows = pl.ds(pl.multiple_of(x * nyl, 8), nyl)
        part = flow(1, x) * v1
        for h in range(halves):
            sig[h, rows, :] = -ALPHA * (sig[h, rows, :] + part[:, h * HALF:(h + 1) * HALF])
        return carry

    by_twos(0, nxl, last_part)
    outs[1].start()

    picked = None
    for h in range(halves):
        both = jnp.dot(hot[h], jnp.concatenate(split(sig[h], 2), axis=1), preferred_element_type=F32)
        term = both[:, :SEG] + both[:, SEG:]
        picked = term if picked is None else picked + term
    settle(fetched.at[others_x], r_send.at[3], r_recv.at[3])
    products = picked * fetched[...].reshape(places, SEG)
    totals = jnp.broadcast_to(jnp.sum(products, axis=1, keepdims=True), (places, HALF)).T[0:8]
    by_px(totals, give, 1)
    spread(npx, at_x, lambda r: give.at[at_x(r)[0]], given.at[me_x], r_send.at[4], r_recv.at[4])
    given[me_x] = give[me_x]
    settle(given.at[others_x], r_send.at[4], r_recv.at[4])
    for p in range(npx):
        stack[p:p + 1, :] = given[p]
    by_py(stack[0:npx, :], gives)
    spread(npy, at_y, lambda r: gives.at[at_y(r)[1]], taken.at[me_y], r_send.at[5], r_recv.at[5])
    taken[me_y] = gives[me_y]
    settle(taken.at[others_y], r_send.at[5], r_recv.at[5])

    values = from_py(taken)
    total = jnp.zeros((npx, HALF), F32)
    for n in range(2 * npy):
        hit = jnp.broadcast_to(labels[:, n:n + 1], (npx, HALF)) == slot_lane
        total = total + jnp.where(hit, jnp.broadcast_to(values[:, n:n + 1], (npx, HALF)), 0.0)
    grad_out[...] = jnp.sum(total, axis=0, keepdims=True)[:, :controls]
    for copy in outs:
        copy.wait()


def main_call(dims, args, owner_rows):
    npx, npy, nxl, nyl, nz = dims
    nx = npx * nxl
    kzl = nz // npx
    kown = kzl // npy
    halves = nz // HALF
    wide = nyl + 16
    cells = nxl * nyl
    pieces = cells // 256
    places = 2 * npx * npy
    vmem = pltpu.VMEM
    anywhere = pl.BlockSpec(memory_space=pl.ANY)
    here = pl.BlockSpec(memory_space=pltpu.VMEM)
    far = pl.BlockSpec(memory_space=pltpu.HBM)
    dma = pltpu.SemaphoreType.DMA
    tables = args[10:13]
    field = vmem((3, halves, nxl + 2, wide, HALF), F32)
    line = vmem((nyl, kzl, nx), F32)
    message = vmem((npx, pieces, kzl, 256), F32)
    scratch = [
        field,
        field,
        vmem((3, cells, nz), BF16),
        vmem((3, cells, nz), BF16),
        vmem((nxl, nyl, nz), jnp.int32),
        vmem((nxl, nyl, HALF), jnp.int32),
        vmem((halves, nxl + 2, nyl, HALF), F32),
        vmem((halves, nxl + 2, wide, HALF), F32),
        vmem((halves, nxl, nyl, HALF), F32),
        vmem((2, 6, halves, nxl, HALF), BF16),
        vmem((2, 6, halves, nxl, HALF), BF16),
        vmem((2, halves, nxl, HALF), F32),
        vmem((2, halves, nxl, HALF), F32),
        vmem((2, OUTLETS, HALF), F32),
        vmem((npx, OUTLETS, HALF), F32),
        vmem((npy, OUTLETS, HALF), F32),
        vmem((halves, cells, HALF), F32),
        message,
        message,
        message,
        vmem((nyl * kzl, nx), F32),
        line,
        line,
        vmem((npy, kown, nx), F32),
        vmem((npy, kown, nx), F32),
        vmem((npy, 2 * kown, nx), F32),
        vmem((npy, 2 * kown, nx), F32),
        vmem((npy, 2 * kown, nx), F32),
        vmem((npy, 2 * kown, nx), F32),
        vmem((2, kzl, nx), F32),
        vmem((halves, nxl + 2, wide, HALF), F32),
        vmem((2, halves, nxl, HALF), F32),
        vmem((2, halves, nxl, HALF), F32),
        vmem((3, nxl, nyl, nz), F32),
        vmem((halves, cells, HALF), F32),
        vmem((nyl, nx), F32),
        vmem((halves, places, cells), BF16),
        vmem((places, 1), jnp.int32),
        vmem((npx, 8 + nyl, HALF), F32),
        vmem((npx, 8 + nyl, HALF), F32),
        vmem((npy, 2, HALF), F32),
        vmem((npy, 2, HALF), F32),
        vmem((places, HALF), BF16),
        vmem((npy, 2 * npx, SEG), F32),
        vmem((npy, 2 * npx, SEG), F32),
        vmem((npx, 2 * npy, SEG), F32),
        vmem((npx, 2 * npy, SEG), F32),
        vmem((npx, 1, HALF), F32),
        vmem((npx, 1, HALF), F32),
        vmem((npy, 2, HALF), F32),
        vmem((npy, 2, HALF), F32),
        vmem((2 * npy, HALF), F32),
        vmem((2, 1, HALF), F32),
    ]
    scratch += [vmem(t.shape, BF16) for t in tables]
    scratch += [
        pltpu.SMEM(a.shape, a.dtype) if n == 5 else vmem(a.shape, a.dtype)
        for n, a in enumerate(args)
        if n > 3 and not 10 <= n < 13
    ]
    scratch += [
        dma((3 * halves + 14,)),
        dma((8,)),
        dma((8,)),
        dma((6,)),
        dma((6,)),
        dma((2,)),
        dma((2,)),
        dma((2 * pieces,)),
        dma((2 * pieces,)),
        dma((2,)),
        dma((2,)),
        dma((npy,)),
        dma((1,)),
        dma((6,)),
        dma((6,)),
        dma((3,)),
    ]
    return pl.pallas_call(
        functools.partial(main_kernel, dims),
        out_shape=(
            jax.ShapeDtypeStruct((3, nxl, nyl, nz), F32),
            jax.ShapeDtypeStruct((1, owner_rows), F32),
        ),
        in_specs=[far] * len(args),
        out_specs=(anywhere, here),
        scratch_shapes=scratch,
        compiler_params=pltpu.CompilerParams(
            collective_id=0, has_side_effects=True, vmem_limit_bytes=58 * 2**20
        ),
        name="project",
    )(*args)


def local(
    base_flow, adjoint_start, source, solid_mask, outlet_ids, resist,
    tile_owner, tile_slot, tile_column, control_basis,
):
    _, nxl, nyl, nz = adjoint_start.shape
    npx, npy = lax.axis_size("px"), lax.axis_size("py")
    nx = npx * nxl
    tz, tx = table_np(nz), table_np(nx)
    tables = [split_np(tz, 3), split_np(tx, 3), split_np(np.ascontiguousarray(tx.T), 2)]
    tables = [jnp.asarray(np.stack(t)) for t in tables]
    lam_x = jnp.asarray(-eigen_np(nx)[None, :])
    depth = np.zeros((nz, HALF), np.float32)
    depth[:, 0] = -eigen_np(nz)
    depth[:, 1] = -0.5 * DT * tz[:, nz - 2]
    depth = jnp.asarray(depth)
    args = (
        adjoint_start,
        base_flow.reshape(3, nxl * nyl, nz),
        source.reshape(3, nxl * nyl, nz),
        solid_mask,
        outlet_ids.T,
        resist,
        tile_owner.reshape(1, -1),
        tile_slot.reshape(1, -1),
        tile_column.reshape(1, -1),
        control_basis,
        *tables,
        lam_x,
        depth,
    )
    velocity, grad = main_call((npx, npy, nxl, nyl, nz), args, control_basis.shape[0])
    return velocity, grad.reshape(-1)


def solution(mesh):
    in_specs = (
        P(None, "px", "py", None),
        P(None, "px", "py", None),
        P(None, "px", "py", None),
        P("px", "py", None),
        P("px", "py"),
        P(),
        P(("px", "py"), None),
        P(("px", "py")),
        P(("px", "py")),
        P(("px", "py"), None),
    )
    out_specs = (P(None, "px", "py", None), P(("px", "py")))
    return jax.shard_map(local, mesh=mesh, in_specs=in_specs, out_specs=out_specs, check_vma=False)
```
